32 devices in a mesh: ens: 2 (over y), wide: 4 (over z), lev: 2 (over x), fld: 2 (over core).
Axes of the slice: x: 2, y: 2, z: 4, core: 2. Of those that a mesh axis runs over, the one named last changes fastest.
Arguments:
- fourier_input_rows: bfloat16 [4, 1280, 4, 4, 256], P('ens', 'wide', None, 'fld', 'lev'), parts along dimension 0, may hold values from -6 to 6
- legendre: bfloat16 [4, 1280, 1280], P('wide', ('lev', 'fld')), may hold values from -0.15625 to 0.15625
- slot_wave: int32 [4], P('wide'), may hold values from 0 to 1279, as said below
- to_modes: bfloat16 [128, 128], replicated, may hold values from -0.5 to 0.5
- from_modes: bfloat16 [128, 128], replicated, may hold values from -0.5 to 0.5
- mode_rate: float32 [128], replicated, may hold values from 0.05 to 5
Outputs:
- fourier_out: bfloat16 [4, 1280, 4, 4, 256], P('ens', 'wide', None, 'fld', 'lev'), parts along dimension 0
- spectral: bfloat16 [8, 1280, 4, 256], P(('ens', 'wide'), None, 'fld', 'lev'), parts along dimension 0
The draws below stay inside these ranges and needn't reach their ends.
There are 2 independent parts, one for each index of `ens`. The reference program is written for one: setup_inputs(seed, part) draws one part's arguments, and reference() takes and returns one part's arrays. A program takes and returns all parts, laid end to end along the dimension named above; an argument that names none is the same for every part. Nothing has to cross between parts.
Inputs may be any that keep to these rules, and one draw needn't show every extreme that they name: `slot_wave`: the wavenumbers of the slots are distinct; one slot holds 0 and one holds 1279.
All inputs are finite; a program needn't handle non-finite values.
Results may differ from the reference program's by a relative error of at most 0.0065.
Values may be sent and summed in bfloat16 or wider, within the bound.
No kernel may reach another device: no remote copies, remote signals or barrier semaphores. Data moves between devices by JAX's collectives and lax.ppermute only.
A program may use at most 64 MiB of HBM per device.

```python
import math
import jax
import jax.numpy as jnp
from jax import lax

DEGREE_LIMIT = 1280
HALF_LATITUDES = 1280
FIELD_TOTAL = 4
SLOT_TOTAL = 4
LEVEL_TOTAL = 128


def draw_slot_wave(key, part):
    first_key, second_random_key = jax.random.split(key)
    inner_loop_body = (jax.random.permutation(first_key, DEGREE_LIMIT - 2) + 1).astype(jnp.int32)
    selected_option = jnp.concatenate((jnp.array([0, DEGREE_LIMIT - 1], dtype=jnp.int32), inner_loop_body[:SLOT_TOTAL - 2]))
    ordering_index = jax.random.permutation(second_random_key, SLOT_TOTAL)
    return selected_option[ordering_index].astype(jnp.int32)


def steps_of(stream_key, shape, cuts, smallest, largest):
    factor_of, own = 1.0, jax.random.fold_in(stream_key, 6)
    for dim, parts in cuts:
        draws = jnp.exp(jax.random.uniform(jax.random.fold_in(own, dim), (parts,), jnp.float32, smallest / len(cuts), largest / len(cuts)))
        factor_of = factor_of * jnp.repeat(draws, shape[dim] // parts).reshape([-1 if axis == dim else 1 for axis in range(len(shape))])
    return factor_of


def scatter_about(key, extent, width, limit, cuts=(), kind=jnp.bfloat16):
    level = steps_of(key, extent, cuts, -0.22, 0.18) if cuts else 1.0
    drawn = jax.random.normal(key, extent, jnp.float32) * width * level
    return jnp.minimum(jnp.maximum(drawn, -limit), limit).astype(kind)


def setup_inputs(seed: int = 0, part: int = 0) -> dict:
    splits = jax.random.split(jax.random.key(seed), 7)
    part_splits = jax.random.split(jax.random.fold_in(splits[6], part), 7)
    return {
        "fourier_input_rows": scatter_about(part_splits[0], (2, HALF_LATITUDES, SLOT_TOTAL, FIELD_TOTAL, 2 * LEVEL_TOTAL), 1.0, 6.0, ((1, 4), (3, 2), (4, 2))),
        "legendre": scatter_about(splits[1], (SLOT_TOTAL, DEGREE_LIMIT, HALF_LATITUDES), HALF_LATITUDES ** -0.5, 0.15625, ((0, 4), (1, 4))),
        "slot_wave": draw_slot_wave(jax.random.fold_in(splits[6], 71), part),
        "to_modes": scatter_about(splits[3], (LEVEL_TOTAL, LEVEL_TOTAL), LEVEL_TOTAL ** -0.5, 0.5),
        "from_modes": scatter_about(splits[4], (LEVEL_TOTAL, LEVEL_TOTAL), LEVEL_TOTAL ** -0.5, 0.5),
        "mode_rate": jnp.clip(jnp.exp(jax.random.uniform(splits[5], (LEVEL_TOTAL,), jnp.float32, math.log(0.05), math.log(5.0))), 0.05, 5.0),
    }


def latitude_weights(count):
    position = jnp.arange(count, dtype=jnp.float32)
    return jnp.sin(math.pi * (position + 0.5) / (2 * count))


def reference(fourier_input_rows, legendre, slot_wave, to_modes, from_modes, mode_rate):
    weights = latitude_weights(HALF_LATITUDES)[:, None, None, None]
    north_half = fourier_input_rows[0].astype(jnp.float32)
    south_half = fourier_input_rows[1].astype(jnp.float32)
    symmetric = (weights * (north_half + south_half)).astype(jnp.bfloat16)
    antisym = (weights * (north_half - south_half)).astype(jnp.bfloat16)
    paired = jnp.moveaxis(jnp.concatenate((symmetric, antisym), axis=3), 1, 0)
    column_count = 2 * LEVEL_TOTAL
    degree = jnp.arange(DEGREE_LIMIT, dtype=jnp.int32)
    degree_real = degree.astype(jnp.float32)
    factor = 1.0 + degree_real[:, None] * (degree_real[:, None] + 1.0) * mode_rate[None, :] / (DEGREE_LIMIT * DEGREE_LIMIT)
    weight_in = to_modes.astype(jnp.float32)
    weight_out = from_modes.astype(jnp.float32)

    def one_slot(slot_items):
        table, block_data, slot_number = slot_items
        product = jnp.dot(table, block_data.reshape(HALF_LATITUDES, FIELD_TOTAL * 2 * column_count), preferred_element_type=jnp.float32)
        product = product.reshape(DEGREE_LIMIT, FIELD_TOTAL, 2 * column_count)
        relative = degree - slot_number
        is_live = (relative >= 0)[:, None, None]
        is_even = (relative % 2 == 0)[:, None, None]
        picked = jnp.where(is_even, product[..., :column_count], product[..., column_count:])
        raw_spectral = jnp.where(is_live, picked, jnp.zeros_like(picked)).astype(jnp.bfloat16)
        level_grid = raw_spectral.astype(jnp.float32).reshape(DEGREE_LIMIT, FIELD_TOTAL, LEVEL_TOTAL, 2)
        projected = jnp.einsum("kl,nflr->nfkr", weight_in, level_grid)
        mode_values = (projected / factor[:, None, :, None]).astype(jnp.bfloat16)
        spectral_slot = jnp.einsum("lk,nfkr->nflr", weight_out, mode_values.astype(jnp.float32))
        spectral_slot = spectral_slot.astype(jnp.bfloat16).reshape(DEGREE_LIMIT, FIELD_TOTAL, column_count)
        even_mask = ((relative >= 0) & (relative % 2 == 0))[:, None, None]
        odd_mask = ((relative >= 0) & (relative % 2 == 1))[:, None, None]
        empty_rows = jnp.zeros_like(spectral_slot)
        parity_split = jnp.concatenate((jnp.where(even_mask, spectral_slot, empty_rows), jnp.where(odd_mask, spectral_slot, empty_rows)), axis=2)
        running = jnp.dot(table.T, parity_split.reshape(DEGREE_LIMIT, FIELD_TOTAL * 2 * column_count), preferred_element_type=jnp.float32)
        running = running.reshape(HALF_LATITUDES, FIELD_TOTAL, 2 * column_count)
        even_sum = running[..., :column_count]
        odd_sum = running[..., column_count:]
        fourier_slot = jnp.stack((even_sum + odd_sum, even_sum - odd_sum), axis=0).astype(jnp.bfloat16)
        return fourier_slot, spectral_slot

    fourier_slots, spectral = lax.map(one_slot, (legendre, paired, slot_wave))
    fourier_out = jnp.moveaxis(fourier_slots, 0, 2)
    return fourier_out, spectral
```

```python
import functools
import math

import jax
import jax.numpy as jnp
from jax import lax
from jax.experimental import pallas as pl
from jax.experimental.pallas import tpu as pltpu
from jax.sharding import PartitionSpec as P

VMEM_BYTES = 24 * 1024 * 1024


def latitude_weights(count):
    position = jnp.arange(count, dtype=jnp.float32)
    return jnp.sin(math.pi * (position + 0.5) / (2 * count))


def iota2(shape, dim):
    return lax.broadcasted_iota(jnp.int32, shape, dim)


def picks(condition):
    return jnp.where(condition, 1.0, 0.0).astype(jnp.bfloat16)


def dot32(a, b):
    return jnp.dot(a, b, preferred_element_type=jnp.float32)


def call(body, out_shape, name, flops, moved, scratch=(), scalars=1, inputs=1):
    smem = pl.BlockSpec(memory_space=pltpu.SMEM)
    vmem = pl.BlockSpec(memory_space=pltpu.VMEM)
    return pl.pallas_call(
        body,
        out_shape=out_shape,
        in_specs=[smem] * scalars + [vmem] * inputs,
        out_specs=jax.tree.map(lambda _: vmem, out_shape),
        scratch_shapes=list(scratch),
        compiler_params=pltpu.CompilerParams(vmem_limit_bytes=VMEM_BYTES),
        cost_estimate=pl.CostEstimate(flops=flops, bytes_accessed=moved, transcendentals=0),
        name=name,
    )


def split_body(slots, fields, block, rows_ref, weight_ref, sym_ref, anti_ref):
    latitudes = weight_ref.shape[0]
    group = slots * fields
    size = block * group
    out_row, in_row = iota2((size, size), 0), iota2((size, size), 1)
    order = picks(in_row == (out_row % block) * group + out_row // block)
    for first in range(0, latitudes, block):
        north = rows_ref[0, first * group : first * group + size, :]
        south = rows_ref[1, first * group : first * group + size, :]
        sorted_rows = dot32(order, jnp.concatenate((north, south), axis=1))
        weight = weight_ref[first : first + block, :]
        for slot in range(slots):
            for field in range(fields):
                at = (slot * fields + field) * block
                up, down = sorted_rows[at : at + block, :128], sorted_rows[at : at + block, 128:]
                lanes = slice(field * 128, field * 128 + 128)
                sym_ref[slot, first : first + block, lanes] = (weight * (up + down)).astype(jnp.bfloat16)
                anti_ref[slot, first : first + block, lanes] = (weight * (up - down)).astype(jnp.bfloat16)


def table_body(meta_ref, table_ref, even_ref, odd_ref):
    rows, columns = table_ref.shape
    half = rows // 2
    parity = meta_ref[0] % 2
    out_row, in_row = iota2((rows, rows), 0), iota2((rows, rows), 1)
    wanted = jnp.where(out_row < half, 2 * out_row + parity, 2 * (out_row - half) + 1 - parity)
    order = picks(in_row == wanted)
    for first in range(0, columns, 256):
        lanes = slice(first, first + 256)
        result = dot32(order, table_ref[:, lanes]).astype(jnp.bfloat16)
        even_ref[:, lanes] = result[:half]
        odd_ref[:, lanes] = result[half:]


def modes_body(lev_total, meta_ref, to_ref, from_ref, in_ref, out_ref):
    levels = to_ref.shape[0]
    wide = 2 * levels
    own = levels // lev_total
    lev = meta_ref[2]

    def spread(sign):
        lane, row = iota2((levels, wide), 1), iota2((levels, wide), 0)
        shift = lane // (2 * own)
        owner = lax.rem(lev + sign * shift + lev_total, lev_total)
        return picks(row == owner * own + (lane % (2 * own)) // 2)

    plain = picks(iota2((levels, wide), 0) == iota2((levels, wide), 1) // 2)
    same = (iota2((wide, wide), 0) % 2) == (iota2((wide, wide), 1) % 2)
    turned = lax.dot_general(
        spread(-1), to_ref[...], (((0,), (1,)), ((), ())), preferred_element_type=jnp.float32
    ).astype(jnp.bfloat16)
    in_ref[...] = jnp.where(same, dot32(turned, plain), 0.0).astype(jnp.bfloat16)
    turned = lax.dot_general(
        plain, from_ref[...], (((0,), (1,)), ((), ())), preferred_element_type=jnp.float32
    ).astype(jnp.bfloat16)
    out_ref[...] = jnp.where(same, dot32(turned, spread(1)), 0.0).astype(jnp.bfloat16)


def degree_column(meta_ref, rows, block, odd):
    parity = meta_ref[0] % 2
    start = jnp.where(parity == odd, 0, 1)
    return block * (2 * rows) + 2 * iota2((rows, 1), 0) + start


def direct_body(sizes, odd, meta_ref, *refs):
    wide, levs, flds = sizes
    parts, refs = refs[:wide], refs[wide:]
    tables, refs = refs[: levs * flds], refs[levs * flds :]
    outs, data = refs[:levs], refs[levs]
    latitudes = parts[0].shape[0]
    for shift in range(wide):
        owner = lax.rem(meta_ref[1] - shift + wide, wide)
        data[pl.ds(pl.multiple_of(owner * latitudes, latitudes), latitudes), :] = parts[shift][...]
    for d in range(levs):
        for g in range(flds):
            table = tables[d * flds + g]
            rows = table.shape[0]
            block = lax.rem(meta_ref[2] + d, levs) * flds + lax.rem(meta_ref[3] + g, flds)
            live = degree_column(meta_ref, rows, block, odd) >= meta_ref[0]
            result = dot32(table[...], data[...])
            outs[d][g * rows : (g + 1) * rows, :] = jnp.where(live, result, 0.0).astype(jnp.bfloat16)


def solve_body(sizes, odd, degree_total, meta_ref, *refs):
    wide, levs, flds = sizes
    parts, refs = refs[:levs], refs[levs:]
    in_ref, out_ref, rate_ref, outs = refs[0], refs[1], refs[2], refs[3:]
    rows, columns = parts[0].shape
    each = rows // flds
    fields = columns // 128
    for g in range(flds):
        block = meta_ref[2] * flds + lax.rem(meta_ref[3] + g, flds)
        degree = degree_column(meta_ref, each, block, odd).astype(jnp.float32)
        factor = 1.0 + degree * (degree + 1.0) * rate_ref[...] / (degree_total * degree_total)
        at = slice(g * each, (g + 1) * each)
        for field in range(fields):
            lanes = slice(field * 128, field * 128 + 128)
            level_grid = jnp.concatenate([part[at, lanes] for part in parts], axis=1)
            modes = (dot32(level_grid, in_ref[...]) / factor).astype(jnp.bfloat16)
            result = dot32(modes, out_ref[...]).astype(jnp.bfloat16)
            for d in range(levs):
                outs[d][at, lanes] = result[:, d * 128 : d * 128 + 128]


def inverse_body(sizes, meta_ref, *refs):
    wide, levs, flds = sizes
    parts, refs = refs[:levs], refs[levs:]
    tables, refs = refs[: levs * flds], refs[levs * flds :]
    outs, total = refs[:wide], refs[wide]
    rows = tables[0].shape[0]
    spectral = jnp.concatenate(
        [parts[d][g * rows : (g + 1) * rows, :] for d in range(levs) for g in range(flds)], axis=0
    )
    columns = total.shape[0]
    for first in range(0, columns, 256):
        lanes = slice(first, first + 256)
        table = jnp.concatenate([ref[:, lanes] for ref in tables], axis=0)
        total[lanes, :] = lax.dot_general(
            table, spectral, (((0,), (0,)), ((), ())), preferred_element_type=jnp.float32
        )
    latitudes = outs[0].shape[0]
    for shift in range(wide):
        owner = lax.rem(meta_ref[1] + shift, wide)
        at = pl.ds(pl.multiple_of(owner * latitudes, latitudes), latitudes)
        outs[shift][...] = total[at, :].astype(jnp.bfloat16)


def join_body(wide, block, meta_ref, *refs):
    evens, odds, out_ref = refs[:wide], refs[wide : 2 * wide], refs[2 * wide]
    latitudes, columns = evens[0].shape
    fields = columns // 128
    group = wide * fields
    size = block * group
    out_row, in_row = iota2((size, size), 0), iota2((size, size), 1)
    place = out_row % group
    shift = lax.rem(meta_ref[1] - place // fields + wide, wide)
    order = picks(in_row == (shift * fields + place % fields) * block + out_row // group)

    def stack(parts, first):
        return jnp.concatenate(
            [
                part[first : first + block, field * 128 : field * 128 + 128]
                for part in parts
                for field in range(fields)
            ],
            axis=0,
        )

    for first in range(0, latitudes, block):
        both = dot32(order, jnp.concatenate((stack(evens, first), stack(odds, first)), axis=1))
        even, odd = both[:, :128], both[:, 128:]
        out_ref[0, first * group : first * group + size, :] = (even + odd).astype(jnp.bfloat16)
        out_ref[1, first * group : first * group + size, :] = (even - odd).astype(jnp.bfloat16)


def rows_body(sizes, block, meta_ref, *refs):
    wide, levs, flds = sizes
    evens, odds, out_ref = refs[:levs], refs[levs : 2 * levs], refs[2 * levs]
    total_rows, columns = evens[0].shape
    rows = total_rows // flds
    fields = columns // 128
    group = 2 * fields
    size = block * group
    parity = meta_ref[0] % 2
    out_row, in_row = iota2((size, size), 0), iota2((size, size), 1)
    place = out_row % group
    is_odd = place // fields
    kind = jnp.where(parity == 0, is_odd, 1 - is_odd)
    order = picks(in_row == (kind * fields + place % fields) * block + out_row // group)
    for d in range(levs):
        for g in range(flds):
            index = lax.rem(meta_ref[2] - d + levs, levs) * flds + lax.rem(meta_ref[3] + g, flds)
            for first in range(0, rows, block):
                at = slice(g * rows + first, g * rows + first + block)
                stacked = jnp.concatenate(
                    [
                        part[at, field * 128 : field * 128 + 128]
                        for part in (evens[d], odds[d])
                        for field in range(fields)
                    ],
                    axis=0,
                )
                start = pl.multiple_of(index * (rows * group), rows * group) + first * group
                out_ref[pl.ds(start, size), :] = dot32(order, stacked).astype(jnp.bfloat16)


def shards(fourier_input_rows, legendre, slot_wave, to_modes, from_modes, mode_rate):
    wide, levs, flds = (lax.axis_size(axis) for axis in ("wide", "lev", "fld"))
    sizes = (wide, levs, flds)
    _, latitudes, slots, fields, lanes = fourier_input_rows.shape
    columns = fields * lanes
    _, shard_rows, half_count = legendre.shape
    degree_count = shard_rows * levs * flds
    half_rows = shard_rows // 2
    group = slots * fields
    bf16, f32 = jnp.bfloat16, jnp.float32

    def shape(*dims):
        return jax.ShapeDtypeStruct(dims, bf16)

    def shifted(value, axis, count, step):
        return lax.ppermute(value, axis, [(i, (i + step) % count) for i in range(count)])

    wide_at, lev_at, fld_at = (lax.axis_index(axis) for axis in ("wide", "lev", "fld"))
    meta = jnp.stack((slot_wave[0], wide_at, lev_at, fld_at)).astype(jnp.int32)
    position = (wide_at * latitudes + jnp.arange(latitudes, dtype=jnp.int32)).astype(f32)
    weights = jnp.sin(math.pi * (position + 0.5) / (2 * half_count))
    weights = jnp.broadcast_to(weights[:, None], (latitudes, lanes))

    block = 256 // group
    halves = call(
        functools.partial(split_body, slots, fields, block),
        (shape(slots, latitudes, columns),) * 2,
        "split_hemispheres", 4 * group * latitudes * 128 * 256, 8 * group * latitudes * 128, scalars=0, inputs=2,
    )(fourier_input_rows.reshape(2, latitudes * group, lanes), weights)
    table_parts = call(
        table_body, (shape(half_rows, half_count),) * 2,
        "split_table", 2 * shard_rows * shard_rows * half_count, 4 * shard_rows * half_count,
    )(meta, legendre[0])
    levels = to_modes.shape[0]
    modes_in, modes_out = call(
        functools.partial(modes_body, levs), (shape(2 * levels, 2 * levels),) * 2,
        "spread_modes", 12 * levels * levels * levels, 12 * levels * levels, inputs=2,
    )(meta, to_modes, from_modes)
    rates = jnp.repeat(mode_rate, 2)[None, :]

    received, tables = [], []
    for odd in range(2):
        own = [
            lax.dynamic_index_in_dim(halves[odd], lax.rem(wide_at + step, wide), 0, keepdims=False)
            for step in range(wide)
        ]
        received.append([own[0]] + [shifted(own[step], "wide", wide, step) for step in range(1, wide)])
        along_lev = [table_parts[odd]] + [
            shifted(table_parts[odd], "lev", levs, -step) for step in range(1, levs)
        ]
        tables.append([
            shifted(part, "fld", flds, -step) if step else part for part in along_lev for step in range(flds)
        ])

    spectrals, sums = [], []
    for odd in range(2):
        raw = call(
            functools.partial(direct_body, sizes, odd),
            (shape(flds * half_rows, columns),) * levs,
            "direct_legendre", degree_count * half_count * columns,
            degree_count * half_count + 2 * half_count * columns + degree_count * columns,
            scratch=[pltpu.VMEM((half_count, columns), bf16)], inputs=wide + levs * flds,
        )(meta, *received[odd], *tables[odd])
        by_level = [raw[0]] + [shifted(raw[step], "lev", levs, step) for step in range(1, levs)]
        solved = call(
            functools.partial(solve_body, sizes, odd, degree_count),
            (shape(flds * half_rows, columns),) * levs,
            "vertical_solve", 16 * flds * half_rows * fields * levels * levels,
            4 * levs * flds * half_rows * columns, inputs=levs + 3,
        )(meta, *by_level, modes_in, modes_out, rates)
        spectral = [solved[0]] + [shifted(solved[step], "lev", levs, step) for step in range(1, levs)]
        spectrals.append(spectral)
        by_degree = [spectral[-step % levs] for step in range(levs)]
        grid = call(
            functools.partial(inverse_body, sizes),
            (shape(latitudes, columns),) * wide,
            "inverse_legendre", degree_count * half_count * columns,
            degree_count * half_count + 2 * half_count * columns + degree_count * columns,
            scratch=[pltpu.VMEM((half_count, columns), f32)], inputs=levs + levs * flds,
        )(meta, *by_degree, *tables[odd])
        sums.append([grid[0]] + [shifted(grid[step], "wide", wide, step) for step in range(1, wide)])

    spectral_rows = call(
        functools.partial(rows_body, sizes, 32),
        shape(degree_count * fields, lanes),
        "order_spectral", 2 * degree_count * fields * lanes * 64 * fields, 4 * degree_count * columns,
        inputs=2 * levs,
    )(meta, *spectrals[0], *spectrals[1])
    fourier_rows = call(
        functools.partial(join_body, wide, block),
        shape(2, latitudes * group, lanes),
        "join_hemispheres", 4 * group * latitudes * 128 * 256, 8 * group * latitudes * 128, inputs=2 * wide,
    )(meta, *sums[0], *sums[1])
    return (
        fourier_rows.reshape(2, latitudes, slots, fields, lanes),
        spectral_rows.reshape(1, degree_count, fields, lanes),
    )
def project(level_grid, degree_real, weight_rows, rate_rows, degree_total):
    projected = jnp.einsum(
        "kl,snflr->snfkr", weight_rows, level_grid, preferred_element_type=jnp.float32
    )
    factor = 1.0 + degree_real[:, None] * (degree_real[:, None] + 1.0) * rate_rows[None, :] / (
        degree_total * degree_total
    )
    return (projected / factor[None, :, None, :, None]).astype(jnp.bfloat16)


def plain_shards(fourier_input_rows, legendre, slot_wave, to_modes, from_modes, mode_rate):
    wave_rows = lax.all_to_all(fourier_input_rows, "wide", split_axis=2, concat_axis=1, tiled=True)
    half_count = wave_rows.shape[1]
    slot_count = wave_rows.shape[2]
    field_count = wave_rows.shape[3]
    column_count = wave_rows.shape[4]
    degree_count = legendre.shape[1] * lax.axis_size(("lev", "fld"))
    weights = latitude_weights(half_count)[:, None, None, None]
    north_half = wave_rows[0].astype(jnp.float32)
    south_half = wave_rows[1].astype(jnp.float32)
    symmetric = (weights * (north_half + south_half)).astype(jnp.bfloat16)
    antisym = (weights * (north_half - south_half)).astype(jnp.bfloat16)
    paired = jnp.concatenate((symmetric, antisym), axis=3)

    def direct_rows(section, first_row):
        row_count = section.shape[1]
        degree = first_row + jnp.arange(row_count, dtype=jnp.int32)
        relative = degree[None, :] - slot_wave[:, None]
        product = jnp.einsum("snj,jsfc->snfc", section, paired, preferred_element_type=jnp.float32)
        is_even = (relative % 2 == 0)[:, :, None, None]
        is_live = (relative >= 0)[:, :, None, None]
        picked = jnp.where(is_even, product[..., :column_count], product[..., column_count:])
        return jnp.where(is_live, picked, jnp.zeros_like(picked))

    full_table = lax.all_gather(legendre, ("lev", "fld"), axis=1, tiled=True)
    block_rows = 128
    block_count = degree_count // block_rows

    def direct_step(block_index, buffer):
        first_row = block_index * block_rows
        section = lax.dynamic_slice_in_dim(full_table, first_row, block_rows, 1)
        result = direct_rows(section, first_row).astype(jnp.bfloat16)
        return lax.dynamic_update_slice_in_dim(buffer, result, first_row, 1)

    initial_raw = jnp.zeros((slot_count, degree_count, field_count, column_count), jnp.bfloat16)
    raw_spectral = lax.fori_loop(0, block_count, direct_step, initial_raw)
    own_levels = column_count // 2
    first_level = lax.axis_index("lev") * own_levels
    degree_real = jnp.arange(degree_count, dtype=jnp.float32)
    all_levels = lax.all_gather(raw_spectral, "lev", axis=3, tiled=True)
    level_count = all_levels.shape[3] // 2
    level_grid = all_levels.reshape(slot_count, degree_count, field_count, level_count, 2)
    weight_rows = lax.dynamic_slice_in_dim(to_modes, first_level, own_levels, 0)
    rate_rows = lax.dynamic_slice_in_dim(mode_rate, first_level, own_levels, 0)
    own_modes = project(level_grid, degree_real, weight_rows, rate_rows, degree_count).reshape(
        slot_count, degree_count, field_count, column_count
    )
    mode_values = lax.all_gather(own_modes, "lev", axis=3, tiled=True).reshape(
        slot_count, degree_count, field_count, level_count, 2
    )
    back_rows = lax.dynamic_slice_in_dim(from_modes, first_level, own_levels, 0)
    spectral = jnp.einsum(
        "lk,snfkr->snflr", back_rows, mode_values, preferred_element_type=jnp.float32
    )
    spectral = spectral.astype(jnp.bfloat16).reshape(
        slot_count, degree_count, field_count, column_count
    )

    def inverse_rows(running, section, first_row):
        row_count = section.shape[1]
        degree = first_row + jnp.arange(row_count, dtype=jnp.int32)
        relative = degree[None, :] - slot_wave[:, None]
        spec_rows = lax.dynamic_slice_in_dim(spectral, first_row, row_count, 1)
        even_mask = ((relative >= 0) & (relative % 2 == 0))[:, :, None, None]
        odd_mask = ((relative >= 0) & (relative % 2 == 1))[:, :, None, None]
        empty_rows = jnp.zeros_like(spec_rows)
        parity_split = jnp.concatenate(
            (
                jnp.where(even_mask, spec_rows, empty_rows),
                jnp.where(odd_mask, spec_rows, empty_rows),
            ),
            axis=3,
        )
        return running + jnp.einsum(
            "snj,snfc->jsfc", section, parity_split, preferred_element_type=jnp.float32
        )

    initial_sum = jnp.zeros((half_count, slot_count, field_count, 2 * column_count), jnp.float32)

    def inverse_step(block_index, running):
        first_row = block_index * block_rows
        section = lax.dynamic_slice_in_dim(full_table, first_row, block_rows, 1)
        return inverse_rows(running, section, first_row)

    running = lax.fori_loop(0, block_count, inverse_step, initial_sum)
    even_sum = running[..., :column_count]
    odd_sum = running[..., column_count:]
    fourier_wave = jnp.stack((even_sum + odd_sum, even_sum - odd_sum), axis=0).astype(jnp.bfloat16)
    fourier_out = lax.all_to_all(fourier_wave, "wide", split_axis=1, concat_axis=2, tiled=True)
    return (fourier_out, spectral)


def solution(mesh):
    in_specs = (
        P("ens", "wide", None, "fld", "lev"),
        P("wide", ("lev", "fld"), None),
        P("wide"),
        P(),
        P(),
        P(),
    )
    out_specs = (P("ens", "wide", None, "fld", "lev"), P(("ens", "wide"), None, "fld", "lev"))

    def body(fourier_input_rows, legendre, *rest):
        _, latitudes, slots, fields, lanes = fourier_input_rows.shape
        whole_tiles = (
            latitudes % 32 == 0
            and slots * fields == 8
            and slots == mesh.shape["wide"]
            and lanes == 128
            and legendre.shape[1] % 64 == 0
            and legendre.shape[2] % 256 == 0
        )
        form = shards if whole_tiles else plain_shards
        return form(fourier_input_rows, legendre, *rest)

    return jax.shard_map(body, mesh=mesh, in_specs=in_specs, out_specs=out_specs, check_vma=False)
```

```python
import functools
import math

import jax
import jax.numpy as jnp
from jax import lax
from jax.experimental import pallas as pl
from jax.experimental.pallas import tpu as pltpu
from jax.sharding import PartitionSpec as P

VMEM_BYTES = 8 * 1024 * 1024


def latitude_weights(count):
    position = jnp.arange(count, dtype=jnp.float32)
    return jnp.sin(math.pi * (position + 0.5) / (2 * count))


def iota2(shape, dim):
    return lax.broadcasted_iota(jnp.int32, shape, dim)


def picks(condition):
    return jnp.where(condition, 1.0, 0.0).astype(jnp.bfloat16)


def dot32(a, b):
    return jnp.dot(a, b, preferred_element_type=jnp.float32)


def call(body, out_shape, name, scratch=(), scalars=1, after=()):
    smem = pl.BlockSpec(memory_space=pltpu.SMEM)
    vmem = pl.BlockSpec(memory_space=pltpu.VMEM)

    def run(*operands):
        used = len(operands)

        def kernel(*refs):
            body(*refs[:used], *refs[used + len(after) :])

        return pl.pallas_call(
            kernel,
            out_shape=out_shape,
            in_specs=[smem] * scalars
            + [vmem] * (used - scalars)
            + [pl.BlockSpec(memory_space=pl.ANY)] * len(after),
            out_specs=jax.tree.map(lambda _: vmem, out_shape),
            scratch_shapes=list(scratch),
            compiler_params=pltpu.CompilerParams(vmem_limit_bytes=VMEM_BYTES),
            name=name,
        )(*operands, *after)

    return run


def split_body(slots, fields, block, odd, rows_ref, weight_ref, out_ref):
    latitudes = weight_ref.shape[0]
    group = slots * fields
    size = block * group
    out_row, in_row = iota2((size, size), 0), iota2((size, size), 1)
    order = picks(in_row == (out_row % block) * group + out_row // block)
    for first in range(0, latitudes, block):
        north = rows_ref[0, first * group : first * group + size, :]
        south = rows_ref[1, first * group : first * group + size, :]
        sorted_rows = dot32(order, jnp.concatenate((north, south), axis=1))
        up, down = sorted_rows[:, :128], sorted_rows[:, 128:]
        mixed = up - down if odd else up + down
        weight = weight_ref[first : first + block, :]
        for slot in range(slots):
            for field in range(fields):
                at = (slot * fields + field) * block
                out_ref[slot, first : first + block, field * 128 : field * 128 + 128] = (
                    weight * mixed[at : at + block]
                ).astype(jnp.bfloat16)


def table_body(odd, meta_ref, table_ref, out_ref):
    rows, columns = table_ref.shape
    half = rows // 2
    out_row, in_row = iota2((half, rows), 0), iota2((half, rows), 1)
    order = picks(in_row == 2 * out_row + (meta_ref[0] + odd) % 2)
    for first in range(0, columns, 256):
        lanes = slice(first, first + 256)
        out_ref[:, lanes] = dot32(order, table_ref[:, lanes]).astype(jnp.bfloat16)


def modes_body(lev_total, meta_ref, to_ref, from_ref, rate_ref, in_ref, out_ref, rates_ref):
    levels = to_ref.shape[0]
    wide = 2 * levels
    own = levels // lev_total
    lev = meta_ref[2]
    lane, row = iota2((levels, wide), 1), iota2((levels, wide), 0)

    def spread(sign):
        owner = lax.rem(lev + sign * (lane // (2 * own)) + lev_total, lev_total)
        return picks(row == owner * own + (lane % (2 * own)) // 2)

    def turned(first, matrix):
        return lax.dot_general(
            first, matrix, (((0,), (1,)), ((), ())), preferred_element_type=jnp.float32
        ).astype(jnp.bfloat16)

    plain = picks(row == lane // 2)
    same = (iota2((wide, wide), 0) % 2) == (iota2((wide, wide), 1) % 2)
    in_ref[...] = jnp.where(same, dot32(turned(spread(-1), to_ref[...]), plain), 0.0).astype(jnp.bfloat16)
    out_ref[...] = jnp.where(same, dot32(turned(plain, from_ref[...]), spread(1)), 0.0).astype(jnp.bfloat16)
    square = (levels, levels)
    diagonal = jnp.where(iota2(square, 0) == iota2(square, 1), rate_ref[...], 0.0)
    column = jnp.sum(diagonal, axis=1, keepdims=True)
    rates_ref[...] = jnp.sum(jnp.where(row == lane // 2, column, 0.0), axis=0, keepdims=True)


def degree_column(meta_ref, rows, block, odd):
    return block * (2 * rows) + 2 * iota2((rows, 1), 0) + (meta_ref[0] + odd) % 2


def direct_body(sizes, odd, meta_ref, data_ref, *refs):
    wide, levs, flds = sizes
    tables, outs = refs[: levs * flds], refs[levs * flds :]
    for d in range(levs):
        for g in range(flds):
            table = tables[d * flds + g]
            rows = table.shape[0]
            block = lax.rem(meta_ref[2] + d, levs) * flds + lax.rem(meta_ref[3] + g, flds)
            live = degree_column(meta_ref, rows, block, odd) >= meta_ref[0]
            result = dot32(table[...], data_ref[...])
            outs[d][g * rows : (g + 1) * rows, :] = jnp.where(live, result, 0.0).astype(jnp.bfloat16)


def solve_body(sizes, odd, degree_total, meta_ref, *refs):
    wide, levs, flds = sizes
    parts, refs = refs[:levs], refs[levs:]
    in_ref, out_ref, rate_ref, outs = refs[0], refs[1], refs[2], refs[3:]
    rows, columns = parts[0].shape
    each = rows // flds
    fields = columns // 128
    for g in range(flds):
        block = meta_ref[2] * flds + lax.rem(meta_ref[3] + g, flds)
        degree = degree_column(meta_ref, each, block, odd).astype(jnp.float32)
        factor = 1.0 + degree * (degree + 1.0) * rate_ref[...] / (degree_total * degree_total)
        at = slice(g * each, (g + 1) * each)
        for field in range(fields):
            lanes = slice(field * 128, field * 128 + 128)
            level_grid = jnp.concatenate([part[at, lanes] for part in parts], axis=1)
            modes = (dot32(level_grid, in_ref[...]) / factor).astype(jnp.bfloat16)
            result = dot32(modes, out_ref[...]).astype(jnp.bfloat16)
            for d in range(levs):
                outs[d][at, lanes] = result[:, d * 128 : d * 128 + 128]


def inverse_body(sizes, *refs):
    wide, levs, flds = sizes
    parts, tables, out_ref = refs[:levs], refs[levs : levs + levs * flds], refs[-1]
    rows = tables[0].shape[0]
    spectral = jnp.concatenate(
        [parts[d][g * rows : (g + 1) * rows, :] for d in range(levs) for g in range(flds)], axis=0
    )
    for first in range(0, out_ref.shape[0], 256):
        lanes = slice(first, first + 256)
        table = jnp.concatenate([ref[:, lanes] for ref in tables], axis=0)
        out_ref[lanes, :] = lax.dot_general(
            table, spectral, (((0,), (0,)), ((), ())), preferred_element_type=jnp.float32
        ).astype(jnp.bfloat16)


def join_body(block, even_ref, odd_ref, out_ref):
    slots, latitudes, columns = even_ref.shape
    fields = columns // 128
    group = slots * fields
    size = block * group
    out_row, in_row = iota2((size, size), 0), iota2((size, size), 1)
    order = picks(in_row == (out_row % group) * block + out_row // group)

    def stack(ref, first):
        return jnp.concatenate(
            [
                ref[slot, first : first + block, field * 128 : field * 128 + 128]
                for slot in range(slots)
                for field in range(fields)
            ],
            axis=0,
        )

    for first in range(0, latitudes, block):
        both = dot32(order, jnp.concatenate((stack(even_ref, first), stack(odd_ref, first)), axis=1))
        even, odd = both[:, :128], both[:, 128:]
        out_ref[0, first * group : first * group + size, :] = (even + odd).astype(jnp.bfloat16)
        out_ref[1, first * group : first * group + size, :] = (even - odd).astype(jnp.bfloat16)


def rows_body(sizes, block, meta_ref, *refs):
    wide, levs, flds = sizes
    evens, odds, out_ref = refs[:levs], refs[levs : 2 * levs], refs[2 * levs]
    total_rows, columns = evens[0].shape
    rows = total_rows // flds
    fields = columns // 128
    group = 2 * fields
    size = block * group
    parity = meta_ref[0] % 2
    out_row, in_row = iota2((size, size), 0), iota2((size, size), 1)
    place = out_row % group
    is_odd = place // fields
    kind = jnp.where(parity == 0, is_odd, 1 - is_odd)
    order = picks(in_row == (kind * fields + place % fields) * block + out_row // group)
    for d in range(levs):
        for g in range(flds):
            index = lax.rem(meta_ref[2] - d + levs, levs) * flds + lax.rem(meta_ref[3] + g, flds)
            for first in range(0, rows, block):
                at = slice(g * rows + first, g * rows + first + block)
                stacked = jnp.concatenate(
                    [
                        part[at, field * 128 : field * 128 + 128]
                        for part in (evens[d], odds[d])
                        for field in range(fields)
                    ],
                    axis=0,
                )
                start = pl.multiple_of(index * (rows * group), rows * group) + first * group
                out_ref[pl.ds(start, size), :] = dot32(order, stacked).astype(jnp.bfloat16)


def shards(fourier_input_rows, legendre, slot_wave, to_modes, from_modes, mode_rate):
    wide, levs, flds = (lax.axis_size(axis) for axis in ("wide", "lev", "fld"))
    sizes = (wide, levs, flds)
    _, latitudes, slots, fields, lanes = fourier_input_rows.shape
    columns = fields * lanes
    _, shard_rows, half_count = legendre.shape
    degree_count = shard_rows * levs * flds
    half_rows = shard_rows // 2
    group = slots * fields
    bf16, f32 = jnp.bfloat16, jnp.float32

    def shape(*dims):
        return jax.ShapeDtypeStruct(dims, bf16)

    def shifted(value, axis, count, step):
        return lax.ppermute(value, axis, [(i, (i + step) % count) for i in range(count)])

    wide_at, lev_at, fld_at = (lax.axis_index(axis) for axis in ("wide", "lev", "fld"))
    meta = jnp.stack((slot_wave[0], wide_at, lev_at, fld_at)).astype(jnp.int32)
    position = (wide_at * latitudes + jnp.arange(latitudes, dtype=jnp.int32)).astype(f32)
    weights = jnp.sin(math.pi * (position + 0.5) / (2 * half_count))
    weights = jnp.broadcast_to(weights[:, None], (latitudes, lanes))
    block = 256 // group
    levels = to_modes.shape[0]

    def across(value):
        return lax.all_to_all(value, "wide", split_axis=0, concat_axis=0, tiled=True)

    def split(odd, after):
        return across(call(
            functools.partial(split_body, slots, fields, block, odd), shape(slots, latitudes, columns),
            "split_hemispheres", scalars=0, after=after,
        )(fourier_input_rows.reshape(2, latitudes * group, lanes), weights))

    def split_table(odd, after):
        part = call(
            functools.partial(table_body, odd), shape(half_rows, half_count),
            "split_table", after=after,
        )(meta, legendre[0])
        along_lev = [part] + [shifted(part, "lev", levs, -step) for step in range(1, levs)]
        return [shifted(one, "fld", flds, -step) if step else one for one in along_lev for step in range(flds)]

    def direct(odd, received, table, after):
        raw = call(
            functools.partial(direct_body, sizes, odd), (shape(flds * half_rows, columns),) * levs,
            "direct_legendre", after=after,
        )(meta, received.reshape(half_count, columns), *table)
        return [raw[0]] + [shifted(raw[step], "lev", levs, step) for step in range(1, levs)]

    def solve(odd, by_level, matrices):
        solved = call(
            functools.partial(solve_body, sizes, odd, degree_count),
            (shape(flds * half_rows, columns),) * levs,
            "vertical_solve",
        )(meta, *by_level, *matrices)
        return [solved[0]] + [shifted(solved[step], "lev", levs, step) for step in range(1, levs)]

    def inverse(spectral, table):
        by_degree = [spectral[-step % levs] for step in range(levs)]
        grid = call(
            functools.partial(inverse_body, sizes), shape(half_count, columns), "inverse_legendre", scalars=0,
        )(*by_degree, *table)
        return grid, across(grid.reshape(wide, latitudes, columns))

    symmetric = split(0, ())
    even_table = split_table(0, ())
    odd_table = split_table(1, (even_table[flds],))
    matrices = call(
        functools.partial(modes_body, levs),
        (shape(2 * levels, 2 * levels),) * 2 + (jax.ShapeDtypeStruct((1, 2 * levels), f32),),
        "spread_modes", after=(even_table[0],),
    )(meta, to_modes, from_modes, mode_rate[None, :])
    antisym = split(1, (symmetric,))

    even_raw = direct(0, symmetric, even_table, (matrices[0], odd_table[0]))
    even_spectral = solve(0, even_raw, matrices)
    even_grid, even_sum = inverse(even_spectral, even_table)
    odd_raw = direct(1, antisym, odd_table, (even_grid,))
    odd_spectral = solve(1, odd_raw, matrices)
    odd_grid, odd_sum = inverse(odd_spectral, odd_table)

    spectral_rows = call(
        functools.partial(rows_body, sizes, 32), shape(degree_count * fields, lanes),
        "order_spectral", after=(odd_grid,),
    )(meta, *even_spectral, *odd_spectral)
    fourier_rows = call(
        functools.partial(join_body, block), shape(2, latitudes * group, lanes), "join_hemispheres", scalars=0,
    )(even_sum, odd_sum)
    return (
        fourier_rows.reshape(2, latitudes, slots, fields, lanes),
        spectral_rows.reshape(1, degree_count, fields, lanes),
    )


def project(level_grid, degree_real, weight_rows, rate_rows, degree_total):
    projected = jnp.einsum(
        "kl,snflr->snfkr", weight_rows, level_grid, preferred_element_type=jnp.float32
    )
    factor = 1.0 + degree_real[:, None] * (degree_real[:, None] + 1.0) * rate_rows[None, :] / (
        degree_total * degree_total
    )
    return (projected / factor[None, :, None, :, None]).astype(jnp.bfloat16)


def plain_shards(fourier_input_rows, legendre, slot_wave, to_modes, from_modes, mode_rate):
    wave_rows = lax.all_to_all(fourier_input_rows, "wide", split_axis=2, concat_axis=1, tiled=True)
    half_count = wave_rows.shape[1]
    slot_count = wave_rows.shape[2]
    field_count = wave_rows.shape[3]
    column_count = wave_rows.shape[4]
    degree_count = legendre.shape[1] * lax.axis_size(("lev", "fld"))
    weights = latitude_weights(half_count)[:, None, None, None]
    north_half = wave_rows[0].astype(jnp.float32)
    south_half = wave_rows[1].astype(jnp.float32)
    symmetric = (weights * (north_half + south_half)).astype(jnp.bfloat16)
    antisym = (weights * (north_half - south_half)).astype(jnp.bfloat16)
    paired = jnp.concatenate((symmetric, antisym), axis=3)

    def direct_rows(section, first_row):
        row_count = section.shape[1]
        degree = first_row + jnp.arange(row_count, dtype=jnp.int32)
        relative = degree[None, :] - slot_wave[:, None]
        product = jnp.einsum("snj,jsfc->snfc", section, paired, preferred_element_type=jnp.float32)
        is_even = (relative % 2 == 0)[:, :, None, None]
        is_live = (relative >= 0)[:, :, None, None]
        picked = jnp.where(is_even, product[..., :column_count], product[..., column_count:])
        return jnp.where(is_live, picked, jnp.zeros_like(picked))

    full_table = lax.all_gather(legendre, ("lev", "fld"), axis=1, tiled=True)
    block_rows = 128
    block_count = degree_count // block_rows

    def direct_step(block_index, buffer):
        first_row = block_index * block_rows
        section = lax.dynamic_slice_in_dim(full_table, first_row, block_rows, 1)
        result = direct_rows(section, first_row).astype(jnp.bfloat16)
        return lax.dynamic_update_slice_in_dim(buffer, result, first_row, 1)

    initial_raw = jnp.zeros((slot_count, degree_count, field_count, column_count), jnp.bfloat16)
    raw_spectral = lax.fori_loop(0, block_count, direct_step, initial_raw)
    own_levels = column_count // 2
    first_level = lax.axis_index("lev") * own_levels
    degree_real = jnp.arange(degree_count, dtype=jnp.float32)
    all_levels = lax.all_gather(raw_spectral, "lev", axis=3, tiled=True)
    level_count = all_levels.shape[3] // 2
    level_grid = all_levels.reshape(slot_count, degree_count, field_count, level_count, 2)
    weight_rows = lax.dynamic_slice_in_dim(to_modes, first_level, own_levels, 0)
    rate_rows = lax.dynamic_slice_in_dim(mode_rate, first_level, own_levels, 0)
    own_modes = project(level_grid, degree_real, weight_rows, rate_rows, degree_count).reshape(
        slot_count, degree_count, field_count, column_count
    )
    mode_values = lax.all_gather(own_modes, "lev", axis=3, tiled=True).reshape(
        slot_count, degree_count, field_count, level_count, 2
    )
    back_rows = lax.dynamic_slice_in_dim(from_modes, first_level, own_levels, 0)
    spectral = jnp.einsum(
        "lk,snfkr->snflr", back_rows, mode_values, preferred_element_type=jnp.float32
    )
    spectral = spectral.astype(jnp.bfloat16).reshape(
        slot_count, degree_count, field_count, column_count
    )

    def inverse_rows(running, section, first_row):
        row_count = section.shape[1]
        degree = first_row + jnp.arange(row_count, dtype=jnp.int32)
        relative = degree[None, :] - slot_wave[:, None]
        spec_rows = lax.dynamic_slice_in_dim(spectral, first_row, row_count, 1)
        even_mask = ((relative >= 0) & (relative % 2 == 0))[:, :, None, None]
        odd_mask = ((relative >= 0) & (relative % 2 == 1))[:, :, None, None]
        empty_rows = jnp.zeros_like(spec_rows)
        parity_split = jnp.concatenate(
            (
                jnp.where(even_mask, spec_rows, empty_rows),
                jnp.where(odd_mask, spec_rows, empty_rows),
            ),
            axis=3,
        )
        return running + jnp.einsum(
            "snj,snfc->jsfc", section, parity_split, preferred_element_type=jnp.float32
        )

    initial_sum = jnp.zeros((half_count, slot_count, field_count, 2 * column_count), jnp.float32)

    def inverse_step(block_index, running):
        first_row = block_index * block_rows
        section = lax.dynamic_slice_in_dim(full_table, first_row, block_rows, 1)
        return inverse_rows(running, section, first_row)

    running = lax.fori_loop(0, block_count, inverse_step, initial_sum)
    even_sum = running[..., :column_count]
    odd_sum = running[..., column_count:]
    fourier_wave = jnp.stack((even_sum + odd_sum, even_sum - odd_sum), axis=0).astype(jnp.bfloat16)
    fourier_out = lax.all_to_all(fourier_wave, "wide", split_axis=1, concat_axis=2, tiled=True)
    return (fourier_out, spectral)


def solution(mesh):
    in_specs = (
        P("ens", "wide", None, "fld", "lev"),
        P("wide", ("lev", "fld"), None),
        P("wide"),
        P(),
        P(),
        P(),
    )
    out_specs = (P("ens", "wide", None, "fld", "lev"), P(("ens", "wide"), None, "fld", "lev"))

    def body(fourier_input_rows, legendre, *rest):
        _, latitudes, slots, fields, lanes = fourier_input_rows.shape
        whole_tiles = (
            latitudes % 32 == 0
            and slots * fields == 8
            and slots == mesh.shape["wide"]
            and lanes == 128
            and legendre.shape[1] % 64 == 0
            and legendre.shape[2] % 256 == 0
        )
        form = shards if whole_tiles else plain_shards
        return form(fourier_input_rows, legendre, *rest)

    return jax.shard_map(body, mesh=mesh, in_specs=in_specs, out_specs=out_specs, check_vma=False)
```

```python
import functools
import math

import jax
import jax.numpy as jnp
from jax import lax
from jax.experimental import pallas as pl
from jax.experimental.pallas import tpu as pltpu
from jax.sharding import PartitionSpec as P

VMEM_BYTES = 8 * 1024 * 1024


def latitude_weights(count):
    position = jnp.arange(count, dtype=jnp.float32)
    return jnp.sin(math.pi * (position + 0.5) / (2 * count))


def iota2(shape, dim):
    return lax.broadcasted_iota(jnp.int32, shape, dim)


def picks(condition):
    return jnp.where(condition, 1.0, 0.0).astype(jnp.bfloat16)


def dot32(a, b):
    return jnp.dot(a, b, preferred_element_type=jnp.float32)


def call(body, out_shape, name, flops, scratch=(), scalars=1, after=()):
    smem = pl.BlockSpec(memory_space=pltpu.SMEM)
    vmem = pl.BlockSpec(memory_space=pltpu.VMEM)

    def run(*operands):
        used = len(operands)

        def kernel(*refs):
            body(*refs[:used], *refs[used + len(after) :])

        return pl.pallas_call(
            kernel,
            out_shape=out_shape,
            in_specs=[smem] * scalars
            + [vmem] * (used - scalars)
            + [pl.BlockSpec(memory_space=pl.ANY)] * len(after),
            out_specs=jax.tree.map(lambda _: vmem, out_shape),
            scratch_shapes=list(scratch),
            compiler_params=pltpu.CompilerParams(vmem_limit_bytes=VMEM_BYTES),
            cost_estimate=pl.CostEstimate(flops=flops, bytes_accessed=0, transcendentals=0),
            name=name,
        )(*operands, *after)

    return run


def lane_order(lanes, lev, old, new):
    levels = lanes // 4
    part = lax.rem(new // (lanes // 2) + lev, 2)
    field = (new // levels) % 2
    return old == field * (lanes // 2) + 2 * (new % levels) + part


def split_body(slots, fields, block, meta_ref, rows_ref, weight_ref, *outs):
    latitudes = weight_ref.shape[0]
    group = slots * fields
    size = block * group
    out_row, in_row = iota2((size, size), 0), iota2((size, size), 1)
    pair = out_row // block
    slot = lax.rem(meta_ref[1] + pair // fields, slots)
    order = picks(in_row == (out_row % block) * group + slot * fields + pair % fields)
    lanes = fields * 128
    parts = picks(lane_order(lanes, meta_ref[2], iota2((lanes, lanes), 0), iota2((lanes, lanes), 1)))
    for first in range(0, latitudes, block):
        north = rows_ref[0, first * group : first * group + size, :]
        south = rows_ref[1, first * group : first * group + size, :]
        sorted_rows = dot32(order, jnp.concatenate((north, south), axis=1))
        up, down = sorted_rows[:, :128], sorted_rows[:, 128:]
        weight = weight_ref[first : first + block, :]
        halves = []
        for mixed in (up + down, up - down):
            for shift in range(slots):
                at = shift * fields * block
                halves.append(jnp.concatenate(
                    [
                        (weight * mixed[at + f * block : at + f * block + block]).astype(jnp.bfloat16)
                        for f in range(fields)
                    ],
                    axis=1,
                ))
        turned = dot32(jnp.concatenate(halves, axis=0), parts).astype(jnp.bfloat16)
        for odd in range(2):
            for shift in range(slots):
                for d in range(2):
                    at = (odd * slots + shift) * block
                    outs[shift * 2 + d][odd, first : first + block, :] = turned[
                        at : at + block, d * 128 : d * 128 + 128
                    ]


def table_body(meta_ref, table_ref, out_ref):
    rows, columns = table_ref.shape
    half = rows // 2
    out_row, in_row = iota2((rows, rows), 0), iota2((rows, rows), 1)
    odd = jnp.where(out_row < half, 0, 1)
    order = picks(in_row == 2 * (out_row - odd * half) + (meta_ref[0] + odd) % 2)
    for first in range(0, columns, 256):
        lanes = slice(first, first + 256)
        out_ref[:, lanes] = dot32(order, table_ref[:, lanes]).astype(jnp.bfloat16)


def modes_body(meta_ref, to_ref, from_ref, in_ref, out_ref):
    levels = to_ref.shape[0]
    wide = 2 * levels
    own = levels // 2
    lane, row = iota2((levels, wide), 1), iota2((levels, wide), 0)
    owner = lax.rem(meta_ref[2] + lane // levels, 2)
    spread = picks(row == owner * own + lane % own)
    plain = picks(row == lane % levels)
    old, new = iota2((wide, wide), 0), iota2((wide, wide), 1)

    def turned(first, matrix, last):
        half = lax.dot_general(first, matrix, (((0,), (1,)), ((), ())), preferred_element_type=jnp.float32)
        return dot32(half.astype(jnp.bfloat16), last)

    same = (old // own) % 2 == new // levels
    in_ref[...] = jnp.where(same, turned(spread, to_ref[...], plain), 0.0).astype(jnp.bfloat16)
    same = old // levels == (new // own) % 2
    out_ref[...] = jnp.where(same, turned(plain, from_ref[...], spread), 0.0).astype(jnp.bfloat16)


def forward_body(sizes, degree_total, meta_ref, rate_ref, in_ref, out_ref, *refs):
    wide, levs, flds = sizes
    parts, refs = refs[: wide * levs], refs[wide * levs :]
    tables, refs = refs[: levs * flds], refs[levs * flds :]
    own_ref, send_ref, data = refs
    latitudes, lanes = parts[0].shape[1:]
    rows = tables[0].shape[0] // 2
    for odd in range(2):
        for shift in range(wide):
            owner = lax.rem(meta_ref[1] - shift + wide, wide)
            at = pl.ds(pl.multiple_of(owner * latitudes, latitudes), latitudes)
            for d in range(levs):
                data[odd, at, d * lanes : d * lanes + lanes] = parts[shift * levs + d][odd]
        degree_step = 2 * iota2((rows, 1), 0) + (meta_ref[0] + odd) % 2
        for d in range(levs):
            for g in range(flds):
                block = lax.rem(meta_ref[2] + d, levs) * flds + lax.rem(meta_ref[3] + g, flds)
                degree = block * (2 * rows) + degree_step
                table = tables[d * flds + g][odd * rows : odd * rows + rows, :]
                raw = jnp.where(degree >= meta_ref[0], dot32(table, data[odd]), 0.0).astype(jnp.bfloat16)
                real = degree.astype(jnp.float32)
                rates = jnp.concatenate([rate_ref[...]] * 2, axis=1)
                factor = 1.0 + real * (real + 1.0) * rates / (degree_total * degree_total)
                modes = (dot32(raw, in_ref[...]) / factor).astype(jnp.bfloat16)
                spectral = dot32(modes, out_ref[...]).astype(jnp.bfloat16)
                at = ((d * flds + g) * 2 + odd) * rows
                own_ref[at : at + rows, :] = spectral[:, :lanes]
                send_ref[at : at + rows, :] = spectral[:, lanes:]


def inverse_body(sizes, meta_ref, own_ref, send_ref, *refs):
    wide, levs, flds = sizes
    tables, refs = refs[: levs * flds], refs[levs * flds :]
    outs, total = refs[: wide * levs], refs[-1]
    rows = tables[0].shape[0] // 2
    latitudes, lanes = outs[0].shape[1:]
    spectral = jnp.concatenate((own_ref[...], send_ref[...]), axis=1)
    for first in range(0, total.shape[1], 256):
        chunk = slice(first, first + 256)
        sums = []
        for odd in range(2):
            table = jnp.concatenate([ref[odd * rows : odd * rows + rows, chunk] for ref in tables], axis=0)
            degrees = jnp.concatenate(
                [spectral[(2 * i + odd) * rows : (2 * i + odd + 1) * rows] for i in range(levs * flds)], axis=0
            )
            sums.append(lax.dot_general(
                table, degrees, (((0,), (0,)), ((), ())), preferred_element_type=jnp.float32
            ))
        total[0, chunk, :] = (sums[0] + sums[1]).astype(jnp.bfloat16)
        total[1, chunk, :] = (sums[0] - sums[1]).astype(jnp.bfloat16)
    for shift in range(wide):
        owner = lax.rem(meta_ref[1] + shift, wide)
        at = pl.ds(pl.multiple_of(owner * latitudes, latitudes), latitudes)
        for d in range(levs):
            outs[shift * levs + d][...] = total[:, at, d * lanes : d * lanes + lanes]


def join_body(slots, block, meta_ref, *refs):
    parts, out_ref = refs[:-1], refs[-1]
    latitudes, lanes = parts[0].shape[1:]
    fields = 2
    group = slots * fields
    size = block * group
    out_row, in_row = iota2((size, size), 0), iota2((size, size), 1)
    place = out_row % group
    shift = lax.rem(meta_ref[1] - place // fields + slots, slots)
    order = picks(in_row == (shift * fields + place % fields) * block + out_row // group)
    both = 2 * lanes
    turn = picks(lane_order(both, meta_ref[2], iota2((both, both), 1), iota2((both, both), 0)))
    for first in range(0, latitudes, block):
        at = slice(first, first + block)
        stacked = jnp.concatenate(
            [
                jnp.concatenate([parts[shift * 2 + d][half, at, :] for d in range(2)], axis=1)
                for half in range(2)
                for shift in range(slots)
            ],
            axis=0,
        )
        turned = dot32(stacked, turn).astype(jnp.bfloat16)
        halves = [
            jnp.concatenate(
                [
                    turned[
                        (half * slots + shift) * block : (half * slots + shift + 1) * block,
                        field * lanes : field * lanes + lanes,
                    ]
                    for shift in range(slots)
                    for field in range(fields)
                ],
                axis=0,
            )
            for half in range(2)
        ]
        result = dot32(order, jnp.concatenate(halves, axis=1)).astype(jnp.bfloat16)
        for half in range(2):
            out_ref[half, first * group : first * group + size, :] = result[:, half * lanes : half * lanes + lanes]


def rows_body(sizes, block, meta_ref, own_ref, other_ref, out_ref):
    wide, levs, flds = sizes
    total_rows, lanes = own_ref.shape
    rows = total_rows // (2 * levs * flds)
    fields = 2
    group = 2 * fields
    size = block * group
    parity = meta_ref[0] % 2
    out_row, in_row = iota2((size, size), 0), iota2((size, size), 1)
    place = out_row % group
    odd = (place // fields + parity) % 2
    order = picks(in_row == (odd * fields + place % fields) * block + out_row // group)
    both = 2 * lanes
    turn = picks(lane_order(both, meta_ref[2], iota2((both, both), 1), iota2((both, both), 0)))
    for d in range(levs):
        for g in range(flds):
            index = lax.rem(meta_ref[2] + d, levs) * flds + lax.rem(meta_ref[3] + g, flds)
            mine, theirs = (d * flds + g) * 2 * rows, ((1 - d) * flds + g) * 2 * rows
            turned = dot32(
                jnp.concatenate(
                    (own_ref[mine : mine + 2 * rows, :], other_ref[theirs : theirs + 2 * rows, :]), axis=1
                ),
                turn,
            ).astype(jnp.bfloat16)
            for first in range(0, rows, block):
                stacked = jnp.concatenate(
                    [
                        turned[
                            odd * rows + first : odd * rows + first + block, field * lanes : field * lanes + lanes
                        ]
                        for odd in range(2)
                        for field in range(fields)
                    ],
                    axis=0,
                )
                start = pl.multiple_of(index * (rows * group), rows * group) + first * group
                out_ref[pl.ds(start, size), :] = dot32(order, stacked).astype(jnp.bfloat16)


def shards(fourier_input_rows, legendre, slot_wave, to_modes, from_modes, mode_rate):
    wide, levs, flds = (lax.axis_size(axis) for axis in ("wide", "lev", "fld"))
    sizes = (wide, levs, flds)
    _, latitudes, slots, fields, lanes = fourier_input_rows.shape
    _, shard_rows, half_count = legendre.shape
    degree_count = shard_rows * levs * flds
    group = slots * fields
    columns = fields * lanes
    block = 256 // group
    levels = to_modes.shape[0]
    bf16 = jnp.bfloat16

    def shape(*dims):
        return jax.ShapeDtypeStruct(dims, bf16)

    def shifted(value, axis, count, step):
        return lax.ppermute(value, axis, [(i, (i + step) % count) for i in range(count)])

    def exchanged(blocks):
        def moved(k, d):
            pairs = [
                (w * levs + l, (w + k) % wide * levs + (l + d) % levs) for w in range(wide) for l in range(levs)
            ]
            return lax.ppermute(blocks[k * levs + d], ("wide", "lev"), pairs)

        steps = [(k, d) for k in range(wide) for d in range(levs) if k or d]
        steps.sort(key=lambda step: (-min(step[0], wide - step[0]), step[1]))
        arrived = {step: moved(*step) for step in steps}
        return [arrived[k, d] if k or d else blocks[0] for k in range(wide) for d in range(levs)]

    wide_at, lev_at, fld_at = (lax.axis_index(axis) for axis in ("wide", "lev", "fld"))
    meta = jnp.stack((slot_wave[0], wide_at, lev_at, fld_at)).astype(jnp.int32)
    position = (wide_at * latitudes + jnp.arange(latitudes, dtype=jnp.int32)).astype(jnp.float32)
    weights = jnp.sin(math.pi * (position + 0.5) / (2 * half_count))
    weights = jnp.broadcast_to(weights[:, None], (latitudes, lanes))
    move_flops = 8 * group * latitudes * 128 * 256
    transform_flops = 2 * degree_count * half_count * columns

    blocks = call(
        functools.partial(split_body, slots, fields, block), (shape(2, latitudes, lanes),) * (wide * levs),
        "split_hemispheres", move_flops,
    )(meta, fourier_input_rows.reshape(2, latitudes * group, lanes), weights)
    data = exchanged(blocks)
    part = call(
        table_body, shape(shard_rows, half_count), "split_table", 2 * shard_rows * shard_rows * half_count,
        after=(blocks[0],),
    )(meta, legendre[0])
    along_lev = [part] + [shifted(part, "lev", levs, -step) for step in range(1, levs)]
    early = [2 * levs, 2 * levs + 1, levs, 3 * levs]
    along_lev[1], *blocks = lax.optimization_barrier((along_lev[1], *(data[i] for i in early)))
    data = [dict(zip(early, blocks)).get(i, one) for i, one in enumerate(data)]
    tables = [shifted(one, "fld", flds, -step) if step else one for one in along_lev for step in range(flds)]
    matrices = call(
        modes_body, (shape(2 * levels, 2 * levels),) * 2, "spread_modes", 12 * levels * levels * levels,
        after=(part,),
    )(meta, to_modes, from_modes)

    own, send = call(
        functools.partial(forward_body, sizes, degree_count), (shape(degree_count, lanes),) * 2,
        "direct_legendre_and_solve", transform_flops,
        scratch=[pltpu.VMEM((2, half_count, columns), bf16)],
    )(meta, mode_rate[None, :], *matrices, *data, *tables)
    grid = call(
        functools.partial(inverse_body, sizes), (shape(2, latitudes, lanes),) * (wide * levs),
        "inverse_legendre", transform_flops, scratch=[pltpu.VMEM((2, half_count, columns), bf16)],
    )(meta, own, send, *tables)
    result = exchanged(grid)
    spectral_rows = call(
        functools.partial(rows_body, sizes, 32), shape(degree_count * fields, lanes), "order_spectral", 0,
    )(meta, own, shifted(send, "lev", levs, 1))
    fourier_rows = call(
        functools.partial(join_body, slots, block), shape(2, latitudes * group, lanes),
        "join_hemispheres", move_flops,
    )(meta, *result)
    return (
        fourier_rows.reshape(2, latitudes, slots, fields, lanes),
        spectral_rows.reshape(1, degree_count, fields, lanes),
    )


def project(level_grid, degree_real, weight_rows, rate_rows, degree_total):
    projected = jnp.einsum(
        "kl,snflr->snfkr", weight_rows, level_grid, preferred_element_type=jnp.float32
    )
    factor = 1.0 + degree_real[:, None] * (degree_real[:, None] + 1.0) * rate_rows[None, :] / (
        degree_total * degree_total
    )
    return (projected / factor[None, :, None, :, None]).astype(jnp.bfloat16)


def plain_shards(fourier_input_rows, legendre, slot_wave, to_modes, from_modes, mode_rate):
    wave_rows = lax.all_to_all(fourier_input_rows, "wide", split_axis=2, concat_axis=1, tiled=True)
    half_count = wave_rows.shape[1]
    slot_count = wave_rows.shape[2]
    field_count = wave_rows.shape[3]
    column_count = wave_rows.shape[4]
    degree_count = legendre.shape[1] * lax.axis_size(("lev", "fld"))
    weights = latitude_weights(half_count)[:, None, None, None]
    north_half = wave_rows[0].astype(jnp.float32)
    south_half = wave_rows[1].astype(jnp.float32)
    symmetric = (weights * (north_half + south_half)).astype(jnp.bfloat16)
    antisym = (weights * (north_half - south_half)).astype(jnp.bfloat16)
    paired = jnp.concatenate((symmetric, antisym), axis=3)

    def direct_rows(section, first_row):
        row_count = section.shape[1]
        degree = first_row + jnp.arange(row_count, dtype=jnp.int32)
        relative = degree[None, :] - slot_wave[:, None]
        product = jnp.einsum("snj,jsfc->snfc", section, paired, preferred_element_type=jnp.float32)
        is_even = (relative % 2 == 0)[:, :, None, None]
        is_live = (relative >= 0)[:, :, None, None]
        picked = jnp.where(is_even, product[..., :column_count], product[..., column_count:])
        return jnp.where(is_live, picked, jnp.zeros_like(picked))

    full_table = lax.all_gather(legendre, ("lev", "fld"), axis=1, tiled=True)
    block_rows = 128
    block_count = degree_count // block_rows

    def direct_step(block_index, buffer):
        first_row = block_index * block_rows
        section = lax.dynamic_slice_in_dim(full_table, first_row, block_rows, 1)
        result = direct_rows(section, first_row).astype(jnp.bfloat16)
        return lax.dynamic_update_slice_in_dim(buffer, result, first_row, 1)

    initial_raw = jnp.zeros((slot_count, degree_count, field_count, column_count), jnp.bfloat16)
    raw_spectral = lax.fori_loop(0, block_count, direct_step, initial_raw)
    own_levels = column_count // 2
    first_level = lax.axis_index("lev") * own_levels
    degree_real = jnp.arange(degree_count, dtype=jnp.float32)
    all_levels = lax.all_gather(raw_spectral, "lev", axis=3, tiled=True)
    level_count = all_levels.shape[3] // 2
    level_grid = all_levels.reshape(slot_count, degree_count, field_count, level_count, 2)
    weight_rows = lax.dynamic_slice_in_dim(to_modes, first_level, own_levels, 0)
    rate_rows = lax.dynamic_slice_in_dim(mode_rate, first_level, own_levels, 0)
    own_modes = project(level_grid, degree_real, weight_rows, rate_rows, degree_count).reshape(
        slot_count, degree_count, field_count, column_count
    )
    mode_values = lax.all_gather(own_modes, "lev", axis=3, tiled=True).reshape(
        slot_count, degree_count, field_count, level_count, 2
    )
    back_rows = lax.dynamic_slice_in_dim(from_modes, first_level, own_levels, 0)
    spectral = jnp.einsum(
        "lk,snfkr->snflr", back_rows, mode_values, preferred_element_type=jnp.float32
    )
    spectral = spectral.astype(jnp.bfloat16).reshape(
        slot_count, degree_count, field_count, column_count
    )

    def inverse_rows(running, section, first_row):
        row_count = section.shape[1]
        degree = first_row + jnp.arange(row_count, dtype=jnp.int32)
        relative = degree[None, :] - slot_wave[:, None]
        spec_rows = lax.dynamic_slice_in_dim(spectral, first_row, row_count, 1)
        even_mask = ((relative >= 0) & (relative % 2 == 0))[:, :, None, None]
        odd_mask = ((relative >= 0) & (relative % 2 == 1))[:, :, None, None]
        empty_rows = jnp.zeros_like(spec_rows)
        parity_split = jnp.concatenate(
            (
                jnp.where(even_mask, spec_rows, empty_rows),
                jnp.where(odd_mask, spec_rows, empty_rows),
            ),
            axis=3,
        )
        return running + jnp.einsum(
            "snj,snfc->jsfc", section, parity_split, preferred_element_type=jnp.float32
        )

    initial_sum = jnp.zeros((half_count, slot_count, field_count, 2 * column_count), jnp.float32)

    def inverse_step(block_index, running):
        first_row = block_index * block_rows
        section = lax.dynamic_slice_in_dim(full_table, first_row, block_rows, 1)
        return inverse_rows(running, section, first_row)

    running = lax.fori_loop(0, block_count, inverse_step, initial_sum)
    even_sum = running[..., :column_count]
    odd_sum = running[..., column_count:]
    fourier_wave = jnp.stack((even_sum + odd_sum, even_sum - odd_sum), axis=0).astype(jnp.bfloat16)
    fourier_out = lax.all_to_all(fourier_wave, "wide", split_axis=1, concat_axis=2, tiled=True)
    return (fourier_out, spectral)


def solution(mesh):
    in_specs = (
        P("ens", "wide", None, "fld", "lev"),
        P("wide", ("lev", "fld"), None),
        P("wide"),
        P(),
        P(),
        P(),
    )
    out_specs = (P("ens", "wide", None, "fld", "lev"), P(("ens", "wide"), None, "fld", "lev"))

    def body(fourier_input_rows, legendre, *rest):
        _, latitudes, slots, fields, lanes = fourier_input_rows.shape
        whole_tiles = (
            latitudes % 32 == 0
            and fields == 2
            and slots == mesh.shape["wide"] == 4
            and mesh.shape["lev"] == 2
            and lanes == 128
            and legendre.shape[1] % 64 == 0
            and legendre.shape[2] % 256 == 0
        )
        form = shards if whole_tiles else plain_shards
        return form(fourier_input_rows, legendre, *rest)

    return jax.shard_map(body, mesh=mesh, in_specs=in_specs, out_specs=out_specs, check_vma=False)
```

```python
import functools
import math

import jax
import jax.numpy as jnp
from jax import lax
from jax.experimental import pallas as pl
from jax.experimental.pallas import tpu as pltpu
from jax.sharding import PartitionSpec as P

VMEM_BYTES = 8 * 1024 * 1024


def latitude_weights(count):
    position = jnp.arange(count, dtype=jnp.float32)
    return jnp.sin(math.pi * (position + 0.5) / (2 * count))


def iota2(shape, dim):
    return lax.broadcasted_iota(jnp.int32, shape, dim)


def picks(condition):
    return jnp.where(condition, 1.0, 0.0).astype(jnp.bfloat16)


def dot32(a, b):
    return jnp.dot(a, b, preferred_element_type=jnp.float32)


def call(body, out_shape, name, flops, scratch=(), scalars=1, after=()):
    smem = pl.BlockSpec(memory_space=pltpu.SMEM)
    vmem = pl.BlockSpec(memory_space=pltpu.VMEM)

    def run(*operands):
        used = len(operands)

        def kernel(*refs):
            body(*refs[:used], *refs[used + len(after) :])

        return pl.pallas_call(
            kernel,
            out_shape=out_shape,
            in_specs=[smem] * scalars
            + [vmem] * (used - scalars)
            + [pl.BlockSpec(memory_space=pl.ANY)] * len(after),
            out_specs=jax.tree.map(lambda _: vmem, out_shape),
            scratch_shapes=list(scratch),
            compiler_params=pltpu.CompilerParams(vmem_limit_bytes=VMEM_BYTES),
            cost_estimate=pl.CostEstimate(flops=flops, bytes_accessed=0, transcendentals=0),
            name=name,
        )(*operands, *after)

    return run


def lane_order(lanes, lev, old, new):
    levels = lanes // 4
    part = lax.rem(new // (lanes // 2) + lev, 2)
    field = (new // levels) % 2
    return old == field * (lanes // 2) + 2 * (new % levels) + part


def first_parity(meta_ref, odd):
    return (meta_ref[0] + meta_ref[4] + odd) % 2


def split_body(slots, fields, block, meta_ref, rows_ref, weight_ref, *outs):
    latitudes = weight_ref.shape[0]
    group = slots * fields
    size = block * group
    out_row, in_row = iota2((size, size), 0), iota2((size, size), 1)
    pair = out_row // block
    slot = lax.rem(meta_ref[1] + pair // fields, slots)
    order = picks(in_row == (out_row % block) * group + slot * fields + pair % fields)
    lanes = fields * 128
    parts = picks(lane_order(lanes, meta_ref[2], iota2((lanes, lanes), 0), iota2((lanes, lanes), 1)))
    for first in range(0, latitudes, block):
        north = rows_ref[0, first * group : first * group + size, :]
        south = rows_ref[1, first * group : first * group + size, :]
        sorted_rows = dot32(order, jnp.concatenate((north, south), axis=1))
        up, down = sorted_rows[:, :128], sorted_rows[:, 128:]
        weight = weight_ref[first : first + block, :]
        halves = []
        sign = 1.0 - 2.0 * meta_ref[4].astype(jnp.float32)
        for mixed in (up + sign * down, up - sign * down):
            for shift in range(slots):
                at = shift * fields * block
                halves.append(jnp.concatenate(
                    [
                        (weight * mixed[at + f * block : at + f * block + block]).astype(jnp.bfloat16)
                        for f in range(fields)
                    ],
                    axis=1,
                ))
        turned = dot32(jnp.concatenate(halves, axis=0), parts).astype(jnp.bfloat16)
        for odd in range(2):
            for shift in range(slots):
                for d in range(2):
                    at = (odd * slots + shift) * block
                    outs[shift * 2 + d][odd, first : first + block, :] = turned[
                        at : at + block, d * 128 : d * 128 + 128
                    ]


def table_body(meta_ref, table_ref, both_ref, first_ref):
    rows, columns = table_ref.shape
    half = rows // 2
    out_row, in_row = iota2((rows, rows), 0), iota2((rows, rows), 1)
    odd = jnp.where(out_row < half, 0, 1)
    order = picks(in_row == 2 * (out_row - odd * half) + first_parity(meta_ref, odd))
    for first in range(0, columns, 256):
        lanes = slice(first, first + 256)
        result = dot32(order, table_ref[:, lanes]).astype(jnp.bfloat16)
        both_ref[:, lanes] = result
        first_ref[:, lanes] = result[:half]


def modes_body(sizes, degree_total, meta_ref, to_ref, from_ref, rate_ref, in_ref, out_ref, scale_ref):
    levels = to_ref.shape[0]
    wide = 2 * levels
    own = levels // 2
    lane, row = iota2((levels, wide), 1), iota2((levels, wide), 0)
    owner = lax.rem(meta_ref[2] + lane // levels, 2)
    spread = picks(row == owner * own + lane % own)
    plain = picks(row == lane % levels)
    old, new = iota2((wide, wide), 0), iota2((wide, wide), 1)

    def turned(first, matrix, last):
        half = lax.dot_general(first, matrix, (((0,), (1,)), ((), ())), preferred_element_type=jnp.float32)
        return dot32(half.astype(jnp.bfloat16), last)

    same = (old // own) % 2 == new // levels
    in_ref[...] = jnp.where(same, turned(spread, to_ref[...], plain), 0.0).astype(jnp.bfloat16)
    same = old // levels == (new // own) % 2
    out_ref[...] = jnp.where(same, turned(plain, from_ref[...], spread), 0.0).astype(jnp.bfloat16)
    wide, levs, flds = sizes
    rows = degree_total // (2 * levs * flds)
    for odd in range(2):
        for d in range(levs):
            for g in range(flds):
                block = lax.rem(meta_ref[2] + d, levs) * flds + lax.rem(meta_ref[3] + g, flds)
                degree = block * (2 * rows) + 2 * iota2((rows, 1), 0) + first_parity(meta_ref, odd)
                real = degree.astype(jnp.float32)
                factor = 1.0 + real * (real + 1.0) * rate_ref[...] / (degree_total * degree_total)
                at = ((odd * levs + d) * flds + g) * rows
                scale_ref[at : at + rows, :] = jnp.where(degree >= meta_ref[0], 1.0 / factor, 0.0)


def rows_of(refs, odd, lanes):
    own, beside, far, far_beside = refs
    rows = own.shape[0] // 2
    half = slice(odd * rows, odd * rows + rows)
    return jnp.concatenate((own[half, lanes], beside[half, lanes], far[:, lanes], far_beside[:, lanes]), axis=0)


def forward_body(wide, odd, meta_ref, in_ref, out_ref, scale_ref, *refs):
    parts, tables, refs = refs[: wide * 2], refs[wide * 2 : -3], refs[-3:]
    own_ref, other_ref, data = refs
    latitudes, lanes = parts[0].shape[1:]
    rows = own_ref.shape[0]
    for shift in range(wide):
        owner = lax.rem(meta_ref[1] - shift + wide, wide)
        at = pl.ds(pl.multiple_of(owner * latitudes, latitudes), latitudes)
        for d in range(2):
            data[at, d * lanes : d * lanes + lanes] = parts[shift * 2 + d][odd]
    raw = dot32(rows_of(tables, odd, slice(None)), data[...]).astype(jnp.bfloat16)
    scale = jnp.concatenate([scale_ref[odd * rows : odd * rows + rows, :]] * 2, axis=1)
    modes = (dot32(raw, in_ref[...]) * scale).astype(jnp.bfloat16)
    spectral = dot32(modes, out_ref[...]).astype(jnp.bfloat16)
    own_ref[...] = spectral[:, :lanes]
    other_ref[...] = spectral[:, lanes:]


def inverse_body(wide, meta_ref, *refs):
    parts, tables, outs, total = refs[:4], (refs[4:8], refs[4:6] + refs[8:10]), refs[10:-1], refs[-1]
    latitudes, lanes = outs[0].shape[1:]
    spectral = [jnp.concatenate((parts[2 * odd][...], parts[2 * odd + 1][...]), axis=1) for odd in range(2)]
    sign = 1.0 - 2.0 * meta_ref[4].astype(jnp.float32)
    for first in range(0, total.shape[1], 256):
        chunk = slice(first, first + 256)
        sums = [
            lax.dot_general(
                rows_of(tables[odd], odd, chunk), spectral[odd], (((0,), (0,)), ((), ())),
                preferred_element_type=jnp.float32,
            )
            for odd in range(2)
        ]
        total[0, chunk, :] = (sums[0] + sums[1]).astype(jnp.bfloat16)
        total[1, chunk, :] = (sign * (sums[0] - sums[1])).astype(jnp.bfloat16)
    for shift in range(wide):
        owner = lax.rem(meta_ref[1] + shift, wide)
        at = pl.ds(pl.multiple_of(owner * latitudes, latitudes), latitudes)
        for d in range(2):
            outs[shift * 2 + d][...] = total[:, at, d * lanes : d * lanes + lanes]


def join_body(slots, block, meta_ref, *refs):
    parts, out_ref = refs[:-1], refs[-1]
    latitudes, lanes = parts[0].shape[1:]
    fields = 2
    group = slots * fields
    size = block * group
    out_row, in_row = iota2((size, size), 0), iota2((size, size), 1)
    place = out_row % group
    shift = lax.rem(meta_ref[1] - place // fields + slots, slots)
    order = picks(in_row == (shift * fields + place % fields) * block + out_row // group)
    both = 2 * lanes
    turn = picks(lane_order(both, meta_ref[2], iota2((both, both), 1), iota2((both, both), 0)))
    for first in range(0, latitudes, block):
        at = slice(first, first + block)
        stacked = jnp.concatenate(
            [
                jnp.concatenate([parts[shift * 2 + d][half, at, :] for d in range(2)], axis=1)
                for half in range(2)
                for shift in range(slots)
            ],
            axis=0,
        )
        turned = dot32(stacked, turn).astype(jnp.bfloat16)
        halves = [
            jnp.concatenate(
                [
                    turned[
                        (half * slots + shift) * block : (half * slots + shift + 1) * block,
                        field * lanes : field * lanes + lanes,
                    ]
                    for shift in range(slots)
                    for field in range(fields)
                ],
                axis=0,
            )
            for half in range(2)
        ]
        result = dot32(order, jnp.concatenate(halves, axis=1)).astype(jnp.bfloat16)
        for half in range(2):
            out_ref[half, first * group : first * group + size, :] = result[:, half * lanes : half * lanes + lanes]


def rows_body(sizes, block, meta_ref, *refs):
    wide, levs, flds = sizes
    own_refs, other_refs, out_ref = refs[:2], refs[2:4], refs[4]
    total_rows, lanes = own_refs[0].shape
    rows = total_rows // (levs * flds)
    fields = 2
    group = 2 * fields
    size = block * group
    out_row, in_row = iota2((size, size), 0), iota2((size, size), 1)
    place = out_row % group
    odd = (place // fields + first_parity(meta_ref, 0)) % 2
    order = picks(in_row == (odd * fields + place % fields) * block + out_row // group)
    both = 2 * lanes
    turn = picks(lane_order(both, meta_ref[2], iota2((both, both), 1), iota2((both, both), 0)))
    for d in range(levs):
        for g in range(flds):
            index = lax.rem(meta_ref[2] + d, levs) * flds + lax.rem(meta_ref[3] + g, flds)
            halves = []
            for odd in range(2):
                mine, theirs = (d * flds + g) * rows, ((1 - d) * flds + g) * rows
                halves.append(jnp.concatenate(
                    (own_refs[odd][mine : mine + rows, :], other_refs[odd][theirs : theirs + rows, :]), axis=1
                ))
            turned = dot32(jnp.concatenate(halves, axis=0), turn).astype(jnp.bfloat16)
            for first in range(0, rows, block):
                stacked = jnp.concatenate(
                    [
                        turned[
                            odd * rows + first : odd * rows + first + block, field * lanes : field * lanes + lanes
                        ]
                        for odd in range(2)
                        for field in range(fields)
                    ],
                    axis=0,
                )
                start = pl.multiple_of(index * (rows * group), rows * group) + first * group
                out_ref[pl.ds(start, size), :] = dot32(order, stacked).astype(jnp.bfloat16)


def shards(fourier_input_rows, legendre, slot_wave, to_modes, from_modes, mode_rate):
    wide, levs, flds = (lax.axis_size(axis) for axis in ("wide", "lev", "fld"))
    sizes = (wide, levs, flds)
    _, latitudes, slots, fields, lanes = fourier_input_rows.shape
    _, shard_rows, half_count = legendre.shape
    degree_count = shard_rows * levs * flds
    group = slots * fields
    columns = fields * lanes
    block = 256 // group
    levels = to_modes.shape[0]
    bf16 = jnp.bfloat16

    def shape(*dims):
        return jax.ShapeDtypeStruct(dims, bf16)

    def shifted(value, axis, count, step):
        return lax.ppermute(value, axis, [(i, (i + step) % count) for i in range(count)])

    def exchanged(blocks):
        arrived = {(0, 0): blocks[0]}
        for k, d, behind in ((0, 1, None), (2, 0, None), (1, 0, None), (3, 0, None), (2, 1, (0, 1)), (1, 1, (1, 0)), (3, 1, (3, 0))):
            value = blocks[k * levs + d]
            if behind:
                value, arrived[behind] = lax.optimization_barrier((value, arrived[behind]))
            pairs = [
                (w * levs + l, (w + k) % wide * levs + (l + d) % levs) for w in range(wide) for l in range(levs)
            ]
            arrived[k, d] = lax.ppermute(value, ("wide", "lev"), pairs)
        return [arrived[k, d] for k in range(wide) for d in range(levs)]

    wide_at, lev_at, fld_at = (lax.axis_index(axis) for axis in ("wide", "lev", "fld"))
    meta = jnp.stack((slot_wave[0], wide_at, lev_at, fld_at, lax.axis_index("ens"))).astype(jnp.int32)
    position = (wide_at * latitudes + jnp.arange(latitudes, dtype=jnp.int32)).astype(jnp.float32)
    weights = jnp.sin(math.pi * (position + 0.5) / (2 * half_count))
    weights = jnp.broadcast_to(weights[:, None], (latitudes, lanes))
    move_flops = 8 * group * latitudes * 128 * 256
    transform_flops = 2 * degree_count * half_count * columns

    blocks = call(
        functools.partial(split_body, slots, fields, block), (shape(2, latitudes, lanes),) * (wide * levs),
        "split_hemispheres", move_flops,
    )(meta, fourier_input_rows.reshape(2, latitudes * group, lanes), weights)
    data = exchanged(blocks)
    part, first = call(
        table_body, (shape(shard_rows, half_count), shape(shard_rows // 2, half_count)), "split_table",
        2 * shard_rows * shard_rows * half_count, after=(blocks[0],),
    )(meta, legendre[0])
    first = shifted(first, "lev", levs, 1)
    ahead = [1, levs, 2 * levs, 3 * levs]
    first, *ahead_data = lax.optimization_barrier((first, *(data[i] for i in ahead)))
    data = [dict(zip(ahead, ahead_data)).get(i, one) for i, one in enumerate(data)]
    second = shifted(first, "ens", 2, 1)
    ahead = [levs + 1, 2 * levs + 1, 3 * levs + 1]
    second, *ahead_data = lax.optimization_barrier((second, *(data[i] for i in ahead)))
    data = [dict(zip(ahead, ahead_data)).get(i, one) for i, one in enumerate(data)]
    near = [part, shifted(part, "fld", flds, 1)]
    far = [[one, shifted(one, "fld", flds, 1)] for one in (first, second)]
    *matrices, scale = call(
        functools.partial(modes_body, sizes, degree_count),
        (shape(2 * levels, 2 * levels),) * 2 + (jax.ShapeDtypeStruct((degree_count, levels), jnp.float32),),
        "spread_modes", 12 * levels * levels * levels, after=(part,),
    )(meta, to_modes, from_modes, mode_rate[None, :])

    half_rows = degree_count // 2
    spectral = [
        call(
            functools.partial(forward_body, wide, odd), (shape(half_rows, lanes),) * 2,
            "direct_legendre_and_solve", transform_flops // 2,
            scratch=[pltpu.VMEM((half_count, columns), bf16)],
        )(meta, *matrices, scale, *data, *near, *far[odd])
        for odd in range(2)
    ]
    grid = call(
        functools.partial(inverse_body, wide), (shape(2, latitudes, lanes),) * (wide * levs),
        "inverse_legendre", transform_flops, scratch=[pltpu.VMEM((2, half_count, columns), bf16)],
    )(meta, *spectral[0], *spectral[1], *near, *far[0], *far[1])
    result = exchanged(grid)
    spectral_rows = call(
        functools.partial(rows_body, sizes, 32), shape(degree_count * fields, lanes), "order_spectral", 0,
    )(meta, *(own for own, _ in spectral), *(shifted(other, "lev", levs, 1) for _, other in spectral))
    fourier_rows = call(
        functools.partial(join_body, slots, block), shape(2, latitudes * group, lanes),
        "join_hemispheres", move_flops, after=(spectral_rows,),
    )(meta, *result)
    return (
        fourier_rows.reshape(2, latitudes, slots, fields, lanes),
        spectral_rows.reshape(1, degree_count, fields, lanes),
    )


def project(level_grid, degree_real, weight_rows, rate_rows, degree_total):
    projected = jnp.einsum(
        "kl,snflr->snfkr", weight_rows, level_grid, preferred_element_type=jnp.float32
    )
    factor = 1.0 + degree_real[:, None] * (degree_real[:, None] + 1.0) * rate_rows[None, :] / (
        degree_total * degree_total
    )
    return (projected / factor[None, :, None, :, None]).astype(jnp.bfloat16)


def plain_shards(fourier_input_rows, legendre, slot_wave, to_modes, from_modes, mode_rate):
    wave_rows = lax.all_to_all(fourier_input_rows, "wide", split_axis=2, concat_axis=1, tiled=True)
    half_count = wave_rows.shape[1]
    slot_count = wave_rows.shape[2]
    field_count = wave_rows.shape[3]
    column_count = wave_rows.shape[4]
    degree_count = legendre.shape[1] * lax.axis_size(("lev", "fld"))
    weights = latitude_weights(half_count)[:, None, None, None]
    north_half = wave_rows[0].astype(jnp.float32)
    south_half = wave_rows[1].astype(jnp.float32)
    symmetric = (weights * (north_half + south_half)).astype(jnp.bfloat16)
    antisym = (weights * (north_half - south_half)).astype(jnp.bfloat16)
    paired = jnp.concatenate((symmetric, antisym), axis=3)

    def direct_rows(section, first_row):
        row_count = section.shape[1]
        degree = first_row + jnp.arange(row_count, dtype=jnp.int32)
        relative = degree[None, :] - slot_wave[:, None]
        product = jnp.einsum("snj,jsfc->snfc", section, paired, preferred_element_type=jnp.float32)
        is_even = (relative % 2 == 0)[:, :, None, None]
        is_live = (relative >= 0)[:, :, None, None]
        picked = jnp.where(is_even, product[..., :column_count], product[..., column_count:])
        return jnp.where(is_live, picked, jnp.zeros_like(picked))

    full_table = lax.all_gather(legendre, ("lev", "fld"), axis=1, tiled=True)
    block_rows = 128
    block_count = degree_count // block_rows

    def direct_step(block_index, buffer):
        first_row = block_index * block_rows
        section = lax.dynamic_slice_in_dim(full_table, first_row, block_rows, 1)
        result = direct_rows(section, first_row).astype(jnp.bfloat16)
        return lax.dynamic_update_slice_in_dim(buffer, result, first_row, 1)

    initial_raw = jnp.zeros((slot_count, degree_count, field_count, column_count), jnp.bfloat16)
    raw_spectral = lax.fori_loop(0, block_count, direct_step, initial_raw)
    own_levels = column_count // 2
    first_level = lax.axis_index("lev") * own_levels
    degree_real = jnp.arange(degree_count, dtype=jnp.float32)
    all_levels = lax.all_gather(raw_spectral, "lev", axis=3, tiled=True)
    level_count = all_levels.shape[3] // 2
    level_grid = all_levels.reshape(slot_count, degree_count, field_count, level_count, 2)
    weight_rows = lax.dynamic_slice_in_dim(to_modes, first_level, own_levels, 0)
    rate_rows = lax.dynamic_slice_in_dim(mode_rate, first_level, own_levels, 0)
    own_modes = project(level_grid, degree_real, weight_rows, rate_rows, degree_count).reshape(
        slot_count, degree_count, field_count, column_count
    )
    mode_values = lax.all_gather(own_modes, "lev", axis=3, tiled=True).reshape(
        slot_count, degree_count, field_count, level_count, 2
    )
    back_rows = lax.dynamic_slice_in_dim(from_modes, first_level, own_levels, 0)
    spectral = jnp.einsum(
        "lk,snfkr->snflr", back_rows, mode_values, preferred_element_type=jnp.float32
    )
    spectral = spectral.astype(jnp.bfloat16).reshape(
        slot_count, degree_count, field_count, column_count
    )

    def inverse_rows(running, section, first_row):
        row_count = section.shape[1]
        degree = first_row + jnp.arange(row_count, dtype=jnp.int32)
        relative = degree[None, :] - slot_wave[:, None]
        spec_rows = lax.dynamic_slice_in_dim(spectral, first_row, row_count, 1)
        even_mask = ((relative >= 0) & (relative % 2 == 0))[:, :, None, None]
        odd_mask = ((relative >= 0) & (relative % 2 == 1))[:, :, None, None]
        empty_rows = jnp.zeros_like(spec_rows)
        parity_split = jnp.concatenate(
            (
                jnp.where(even_mask, spec_rows, empty_rows),
                jnp.where(odd_mask, spec_rows, empty_rows),
            ),
            axis=3,
        )
        return running + jnp.einsum(
            "snj,snfc->jsfc", section, parity_split, preferred_element_type=jnp.float32
        )

    initial_sum = jnp.zeros((half_count, slot_count, field_count, 2 * column_count), jnp.float32)

    def inverse_step(block_index, running):
        first_row = block_index * block_rows
        section = lax.dynamic_slice_in_dim(full_table, first_row, block_rows, 1)
        return inverse_rows(running, section, first_row)

    running = lax.fori_loop(0, block_count, inverse_step, initial_sum)
    even_sum = running[..., :column_count]
    odd_sum = running[..., column_count:]
    fourier_wave = jnp.stack((even_sum + odd_sum, even_sum - odd_sum), axis=0).astype(jnp.bfloat16)
    fourier_out = lax.all_to_all(fourier_wave, "wide", split_axis=1, concat_axis=2, tiled=True)
    return (fourier_out, spectral)


def solution(mesh):
    in_specs = (
        P("ens", "wide", None, "fld", "lev"),
        P("wide", ("lev", "fld"), None),
        P("wide"),
        P(),
        P(),
        P(),
    )
    out_specs = (P("ens", "wide", None, "fld", "lev"), P(("ens", "wide"), None, "fld", "lev"))

    def body(fourier_input_rows, legendre, *rest):
        _, latitudes, slots, fields, lanes = fourier_input_rows.shape
        whole_tiles = (
            latitudes % 32 == 0
            and fields == 2
            and slots == mesh.shape["wide"] == 4
            and mesh.shape["ens"] == mesh.shape["lev"] == mesh.shape["fld"] == 2
            and lanes == 128
            and legendre.shape[1] % 64 == 0
            and legendre.shape[2] % 256 == 0
        )
        form = shards if whole_tiles else plain_shards
        return form(fourier_input_rows, legendre, *rest)

    return jax.shard_map(body, mesh=mesh, in_specs=in_specs, out_specs=out_specs, check_vma=False)
```

```python
import functools
import math

import jax
import jax.numpy as jnp
from jax import lax
from jax.experimental import pallas as pl
from jax.experimental.pallas import tpu as pltpu
from jax.sharding import PartitionSpec as P

VMEM_BYTES = 8 * 1024 * 1024


def latitude_weights(count):
    position = jnp.arange(count, dtype=jnp.float32)
    return jnp.sin(math.pi * (position + 0.5) / (2 * count))


def iota2(shape, dim):
    return lax.broadcasted_iota(jnp.int32, shape, dim)


def picks(condition):
    return jnp.where(condition, 1.0, 0.0).astype(jnp.bfloat16)


def dot32(a, b):
    return jnp.dot(a, b, preferred_element_type=jnp.float32)


def call(body, out_shape, name, flops, scratch=(), scalars=1, after=()):
    smem = pl.BlockSpec(memory_space=pltpu.SMEM)
    vmem = pl.BlockSpec(memory_space=pltpu.VMEM)

    def run(*operands):
        used = len(operands)

        def kernel(*refs):
            body(*refs[:used], *refs[used + len(after) :])

        return pl.pallas_call(
            kernel,
            out_shape=out_shape,
            in_specs=[smem] * scalars
            + [vmem] * (used - scalars)
            + [pl.BlockSpec(memory_space=pl.ANY)] * len(after),
            out_specs=jax.tree.map(lambda _: vmem, out_shape),
            scratch_shapes=list(scratch),
            compiler_params=pltpu.CompilerParams(vmem_limit_bytes=VMEM_BYTES),
            cost_estimate=pl.CostEstimate(flops=flops, bytes_accessed=0, transcendentals=0),
            name=name,
        )(*operands, *after)

    return run


def split_body(slots, fields, block, odd, meta_ref, rows_ref, weight_ref, *outs):
    latitudes = weight_ref.shape[0]
    group = slots * fields
    size = block * group
    out_row, in_row = iota2((size, size), 0), iota2((size, size), 1)
    pair = out_row // block
    slot = lax.rem(meta_ref[1] + pair // fields, slots)
    order = picks(in_row == (out_row % block) * group + slot * fields + pair % fields)
    for first in range(0, latitudes, block):
        north = rows_ref[0, first * group : first * group + size, :]
        south = rows_ref[1, first * group : first * group + size, :]
        sorted_rows = dot32(order, jnp.concatenate((north, south), axis=1))
        up, down = sorted_rows[:, :128], sorted_rows[:, 128:]
        mixed = up - down if odd else up + down
        weight = weight_ref[first : first + block, :]
        for shift in range(slots):
            for field in range(fields):
                at = (shift * fields + field) * block
                outs[shift][first : first + block, field * 128 : field * 128 + 128] = (
                    weight * mixed[at : at + block]
                ).astype(jnp.bfloat16)


def table_body(odd, meta_ref, table_ref, out_ref):
    rows, columns = table_ref.shape
    half = rows // 2
    out_row, in_row = iota2((half, rows), 0), iota2((half, rows), 1)
    order = picks(in_row == 2 * out_row + (meta_ref[0] + odd) % 2)
    for first in range(0, columns, 256):
        lanes = slice(first, first + 256)
        out_ref[:, lanes] = dot32(order, table_ref[:, lanes]).astype(jnp.bfloat16)


def modes_body(flds, degree_total, meta_ref, to_ref, from_ref, rate_ref, in_ref, out_ref, scale_ref):
    levels = to_ref.shape[0]
    wide = 2 * levels
    own = levels // 2
    lane, row = iota2((levels, wide), 1), iota2((levels, wide), 0)
    owner = lax.rem(meta_ref[2] + lane // (2 * own), 2)
    spread = picks(row == owner * own + (lane % (2 * own)) // 2)
    plain = picks(row == lane // 2)
    same = (iota2((wide, wide), 0) % 2) == (iota2((wide, wide), 1) % 2)

    def turned(first, matrix, last):
        half = lax.dot_general(first, matrix, (((0,), (1,)), ((), ())), preferred_element_type=jnp.float32)
        return jnp.where(same, dot32(half.astype(jnp.bfloat16), last), 0.0).astype(jnp.bfloat16)

    in_ref[...] = turned(spread, to_ref[...], plain)
    out_ref[...] = turned(plain, from_ref[...], spread)
    square = (levels, levels)
    diagonal = jnp.where(iota2(square, 0) == iota2(square, 1), rate_ref[...], 0.0)
    column = jnp.sum(diagonal, axis=1, keepdims=True)
    rates = jnp.sum(jnp.where(row == lane // 2, column, 0.0), axis=0, keepdims=True)
    rows = scale_ref.shape[0] // (2 * flds)
    for odd in range(2):
        for g in range(flds):
            block = (1 - meta_ref[2]) * flds + lax.rem(meta_ref[3] + g, flds)
            degree = block * (2 * rows) + 2 * iota2((rows, 1), 0) + (meta_ref[0] + odd) % 2
            real = degree.astype(jnp.float32)
            factor = 1.0 + real * (real + 1.0) * rates / (degree_total * degree_total)
            at = (odd * flds + g) * rows
            scale_ref[at : at + rows, :] = jnp.where(degree >= meta_ref[0], 1.0 / factor, 0.0)


def near_body(meta_ref, *refs):
    parts, tables, (out_ref, data_ref) = refs[:-4], refs[-4:-2], refs[-2:]
    wide, latitudes = len(parts), parts[0].shape[0]
    for shift in range(wide):
        owner = lax.rem(meta_ref[1] - shift + wide, wide)
        data_ref[pl.ds(pl.multiple_of(owner * latitudes, latitudes), latitudes), :] = parts[shift][...]
    table = jnp.concatenate([ref[...] for ref in tables], axis=0)
    out_ref[...] = dot32(table, data_ref[...]).astype(jnp.bfloat16)


def far_body(data_ref, first_ref, second_ref, out_ref):
    table = jnp.concatenate((first_ref[...], second_ref[...]), axis=0)
    out_ref[...] = dot32(table, data_ref[...]).astype(jnp.bfloat16)


def solve_body(odd, own_ref, other_ref, in_ref, out_ref, scale_ref, to_own_ref, to_other_ref):
    rows, columns = own_ref.shape
    for lanes in (slice(first, first + 128) for first in range(0, columns, 128)):
        level_grid = jnp.concatenate((own_ref[:, lanes], other_ref[:, lanes]), axis=1)
        scale = scale_ref[odd * rows : odd * rows + rows, :]
        modes = (dot32(level_grid, in_ref[...]) * scale).astype(jnp.bfloat16)
        result = dot32(modes, out_ref[...]).astype(jnp.bfloat16)
        to_own_ref[:, lanes] = result[:, :128]
        to_other_ref[:, lanes] = result[:, 128:]


def turned_dot(tables, spectral, chunk):
    table = jnp.concatenate([ref[:, chunk] for ref in tables], axis=0)
    return lax.dot_general(table, spectral, (((0,), (0,)), ((), ())), preferred_element_type=jnp.float32)


def inverse_far_body(spectral_ref, first_ref, second_ref, out_ref):
    for first in range(0, out_ref.shape[0], 256):
        chunk = slice(first, first + 256)
        out_ref[chunk, :] = turned_dot((first_ref, second_ref), spectral_ref[...], chunk)


def inverse_near_body(meta_ref, sum_ref, spectral_ref, first_ref, second_ref, *refs):
    outs, total = refs[:-1], refs[-1]
    wide, latitudes = len(outs), outs[0].shape[0]
    for first in range(0, total.shape[0], 256):
        chunk = slice(first, first + 256)
        more = turned_dot((first_ref, second_ref), spectral_ref[...], chunk)
        total[chunk, :] = (sum_ref[chunk, :] + more).astype(jnp.bfloat16)
    for shift in range(wide):
        owner = lax.rem(meta_ref[1] + shift, wide)
        outs[shift][...] = total[pl.ds(pl.multiple_of(owner * latitudes, latitudes), latitudes), :]


def join_body(wide, block, meta_ref, *refs):
    evens, odds, out_ref = refs[:wide], refs[wide : 2 * wide], refs[2 * wide]
    latitudes, columns = evens[0].shape
    fields = columns // 128
    group = wide * fields
    size = block * group
    out_row, in_row = iota2((size, size), 0), iota2((size, size), 1)
    place = out_row % group
    shift = lax.rem(meta_ref[1] - place // fields + wide, wide)
    order = picks(in_row == (shift * fields + place % fields) * block + out_row // group)

    def stack(parts, first):
        return jnp.concatenate(
            [
                part[first : first + block, field * 128 : field * 128 + 128]
                for part in parts
                for field in range(fields)
            ],
            axis=0,
        )

    for first in range(0, latitudes, block):
        both = dot32(order, jnp.concatenate((stack(evens, first), stack(odds, first)), axis=1))
        even, odd = both[:, :128], both[:, 128:]
        out_ref[0, first * group : first * group + size, :] = (even + odd).astype(jnp.bfloat16)
        out_ref[1, first * group : first * group + size, :] = (even - odd).astype(jnp.bfloat16)


def rows_body(flds, block, meta_ref, *refs):
    parts, out_ref = (refs[:2], refs[2:4]), refs[4]
    total_rows, columns = refs[0].shape
    rows = total_rows // flds
    fields = columns // 128
    group = 2 * fields
    size = block * group
    parity = meta_ref[0] % 2
    out_row, in_row = iota2((size, size), 0), iota2((size, size), 1)
    place = out_row % group
    odd = (place // fields + parity) % 2
    order = picks(in_row == (odd * fields + place % fields) * block + out_row // group)
    for d in range(2):
        for g in range(flds):
            index = lax.rem(meta_ref[2] + d, 2) * flds + lax.rem(meta_ref[3] + g, flds)
            for first in range(0, rows, block):
                at = slice(g * rows + first, g * rows + first + block)
                stacked = jnp.concatenate(
                    [
                        part[d][at, field * 128 : field * 128 + 128]
                        for part in parts
                        for field in range(fields)
                    ],
                    axis=0,
                )
                start = pl.multiple_of(index * (rows * group), rows * group) + first * group
                out_ref[pl.ds(start, size), :] = dot32(order, stacked).astype(jnp.bfloat16)


def shards(fourier_input_rows, legendre, slot_wave, to_modes, from_modes, mode_rate):
    wide, levs, flds = (lax.axis_size(axis) for axis in ("wide", "lev", "fld"))
    _, latitudes, slots, fields, lanes = fourier_input_rows.shape
    _, shard_rows, half_count = legendre.shape
    degree_count = shard_rows * levs * flds
    columns = fields * lanes
    group = slots * fields
    half_rows = shard_rows // 2
    share = flds * half_rows
    levels = to_modes.shape[0]
    block = 256 // group
    bf16, f32 = jnp.bfloat16, jnp.float32

    def shape(*dims, kind=bf16):
        return jax.ShapeDtypeStruct(dims, kind)

    def shifted(value, axis, count, step):
        return lax.ppermute(value, axis, [(i, (i + step) % count) for i in range(count)])

    def across(value, step):
        return shifted(value, "wide", wide, step)

    def behind(value, *others):
        return lax.optimization_barrier((value, *others))

    wide_at, lev_at, fld_at = (lax.axis_index(axis) for axis in ("wide", "lev", "fld"))
    meta = jnp.stack((slot_wave[0], wide_at, lev_at, fld_at)).astype(jnp.int32)
    position = (wide_at * latitudes + jnp.arange(latitudes, dtype=jnp.int32)).astype(f32)
    weights = jnp.sin(math.pi * (position + 0.5) / (2 * half_count))
    weights = jnp.broadcast_to(weights[:, None], (latitudes, lanes))
    move_flops = 4 * group * latitudes * 128 * 256
    share_flops = 2 * share * half_count * columns

    def split(odd, after=()):
        return call(
            functools.partial(split_body, slots, fields, block, odd), (shape(latitudes, columns),) * wide,
            "split_hemispheres", move_flops, after=after,
        )(meta, fourier_input_rows.reshape(2, latitudes * group, lanes), weights)

    def split_table(odd, after):
        return call(
            functools.partial(table_body, odd), shape(half_rows, half_count), "split_table",
            shard_rows * shard_rows * half_count, after=after,
        )(meta, legendre[0])

    def direct_near(received, table):
        return call(
            near_body, (shape(share, columns), shape(half_count, columns)), "direct_legendre_near", share_flops
        )(meta, *received, *table)

    def direct_far(data, table):
        return call(far_body, shape(share, columns), "direct_legendre_far", share_flops, scalars=0)(data, *table)

    def solve(odd, own, other):
        return call(
            functools.partial(solve_body, odd), (shape(share, columns),) * 2, "vertical_solve",
            16 * share * fields * levels * levels, scalars=0,
        )(own, other, *matrices)

    def inverse_far(spectral, table):
        return call(
            inverse_far_body, shape(half_count, columns, kind=f32), "inverse_legendre_far", share_flops, scalars=0,
        )(spectral, *table)

    def inverse_near(total, spectral, table):
        return call(
            inverse_near_body, (shape(latitudes, columns),) * wide, "inverse_legendre_near", share_flops,
            scratch=[pltpu.VMEM((half_count, columns), bf16)],
        )(meta, total, spectral, *table)

    def over_lev(value):
        return shifted(value, "lev", levs, 1)

    def beside(value):
        return shifted(value, "fld", flds, 1)

    even = split(0)
    even_in = [even[0]] + [across(even[step], step) for step in range(1, wide)]
    part = split_table(0, (even[0],))
    even_near, even_far = [part, beside(part)], over_lev(part)
    even_far, *even_in[1:] = behind(even_far, *even_in[1:])
    even_far = [even_far, beside(even_far)]
    odd = split(1, (even_near[1],))
    odd_part = split_table(1, (odd[0],))
    *matrices, scale = call(
        functools.partial(modes_body, flds, degree_count),
        (shape(2 * levels, 2 * levels),) * 2 + (shape(2 * share, 2 * levels, kind=f32),),
        "spread_modes", 12 * levels * levels * levels, after=(odd_part,),
    )(meta, to_modes, from_modes, mode_rate[None, :])
    matrices = (*matrices, scale)

    odd_in = [odd[0]] + [across(odd[step], step) for step in range(1, wide)]
    odd_near, odd_far = [odd_part, beside(odd_part)], over_lev(odd_part)
    odd_far = [odd_far, beside(odd_far)]
    raw, data = direct_near(even_in, even_near)
    other, odd_in[2] = behind(over_lev(raw), odd_in[2])
    to_own, to_other = solve(0, direct_far(data, even_far), other)
    total = inverse_far(to_own, even_far)
    from_other, odd_in[1], odd_in[3] = behind(over_lev(to_other), odd_in[1], odd_in[3])
    even_spectral = [from_other, to_own]
    grid = inverse_near(total, from_other, even_near)

    even_out = [grid[0]] + [across(grid[step], step) for step in range(1, wide)]
    raw, data = direct_near(odd_in, odd_near)
    other, even_out[2] = behind(over_lev(raw), even_out[2])
    to_own, to_other = solve(1, direct_far(data, odd_far), other)
    total = inverse_far(to_own, odd_far)
    from_other, even_out[1], even_out[3] = behind(over_lev(to_other), even_out[1], even_out[3])
    odd_spectral = [from_other, to_own]
    grid = inverse_near(total, from_other, odd_near)
    odd_out = [grid[0]] + [across(grid[step], step) for step in range(1, wide)]

    spectral_rows = call(
        functools.partial(rows_body, flds, 32), shape(degree_count * fields, lanes), "order_spectral", 0,
        after=(grid[0],),
    )(meta, *even_spectral, *odd_spectral)
    fourier_rows = call(
        functools.partial(join_body, wide, block), shape(2, latitudes * group, lanes), "join_hemispheres", move_flops,
    )(meta, *even_out, *odd_out)
    return (
        fourier_rows.reshape(2, latitudes, slots, fields, lanes),
        spectral_rows.reshape(1, degree_count, fields, lanes),
    )


def project(level_grid, degree_real, weight_rows, rate_rows, degree_total):
    projected = jnp.einsum(
        "kl,snflr->snfkr", weight_rows, level_grid, preferred_element_type=jnp.float32
    )
    factor = 1.0 + degree_real[:, None] * (degree_real[:, None] + 1.0) * rate_rows[None, :] / (
        degree_total * degree_total
    )
    return (projected / factor[None, :, None, :, None]).astype(jnp.bfloat16)


def plain_shards(fourier_input_rows, legendre, slot_wave, to_modes, from_modes, mode_rate):
    wave_rows = lax.all_to_all(fourier_input_rows, "wide", split_axis=2, concat_axis=1, tiled=True)
    half_count = wave_rows.shape[1]
    slot_count = wave_rows.shape[2]
    field_count = wave_rows.shape[3]
    column_count = wave_rows.shape[4]
    degree_count = legendre.shape[1] * lax.axis_size(("lev", "fld"))
    weights = latitude_weights(half_count)[:, None, None, None]
    north_half = wave_rows[0].astype(jnp.float32)
    south_half = wave_rows[1].astype(jnp.float32)
    symmetric = (weights * (north_half + south_half)).astype(jnp.bfloat16)
    antisym = (weights * (north_half - south_half)).astype(jnp.bfloat16)
    paired = jnp.concatenate((symmetric, antisym), axis=3)

    def direct_rows(section, first_row):
        row_count = section.shape[1]
        degree = first_row + jnp.arange(row_count, dtype=jnp.int32)
        relative = degree[None, :] - slot_wave[:, None]
        product = jnp.einsum("snj,jsfc->snfc", section, paired, preferred_element_type=jnp.float32)
        is_even = (relative % 2 == 0)[:, :, None, None]
        is_live = (relative >= 0)[:, :, None, None]
        picked = jnp.where(is_even, product[..., :column_count], product[..., column_count:])
        return jnp.where(is_live, picked, jnp.zeros_like(picked))

    full_table = lax.all_gather(legendre, ("lev", "fld"), axis=1, tiled=True)
    block_rows = 128
    block_count = degree_count // block_rows

    def direct_step(block_index, buffer):
        first_row = block_index * block_rows
        section = lax.dynamic_slice_in_dim(full_table, first_row, block_rows, 1)
        result = direct_rows(section, first_row).astype(jnp.bfloat16)
        return lax.dynamic_update_slice_in_dim(buffer, result, first_row, 1)

    initial_raw = jnp.zeros((slot_count, degree_count, field_count, column_count), jnp.bfloat16)
    raw_spectral = lax.fori_loop(0, block_count, direct_step, initial_raw)
    own_levels = column_count // 2
    first_level = lax.axis_index("lev") * own_levels
    degree_real = jnp.arange(degree_count, dtype=jnp.float32)
    all_levels = lax.all_gather(raw_spectral, "lev", axis=3, tiled=True)
    level_count = all_levels.shape[3] // 2
    level_grid = all_levels.reshape(slot_count, degree_count, field_count, level_count, 2)
    weight_rows = lax.dynamic_slice_in_dim(to_modes, first_level, own_levels, 0)
    rate_rows = lax.dynamic_slice_in_dim(mode_rate, first_level, own_levels, 0)
    own_modes = project(level_grid, degree_real, weight_rows, rate_rows, degree_count).reshape(
        slot_count, degree_count, field_count, column_count
    )
    mode_values = lax.all_gather(own_modes, "lev", axis=3, tiled=True).reshape(
        slot_count, degree_count, field_count, level_count, 2
    )
    back_rows = lax.dynamic_slice_in_dim(from_modes, first_level, own_levels, 0)
    spectral = jnp.einsum(
        "lk,snfkr->snflr", back_rows, mode_values, preferred_element_type=jnp.float32
    )
    spectral = spectral.astype(jnp.bfloat16).reshape(
        slot_count, degree_count, field_count, column_count
    )

    def inverse_rows(running, section, first_row):
        row_count = section.shape[1]
        degree = first_row + jnp.arange(row_count, dtype=jnp.int32)
        relative = degree[None, :] - slot_wave[:, None]
        spec_rows = lax.dynamic_slice_in_dim(spectral, first_row, row_count, 1)
        even_mask = ((relative >= 0) & (relative % 2 == 0))[:, :, None, None]
        odd_mask = ((relative >= 0) & (relative % 2 == 1))[:, :, None, None]
        empty_rows = jnp.zeros_like(spec_rows)
        parity_split = jnp.concatenate(
            (
                jnp.where(even_mask, spec_rows, empty_rows),
                jnp.where(odd_mask, spec_rows, empty_rows),
            ),
            axis=3,
        )
        return running + jnp.einsum(
            "snj,snfc->jsfc", section, parity_split, preferred_element_type=jnp.float32
        )

    initial_sum = jnp.zeros((half_count, slot_count, field_count, 2 * column_count), jnp.float32)

    def inverse_step(block_index, running):
        first_row = block_index * block_rows
        section = lax.dynamic_slice_in_dim(full_table, first_row, block_rows, 1)
        return inverse_rows(running, section, first_row)

    running = lax.fori_loop(0, block_count, inverse_step, initial_sum)
    even_sum = running[..., :column_count]
    odd_sum = running[..., column_count:]
    fourier_wave = jnp.stack((even_sum + odd_sum, even_sum - odd_sum), axis=0).astype(jnp.bfloat16)
    fourier_out = lax.all_to_all(fourier_wave, "wide", split_axis=1, concat_axis=2, tiled=True)
    return (fourier_out, spectral)


def solution(mesh):
    in_specs = (
        P("ens", "wide", None, "fld", "lev"),
        P("wide", ("lev", "fld"), None),
        P("wide"),
        P(),
        P(),
        P(),
    )
    out_specs = (P("ens", "wide", None, "fld", "lev"), P(("ens", "wide"), None, "fld", "lev"))

    def body(fourier_input_rows, legendre, *rest):
        _, latitudes, slots, fields, lanes = fourier_input_rows.shape
        whole_tiles = (
            latitudes % 32 == 0
            and fields == 2
            and slots == mesh.shape["wide"] == 4
            and mesh.shape["ens"] == mesh.shape["lev"] == mesh.shape["fld"] == 2
            and lanes == 128
            and legendre.shape[1] % 64 == 0
            and legendre.shape[2] % 256 == 0
        )
        form = shards if whole_tiles else plain_shards
        return form(fourier_input_rows, legendre, *rest)

    return jax.shard_map(body, mesh=mesh, in_specs=in_specs, out_specs=out_specs, check_vma=False)
```

```python
import functools
import math

import jax
import jax.numpy as jnp
from jax import lax
from jax.experimental import pallas as pl
from jax.experimental.pallas import tpu as pltpu
from jax.sharding import PartitionSpec as P

VMEM_BYTES = 8 * 1024 * 1024


def latitude_weights(count):
    position = jnp.arange(count, dtype=jnp.float32)
    return jnp.sin(math.pi * (position + 0.5) / (2 * count))


def iota2(shape, dim):
    return lax.broadcasted_iota(jnp.int32, shape, dim)


def picks(condition):
    return jnp.where(condition, 1.0, 0.0).astype(jnp.bfloat16)


def dot32(a, b):
    return jnp.dot(a, b, preferred_element_type=jnp.float32)


def call(body, out_shape, name, flops, scratch=(), scalars=1, after=()):
    smem = pl.BlockSpec(memory_space=pltpu.SMEM)
    vmem = pl.BlockSpec(memory_space=pltpu.VMEM)

    def run(*operands):
        used = len(operands)

        def kernel(*refs):
            body(*refs[:used], *refs[used + len(after) :])

        return pl.pallas_call(
            kernel,
            out_shape=out_shape,
            in_specs=[smem] * scalars
            + [vmem] * (used - scalars)
            + [pl.BlockSpec(memory_space=pl.ANY)] * len(after),
            out_specs=jax.tree.map(lambda _: vmem, out_shape),
            scratch_shapes=list(scratch),
            compiler_params=pltpu.CompilerParams(vmem_limit_bytes=VMEM_BYTES),
            cost_estimate=pl.CostEstimate(flops=flops, bytes_accessed=0, transcendentals=0),
            name=name,
        )(*operands, *after)

    return run


def split_body(slots, fields, block, meta_ref, rows_ref, weight_ref, *outs):
    latitudes = weight_ref.shape[0]
    group = slots * fields
    size = block * group
    out_row, in_row = iota2((size, size), 0), iota2((size, size), 1)
    pair = out_row // block
    slot = lax.rem(meta_ref[1] + pair // fields, slots)
    order = picks(in_row == (out_row % block) * group + slot * fields + pair % fields)
    for first in range(0, latitudes, block):
        north = rows_ref[0, first * group : first * group + size, :]
        south = rows_ref[1, first * group : first * group + size, :]
        sorted_rows = dot32(order, jnp.concatenate((north, south), axis=1))
        up, down = sorted_rows[:, :128], sorted_rows[:, 128:]
        weight = weight_ref[first : first + block, :]
        for odd, mixed in enumerate((up + down, up - down)):
            for shift in range(slots):
                for field in range(fields):
                    at = (shift * fields + field) * block
                    outs[odd * slots + shift][first : first + block, field * 128 : field * 128 + 128] = (
                        weight * mixed[at : at + block]
                    ).astype(jnp.bfloat16)


def table_body(meta_ref, first_ref, second_ref, even_ref, odd_ref):
    rows, columns = first_ref.shape
    half = rows // 2
    out_row, in_row = iota2((rows, rows), 0), iota2((rows, rows), 1)
    odd = jnp.where(out_row < half, 0, 1)
    order = picks(in_row == 2 * (out_row - odd * half) + (meta_ref[0] + odd) % 2)
    for g, table_ref in enumerate((first_ref, second_ref)):
        at = slice(g * half, g * half + half)
        for first in range(0, columns, 256):
            lanes = slice(first, first + 256)
            result = dot32(order, table_ref[:, lanes]).astype(jnp.bfloat16)
            even_ref[at, lanes] = result[:half]
            odd_ref[at, lanes] = result[half:]


def modes_body(flds, degree_total, meta_ref, to_ref, from_ref, rate_ref, in_ref, out_ref, scale_ref):
    levels = to_ref.shape[0]
    wide = 2 * levels
    own = levels // 2
    lane, row = iota2((levels, wide), 1), iota2((levels, wide), 0)
    owner = lax.rem(meta_ref[2] + lane // (2 * own), 2)
    spread = picks(row == owner * own + (lane % (2 * own)) // 2)
    plain = picks(row == lane // 2)
    same = (iota2((wide, wide), 0) % 2) == (iota2((wide, wide), 1) % 2)

    def turned(first, matrix, last):
        half = lax.dot_general(first, matrix, (((0,), (1,)), ((), ())), preferred_element_type=jnp.float32)
        return jnp.where(same, dot32(half.astype(jnp.bfloat16), last), 0.0).astype(jnp.bfloat16)

    in_ref[...] = turned(spread, to_ref[...], plain)
    out_ref[...] = turned(plain, from_ref[...], spread)
    square = (levels, levels)
    diagonal = jnp.where(iota2(square, 0) == iota2(square, 1), rate_ref[...], 0.0)
    column = jnp.sum(diagonal, axis=1, keepdims=True)
    rates = jnp.sum(jnp.where(row == lane // 2, column, 0.0), axis=0, keepdims=True)
    rows = scale_ref.shape[0] // (2 * flds)
    for odd in range(2):
        for g in range(flds):
            block = (1 - meta_ref[2]) * flds + lax.rem(meta_ref[3] + g, flds)
            degree = block * (2 * rows) + 2 * iota2((rows, 1), 0) + (meta_ref[0] + odd) % 2
            real = degree.astype(jnp.float32)
            factor = 1.0 + real * (real + 1.0) * rates / (degree_total * degree_total)
            at = (odd * flds + g) * rows
            scale_ref[at : at + rows, :] = jnp.where(degree >= meta_ref[0], 1.0 / factor, 0.0)


def near_body(meta_ref, *refs):
    parts, (table_ref, out_ref, data_ref) = refs[:-3], refs[-3:]
    wide, latitudes = len(parts), parts[0].shape[0]
    for shift in range(wide):
        owner = lax.rem(meta_ref[1] - shift + wide, wide)
        data_ref[pl.ds(pl.multiple_of(owner * latitudes, latitudes), latitudes), :] = parts[shift][...]
    out_ref[...] = dot32(table_ref[...], data_ref[...]).astype(jnp.bfloat16)


def far_body(data_ref, table_ref, out_ref):
    out_ref[...] = dot32(table_ref[...], data_ref[...]).astype(jnp.bfloat16)


def solve_body(odd, own_ref, other_ref, in_ref, out_ref, scale_ref, to_own_ref, to_other_ref):
    rows, columns = own_ref.shape
    for lanes in (slice(first, first + 128) for first in range(0, columns, 128)):
        level_grid = jnp.concatenate((own_ref[:, lanes], other_ref[:, lanes]), axis=1)
        scale = scale_ref[odd * rows : odd * rows + rows, :]
        modes = (dot32(level_grid, in_ref[...]) * scale).astype(jnp.bfloat16)
        result = dot32(modes, out_ref[...]).astype(jnp.bfloat16)
        to_own_ref[:, lanes] = result[:, :128]
        to_other_ref[:, lanes] = result[:, 128:]


def turned_dot(table_ref, spectral_ref, chunk):
    return lax.dot_general(
        table_ref[:, chunk], spectral_ref[...], (((0,), (0,)), ((), ())), preferred_element_type=jnp.float32
    )


def inverse_far_body(spectral_ref, table_ref, out_ref):
    for first in range(0, out_ref.shape[0], 256):
        chunk = slice(first, first + 256)
        out_ref[chunk, :] = turned_dot(table_ref, spectral_ref, chunk)


def inverse_near_body(meta_ref, sum_ref, spectral_ref, table_ref, *refs):
    outs, total = refs[:-1], refs[-1]
    wide, latitudes = len(outs), outs[0].shape[0]
    for first in range(0, total.shape[0], 256):
        chunk = slice(first, first + 256)
        total[chunk, :] = (sum_ref[chunk, :] + turned_dot(table_ref, spectral_ref, chunk)).astype(jnp.bfloat16)
    for shift in range(wide):
        owner = lax.rem(meta_ref[1] + shift, wide)
        outs[shift][...] = total[pl.ds(pl.multiple_of(owner * latitudes, latitudes), latitudes), :]


def join_body(wide, block, meta_ref, *refs):
    evens, odds, out_ref = refs[:wide], refs[wide : 2 * wide], refs[2 * wide]
    latitudes, columns = evens[0].shape
    fields = columns // 128
    group = wide * fields
    size = block * group
    out_row, in_row = iota2((size, size), 0), iota2((size, size), 1)
    place = out_row % group
    shift = lax.rem(meta_ref[1] - place // fields + wide, wide)
    order = picks(in_row == (shift * fields + place % fields) * block + out_row // group)

    def stack(parts, first):
        return jnp.concatenate(
            [
                part[first : first + block, field * 128 : field * 128 + 128]
                for part in parts
                for field in range(fields)
            ],
            axis=0,
        )

    for first in range(0, latitudes, block):
        both = dot32(order, jnp.concatenate((stack(evens, first), stack(odds, first)), axis=1))
        even, odd = both[:, :128], both[:, 128:]
        out_ref[0, first * group : first * group + size, :] = (even + odd).astype(jnp.bfloat16)
        out_ref[1, first * group : first * group + size, :] = (even - odd).astype(jnp.bfloat16)


def rows_body(flds, block, meta_ref, *refs):
    parts, out_ref = (refs[:2], refs[2:4]), refs[4]
    total_rows, columns = refs[0].shape
    rows = total_rows // flds
    fields = columns // 128
    group = 2 * fields
    size = block * group
    parity = meta_ref[0] % 2
    out_row, in_row = iota2((size, size), 0), iota2((size, size), 1)
    place = out_row % group
    odd = (place // fields + parity) % 2
    order = picks(in_row == (odd * fields + place % fields) * block + out_row // group)
    for d in range(2):
        for g in range(flds):
            index = lax.rem(meta_ref[2] + d, 2) * flds + lax.rem(meta_ref[3] + g, flds)
            for first in range(0, rows, block):
                at = slice(g * rows + first, g * rows + first + block)
                stacked = jnp.concatenate(
                    [
                        part[d][at, field * 128 : field * 128 + 128]
                        for part in parts
                        for field in range(fields)
                    ],
                    axis=0,
                )
                start = pl.multiple_of(index * (rows * group), rows * group) + first * group
                out_ref[pl.ds(start, size), :] = dot32(order, stacked).astype(jnp.bfloat16)


def shards(fourier_input_rows, legendre, slot_wave, to_modes, from_modes, mode_rate):
    wide, levs, flds = (lax.axis_size(axis) for axis in ("wide", "lev", "fld"))
    _, latitudes, slots, fields, lanes = fourier_input_rows.shape
    _, shard_rows, half_count = legendre.shape
    degree_count = shard_rows * levs * flds
    columns = fields * lanes
    group = slots * fields
    half_rows = shard_rows // 2
    share = flds * half_rows
    levels = to_modes.shape[0]
    block = 256 // group
    bf16, f32 = jnp.bfloat16, jnp.float32

    def shape(*dims, kind=bf16):
        return jax.ShapeDtypeStruct(dims, kind)

    def shifted(value, axis, count, step):
        return lax.ppermute(value, axis, [(i, (i + step) % count) for i in range(count)])

    def across(value, step):
        return shifted(value, "wide", wide, step)

    def behind(value, *others):
        return lax.optimization_barrier((value, *others))

    wide_at, lev_at, fld_at = (lax.axis_index(axis) for axis in ("wide", "lev", "fld"))
    meta = jnp.stack((slot_wave[0], wide_at, lev_at, fld_at)).astype(jnp.int32)
    position = (wide_at * latitudes + jnp.arange(latitudes, dtype=jnp.int32)).astype(f32)
    weights = jnp.sin(math.pi * (position + 0.5) / (2 * half_count))
    weights = jnp.broadcast_to(weights[:, None], (latitudes, lanes))
    move_flops = 4 * group * latitudes * 128 * 256
    share_flops = 2 * share * half_count * columns

    def direct_near(received, table, after=()):
        return call(
            near_body, (shape(share, columns), shape(half_count, columns)), "direct_legendre_near", share_flops,
            after=after,
        )(meta, *received, table)

    def direct_far(data, table):
        return call(far_body, shape(share, columns), "direct_legendre_far", share_flops, scalars=0)(data, table)

    def solve(odd, own, other):
        return call(
            functools.partial(solve_body, odd), (shape(share, columns),) * 2, "vertical_solve",
            16 * share * fields * levels * levels, scalars=0,
        )(own, other, *matrices)

    def inverse_far(spectral, table):
        return call(
            inverse_far_body, shape(half_count, columns, kind=f32), "inverse_legendre_far", share_flops, scalars=0,
        )(spectral, table)

    def inverse_near(total, spectral, table):
        return call(
            inverse_near_body, (shape(latitudes, columns),) * wide, "inverse_legendre_near", share_flops,
            scratch=[pltpu.VMEM((half_count, columns), bf16)],
        )(meta, total, spectral, table)

    def over_lev(value):
        return shifted(value, "lev", levs, 1)

    def beside(value):
        return shifted(value, "fld", flds, 1)

    blocks = call(
        functools.partial(split_body, slots, fields, block), (shape(latitudes, columns),) * (2 * wide),
        "split_hemispheres", move_flops,
    )(meta, fourier_input_rows.reshape(2, latitudes * group, lanes), weights)
    table_beside, *blocks = behind(beside(legendre[0]), *blocks)
    even_in, odd_in = (
        [half[0]] + [across(half[step], step) for step in range(1, wide)] for half in (blocks[:wide], blocks[wide:])
    )
    def split_table(first, second, after=()):
        return call(
            table_body, (shape(flds * half_rows, half_count),) * 2, "split_table",
            4 * shard_rows * shard_rows * half_count, after=after,
        )(meta, first, second)

    far_part = over_lev(legendre[0])
    even_near, odd_near = split_table(legendre[0], table_beside)
    *matrices, scale = call(
        functools.partial(modes_body, flds, degree_count),
        (shape(2 * levels, 2 * levels),) * 2 + (shape(2 * share, 2 * levels, kind=f32),),
        "spread_modes", 12 * levels * levels * levels, after=(blocks[0],),
    )(meta, to_modes, from_modes, mode_rate[None, :])
    matrices = (*matrices, scale)

    even_in[1], odd_in[1] = behind(even_in[1], odd_in[1])
    raw, data = direct_near(even_in, even_near, (scale,))
    far_part, raw = behind(far_part, raw)
    even_far, odd_far = split_table(far_part, beside(far_part))
    other, odd_in[2] = behind(over_lev(raw), odd_in[2])
    to_own, to_other = solve(0, direct_far(data, even_far), other)
    total = inverse_far(to_own, even_far)
    from_other = over_lev(to_other)
    even_spectral = [from_other, to_own]
    grid = inverse_near(total, from_other, even_near)

    even_out = [grid[0]] + [across(grid[step], step) for step in range(1, wide)]
    raw, data = direct_near(odd_in, odd_near, (grid[0],))
    other, even_out[1] = behind(over_lev(raw), even_out[1])
    to_own, to_other = solve(1, direct_far(data, odd_far), other)
    total = inverse_far(to_own, odd_far)
    from_other, even_out[2], even_out[3] = behind(over_lev(to_other), even_out[2], even_out[3])
    odd_spectral = [from_other, to_own]
    grid = inverse_near(total, from_other, odd_near)
    odd_out = [grid[0]] + [across(grid[step], step) for step in range(1, wide)]

    spectral_rows = call(
        functools.partial(rows_body, flds, 32), shape(degree_count * fields, lanes), "order_spectral", 0,
        after=(grid[0],),
    )(meta, *even_spectral, *odd_spectral)
    fourier_rows = call(
        functools.partial(join_body, wide, block), shape(2, latitudes * group, lanes), "join_hemispheres", move_flops,
    )(meta, *even_out, *odd_out)
    return (
        fourier_rows.reshape(2, latitudes, slots, fields, lanes),
        spectral_rows.reshape(1, degree_count, fields, lanes),
    )


def project(level_grid, degree_real, weight_rows, rate_rows, degree_total):
    projected = jnp.einsum(
        "kl,snflr->snfkr", weight_rows, level_grid, preferred_element_type=jnp.float32
    )
    factor = 1.0 + degree_real[:, None] * (degree_real[:, None] + 1.0) * rate_rows[None, :] / (
        degree_total * degree_total
    )
    return (projected / factor[None, :, None, :, None]).astype(jnp.bfloat16)


def plain_shards(fourier_input_rows, legendre, slot_wave, to_modes, from_modes, mode_rate):
    wave_rows = lax.all_to_all(fourier_input_rows, "wide", split_axis=2, concat_axis=1, tiled=True)
    half_count = wave_rows.shape[1]
    slot_count = wave_rows.shape[2]
    field_count = wave_rows.shape[3]
    column_count = wave_rows.shape[4]
    degree_count = legendre.shape[1] * lax.axis_size(("lev", "fld"))
    weights = latitude_weights(half_count)[:, None, None, None]
    north_half = wave_rows[0].astype(jnp.float32)
    south_half = wave_rows[1].astype(jnp.float32)
    symmetric = (weights * (north_half + south_half)).astype(jnp.bfloat16)
    antisym = (weights * (north_half - south_half)).astype(jnp.bfloat16)
    paired = jnp.concatenate((symmetric, antisym), axis=3)

    def direct_rows(section, first_row):
        row_count = section.shape[1]
        degree = first_row + jnp.arange(row_count, dtype=jnp.int32)
        relative = degree[None, :] - slot_wave[:, None]
        product = jnp.einsum("snj,jsfc->snfc", section, paired, preferred_element_type=jnp.float32)
        is_even = (relative % 2 == 0)[:, :, None, None]
        is_live = (relative >= 0)[:, :, None, None]
        picked = jnp.where(is_even, product[..., :column_count], product[..., column_count:])
        return jnp.where(is_live, picked, jnp.zeros_like(picked))

    full_table = lax.all_gather(legendre, ("lev", "fld"), axis=1, tiled=True)
    block_rows = 128
    block_count = degree_count // block_rows

    def direct_step(block_index, buffer):
        first_row = block_index * block_rows
        section = lax.dynamic_slice_in_dim(full_table, first_row, block_rows, 1)
        result = direct_rows(section, first_row).astype(jnp.bfloat16)
        return lax.dynamic_update_slice_in_dim(buffer, result, first_row, 1)

    initial_raw = jnp.zeros((slot_count, degree_count, field_count, column_count), jnp.bfloat16)
    raw_spectral = lax.fori_loop(0, block_count, direct_step, initial_raw)
    own_levels = column_count // 2
    first_level = lax.axis_index("lev") * own_levels
    degree_real = jnp.arange(degree_count, dtype=jnp.float32)
    all_levels = lax.all_gather(raw_spectral, "lev", axis=3, tiled=True)
    level_count = all_levels.shape[3] // 2
    level_grid = all_levels.reshape(slot_count, degree_count, field_count, level_count, 2)
    weight_rows = lax.dynamic_slice_in_dim(to_modes, first_level, own_levels, 0)
    rate_rows = lax.dynamic_slice_in_dim(mode_rate, first_level, own_levels, 0)
    own_modes = project(level_grid, degree_real, weight_rows, rate_rows, degree_count).reshape(
        slot_count, degree_count, field_count, column_count
    )
    mode_values = lax.all_gather(own_modes, "lev", axis=3, tiled=True).reshape(
        slot_count, degree_count, field_count, level_count, 2
    )
    back_rows = lax.dynamic_slice_in_dim(from_modes, first_level, own_levels, 0)
    spectral = jnp.einsum(
        "lk,snfkr->snflr", back_rows, mode_values, preferred_element_type=jnp.float32
    )
    spectral = spectral.astype(jnp.bfloat16).reshape(
        slot_count, degree_count, field_count, column_count
    )

    def inverse_rows(running, section, first_row):
        row_count = section.shape[1]
        degree = first_row + jnp.arange(row_count, dtype=jnp.int32)
        relative = degree[None, :] - slot_wave[:, None]
        spec_rows = lax.dynamic_slice_in_dim(spectral, first_row, row_count, 1)
        even_mask = ((relative >= 0) & (relative % 2 == 0))[:, :, None, None]
        odd_mask = ((relative >= 0) & (relative % 2 == 1))[:, :, None, None]
        empty_rows = jnp.zeros_like(spec_rows)
        parity_split = jnp.concatenate(
            (
                jnp.where(even_mask, spec_rows, empty_rows),
                jnp.where(odd_mask, spec_rows, empty_rows),
            ),
            axis=3,
        )
        return running + jnp.einsum(
            "snj,snfc->jsfc", section, parity_split, preferred_element_type=jnp.float32
        )

    initial_sum = jnp.zeros((half_count, slot_count, field_count, 2 * column_count), jnp.float32)

    def inverse_step(block_index, running):
        first_row = block_index * block_rows
        section = lax.dynamic_slice_in_dim(full_table, first_row, block_rows, 1)
        return inverse_rows(running, section, first_row)

    running = lax.fori_loop(0, block_count, inverse_step, initial_sum)
    even_sum = running[..., :column_count]
    odd_sum = running[..., column_count:]
    fourier_wave = jnp.stack((even_sum + odd_sum, even_sum - odd_sum), axis=0).astype(jnp.bfloat16)
    fourier_out = lax.all_to_all(fourier_wave, "wide", split_axis=1, concat_axis=2, tiled=True)
    return (fourier_out, spectral)


def solution(mesh):
    in_specs = (
        P("ens", "wide", None, "fld", "lev"),
        P("wide", ("lev", "fld"), None),
        P("wide"),
        P(),
        P(),
        P(),
    )
    out_specs = (P("ens", "wide", None, "fld", "lev"), P(("ens", "wide"), None, "fld", "lev"))

    def body(fourier_input_rows, legendre, *rest):
        _, latitudes, slots, fields, lanes = fourier_input_rows.shape
        whole_tiles = (
            latitudes % 32 == 0
            and fields == 2
            and slots == mesh.shape["wide"] == 4
            and mesh.shape["ens"] == mesh.shape["lev"] == mesh.shape["fld"] == 2
            and lanes == 128
            and legendre.shape[1] % 64 == 0
            and legendre.shape[2] % 256 == 0
        )
        form = shards if whole_tiles else plain_shards
        return form(fourier_input_rows, legendre, *rest)

    return jax.shard_map(body, mesh=mesh, in_specs=in_specs, out_specs=out_specs, check_vma=False)
```

```python
import functools
import math

import jax
import jax.numpy as jnp
from jax import lax
from jax.experimental import pallas as pl
from jax.experimental.pallas import tpu as pltpu
from jax.sharding import PartitionSpec as P

VMEM_BYTES = 8 * 1024 * 1024
RELAYS = (2, 1, 3, 0)


def latitude_weights(count):
    position = jnp.arange(count, dtype=jnp.float32)
    return jnp.sin(math.pi * (position + 0.5) / (2 * count))


def iota2(shape, dim):
    return lax.broadcasted_iota(jnp.int32, shape, dim)


def picks(condition):
    return jnp.where(condition, 1.0, 0.0).astype(jnp.bfloat16)


def dot32(a, b):
    return jnp.dot(a, b, preferred_element_type=jnp.float32)


def call(body, out_shape, name, flops, scratch=(), scalars=1, after=()):
    smem = pl.BlockSpec(memory_space=pltpu.SMEM)
    vmem = pl.BlockSpec(memory_space=pltpu.VMEM)

    def run(*operands):
        used = len(operands)

        def kernel(*refs):
            body(*refs[:used], *refs[used + len(after) :])

        return pl.pallas_call(
            kernel,
            out_shape=out_shape,
            in_specs=[smem] * scalars
            + [vmem] * (used - scalars)
            + [pl.BlockSpec(memory_space=pl.ANY)] * len(after),
            out_specs=jax.tree.map(lambda _: vmem, out_shape),
            scratch_shapes=list(scratch),
            compiler_params=pltpu.CompilerParams(vmem_limit_bytes=VMEM_BYTES),
            cost_estimate=pl.CostEstimate(flops=flops, bytes_accessed=0, transcendentals=0),
            name=name,
        )(*operands, *after)

    return run


def lane_order(lanes, lev, old, new):
    levels = lanes // 4
    part = lax.rem(new // (lanes // 2) + lev, 2)
    field = (new // levels) % 2
    return old == field * (lanes // 2) + 2 * (new % levels) + part


def split_body(slots, fields, block, meta_ref, rows_ref, weight_ref, *outs):
    latitudes = weight_ref.shape[0]
    group = slots * fields
    size = block * group
    out_row, in_row = iota2((size, size), 0), iota2((size, size), 1)
    pair = out_row // block
    slot = lax.rem(meta_ref[1] + pair // fields, slots)
    order = picks(in_row == (out_row % block) * group + slot * fields + pair % fields)
    lanes = fields * 128
    parts = picks(lane_order(lanes, meta_ref[2], iota2((lanes, lanes), 0), iota2((lanes, lanes), 1)))
    for first in range(0, latitudes, block):
        north = rows_ref[0, first * group : first * group + size, :]
        south = rows_ref[1, first * group : first * group + size, :]
        sorted_rows = dot32(order, jnp.concatenate((north, south), axis=1))
        up, down = sorted_rows[:, :128], sorted_rows[:, 128:]
        weight = weight_ref[first : first + block, :]
        halves = []
        for mixed in (up + down, up - down):
            for shift in range(slots):
                at = shift * fields * block
                halves.append(jnp.concatenate(
                    [
                        (weight * mixed[at + f * block : at + f * block + block]).astype(jnp.bfloat16)
                        for f in range(fields)
                    ],
                    axis=1,
                ))
        turned = dot32(jnp.concatenate(halves, axis=0), parts).astype(jnp.bfloat16)
        for odd in range(2):
            for shift in range(slots):
                at = (odd * slots + shift) * block
                outs[shift][odd, first : first + block, :] = turned[at : at + block, :128]
                pair, place = divmod(RELAYS.index(shift), 2)
                outs[slots + pair][place, odd, first : first + block, :] = turned[at : at + block, 128:]


def by_parity(meta_ref, rows):
    half = rows // 2
    out_row, in_row = iota2((rows, rows), 0), iota2((rows, rows), 1)
    odd = jnp.where(out_row < half, 0, 1)
    return picks(in_row == 2 * (out_row - odd * half) + (meta_ref[0] + odd) % 2)


def near_table_body(meta_ref, own_ref, beside_ref, even_ref, odd_ref):
    rows, columns = own_ref.shape
    half = rows // 2
    order = by_parity(meta_ref, rows)
    for g, table_ref in enumerate((own_ref, beside_ref)):
        at = slice(g * half, g * half + half)
        for first in range(0, columns, 256):
            lanes = slice(first, first + 256)
            result = dot32(order, table_ref[:, lanes]).astype(jnp.bfloat16)
            even_ref[at, lanes] = result[:half]
            odd_ref[at, lanes] = result[half:]


def far_table_body(meta_ref, first_ref, second_ref, out_ref, whole):
    half, columns = first_ref.shape
    for ens, ref in ((meta_ref[4], first_ref), (1 - meta_ref[4], second_ref)):
        whole[pl.ds(pl.multiple_of(ens * half, half), half), :] = ref[...]
    order = by_parity(meta_ref, 2 * half)
    for first in range(0, columns, 256):
        lanes = slice(first, first + 256)
        out_ref[:, lanes] = dot32(order, whole[:, lanes]).astype(jnp.bfloat16)


def modes_body(sizes, degree_total, meta_ref, to_ref, from_ref, rate_ref, in_ref, out_ref, scale_ref):
    levels = to_ref.shape[0]
    wide = 2 * levels
    own = levels // 2
    lane, row = iota2((levels, wide), 1), iota2((levels, wide), 0)
    owner = lax.rem(meta_ref[2] + lane // levels, 2)
    spread = picks(row == owner * own + lane % own)
    plain = picks(row == lane % levels)
    old, new = iota2((wide, wide), 0), iota2((wide, wide), 1)

    def turned(first, matrix, last):
        half = lax.dot_general(first, matrix, (((0,), (1,)), ((), ())), preferred_element_type=jnp.float32)
        return dot32(half.astype(jnp.bfloat16), last)

    same = (old // own) % 2 == new // levels
    in_ref[...] = jnp.where(same, turned(spread, to_ref[...], plain), 0.0).astype(jnp.bfloat16)
    same = old // levels == (new // own) % 2
    out_ref[...] = jnp.where(same, turned(plain, from_ref[...], spread), 0.0).astype(jnp.bfloat16)
    wide, levs, flds = sizes
    rows = degree_total // (2 * levs * flds)
    for odd in range(2):
        for d in range(levs):
            for g in range(flds):
                block = lax.rem(meta_ref[2] + d, levs) * flds + lax.rem(meta_ref[3] + g, flds)
                degree = block * (2 * rows) + 2 * iota2((rows, 1), 0) + (meta_ref[0] + odd) % 2
                real = degree.astype(jnp.float32)
                factor = 1.0 + real * (real + 1.0) * rate_ref[...] / (degree_total * degree_total)
                at = ((odd * levs + d) * flds + g) * rows
                scale_ref[at : at + rows, :] = jnp.where(degree >= meta_ref[0], 1.0 / factor, 0.0)


def rows_of(refs, odd, lanes):
    near, far, far_beside = refs
    rows = far.shape[0] // 2
    half = slice(odd * rows, odd * rows + rows)
    return jnp.concatenate((near[:, lanes], far[half, lanes], far_beside[half, lanes]), axis=0)


def forward_body(wide, odd, meta_ref, in_ref, out_ref, scale_ref, *refs):
    parts, tables, refs = refs[: wide * 2], refs[wide * 2 : -3], refs[-3:]
    own_ref, other_ref, data = refs
    latitudes, lanes = parts[0].shape[1:]
    rows = own_ref.shape[0]
    for shift in range(wide):
        owner = lax.rem(meta_ref[1] - shift + wide, wide)
        at = pl.ds(pl.multiple_of(owner * latitudes, latitudes), latitudes)
        for d in range(2):
            data[at, d * lanes : d * lanes + lanes] = parts[shift * 2 + d][odd]
    raw = dot32(rows_of(tables, odd, slice(None)), data[...]).astype(jnp.bfloat16)
    scale = jnp.concatenate([scale_ref[odd * rows : odd * rows + rows, :]] * 2, axis=1)
    modes = (dot32(raw, in_ref[...]) * scale).astype(jnp.bfloat16)
    spectral = dot32(modes, out_ref[...]).astype(jnp.bfloat16)
    own_ref[...] = spectral[:, :lanes]
    other_ref[...] = spectral[:, lanes:]


def inverse_body(wide, meta_ref, *refs):
    parts, tables, outs, total = refs[:4], (refs[4:5] + refs[6:8], refs[5:8]), refs[8:-1], refs[-1]
    latitudes, lanes = outs[0].shape[1:]
    spectral = [jnp.concatenate((parts[2 * odd][...], parts[2 * odd + 1][...]), axis=1) for odd in range(2)]
    for first in range(0, total.shape[1], 256):
        chunk = slice(first, first + 256)
        sums = [
            lax.dot_general(
                rows_of(tables[odd], odd, chunk), spectral[odd], (((0,), (0,)), ((), ())),
                preferred_element_type=jnp.float32,
            )
            for odd in range(2)
        ]
        total[0, chunk, :] = (sums[0] + sums[1]).astype(jnp.bfloat16)
        total[1, chunk, :] = (sums[0] - sums[1]).astype(jnp.bfloat16)
    for shift in range(wide):
        owner = lax.rem(meta_ref[1] + shift, wide)
        at = pl.ds(pl.multiple_of(owner * latitudes, latitudes), latitudes)
        for d in range(2):
            outs[shift * 2 + d][...] = total[:, at, d * lanes : d * lanes + lanes]


def join_body(slots, block, meta_ref, *refs):
    parts, out_ref = refs[:-1], refs[-1]
    latitudes, lanes = parts[0].shape[1:]
    fields = 2
    group = slots * fields
    size = block * group
    out_row, in_row = iota2((size, size), 0), iota2((size, size), 1)
    place = out_row % group
    shift = lax.rem(meta_ref[1] - place // fields + slots, slots)
    order = picks(in_row == (shift * fields + place % fields) * block + out_row // group)
    both = 2 * lanes
    turn = picks(lane_order(both, meta_ref[2], iota2((both, both), 1), iota2((both, both), 0)))
    for first in range(0, latitudes, block):
        at = slice(first, first + block)
        stacked = jnp.concatenate(
            [
                jnp.concatenate([parts[shift * 2 + d][half, at, :] for d in range(2)], axis=1)
                for half in range(2)
                for shift in range(slots)
            ],
            axis=0,
        )
        turned = dot32(stacked, turn).astype(jnp.bfloat16)
        halves = [
            jnp.concatenate(
                [
                    turned[
                        (half * slots + shift) * block : (half * slots + shift + 1) * block,
                        field * lanes : field * lanes + lanes,
                    ]
                    for shift in range(slots)
                    for field in range(fields)
                ],
                axis=0,
            )
            for half in range(2)
        ]
        result = dot32(order, jnp.concatenate(halves, axis=1)).astype(jnp.bfloat16)
        for half in range(2):
            out_ref[half, first * group : first * group + size, :] = result[:, half * lanes : half * lanes + lanes]


def rows_body(sizes, block, meta_ref, *refs):
    wide, levs, flds = sizes
    own_refs, other_refs, out_ref = refs[:2], refs[2:4], refs[4]
    total_rows, lanes = own_refs[0].shape
    rows = total_rows // (levs * flds)
    fields = 2
    group = 2 * fields
    size = block * group
    out_row, in_row = iota2((size, size), 0), iota2((size, size), 1)
    place = out_row % group
    odd = (place // fields + meta_ref[0] % 2) % 2
    order = picks(in_row == (odd * fields + place % fields) * block + out_row // group)
    both = 2 * lanes
    turn = picks(lane_order(both, meta_ref[2], iota2((both, both), 1), iota2((both, both), 0)))
    for d in range(levs):
        for g in range(flds):
            index = lax.rem(meta_ref[2] + d, levs) * flds + lax.rem(meta_ref[3] + g, flds)
            halves = []
            for odd in range(2):
                mine, theirs = (d * flds + g) * rows, ((1 - d) * flds + g) * rows
                halves.append(jnp.concatenate(
                    (own_refs[odd][mine : mine + rows, :], other_refs[odd][theirs : theirs + rows, :]), axis=1
                ))
            turned = dot32(jnp.concatenate(halves, axis=0), turn).astype(jnp.bfloat16)
            for first in range(0, rows, block):
                stacked = jnp.concatenate(
                    [
                        turned[
                            odd * rows + first : odd * rows + first + block, field * lanes : field * lanes + lanes
                        ]
                        for odd in range(2)
                        for field in range(fields)
                    ],
                    axis=0,
                )
                start = pl.multiple_of(index * (rows * group), rows * group) + first * group
                out_ref[pl.ds(start, size), :] = dot32(order, stacked).astype(jnp.bfloat16)


def shards(fourier_input_rows, legendre, slot_wave, to_modes, from_modes, mode_rate):
    wide, levs, flds = (lax.axis_size(axis) for axis in ("wide", "lev", "fld"))
    sizes = (wide, levs, flds)
    _, latitudes, slots, fields, lanes = fourier_input_rows.shape
    _, shard_rows, half_count = legendre.shape
    degree_count = shard_rows * levs * flds
    group = slots * fields
    columns = fields * lanes
    block = 256 // group
    levels = to_modes.shape[0]
    bf16 = jnp.bfloat16

    def shape(*dims):
        return jax.ShapeDtypeStruct(dims, bf16)

    def shifted(value, axis, count, step):
        return lax.ppermute(value, axis, [(i, (i + step) % count) for i in range(count)])

    def across(value, step):
        return shifted(value, "wide", wide, step)

    def over_lev(value):
        return shifted(value, "lev", levs, 1)

    def beside(value):
        return shifted(value, "fld", flds, 1)

    def behind(value, *others):
        return lax.optimization_barrier((value, *others))

    wide_at, lev_at, fld_at = (lax.axis_index(axis) for axis in ("wide", "lev", "fld"))
    meta = jnp.stack((slot_wave[0], wide_at, lev_at, fld_at, lax.axis_index("ens"))).astype(jnp.int32)
    position = (wide_at * latitudes + jnp.arange(latitudes, dtype=jnp.int32)).astype(jnp.float32)
    weights = jnp.sin(math.pi * (position + 0.5) / (2 * half_count))
    weights = jnp.broadcast_to(weights[:, None], (latitudes, lanes))
    move_flops = 8 * group * latitudes * 128 * 256
    transform_flops = 2 * degree_count * half_count * columns

    *own_blocks, early, late = call(
        functools.partial(split_body, slots, fields, block),
        (shape(2, latitudes, lanes),) * wide + (shape(2, 2, latitudes, lanes),) * 2,
        "split_hemispheres", move_flops,
    )(meta, fourier_input_rows.reshape(2, latitudes * group, lanes), weights)
    direct = [own_blocks[0]] + [across(own_blocks[step], step) for step in range(1, wide)]
    early, late = over_lev(early), over_lev(late)
    half_shard = shard_rows // 2
    own_table, own_blocks[0] = behind(legendre[0], own_blocks[0])
    first = lax.dynamic_slice_in_dim(own_table, lax.axis_index("ens") * half_shard, half_shard, 0)
    first, early, *direct = behind(over_lev(first), early, *direct)
    second = shifted(first, "ens", 2, 1)
    own_table, early = behind(own_table, early)
    relayed = {step: across(early[i], step) for i, step in enumerate(RELAYS[:2])}
    second, late, relayed[1], relayed[2] = behind(second, late, relayed[1], relayed[2])
    relayed |= {3: across(late[0], 3), 0: late[1]}
    data = [one for step in range(wide) for one in (direct[step], relayed[step])]
    near = call(
        near_table_body, (shape(shard_rows, half_count),) * 2, "split_table",
        4 * shard_rows * shard_rows * half_count,
    )(meta, legendre[0], beside(own_table))
    far = call(
        far_table_body, shape(shard_rows, half_count), "split_table", 2 * shard_rows * shard_rows * half_count,
        scratch=[pltpu.VMEM((shard_rows, half_count), bf16)],
    )(meta, first, second)
    far = [far, beside(far)]
    *matrices, scale = call(
        functools.partial(modes_body, sizes, degree_count),
        (shape(2 * levels, 2 * levels),) * 2 + (jax.ShapeDtypeStruct((degree_count, levels), jnp.float32),),
        "spread_modes", 12 * levels * levels * levels, after=(own_blocks[0],),
    )(meta, to_modes, from_modes, mode_rate[None, :])

    half_rows = degree_count // 2
    spectral = [
        call(
            functools.partial(forward_body, wide, odd), (shape(half_rows, lanes),) * 2,
            "direct_legendre_and_solve", transform_flops // 2,
            scratch=[pltpu.VMEM((half_count, columns), bf16)],
        )(meta, *matrices, scale, *data, near[odd], *far)
        for odd in range(2)
    ]
    grid = call(
        functools.partial(inverse_body, wide), (shape(2, latitudes, lanes),) * (wide * levs),
        "inverse_legendre", transform_flops, scratch=[pltpu.VMEM((2, half_count, columns), bf16)],
    )(meta, *spectral[0], *spectral[1], *near, *far)
    relayed = [over_lev(grid[1])] + [None] * (wide - 1)
    direct = [grid[0]] + [None] * (wide - 1)
    for step in RELAYS[:-1]:
        crossed = across(grid[2 * step + 1], step)
        block, crossed = behind(grid[2 * step], crossed)
        direct[step] = across(block, step)
        relayed[step] = over_lev(crossed)
    result = [one for step in range(wide) for one in (direct[step], relayed[step])]
    spectral_rows = call(
        functools.partial(rows_body, sizes, 32), shape(degree_count * fields, lanes), "order_spectral", 0,
    )(meta, *(own for own, _ in spectral), *(shifted(other, "lev", levs, 1) for _, other in spectral))
    fourier_rows = call(
        functools.partial(join_body, slots, 256 // group), shape(2, latitudes * group, lanes),
        "join_hemispheres", move_flops, after=(spectral_rows,),
    )(meta, *result)
    return (
        fourier_rows.reshape(2, latitudes, slots, fields, lanes),
        spectral_rows.reshape(1, degree_count, fields, lanes),
    )


def project(level_grid, degree_real, weight_rows, rate_rows, degree_total):
    projected = jnp.einsum(
        "kl,snflr->snfkr", weight_rows, level_grid, preferred_element_type=jnp.float32
    )
    factor = 1.0 + degree_real[:, None] * (degree_real[:, None] + 1.0) * rate_rows[None, :] / (
        degree_total * degree_total
    )
    return (projected / factor[None, :, None, :, None]).astype(jnp.bfloat16)


def plain_shards(fourier_input_rows, legendre, slot_wave, to_modes, from_modes, mode_rate):
    wave_rows = lax.all_to_all(fourier_input_rows, "wide", split_axis=2, concat_axis=1, tiled=True)
    half_count = wave_rows.shape[1]
    slot_count = wave_rows.shape[2]
    field_count = wave_rows.shape[3]
    column_count = wave_rows.shape[4]
    degree_count = legendre.shape[1] * lax.axis_size(("lev", "fld"))
    weights = latitude_weights(half_count)[:, None, None, None]
    north_half = wave_rows[0].astype(jnp.float32)
    south_half = wave_rows[1].astype(jnp.float32)
    symmetric = (weights * (north_half + south_half)).astype(jnp.bfloat16)
    antisym = (weights * (north_half - south_half)).astype(jnp.bfloat16)
    paired = jnp.concatenate((symmetric, antisym), axis=3)

    def direct_rows(section, first_row):
        row_count = section.shape[1]
        degree = first_row + jnp.arange(row_count, dtype=jnp.int32)
        relative = degree[None, :] - slot_wave[:, None]
        product = jnp.einsum("snj,jsfc->snfc", section, paired, preferred_element_type=jnp.float32)
        is_even = (relative % 2 == 0)[:, :, None, None]
        is_live = (relative >= 0)[:, :, None, None]
        picked = jnp.where(is_even, product[..., :column_count], product[..., column_count:])
        return jnp.where(is_live, picked, jnp.zeros_like(picked))

    full_table = lax.all_gather(legendre, ("lev", "fld"), axis=1, tiled=True)
    block_rows = 128
    block_count = degree_count // block_rows

    def direct_step(block_index, buffer):
        first_row = block_index * block_rows
        section = lax.dynamic_slice_in_dim(full_table, first_row, block_rows, 1)
        result = direct_rows(section, first_row).astype(jnp.bfloat16)
        return lax.dynamic_update_slice_in_dim(buffer, result, first_row, 1)

    initial_raw = jnp.zeros((slot_count, degree_count, field_count, column_count), jnp.bfloat16)
    raw_spectral = lax.fori_loop(0, block_count, direct_step, initial_raw)
    own_levels = column_count // 2
    first_level = lax.axis_index("lev") * own_levels
    degree_real = jnp.arange(degree_count, dtype=jnp.float32)
    all_levels = lax.all_gather(raw_spectral, "lev", axis=3, tiled=True)
    level_count = all_levels.shape[3] // 2
    level_grid = all_levels.reshape(slot_count, degree_count, field_count, level_count, 2)
    weight_rows = lax.dynamic_slice_in_dim(to_modes, first_level, own_levels, 0)
    rate_rows = lax.dynamic_slice_in_dim(mode_rate, first_level, own_levels, 0)
    own_modes = project(level_grid, degree_real, weight_rows, rate_rows, degree_count).reshape(
        slot_count, degree_count, field_count, column_count
    )
    mode_values = lax.all_gather(own_modes, "lev", axis=3, tiled=True).reshape(
        slot_count, degree_count, field_count, level_count, 2
    )
    back_rows = lax.dynamic_slice_in_dim(from_modes, first_level, own_levels, 0)
    spectral = jnp.einsum(
        "lk,snfkr->snflr", back_rows, mode_values, preferred_element_type=jnp.float32
    )
    spectral = spectral.astype(jnp.bfloat16).reshape(
        slot_count, degree_count, field_count, column_count
    )

    def inverse_rows(running, section, first_row):
        row_count = section.shape[1]
        degree = first_row + jnp.arange(row_count, dtype=jnp.int32)
        relative = degree[None, :] - slot_wave[:, None]
        spec_rows = lax.dynamic_slice_in_dim(spectral, first_row, row_count, 1)
        even_mask = ((relative >= 0) & (relative % 2 == 0))[:, :, None, None]
        odd_mask = ((relative >= 0) & (relative % 2 == 1))[:, :, None, None]
        empty_rows = jnp.zeros_like(spec_rows)
        parity_split = jnp.concatenate(
            (
                jnp.where(even_mask, spec_rows, empty_rows),
                jnp.where(odd_mask, spec_rows, empty_rows),
            ),
            axis=3,
        )
        return running + jnp.einsum(
            "snj,snfc->jsfc", section, parity_split, preferred_element_type=jnp.float32
        )

    initial_sum = jnp.zeros((half_count, slot_count, field_count, 2 * column_count), jnp.float32)

    def inverse_step(block_index, running):
        first_row = block_index * block_rows
        section = lax.dynamic_slice_in_dim(full_table, first_row, block_rows, 1)
        return inverse_rows(running, section, first_row)

    running = lax.fori_loop(0, block_count, inverse_step, initial_sum)
    even_sum = running[..., :column_count]
    odd_sum = running[..., column_count:]
    fourier_wave = jnp.stack((even_sum + odd_sum, even_sum - odd_sum), axis=0).astype(jnp.bfloat16)
    fourier_out = lax.all_to_all(fourier_wave, "wide", split_axis=1, concat_axis=2, tiled=True)
    return (fourier_out, spectral)


def solution(mesh):
    in_specs = (
        P("ens", "wide", None, "fld", "lev"),
        P("wide", ("lev", "fld"), None),
        P("wide"),
        P(),
        P(),
        P(),
    )
    out_specs = (P("ens", "wide", None, "fld", "lev"), P(("ens", "wide"), None, "fld", "lev"))

    def body(fourier_input_rows, legendre, *rest):
        _, latitudes, slots, fields, lanes = fourier_input_rows.shape
        whole_tiles = (
            latitudes % 32 == 0
            and fields == 2
            and slots == mesh.shape["wide"] == 4
            and mesh.shape["ens"] == mesh.shape["lev"] == mesh.shape["fld"] == 2
            and lanes == 128
            and legendre.shape[1] % 64 == 0
            and legendre.shape[2] % 256 == 0
        )
        form = shards if whole_tiles else plain_shards
        return form(fourier_input_rows, legendre, *rest)

    return jax.shard_map(body, mesh=mesh, in_specs=in_specs, out_specs=out_specs, check_vma=False)
```

```python
import functools
import math

import jax
import jax.numpy as jnp
from jax import lax
from jax.experimental import pallas as pl
from jax.experimental.pallas import tpu as pltpu
from jax.sharding import PartitionSpec as P

VMEM_BYTES = 8 * 1024 * 1024


def latitude_weights(count):
    position = jnp.arange(count, dtype=jnp.float32)
    return jnp.sin(math.pi * (position + 0.5) / (2 * count))


def iota2(shape, dim):
    return lax.broadcasted_iota(jnp.int32, shape, dim)


def picks(condition):
    return jnp.where(condition, 1.0, 0.0).astype(jnp.bfloat16)


def dot32(a, b):
    return jnp.dot(a, b, preferred_element_type=jnp.float32)


def call(body, out_shape, name, flops, scratch=(), scalars=1, after=()):
    smem = pl.BlockSpec(memory_space=pltpu.SMEM)
    vmem = pl.BlockSpec(memory_space=pltpu.VMEM)

    def run(*operands):
        used = len(operands)

        def kernel(*refs):
            body(*refs[:used], *refs[used + len(after) :])

        return pl.pallas_call(
            kernel,
            out_shape=out_shape,
            in_specs=[smem] * scalars
            + [vmem] * (used - scalars)
            + [pl.BlockSpec(memory_space=pl.ANY)] * len(after),
            out_specs=jax.tree.map(lambda _: vmem, out_shape),
            scratch_shapes=list(scratch),
            compiler_params=pltpu.CompilerParams(vmem_limit_bytes=VMEM_BYTES),
            cost_estimate=pl.CostEstimate(flops=flops, bytes_accessed=0, transcendentals=0),
            name=name,
        )(*operands, *after)

    return run


def lane_order(lanes, lev, old, new):
    levels = lanes // 4
    part = lax.rem(new // (lanes // 2) + lev, 2)
    field = (new // levels) % 2
    return old == field * (lanes // 2) + 2 * (new % levels) + part


def split_body(slots, fields, block, meta_ref, rows_ref, weight_ref, *outs):
    latitudes = weight_ref.shape[0]
    group = slots * fields
    size = block * group
    out_row, in_row = iota2((size, size), 0), iota2((size, size), 1)
    pair = out_row // block
    slot = lax.rem(meta_ref[1] + pair // fields, slots)
    order = picks(in_row == (out_row % block) * group + slot * fields + pair % fields)
    lanes = fields * 128
    parts = picks(lane_order(lanes, meta_ref[2], iota2((lanes, lanes), 0), iota2((lanes, lanes), 1)))
    for first in range(0, latitudes, block):
        north = rows_ref[0, first * group : first * group + size, :]
        south = rows_ref[1, first * group : first * group + size, :]
        sorted_rows = dot32(order, jnp.concatenate((north, south), axis=1))
        up, down = sorted_rows[:, :128], sorted_rows[:, 128:]
        weight = weight_ref[first : first + block, :]
        halves = []
        for mixed in (up + down, up - down):
            for shift in range(slots):
                at = shift * fields * block
                halves.append(jnp.concatenate(
                    [
                        (weight * mixed[at + f * block : at + f * block + block]).astype(jnp.bfloat16)
                        for f in range(fields)
                    ],
                    axis=1,
                ))
        turned = dot32(jnp.concatenate(halves, axis=0), parts).astype(jnp.bfloat16)
        for odd in range(2):
            for shift in range(slots):
                at = (odd * slots + shift) * block
                for d in range(2):
                    outs[shift * 2 + d][odd, first : first + block, :] = turned[
                        at : at + block, d * 128 : d * 128 + 128
                    ]


def by_parity(meta_ref, rows):
    half = rows // 2
    out_row, in_row = iota2((rows, rows), 0), iota2((rows, rows), 1)
    odd = jnp.where(out_row < half, 0, 1)
    return picks(in_row == 2 * (out_row - odd * half) + (meta_ref[0] + odd) % 2)


def near_table_body(meta_ref, own_ref, beside_ref, even_ref, odd_ref):
    rows, columns = own_ref.shape
    half = rows // 2
    order = by_parity(meta_ref, rows)
    for g, table_ref in enumerate((own_ref, beside_ref)):
        at = slice(g * half, g * half + half)
        for first in range(0, columns, 256):
            lanes = slice(first, first + 256)
            result = dot32(order, table_ref[:, lanes]).astype(jnp.bfloat16)
            even_ref[at, lanes] = result[:half]
            odd_ref[at, lanes] = result[half:]


def far_table_body(meta_ref, first_ref, second_ref, out_ref, whole):
    half, columns = first_ref.shape
    for ens, ref in ((meta_ref[4], first_ref), (1 - meta_ref[4], second_ref)):
        whole[pl.ds(pl.multiple_of(ens * half, half), half), :] = ref[...]
    order = by_parity(meta_ref, 2 * half)
    for first in range(0, columns, 256):
        lanes = slice(first, first + 256)
        out_ref[:, lanes] = dot32(order, whole[:, lanes]).astype(jnp.bfloat16)


def modes_body(sizes, degree_total, meta_ref, to_ref, from_ref, rate_ref, in_ref, out_ref, scale_ref):
    levels = to_ref.shape[0]
    wide = 2 * levels
    own = levels // 2
    lane, row = iota2((levels, wide), 1), iota2((levels, wide), 0)
    owner = lax.rem(meta_ref[2] + lane // levels, 2)
    spread = picks(row == owner * own + lane % own)
    plain = picks(row == lane % levels)
    old, new = iota2((wide, wide), 0), iota2((wide, wide), 1)

    def turned(first, matrix, last):
        half = lax.dot_general(first, matrix, (((0,), (1,)), ((), ())), preferred_element_type=jnp.float32)
        return dot32(half.astype(jnp.bfloat16), last)

    same = (old // own) % 2 == new // levels
    in_ref[...] = jnp.where(same, turned(spread, to_ref[...], plain), 0.0).astype(jnp.bfloat16)
    same = old // levels == (new // own) % 2
    out_ref[...] = jnp.where(same, turned(plain, from_ref[...], spread), 0.0).astype(jnp.bfloat16)
    wide, levs, flds = sizes
    rows = degree_total // (2 * levs * flds)
    for odd in range(2):
        for d in range(levs):
            for g in range(flds):
                block = lax.rem(meta_ref[2] + d, levs) * flds + lax.rem(meta_ref[3] + g, flds)
                degree = block * (2 * rows) + 2 * iota2((rows, 1), 0) + (meta_ref[0] + odd) % 2
                real = degree.astype(jnp.float32)
                factor = 1.0 + real * (real + 1.0) * rate_ref[...] / (degree_total * degree_total)
                at = ((d * 2 + odd) * flds + g) * rows
                scale_ref[at : at + rows, :] = jnp.where(degree >= meta_ref[0], 1.0 / factor, 0.0)


def transform(tables, data, scale_ref, in_ref, out_ref, own_ref, other_ref):
    lanes = own_ref.shape[1]
    rows = own_ref.shape[0] // 2
    for odd in range(2):
        at = slice(odd * rows, odd * rows + rows)
        raw = dot32(tables[odd], data[odd]).astype(jnp.bfloat16)
        scale = jnp.concatenate([scale_ref[at, :]] * 2, axis=1)
        modes = (dot32(raw, in_ref[...]) * scale).astype(jnp.bfloat16)
        spectral = dot32(modes, out_ref[...]).astype(jnp.bfloat16)
        own_ref[at, :] = spectral[:, :lanes]
        other_ref[at, :] = spectral[:, lanes:]


def near_body(wide, meta_ref, in_ref, out_ref, scale_ref, even_ref, odd_ref, *refs):
    parts, (own_ref, other_ref, data_ref) = refs[:-3], refs[-3:]
    latitudes, lanes = parts[0].shape[1:]
    for shift in range(wide):
        owner = lax.rem(meta_ref[1] - shift + wide, wide)
        at = pl.ds(pl.multiple_of(owner * latitudes, latitudes), latitudes)
        for d in range(2):
            data_ref[:, at, d * lanes : d * lanes + lanes] = parts[shift * 2 + d][...]
    scale = scale_ref.at[: scale_ref.shape[0] // 2]
    transform((even_ref[...], odd_ref[...]), data_ref, scale, in_ref, out_ref, own_ref, other_ref)


def far_body(in_ref, out_ref, scale_ref, first_ref, second_ref, data_ref, own_ref, other_ref):
    rows = first_ref.shape[0] // 2
    tables = [
        jnp.concatenate([ref[odd * rows : odd * rows + rows, :] for ref in (first_ref, second_ref)], axis=0)
        for odd in range(2)
    ]
    scale = scale_ref.at[scale_ref.shape[0] // 2 :]
    transform(tables, data_ref, scale, in_ref, out_ref, own_ref, other_ref)


def inverse_body(wide, meta_ref, *refs):
    parts, near, far, outs, total = refs[:4], refs[4:6], refs[6:8], refs[8:-1], refs[-1]
    latitudes, lanes = outs[0].shape[1:]
    rows = parts[0].shape[0] // 2
    spectral = [
        jnp.concatenate(
            [
                jnp.concatenate([ref[odd * rows : odd * rows + rows, :] for ref in pair], axis=1)
                for pair in (parts[:2], parts[2:])
            ],
            axis=0,
        )
        for odd in range(2)
    ]
    for first in range(0, total.shape[1], 256):
        chunk = slice(first, first + 256)
        sums = []
        for odd in range(2):
            at = slice(odd * (rows // 2), (odd + 1) * (rows // 2))
            table = jnp.concatenate([near[odd][:, chunk]] + [ref[at, chunk] for ref in far], axis=0)
            sums.append(lax.dot_general(
                table, spectral[odd], (((0,), (0,)), ((), ())), preferred_element_type=jnp.float32
            ))
        total[0, chunk, :] = (sums[0] + sums[1]).astype(jnp.bfloat16)
        total[1, chunk, :] = (sums[0] - sums[1]).astype(jnp.bfloat16)
    for shift in range(wide):
        owner = lax.rem(meta_ref[1] + shift, wide)
        at = pl.ds(pl.multiple_of(owner * latitudes, latitudes), latitudes)
        for d in range(2):
            outs[shift * 2 + d][...] = total[:, at, d * lanes : d * lanes + lanes]


def join_body(slots, block, meta_ref, *refs):
    parts, out_ref = refs[:-1], refs[-1]
    latitudes, lanes = parts[0].shape[1:]
    fields = 2
    group = slots * fields
    size = block * group
    out_row, in_row = iota2((size, size), 0), iota2((size, size), 1)
    place = out_row % group
    shift = lax.rem(meta_ref[1] - place // fields + slots, slots)
    order = picks(in_row == (shift * fields + place % fields) * block + out_row // group)
    both = 2 * lanes
    turn = picks(lane_order(both, meta_ref[2], iota2((both, both), 1), iota2((both, both), 0)))
    for first in range(0, latitudes, block):
        at = slice(first, first + block)
        stacked = jnp.concatenate(
            [
                jnp.concatenate([parts[shift * 2 + d][half, at, :] for d in range(2)], axis=1)
                for half in range(2)
                for shift in range(slots)
            ],
            axis=0,
        )
        turned = dot32(stacked, turn).astype(jnp.bfloat16)
        halves = [
            jnp.concatenate(
                [
                    turned[
                        (half * slots + shift) * block : (half * slots + shift + 1) * block,
                        field * lanes : field * lanes + lanes,
                    ]
                    for shift in range(slots)
                    for field in range(fields)
                ],
                axis=0,
            )
            for half in range(2)
        ]
        result = dot32(order, jnp.concatenate(halves, axis=1)).astype(jnp.bfloat16)
        for half in range(2):
            out_ref[half, first * group : first * group + size, :] = result[:, half * lanes : half * lanes + lanes]


def rows_body(sizes, block, meta_ref, *refs):
    wide, levs, flds = sizes
    own_refs, other_refs, out_ref = refs[:2], refs[2:4], refs[4]
    total_rows, lanes = own_refs[0].shape
    rows = total_rows // (2 * flds)
    fields = 2
    group = 2 * fields
    size = block * group
    out_row, in_row = iota2((size, size), 0), iota2((size, size), 1)
    place = out_row % group
    odd = (place // fields + meta_ref[0] % 2) % 2
    order = picks(in_row == (odd * fields + place % fields) * block + out_row // group)
    both = 2 * lanes
    turn = picks(lane_order(both, meta_ref[2], iota2((both, both), 1), iota2((both, both), 0)))
    for d in range(levs):
        for g in range(flds):
            index = lax.rem(meta_ref[2] + d, levs) * flds + lax.rem(meta_ref[3] + g, flds)
            halves = []
            for odd in range(2):
                at = slice((odd * flds + g) * rows, (odd * flds + g + 1) * rows)
                halves.append(jnp.concatenate((own_refs[d][at, :], other_refs[1 - d][at, :]), axis=1))
            turned = dot32(jnp.concatenate(halves, axis=0), turn).astype(jnp.bfloat16)
            for first in range(0, rows, block):
                stacked = jnp.concatenate(
                    [
                        turned[
                            odd * rows + first : odd * rows + first + block, field * lanes : field * lanes + lanes
                        ]
                        for odd in range(2)
                        for field in range(fields)
                    ],
                    axis=0,
                )
                start = pl.multiple_of(index * (rows * group), rows * group) + first * group
                out_ref[pl.ds(start, size), :] = dot32(order, stacked).astype(jnp.bfloat16)


def shards(fourier_input_rows, legendre, slot_wave, to_modes, from_modes, mode_rate):
    wide, levs, flds = (lax.axis_size(axis) for axis in ("wide", "lev", "fld"))
    sizes = (wide, levs, flds)
    _, latitudes, slots, fields, lanes = fourier_input_rows.shape
    _, shard_rows, half_count = legendre.shape
    degree_count = shard_rows * levs * flds
    group = slots * fields
    columns = fields * lanes
    block = 256 // group
    levels = to_modes.shape[0]
    bf16 = jnp.bfloat16

    def shape(*dims):
        return jax.ShapeDtypeStruct(dims, bf16)

    def shifted(value, axis, count, step):
        return lax.ppermute(value, axis, [(i, (i + step) % count) for i in range(count)])

    def over_lev(value):
        return shifted(value, "lev", levs, 1)

    def beside(value):
        return shifted(value, "fld", flds, 1)

    def moved(value, k, d):
        pairs = [(w * levs + l, (w + k) % wide * levs + (l + d) % levs) for w in range(wide) for l in range(levs)]
        return lax.ppermute(value, ("wide", "lev"), pairs)

    def behind(value, *others):
        return lax.optimization_barrier((value, *others))

    wide_at, lev_at, fld_at = (lax.axis_index(axis) for axis in ("wide", "lev", "fld"))
    meta = jnp.stack((slot_wave[0], wide_at, lev_at, fld_at, lax.axis_index("ens"))).astype(jnp.int32)
    position = (wide_at * latitudes + jnp.arange(latitudes, dtype=jnp.int32)).astype(jnp.float32)
    weights = jnp.sin(math.pi * (position + 0.5) / (2 * half_count))
    weights = jnp.broadcast_to(weights[:, None], (latitudes, lanes))
    move_flops = 8 * group * latitudes * 128 * 256
    transform_flops = 2 * degree_count * half_count * columns

    table_beside = beside(legendre[0])
    blocks = call(
        functools.partial(split_body, slots, fields, block), (shape(2, latitudes, lanes),) * (wide * levs),
        "split_hemispheres", move_flops,
    )(meta, fourier_input_rows.reshape(2, latitudes * group, lanes), weights)
    table_beside, *blocks = behind(table_beside, *blocks)
    *matrices, scale = call(
        functools.partial(modes_body, sizes, degree_count),
        (shape(2 * levels, 2 * levels),) * 2 + (jax.ShapeDtypeStruct((degree_count, levels), jnp.float32),),
        "spread_modes", 12 * levels * levels * levels, after=(blocks[0],),
    )(meta, to_modes, from_modes, mode_rate[None, :])
    near = call(
        near_table_body, (shape(shard_rows, half_count),) * 2, "split_table",
        4 * shard_rows * shard_rows * half_count, after=(scale,),
    )(meta, legendre[0], table_beside)

    def exchanged(blocks, ahead):
        arrived = {(0, 0): blocks[0]}
        for k, d in ((2, 0), (1, 0), (3, 0), (0, 1)):
            arrived[k, d] = moved(blocks[k * levs + d], k, d)
        for k, first in ((2, (0, 1)), (1, (1, 0)), (3, (3, 0))):
            value, arrived[first], *_ = behind(blocks[k * levs + 1], arrived[first], *ahead)
            arrived[k, 1] = moved(value, k, 1)
        return arrived

    def listed(arrived):
        return [arrived[k, d] for k in range(wide) for d in range(levs)]

    arrived = exchanged(blocks, (near[0], scale))
    half_shard = shard_rows // 2
    own_table, _ = behind(legendre[0], blocks[0])
    first = over_lev(lax.dynamic_slice_in_dim(own_table, lax.axis_index("ens") * half_shard, half_shard, 0))
    steps = [(1, 0), (2, 0), (3, 0), (0, 1)]
    first, *ahead = behind(first, *(arrived[step] for step in steps))
    arrived |= dict(zip(steps, ahead))
    second = shifted(first, "ens", 2, 1)
    steps = [(1, 1), (2, 1), (3, 1)]
    second, *ahead = behind(second, *(arrived[step] for step in steps))
    arrived |= dict(zip(steps, ahead))
    far = call(
        far_table_body, shape(shard_rows, half_count), "split_table", 2 * shard_rows * shard_rows * half_count,
        scratch=[pltpu.VMEM((shard_rows, half_count), bf16)],
    )(meta, first, second)
    far = [far, beside(far)]

    half_rows = degree_count // 2
    *near_spectral, data = call(
        functools.partial(near_body, wide), (shape(half_rows, lanes),) * 2 + (shape(2, half_count, columns),),
        "direct_legendre_and_solve", transform_flops // 2,
    )(meta, *matrices, scale, *near, *listed(arrived))
    far_spectral = call(
        far_body, (shape(half_rows, lanes),) * 2, "direct_legendre_and_solve", transform_flops // 2, scalars=0,
    )(*matrices, scale, *far, data)
    spectral = (near_spectral, far_spectral)
    grid = call(
        functools.partial(inverse_body, wide), (shape(2, latitudes, lanes),) * (wide * levs),
        "inverse_legendre", transform_flops, scratch=[pltpu.VMEM((2, half_count, columns), bf16)],
    )(meta, *near_spectral, *far_spectral, *near, *far)
    arrived = exchanged(grid, ())
    others = [other for _, other in spectral]
    arrived[0, 1], *others = behind(arrived[0, 1], *others)
    result = listed(arrived)
    spectral_rows = call(
        functools.partial(rows_body, sizes, 32), shape(degree_count * fields, lanes), "order_spectral", move_flops,
    )(meta, *(own for own, _ in spectral), *(over_lev(other) for other in others))
    fourier_rows = call(
        functools.partial(join_body, slots, 256 // group), shape(2, latitudes * group, lanes),
        "join_hemispheres", move_flops,
    )(meta, *result)
    return (
        fourier_rows.reshape(2, latitudes, slots, fields, lanes),
        spectral_rows.reshape(1, degree_count, fields, lanes),
    )


def project(level_grid, degree_real, weight_rows, rate_rows, degree_total):
    projected = jnp.einsum(
        "kl,snflr->snfkr", weight_rows, level_grid, preferred_element_type=jnp.float32
    )
    factor = 1.0 + degree_real[:, None] * (degree_real[:, None] + 1.0) * rate_rows[None, :] / (
        degree_total * degree_total
    )
    return (projected / factor[None, :, None, :, None]).astype(jnp.bfloat16)


def plain_shards(fourier_input_rows, legendre, slot_wave, to_modes, from_modes, mode_rate):
    wave_rows = lax.all_to_all(fourier_input_rows, "wide", split_axis=2, concat_axis=1, tiled=True)
    half_count = wave_rows.shape[1]
    slot_count = wave_rows.shape[2]
    field_count = wave_rows.shape[3]
    column_count = wave_rows.shape[4]
    degree_count = legendre.shape[1] * lax.axis_size(("lev", "fld"))
    weights = latitude_weights(half_count)[:, None, None, None]
    north_half = wave_rows[0].astype(jnp.float32)
    south_half = wave_rows[1].astype(jnp.float32)
    symmetric = (weights * (north_half + south_half)).astype(jnp.bfloat16)
    antisym = (weights * (north_half - south_half)).astype(jnp.bfloat16)
    paired = jnp.concatenate((symmetric, antisym), axis=3)

    def direct_rows(section, first_row):
        row_count = section.shape[1]
        degree = first_row + jnp.arange(row_count, dtype=jnp.int32)
        relative = degree[None, :] - slot_wave[:, None]
        product = jnp.einsum("snj,jsfc->snfc", section, paired, preferred_element_type=jnp.float32)
        is_even = (relative % 2 == 0)[:, :, None, None]
        is_live = (relative >= 0)[:, :, None, None]
        picked = jnp.where(is_even, product[..., :column_count], product[..., column_count:])
        return jnp.where(is_live, picked, jnp.zeros_like(picked))

    full_table = lax.all_gather(legendre, ("lev", "fld"), axis=1, tiled=True)
    block_rows = 128
    block_count = degree_count // block_rows

    def direct_step(block_index, buffer):
        first_row = block_index * block_rows
        section = lax.dynamic_slice_in_dim(full_table, first_row, block_rows, 1)
        result = direct_rows(section, first_row).astype(jnp.bfloat16)
        return lax.dynamic_update_slice_in_dim(buffer, result, first_row, 1)

    initial_raw = jnp.zeros((slot_count, degree_count, field_count, column_count), jnp.bfloat16)
    raw_spectral = lax.fori_loop(0, block_count, direct_step, initial_raw)
    own_levels = column_count // 2
    first_level = lax.axis_index("lev") * own_levels
    degree_real = jnp.arange(degree_count, dtype=jnp.float32)
    all_levels = lax.all_gather(raw_spectral, "lev", axis=3, tiled=True)
    level_count = all_levels.shape[3] // 2
    level_grid = all_levels.reshape(slot_count, degree_count, field_count, level_count, 2)
    weight_rows = lax.dynamic_slice_in_dim(to_modes, first_level, own_levels, 0)
    rate_rows = lax.dynamic_slice_in_dim(mode_rate, first_level, own_levels, 0)
    own_modes = project(level_grid, degree_real, weight_rows, rate_rows, degree_count).reshape(
        slot_count, degree_count, field_count, column_count
    )
    mode_values = lax.all_gather(own_modes, "lev", axis=3, tiled=True).reshape(
        slot_count, degree_count, field_count, level_count, 2
    )
    back_rows = lax.dynamic_slice_in_dim(from_modes, first_level, own_levels, 0)
    spectral = jnp.einsum(
        "lk,snfkr->snflr", back_rows, mode_values, preferred_element_type=jnp.float32
    )
    spectral = spectral.astype(jnp.bfloat16).reshape(
        slot_count, degree_count, field_count, column_count
    )

    def inverse_rows(running, section, first_row):
        row_count = section.shape[1]
        degree = first_row + jnp.arange(row_count, dtype=jnp.int32)
        relative = degree[None, :] - slot_wave[:, None]
        spec_rows = lax.dynamic_slice_in_dim(spectral, first_row, row_count, 1)
        even_mask = ((relative >= 0) & (relative % 2 == 0))[:, :, None, None]
        odd_mask = ((relative >= 0) & (relative % 2 == 1))[:, :, None, None]
        empty_rows = jnp.zeros_like(spec_rows)
        parity_split = jnp.concatenate(
            (
                jnp.where(even_mask, spec_rows, empty_rows),
                jnp.where(odd_mask, spec_rows, empty_rows),
            ),
            axis=3,
        )
        return running + jnp.einsum(
            "snj,snfc->jsfc", section, parity_split, preferred_element_type=jnp.float32
        )

    initial_sum = jnp.zeros((half_count, slot_count, field_count, 2 * column_count), jnp.float32)

    def inverse_step(block_index, running):
        first_row = block_index * block_rows
        section = lax.dynamic_slice_in_dim(full_table, first_row, block_rows, 1)
        return inverse_rows(running, section, first_row)

    running = lax.fori_loop(0, block_count, inverse_step, initial_sum)
    even_sum = running[..., :column_count]
    odd_sum = running[..., column_count:]
    fourier_wave = jnp.stack((even_sum + odd_sum, even_sum - odd_sum), axis=0).astype(jnp.bfloat16)
    fourier_out = lax.all_to_all(fourier_wave, "wide", split_axis=1, concat_axis=2, tiled=True)
    return (fourier_out, spectral)


def solution(mesh):
    in_specs = (
        P("ens", "wide", None, "fld", "lev"),
        P("wide", ("lev", "fld"), None),
        P("wide"),
        P(),
        P(),
        P(),
    )
    out_specs = (P("ens", "wide", None, "fld", "lev"), P(("ens", "wide"), None, "fld", "lev"))

    def body(fourier_input_rows, legendre, *rest):
        _, latitudes, slots, fields, lanes = fourier_input_rows.shape
        whole_tiles = (
            latitudes % 32 == 0
            and fields == 2
            and slots == mesh.shape["wide"] == 4
            and mesh.shape["ens"] == mesh.shape["lev"] == mesh.shape["fld"] == 2
            and lanes == 128
            and legendre.shape[1] % 64 == 0
            and legendre.shape[2] % 256 == 0
        )
        form = shards if whole_tiles else plain_shards
        return form(fourier_input_rows, legendre, *rest)

    return jax.shard_map(body, mesh=mesh, in_specs=in_specs, out_specs=out_specs, check_vma=False)
```

```python
import functools
import math

import jax
import jax.numpy as jnp
from jax import lax
from jax.experimental import pallas as pl
from jax.experimental.pallas import tpu as pltpu
from jax.sharding import PartitionSpec as P

VMEM_BYTES = 8 * 1024 * 1024


def latitude_weights(count):
    position = jnp.arange(count, dtype=jnp.float32)
    return jnp.sin(math.pi * (position + 0.5) / (2 * count))


def iota2(shape, dim):
    return lax.broadcasted_iota(jnp.int32, shape, dim)


def picks(condition):
    return jnp.where(condition, 1.0, 0.0).astype(jnp.bfloat16)


def dot32(a, b):
    return jnp.dot(a, b, preferred_element_type=jnp.float32)


def call_by_latitude(body, steps, out_shape, name, flops):
    def block_of(array):
        dims = array.shape
        if len(dims) == 2:
            return pl.BlockSpec((dims[0] // steps, dims[1]), lambda i: (i, 0))
        return pl.BlockSpec((dims[0], dims[1] // steps, dims[2]), lambda i: (0, i, 0))

    def run(meta, *operands):
        return pl.pallas_call(
            body,
            grid=(steps,),
            out_shape=out_shape,
            in_specs=[pl.BlockSpec(memory_space=pltpu.SMEM)] + [block_of(one) for one in operands],
            out_specs=jax.tree.map(block_of, out_shape),
            compiler_params=pltpu.CompilerParams(vmem_limit_bytes=VMEM_BYTES),
            cost_estimate=pl.CostEstimate(flops=flops, bytes_accessed=0, transcendentals=0),
            name=name,
        )(meta, *operands)

    return run


def call(body, out_shape, name, flops, scratch=(), scalars=1, after=()):
    smem = pl.BlockSpec(memory_space=pltpu.SMEM)
    vmem = pl.BlockSpec(memory_space=pltpu.VMEM)

    def run(*operands):
        used = len(operands)

        def kernel(*refs):
            body(*refs[:used], *refs[used + len(after) :])

        return pl.pallas_call(
            kernel,
            out_shape=out_shape,
            in_specs=[smem] * scalars
            + [vmem] * (used - scalars)
            + [pl.BlockSpec(memory_space=pl.ANY)] * len(after),
            out_specs=jax.tree.map(lambda _: vmem, out_shape),
            scratch_shapes=list(scratch),
            compiler_params=pltpu.CompilerParams(vmem_limit_bytes=VMEM_BYTES),
            cost_estimate=pl.CostEstimate(flops=flops, bytes_accessed=0, transcendentals=0),
            name=name,
        )(*operands, *after)

    return run


def lane_order(lanes, lev, old, new):
    levels = lanes // 4
    part = lax.rem(new // (lanes // 2) + lev, 2)
    field = (new // levels) % 2
    return old == field * (lanes // 2) + 2 * (new % levels) + part


def split_body(slots, fields, block, meta_ref, rows_ref, weight_ref, *outs):
    latitudes = weight_ref.shape[0]
    group = slots * fields
    size = block * group
    out_row, in_row = iota2((size, size), 0), iota2((size, size), 1)
    pair = out_row // block
    slot = lax.rem(meta_ref[1] + pair // fields, slots)
    order = picks(in_row == (out_row % block) * group + slot * fields + pair % fields)
    lanes = fields * 128
    parts = picks(lane_order(lanes, meta_ref[2], iota2((lanes, lanes), 0), iota2((lanes, lanes), 1)))
    for first in range(0, latitudes, block):
        north = rows_ref[0, first * group : first * group + size, :]
        south = rows_ref[1, first * group : first * group + size, :]
        sorted_rows = dot32(order, jnp.concatenate((north, south), axis=1))
        up, down = sorted_rows[:, :128], sorted_rows[:, 128:]
        weight = weight_ref[first : first + block, :]
        halves = []
        for mixed in (up + down, up - down):
            for shift in range(slots):
                at = shift * fields * block
                halves.append(jnp.concatenate(
                    [
                        (weight * mixed[at + f * block : at + f * block + block]).astype(jnp.bfloat16)
                        for f in range(fields)
                    ],
                    axis=1,
                ))
        turned = dot32(jnp.concatenate(halves, axis=0), parts).astype(jnp.bfloat16)
        for odd in range(2):
            for shift in range(slots):
                at = (odd * slots + shift) * block
                for d in range(2):
                    outs[shift * 2 + d][odd, first : first + block, :] = turned[
                        at : at + block, d * 128 : d * 128 + 128
                    ]


def by_parity(meta_ref, rows):
    half = rows // 2
    out_row, in_row = iota2((rows, rows), 0), iota2((rows, rows), 1)
    odd = jnp.where(out_row < half, 0, 1)
    return picks(in_row == 2 * (out_row - odd * half) + (meta_ref[0] + odd) % 2)


def near_table_body(meta_ref, own_ref, beside_ref, even_ref, odd_ref):
    rows, columns = own_ref.shape
    half = rows // 2
    order = by_parity(meta_ref, rows)
    for g, table_ref in enumerate((own_ref, beside_ref)):
        at = slice(g * half, g * half + half)
        for first in range(0, columns, 256):
            lanes = slice(first, first + 256)
            result = dot32(order, table_ref[:, lanes]).astype(jnp.bfloat16)
            even_ref[at, lanes] = result[:half]
            odd_ref[at, lanes] = result[half:]


def far_table_body(meta_ref, first_ref, second_ref, out_ref, whole):
    half, columns = first_ref.shape
    for ens, ref in ((meta_ref[4], first_ref), (1 - meta_ref[4], second_ref)):
        whole[pl.ds(pl.multiple_of(ens * half, half), half), :] = ref[...]
    order = by_parity(meta_ref, 2 * half)
    for first in range(0, columns, 256):
        lanes = slice(first, first + 256)
        out_ref[:, lanes] = dot32(order, whole[:, lanes]).astype(jnp.bfloat16)


def modes_body(sizes, degree_total, meta_ref, to_ref, from_ref, rate_ref, in_ref, out_ref, scale_ref):
    levels = to_ref.shape[0]
    wide = 2 * levels
    own = levels // 2
    lane, row = iota2((levels, wide), 1), iota2((levels, wide), 0)
    owner = lax.rem(meta_ref[2] + lane // levels, 2)
    spread = picks(row == owner * own + lane % own)
    plain = picks(row == lane % levels)
    old, new = iota2((wide, wide), 0), iota2((wide, wide), 1)

    def turned(first, matrix, last):
        half = lax.dot_general(first, matrix, (((0,), (1,)), ((), ())), preferred_element_type=jnp.float32)
        return dot32(half.astype(jnp.bfloat16), last)

    same = (old // own) % 2 == new // levels
    in_ref[...] = jnp.where(same, turned(spread, to_ref[...], plain), 0.0).astype(jnp.bfloat16)
    same = old // levels == (new // own) % 2
    out_ref[...] = jnp.where(same, turned(plain, from_ref[...], spread), 0.0).astype(jnp.bfloat16)
    wide, levs, flds = sizes
    rows = degree_total // (2 * levs * flds)
    for odd in range(2):
        for d in range(levs):
            for g in range(flds):
                block = lax.rem(meta_ref[2] + d, levs) * flds + lax.rem(meta_ref[3] + g, flds)
                degree = block * (2 * rows) + 2 * iota2((rows, 1), 0) + (meta_ref[0] + odd) % 2
                real = degree.astype(jnp.float32)
                factor = 1.0 + real * (real + 1.0) * rate_ref[...] / (degree_total * degree_total)
                at = ((d * 2 + odd) * flds + g) * rows
                scale_ref[at : at + rows, :] = jnp.where(degree >= meta_ref[0], 1.0 / factor, 0.0)


def transform(tables, data, scale_ref, in_ref, out_ref, own_ref, other_ref):
    lanes = own_ref.shape[1]
    rows = own_ref.shape[0] // 2
    for odd in range(2):
        at = slice(odd * rows, odd * rows + rows)
        raw = dot32(tables[odd], data[odd]).astype(jnp.bfloat16)
        scale = jnp.concatenate([scale_ref[at, :]] * 2, axis=1)
        modes = (dot32(raw, in_ref[...]) * scale).astype(jnp.bfloat16)
        spectral = dot32(modes, out_ref[...]).astype(jnp.bfloat16)
        own_ref[at, :] = spectral[:, :lanes]
        other_ref[at, :] = spectral[:, lanes:]


def near_body(wide, meta_ref, in_ref, out_ref, scale_ref, even_ref, odd_ref, *refs):
    parts, (own_ref, other_ref, data_ref) = refs[:-3], refs[-3:]
    latitudes, lanes = parts[0].shape[1:]
    for shift in range(wide):
        owner = lax.rem(meta_ref[1] - shift + wide, wide)
        at = pl.ds(pl.multiple_of(owner * latitudes, latitudes), latitudes)
        for d in range(2):
            data_ref[:, at, d * lanes : d * lanes + lanes] = parts[shift * 2 + d][...]
    scale = scale_ref.at[: scale_ref.shape[0] // 2]
    transform((even_ref[...], odd_ref[...]), data_ref, scale, in_ref, out_ref, own_ref, other_ref)


def far_body(in_ref, out_ref, scale_ref, first_ref, second_ref, data_ref, own_ref, other_ref):
    rows = first_ref.shape[0] // 2
    tables = [
        jnp.concatenate([ref[odd * rows : odd * rows + rows, :] for ref in (first_ref, second_ref)], axis=0)
        for odd in range(2)
    ]
    scale = scale_ref.at[scale_ref.shape[0] // 2 :]
    transform(tables, data_ref, scale, in_ref, out_ref, own_ref, other_ref)


def inverse_body(wide, meta_ref, *refs):
    parts, near, far, outs, total = refs[:4], refs[4:6], refs[6:8], refs[8:-1], refs[-1]
    latitudes, lanes = outs[0].shape[1:]
    rows = parts[0].shape[0] // 2
    spectral = [
        jnp.concatenate(
            [
                jnp.concatenate([ref[odd * rows : odd * rows + rows, :] for ref in pair], axis=1)
                for pair in (parts[:2], parts[2:])
            ],
            axis=0,
        )
        for odd in range(2)
    ]
    for first in range(0, total.shape[1], 256):
        chunk = slice(first, first + 256)
        sums = []
        for odd in range(2):
            at = slice(odd * (rows // 2), (odd + 1) * (rows // 2))
            table = jnp.concatenate([near[odd][:, chunk]] + [ref[at, chunk] for ref in far], axis=0)
            sums.append(lax.dot_general(
                table, spectral[odd], (((0,), (0,)), ((), ())), preferred_element_type=jnp.float32
            ))
        total[0, chunk, :] = (sums[0] + sums[1]).astype(jnp.bfloat16)
        total[1, chunk, :] = (sums[0] - sums[1]).astype(jnp.bfloat16)
    for shift in range(wide):
        owner = lax.rem(meta_ref[1] + shift, wide)
        at = pl.ds(pl.multiple_of(owner * latitudes, latitudes), latitudes)
        for d in range(2):
            outs[shift * 2 + d][...] = total[:, at, d * lanes : d * lanes + lanes]


def join_body(slots, block, meta_ref, *refs):
    parts, out_ref = refs[:-1], refs[-1]
    latitudes, lanes = parts[0].shape[1:]
    fields = 2
    group = slots * fields
    size = block * group
    out_row, in_row = iota2((size, size), 0), iota2((size, size), 1)
    place = out_row % group
    shift = lax.rem(meta_ref[1] - place // fields + slots, slots)
    order = picks(in_row == (shift * fields + place % fields) * block + out_row // group)
    both = 2 * lanes
    turn = picks(lane_order(both, meta_ref[2], iota2((both, both), 1), iota2((both, both), 0)))
    for first in range(0, latitudes, block):
        at = slice(first, first + block)
        stacked = jnp.concatenate(
            [
                jnp.concatenate([parts[shift * 2 + d][half, at, :] for d in range(2)], axis=1)
                for half in range(2)
                for shift in range(slots)
            ],
            axis=0,
        )
        turned = dot32(stacked, turn).astype(jnp.bfloat16)
        halves = [
            jnp.concatenate(
                [
                    turned[
                        (half * slots + shift) * block : (half * slots + shift + 1) * block,
                        field * lanes : field * lanes + lanes,
                    ]
                    for shift in range(slots)
                    for field in range(fields)
                ],
                axis=0,
            )
            for half in range(2)
        ]
        result = dot32(order, jnp.concatenate(halves, axis=1)).astype(jnp.bfloat16)
        for half in range(2):
            out_ref[half, first * group : first * group + size, :] = result[:, half * lanes : half * lanes + lanes]


def rows_body(sizes, block, meta_ref, *refs):
    wide, levs, flds = sizes
    own_refs, other_refs, out_ref = refs[:2], refs[2:4], refs[4]
    total_rows, lanes = own_refs[0].shape
    rows = total_rows // (2 * flds)
    fields = 2
    group = 2 * fields
    size = block * group
    out_row, in_row = iota2((size, size), 0), iota2((size, size), 1)
    place = out_row % group
    odd = (place // fields + meta_ref[0] % 2) % 2
    order = picks(in_row == (odd * fields + place % fields) * block + out_row // group)
    both = 2 * lanes
    turn = picks(lane_order(both, meta_ref[2], iota2((both, both), 1), iota2((both, both), 0)))
    for d in range(levs):
        for g in range(flds):
            index = lax.rem(meta_ref[2] + d, levs) * flds + lax.rem(meta_ref[3] + g, flds)
            halves = []
            for odd in range(2):
                at = slice((odd * flds + g) * rows, (odd * flds + g + 1) * rows)
                halves.append(jnp.concatenate((own_refs[d][at, :], other_refs[1 - d][at, :]), axis=1))
            turned = dot32(jnp.concatenate(halves, axis=0), turn).astype(jnp.bfloat16)
            for first in range(0, rows, block):
                stacked = jnp.concatenate(
                    [
                        turned[
                            odd * rows + first : odd * rows + first + block, field * lanes : field * lanes + lanes
                        ]
                        for odd in range(2)
                        for field in range(fields)
                    ],
                    axis=0,
                )
                start = pl.multiple_of(index * (rows * group), rows * group) + first * group
                out_ref[pl.ds(start, size), :] = dot32(order, stacked).astype(jnp.bfloat16)


def shards(fourier_input_rows, legendre, slot_wave, to_modes, from_modes, mode_rate):
    wide, levs, flds = (lax.axis_size(axis) for axis in ("wide", "lev", "fld"))
    sizes = (wide, levs, flds)
    _, latitudes, slots, fields, lanes = fourier_input_rows.shape
    _, shard_rows, half_count = legendre.shape
    degree_count = shard_rows * levs * flds
    group = slots * fields
    columns = fields * lanes
    block = 256 // group
    levels = to_modes.shape[0]
    bf16 = jnp.bfloat16

    def shape(*dims):
        return jax.ShapeDtypeStruct(dims, bf16)

    def shifted(value, axis, count, step):
        return lax.ppermute(value, axis, [(i, (i + step) % count) for i in range(count)])

    def over_lev(value):
        return shifted(value, "lev", levs, 1)

    def beside(value):
        return shifted(value, "fld", flds, 1)

    def moved(value, k, d):
        pairs = [(w * levs + l, (w + k) % wide * levs + (l + d) % levs) for w in range(wide) for l in range(levs)]
        return lax.ppermute(value, ("wide", "lev"), pairs)

    def behind(value, *others):
        return lax.optimization_barrier((value, *others))

    wide_at, lev_at, fld_at = (lax.axis_index(axis) for axis in ("wide", "lev", "fld"))
    meta = jnp.stack((slot_wave[0], wide_at, lev_at, fld_at, lax.axis_index("ens"))).astype(jnp.int32)
    position = (wide_at * latitudes + jnp.arange(latitudes, dtype=jnp.int32)).astype(jnp.float32)
    weights = jnp.sin(math.pi * (position + 0.5) / (2 * half_count))
    weights = jnp.broadcast_to(weights[:, None], (latitudes, lanes))
    move_flops = 8 * group * latitudes * 128 * 256
    transform_flops = 2 * degree_count * half_count * columns

    table_beside = beside(legendre[0])
    pieces = latitudes // (2 * block)
    blocks = call_by_latitude(
        functools.partial(split_body, slots, fields, block), pieces, (shape(2, latitudes, lanes),) * (wide * levs),
        "split_hemispheres", move_flops,
    )(meta, fourier_input_rows.reshape(2, latitudes * group, lanes), weights)
    table_beside, *blocks = behind(table_beside, *blocks)
    *matrices, scale = call(
        functools.partial(modes_body, sizes, degree_count),
        (shape(2 * levels, 2 * levels),) * 2 + (jax.ShapeDtypeStruct((degree_count, levels), jnp.float32),),
        "spread_modes", 12 * levels * levels * levels, after=(blocks[0],),
    )(meta, to_modes, from_modes, mode_rate[None, :])
    near = call(
        near_table_body, (shape(shard_rows, half_count),) * 2, "split_table",
        4 * shard_rows * shard_rows * half_count, after=(scale,),
    )(meta, legendre[0], table_beside)

    def exchanged(blocks, ahead, leads, over=()):
        arrived = {(0, 0): blocks[0]}
        for k, d in ((2, 0), (1, 0), (3, 0), (0, 1)):
            arrived[k, d] = moved(blocks[k * levs + d], k, d)
        over = list(over)
        if over:
            over[1], arrived[0, 1] = behind(over[1], arrived[0, 1])
            over = [over_lev(one) for one in over]
        for k, first in zip((2, 1, 3), leads):
            value, arrived[first], *rest = behind(blocks[k * levs + 1], arrived[first], *(over or ahead))
            over = rest if over else over
            arrived[k, 1] = moved(value, k, 1)
        return arrived, over

    def listed(arrived):
        return [arrived[k, d] for k in range(wide) for d in range(levs)]

    arrived, _ = exchanged(blocks, (near[0], scale), ((0, 1), (1, 0), (3, 0)))
    half_shard = shard_rows // 2
    first = over_lev(lax.dynamic_slice_in_dim(legendre[0], lax.axis_index("ens") * half_shard, half_shard, 0))
    steps = [(1, 0), (2, 0), (3, 0), (0, 1)]
    first, *ahead = behind(first, *(arrived[step] for step in steps))
    arrived |= dict(zip(steps, ahead))
    second = shifted(first, "ens", 2, 1)
    steps = [(1, 1), (2, 1), (3, 1)]
    second, *ahead = behind(second, *(arrived[step] for step in steps))
    arrived |= dict(zip(steps, ahead))
    far = call(
        far_table_body, shape(shard_rows, half_count), "split_table", 2 * shard_rows * shard_rows * half_count,
        scratch=[pltpu.VMEM((shard_rows, half_count), bf16)],
    )(meta, first, second)
    far = [far, beside(far)]

    half_rows = degree_count // 2
    *near_spectral, data = call(
        functools.partial(near_body, wide), (shape(half_rows, lanes),) * 2 + (shape(2, half_count, columns),),
        "direct_legendre_and_solve", transform_flops // 2,
    )(meta, *matrices, scale, *near, *listed(arrived))
    far_spectral = call(
        far_body, (shape(half_rows, lanes),) * 2, "direct_legendre_and_solve", transform_flops // 2, scalars=0,
    )(*matrices, scale, *far, data)
    spectral = (near_spectral, far_spectral)
    grid = call(
        functools.partial(inverse_body, wide), (shape(2, latitudes, lanes),) * (wide * levs),
        "inverse_legendre", transform_flops, scratch=[pltpu.VMEM((2, half_count, columns), bf16)],
    )(meta, *near_spectral, *far_spectral, *near, *far)
    leads = ((2, 0), (1, 0), (3, 0))
    arrived, others = exchanged(grid, (), leads, [other for _, other in spectral])
    result = listed(arrived)
    spectral_rows = call(
        functools.partial(rows_body, sizes, 32), shape(degree_count * fields, lanes), "order_spectral", move_flops,
    )(meta, *(own for own, _ in spectral), *others)
    fourier_rows = call_by_latitude(
        functools.partial(join_body, slots, block), pieces, shape(2, latitudes * group, lanes),
        "join_hemispheres", move_flops,
    )(meta, *result)
    return (
        fourier_rows.reshape(2, latitudes, slots, fields, lanes),
        spectral_rows.reshape(1, degree_count, fields, lanes),
    )


def project(level_grid, degree_real, weight_rows, rate_rows, degree_total):
    projected = jnp.einsum(
        "kl,snflr->snfkr", weight_rows, level_grid, preferred_element_type=jnp.float32
    )
    factor = 1.0 + degree_real[:, None] * (degree_real[:, None] + 1.0) * rate_rows[None, :] / (
        degree_total * degree_total
    )
    return (projected / factor[None, :, None, :, None]).astype(jnp.bfloat16)


def plain_shards(fourier_input_rows, legendre, slot_wave, to_modes, from_modes, mode_rate):
    wave_rows = lax.all_to_all(fourier_input_rows, "wide", split_axis=2, concat_axis=1, tiled=True)
    half_count = wave_rows.shape[1]
    slot_count = wave_rows.shape[2]
    field_count = wave_rows.shape[3]
    column_count = wave_rows.shape[4]
    degree_count = legendre.shape[1] * lax.axis_size(("lev", "fld"))
    weights = latitude_weights(half_count)[:, None, None, None]
    north_half = wave_rows[0].astype(jnp.float32)
    south_half = wave_rows[1].astype(jnp.float32)
    symmetric = (weights * (north_half + south_half)).astype(jnp.bfloat16)
    antisym = (weights * (north_half - south_half)).astype(jnp.bfloat16)
    paired = jnp.concatenate((symmetric, antisym), axis=3)

    def direct_rows(section, first_row):
        row_count = section.shape[1]
        degree = first_row + jnp.arange(row_count, dtype=jnp.int32)
        relative = degree[None, :] - slot_wave[:, None]
        product = jnp.einsum("snj,jsfc->snfc", section, paired, preferred_element_type=jnp.float32)
        is_even = (relative % 2 == 0)[:, :, None, None]
        is_live = (relative >= 0)[:, :, None, None]
        picked = jnp.where(is_even, product[..., :column_count], product[..., column_count:])
        return jnp.where(is_live, picked, jnp.zeros_like(picked))

    full_table = lax.all_gather(legendre, ("lev", "fld"), axis=1, tiled=True)
    block_rows = 128
    block_count = degree_count // block_rows

    def direct_step(block_index, buffer):
        first_row = block_index * block_rows
        section = lax.dynamic_slice_in_dim(full_table, first_row, block_rows, 1)
        result = direct_rows(section, first_row).astype(jnp.bfloat16)
        return lax.dynamic_update_slice_in_dim(buffer, result, first_row, 1)

    initial_raw = jnp.zeros((slot_count, degree_count, field_count, column_count), jnp.bfloat16)
    raw_spectral = lax.fori_loop(0, block_count, direct_step, initial_raw)
    own_levels = column_count // 2
    first_level = lax.axis_index("lev") * own_levels
    degree_real = jnp.arange(degree_count, dtype=jnp.float32)
    all_levels = lax.all_gather(raw_spectral, "lev", axis=3, tiled=True)
    level_count = all_levels.shape[3] // 2
    level_grid = all_levels.reshape(slot_count, degree_count, field_count, level_count, 2)
    weight_rows = lax.dynamic_slice_in_dim(to_modes, first_level, own_levels, 0)
    rate_rows = lax.dynamic_slice_in_dim(mode_rate, first_level, own_levels, 0)
    own_modes = project(level_grid, degree_real, weight_rows, rate_rows, degree_count).reshape(
        slot_count, degree_count, field_count, column_count
    )
    mode_values = lax.all_gather(own_modes, "lev", axis=3, tiled=True).reshape(
        slot_count, degree_count, field_count, level_count, 2
    )
    back_rows = lax.dynamic_slice_in_dim(from_modes, first_level, own_levels, 0)
    spectral = jnp.einsum(
        "lk,snfkr->snflr", back_rows, mode_values, preferred_element_type=jnp.float32
    )
    spectral = spectral.astype(jnp.bfloat16).reshape(
        slot_count, degree_count, field_count, column_count
    )

    def inverse_rows(running, section, first_row):
        row_count = section.shape[1]
        degree = first_row + jnp.arange(row_count, dtype=jnp.int32)
        relative = degree[None, :] - slot_wave[:, None]
        spec_rows = lax.dynamic_slice_in_dim(spectral, first_row, row_count, 1)
        even_mask = ((relative >= 0) & (relative % 2 == 0))[:, :, None, None]
        odd_mask = ((relative >= 0) & (relative % 2 == 1))[:, :, None, None]
        empty_rows = jnp.zeros_like(spec_rows)
        parity_split = jnp.concatenate(
            (
                jnp.where(even_mask, spec_rows, empty_rows),
                jnp.where(odd_mask, spec_rows, empty_rows),
            ),
            axis=3,
        )
        return running + jnp.einsum(
            "snj,snfc->jsfc", section, parity_split, preferred_element_type=jnp.float32
        )

    initial_sum = jnp.zeros((half_count, slot_count, field_count, 2 * column_count), jnp.float32)

    def inverse_step(block_index, running):
        first_row = block_index * block_rows
        section = lax.dynamic_slice_in_dim(full_table, first_row, block_rows, 1)
        return inverse_rows(running, section, first_row)

    running = lax.fori_loop(0, block_count, inverse_step, initial_sum)
    even_sum = running[..., :column_count]
    odd_sum = running[..., column_count:]
    fourier_wave = jnp.stack((even_sum + odd_sum, even_sum - odd_sum), axis=0).astype(jnp.bfloat16)
    fourier_out = lax.all_to_all(fourier_wave, "wide", split_axis=1, concat_axis=2, tiled=True)
    return (fourier_out, spectral)


def solution(mesh):
    in_specs = (
        P("ens", "wide", None, "fld", "lev"),
        P("wide", ("lev", "fld"), None),
        P("wide"),
        P(),
        P(),
        P(),
    )
    out_specs = (P("ens", "wide", None, "fld", "lev"), P(("ens", "wide"), None, "fld", "lev"))

    def body(fourier_input_rows, legendre, *rest):
        _, latitudes, slots, fields, lanes = fourier_input_rows.shape
        whole_tiles = (
            latitudes % 64 == 0
            and fields == 2
            and slots == mesh.shape["wide"] == 4
            and mesh.shape["ens"] == mesh.shape["lev"] == mesh.shape["fld"] == 2
            and lanes == 128
            and legendre.shape[1] % 64 == 0
            and legendre.shape[2] % 256 == 0
        )
        form = shards if whole_tiles else plain_shards
        return form(fourier_input_rows, legendre, *rest)

    return jax.shard_map(body, mesh=mesh, in_specs=in_specs, out_specs=out_specs, check_vma=False)
```

```python
import functools
import math

import jax
import jax.numpy as jnp
from jax import lax
from jax.experimental import pallas as pl
from jax.experimental.pallas import tpu as pltpu
from jax.sharding import PartitionSpec as P

VMEM_BYTES = 8 * 1024 * 1024


def latitude_weights(count):
    position = jnp.arange(count, dtype=jnp.float32)
    return jnp.sin(math.pi * (position + 0.5) / (2 * count))


def iota2(shape, dim):
    return lax.broadcasted_iota(jnp.int32, shape, dim)


def picks(condition):
    return jnp.where(condition, 1.0, 0.0).astype(jnp.bfloat16)


def dot32(a, b):
    return jnp.dot(a, b, preferred_element_type=jnp.float32)


def call(body, out_shape, name, flops, scratch=(), scalars=1, after=()):
    smem = pl.BlockSpec(memory_space=pltpu.SMEM)
    vmem = pl.BlockSpec(memory_space=pltpu.VMEM)

    def run(*operands):
        used = len(operands)

        def kernel(*refs):
            body(*refs[:used], *refs[used + len(after) :])

        return pl.pallas_call(
            kernel,
            out_shape=out_shape,
            in_specs=[smem] * scalars
            + [vmem] * (used - scalars)
            + [pl.BlockSpec(memory_space=pl.ANY)] * len(after),
            out_specs=jax.tree.map(lambda _: vmem, out_shape),
            scratch_shapes=list(scratch),
            compiler_params=pltpu.CompilerParams(vmem_limit_bytes=VMEM_BYTES),
            cost_estimate=pl.CostEstimate(flops=flops, bytes_accessed=0, transcendentals=0),
            name=name,
        )(*operands, *after)

    return run


def lane_order(lanes, lev, old, new):
    levels = lanes // 4
    part = lax.rem(new // (lanes // 2) + lev, 2)
    field = (new // levels) % 2
    return old == field * (lanes // 2) + 2 * (new % levels) + part


def split_body(slots, fields, block, meta_ref, rows_ref, weight_ref, *outs):
    latitudes = weight_ref.shape[0]
    group = slots * fields
    size = block * group
    out_row, in_row = iota2((size, size), 0), iota2((size, size), 1)
    pair = out_row // block
    slot = lax.rem(meta_ref[1] + pair // fields, slots)
    order = picks(in_row == (out_row % block) * group + slot * fields + pair % fields)
    lanes = fields * 128
    parts = picks(lane_order(lanes, meta_ref[2], iota2((lanes, lanes), 0), iota2((lanes, lanes), 1)))
    for first in range(0, latitudes, block):
        north = rows_ref[0, first * group : first * group + size, :]
        south = rows_ref[1, first * group : first * group + size, :]
        sorted_rows = dot32(order, jnp.concatenate((north, south), axis=1))
        up, down = sorted_rows[:, :128], sorted_rows[:, 128:]
        weight = weight_ref[first : first + block, :]
        halves = []
        for mixed in (up + down, up - down):
            for shift in range(slots):
                at = shift * fields * block
                halves.append(jnp.concatenate(
                    [
                        (weight * mixed[at + f * block : at + f * block + block]).astype(jnp.bfloat16)
                        for f in range(fields)
                    ],
                    axis=1,
                ))
        turned = dot32(jnp.concatenate(halves, axis=0), parts).astype(jnp.bfloat16)
        for odd in range(2):
            for shift in range(slots):
                at = (odd * slots + shift) * block
                outs[shift][odd, first : first + block, :] = turned[at : at + block, :]


def by_parity(meta_ref, rows):
    half = rows // 2
    out_row, in_row = iota2((rows, rows), 0), iota2((rows, rows), 1)
    odd = jnp.where(out_row < half, 0, 1)
    return picks(in_row == 2 * (out_row - odd * half) + (meta_ref[0] + odd) % 2)


def table_body(meta_ref, own_ref, beside_ref, even_ref, odd_ref):
    rows, columns = own_ref.shape
    half = rows // 2
    order = by_parity(meta_ref, rows)
    for g, table_ref in enumerate((own_ref, beside_ref)):
        at = slice(g * half, g * half + half)
        for first in range(0, columns, 256):
            lanes = slice(first, first + 256)
            result = dot32(order, table_ref[:, lanes]).astype(jnp.bfloat16)
            even_ref[at, lanes] = result[:half]
            odd_ref[at, lanes] = result[half:]


def modes_body(sizes, degree_total, meta_ref, to_ref, from_ref, rate_ref, in_ref, out_ref, scale_ref):
    levels = to_ref.shape[0]
    wide = 2 * levels
    own = levels // 2
    lane, row = iota2((levels, wide), 1), iota2((levels, wide), 0)
    owner = lax.rem(meta_ref[2] + lane // levels, 2)
    spread = picks(row == owner * own + lane % own)
    plain = picks(row == lane % levels)
    old, new = iota2((wide, wide), 0), iota2((wide, wide), 1)

    def turned(first, matrix, last):
        half = lax.dot_general(first, matrix, (((0,), (1,)), ((), ())), preferred_element_type=jnp.float32)
        return dot32(half.astype(jnp.bfloat16), last)

    same = (old // own) % 2 == new // levels
    in_ref[...] = jnp.where(same, turned(spread, to_ref[...], plain), 0.0).astype(jnp.bfloat16)
    same = old // levels == (new // own) % 2
    out_ref[...] = jnp.where(same, turned(plain, from_ref[...], spread), 0.0).astype(jnp.bfloat16)
    wide, levs, flds = sizes
    rows = degree_total // (2 * levs * flds)
    for odd in range(2):
        for d in range(levs):
            for g in range(flds):
                block = lax.rem(meta_ref[2] + d, levs) * flds + lax.rem(meta_ref[3] + g, flds)
                degree = block * (2 * rows) + 2 * iota2((rows, 1), 0) + (meta_ref[0] + odd) % 2
                real = degree.astype(jnp.float32)
                factor = 1.0 + real * (real + 1.0) * rate_ref[...] / (degree_total * degree_total)
                at = ((d * 2 + odd) * flds + g) * rows
                scale_ref[at : at + rows, :] = jnp.where(degree >= meta_ref[0], 1.0 / factor, 0.0)


def transform(even_ref, odd_ref, data_ref, own_ref, other_ref):
    rows, lanes = even_ref.shape[0], own_ref.shape[1]
    for odd, table_ref in enumerate((even_ref, odd_ref)):
        at = slice(odd * rows, odd * rows + rows)
        raw = dot32(table_ref[...], data_ref[odd]).astype(jnp.bfloat16)
        own_ref[at, :] = raw[:, :lanes]
        other_ref[at, :] = raw[:, lanes:]


def near_body(meta_ref, *refs):
    parts, (even_ref, odd_ref, own_ref, other_ref, data_ref) = refs[:-5], refs[-5:]
    wide, latitudes = len(parts), parts[0].shape[1]
    for shift in range(wide):
        owner = lax.rem(meta_ref[1] - shift + wide, wide)
        data_ref[:, pl.ds(pl.multiple_of(owner * latitudes, latitudes), latitudes), :] = parts[shift][...]
    transform(even_ref, odd_ref, data_ref, own_ref, other_ref)


def far_body(data_ref, even_ref, odd_ref, own_ref, other_ref):
    transform(even_ref, odd_ref, data_ref, own_ref, other_ref)


def solve_body(far, in_ref, out_ref, scale_ref, mine_ref, theirs_ref, own_ref, other_ref):
    rows, lanes = mine_ref.shape
    raw = jnp.concatenate((mine_ref[...], theirs_ref[...]), axis=1)
    scale = jnp.concatenate([scale_ref[far * rows : far * rows + rows, :]] * 2, axis=1)
    modes = (dot32(raw, in_ref[...]) * scale).astype(jnp.bfloat16)
    spectral = dot32(modes, out_ref[...]).astype(jnp.bfloat16)
    own_ref[...] = spectral[:, :lanes]
    other_ref[...] = spectral[:, lanes:]


def hemispheres(own_ref, other_ref, even_ref, odd_ref, chunk):
    rows = even_ref.shape[0]
    even, odd = (
        lax.dot_general(
            table_ref[:, chunk],
            jnp.concatenate((own_ref[at : at + rows, :], other_ref[at : at + rows, :]), axis=1),
            (((0,), (0,)), ((), ())),
            preferred_element_type=jnp.float32,
        )
        for table_ref, at in ((even_ref, 0), (odd_ref, rows))
    )
    return even + odd, even - odd


def inverse_far_body(own_ref, other_ref, even_ref, odd_ref, out_ref):
    for first in range(0, out_ref.shape[1], 256):
        chunk = slice(first, first + 256)
        out_ref[0, chunk, :], out_ref[1, chunk, :] = hemispheres(own_ref, other_ref, even_ref, odd_ref, chunk)


def inverse_near_body(wide, meta_ref, sum_ref, own_ref, other_ref, even_ref, odd_ref, *refs):
    outs, total = refs[:-1], refs[-1]
    latitudes, lanes = outs[0].shape[1:]
    for first in range(0, total.shape[1], 256):
        chunk = slice(first, first + 256)
        for half, more in enumerate(hemispheres(own_ref, other_ref, even_ref, odd_ref, chunk)):
            total[half, chunk, :] = (sum_ref[half, chunk, :] + more).astype(jnp.bfloat16)
    for shift in range(wide):
        owner = lax.rem(meta_ref[1] + shift, wide)
        at = pl.ds(pl.multiple_of(owner * latitudes, latitudes), latitudes)
        for d in range(2):
            outs[shift * 2 + d][...] = total[:, at, d * lanes : d * lanes + lanes]


def join_body(slots, block, meta_ref, *refs):
    parts, out_ref = refs[:-1], refs[-1]
    latitudes, lanes = parts[0].shape[1:]
    fields = 2
    group = slots * fields
    size = block * group
    out_row, in_row = iota2((size, size), 0), iota2((size, size), 1)
    place = out_row % group
    shift = lax.rem(meta_ref[1] - place // fields + slots, slots)
    order = picks(in_row == (shift * fields + place % fields) * block + out_row // group)
    both = 2 * lanes
    turn = picks(lane_order(both, meta_ref[2], iota2((both, both), 1), iota2((both, both), 0)))
    for first in range(0, latitudes, block):
        at = slice(first, first + block)
        stacked = jnp.concatenate(
            [
                jnp.concatenate([parts[shift * 2 + d][half, at, :] for d in range(2)], axis=1)
                for half in range(2)
                for shift in range(slots)
            ],
            axis=0,
        )
        turned = dot32(stacked, turn).astype(jnp.bfloat16)
        halves = [
            jnp.concatenate(
                [
                    turned[
                        (half * slots + shift) * block : (half * slots + shift + 1) * block,
                        field * lanes : field * lanes + lanes,
                    ]
                    for shift in range(slots)
                    for field in range(fields)
                ],
                axis=0,
            )
            for half in range(2)
        ]
        result = dot32(order, jnp.concatenate(halves, axis=1)).astype(jnp.bfloat16)
        for half in range(2):
            out_ref[half, first * group : first * group + size, :] = result[:, half * lanes : half * lanes + lanes]


def rows_body(sizes, block, meta_ref, *refs):
    wide, levs, flds = sizes
    own_refs, other_refs, out_ref = refs[:2], refs[2:4], refs[4]
    total_rows, lanes = own_refs[0].shape
    rows = total_rows // (2 * flds)
    fields = 2
    group = 2 * fields
    size = block * group
    out_row, in_row = iota2((size, size), 0), iota2((size, size), 1)
    place = out_row % group
    odd = (place // fields + meta_ref[0] % 2) % 2
    order = picks(in_row == (odd * fields + place % fields) * block + out_row // group)
    both = 2 * lanes
    turn = picks(lane_order(both, meta_ref[2], iota2((both, both), 1), iota2((both, both), 0)))
    for d in range(levs):
        for g in range(flds):
            index = lax.rem(meta_ref[2] + d, levs) * flds + lax.rem(meta_ref[3] + g, flds)
            halves = []
            for odd in range(2):
                at = slice((odd * flds + g) * rows, (odd * flds + g + 1) * rows)
                halves.append(jnp.concatenate((own_refs[d][at, :], other_refs[1 - d][at, :]), axis=1))
            turned = dot32(jnp.concatenate(halves, axis=0), turn).astype(jnp.bfloat16)
            for first in range(0, rows, block):
                stacked = jnp.concatenate(
                    [
                        turned[
                            odd * rows + first : odd * rows + first + block, field * lanes : field * lanes + lanes
                        ]
                        for odd in range(2)
                        for field in range(fields)
                    ],
                    axis=0,
                )
                start = pl.multiple_of(index * (rows * group), rows * group) + first * group
                out_ref[pl.ds(start, size), :] = dot32(order, stacked).astype(jnp.bfloat16)


def shards(fourier_input_rows, legendre, slot_wave, to_modes, from_modes, mode_rate):
    wide, levs, flds = (lax.axis_size(axis) for axis in ("wide", "lev", "fld"))
    sizes = (wide, levs, flds)
    _, latitudes, slots, fields, lanes = fourier_input_rows.shape
    _, shard_rows, half_count = legendre.shape
    degree_count = shard_rows * levs * flds
    group = slots * fields
    columns = fields * lanes
    block = 256 // group
    levels = to_modes.shape[0]
    bf16 = jnp.bfloat16

    def shape(*dims):
        return jax.ShapeDtypeStruct(dims, bf16)

    def shifted(value, axis, count, step):
        return lax.ppermute(value, axis, [(i, (i + step) % count) for i in range(count)])

    def moved(value, k, d):
        pairs = [(w * levs + l, (w + k) % wide * levs + (l + d) % levs) for w in range(wide) for l in range(levs)]
        return lax.ppermute(value, ("wide", "lev"), pairs)

    def over_lev(value):
        return shifted(value, "lev", levs, 1)

    def beside(value):
        return shifted(value, "fld", flds, 1)

    def behind(value, *others):
        return lax.optimization_barrier((value, *others))

    wide_at, lev_at, fld_at = (lax.axis_index(axis) for axis in ("wide", "lev", "fld"))
    meta = jnp.stack((slot_wave[0], wide_at, lev_at, fld_at)).astype(jnp.int32)
    position = (wide_at * latitudes + jnp.arange(latitudes, dtype=jnp.int32)).astype(jnp.float32)
    weights = jnp.sin(math.pi * (position + 0.5) / (2 * half_count))
    weights = jnp.broadcast_to(weights[:, None], (latitudes, lanes))
    move_flops = 8 * group * latitudes * 128 * 256
    transform_flops = 2 * degree_count * half_count * columns

    def split_table(first, second, after=()):
        return call(
            table_body, (shape(shard_rows, half_count),) * 2, "split_table",
            4 * shard_rows * shard_rows * half_count, after=after,
        )(meta, first, second)

    table_far, table_beside = over_lev(legendre[0]), beside(legendre[0])
    blocks = call(
        functools.partial(split_body, slots, fields, block), (shape(2, latitudes, columns),) * wide,
        "split_hemispheres", move_flops,
    )(meta, fourier_input_rows.reshape(2, latitudes * group, lanes), weights)
    table_beside, *blocks = behind(table_beside, *blocks)
    data = [blocks[0]] + [moved(blocks[k], k, 0) for k in range(1, wide)]
    *matrices, scale = call(
        functools.partial(modes_body, sizes, degree_count),
        (shape(2 * levels, 2 * levels),) * 2 + (jax.ShapeDtypeStruct((degree_count, levels), jnp.float32),),
        "spread_modes", 12 * levels * levels * levels, after=(blocks[0],),
    )(meta, to_modes, from_modes, mode_rate[None, :])
    near = split_table(legendre[0], table_beside, (scale,))
    table_far, scale, *near = behind(table_far, scale, *near)
    table_far, *arrived = behind(table_far, *data[1:])
    data[1:] = arrived
    far = split_table(table_far, beside(table_far))

    half_rows = degree_count // 2
    raw = (shape(half_rows, lanes),) * 2
    *near_raw, gathered = call(
        near_body, raw + (shape(2, half_count, columns),), "direct_legendre_near", transform_flops // 2
    )(meta, *data, *near)
    far_raw = call(far_body, raw, "direct_legendre_far", transform_flops // 2, scalars=0)(gathered, *far)
    spectral = [
        call(functools.partial(solve_body, i), raw, "vertical_solve", move_flops, scalars=0)(
            *matrices, scale, mine, over_lev(other)
        )
        for i, (mine, other) in enumerate(((near_raw[0], far_raw[1]), (far_raw[0], near_raw[1])))
    ]
    far_sum = call(
        inverse_far_body, jax.ShapeDtypeStruct((2, half_count, columns), jnp.float32), "inverse_legendre_far",
        transform_flops // 2, scalars=0,
    )(*spectral[1], *far)
    grid = call(
        functools.partial(inverse_near_body, wide), (shape(2, latitudes, lanes),) * (wide * levs),
        "inverse_legendre_near", transform_flops // 2, scratch=[pltpu.VMEM((2, half_count, columns), bf16)],
    )(meta, far_sum, *spectral[0], *near)

    arrived = {(k, 0): moved(grid[k * levs], k, 0) if k else grid[0] for k in range(wide)}
    arrived[0, 1] = moved(grid[1], 0, 1)
    for k in range(1, wide):
        value, arrived[k, 0] = behind(grid[k * levs + 1], arrived[k, 0])
        if k == 1:
            value, arrived[0, 1] = behind(value, arrived[0, 1])
        arrived[k, 1] = moved(value, k, 1)
    result = [arrived[k, d] for k in range(wide) for d in range(levs)]
    spectral_rows = call(
        functools.partial(rows_body, sizes, 32), shape(degree_count * fields, lanes), "order_spectral", move_flops,
    )(meta, *(own for own, _ in spectral), *(over_lev(other) for _, other in spectral))
    fourier_rows = call(
        functools.partial(join_body, slots, 256 // group), shape(2, latitudes * group, lanes),
        "join_hemispheres", move_flops,
    )(meta, *result)
    return (
        fourier_rows.reshape(2, latitudes, slots, fields, lanes),
        spectral_rows.reshape(1, degree_count, fields, lanes),
    )


def project(level_grid, degree_real, weight_rows, rate_rows, degree_total):
    projected = jnp.einsum(
        "kl,snflr->snfkr", weight_rows, level_grid, preferred_element_type=jnp.float32
    )
    factor = 1.0 + degree_real[:, None] * (degree_real[:, None] + 1.0) * rate_rows[None, :] / (
        degree_total * degree_total
    )
    return (projected / factor[None, :, None, :, None]).astype(jnp.bfloat16)


def plain_shards(fourier_input_rows, legendre, slot_wave, to_modes, from_modes, mode_rate):
    wave_rows = lax.all_to_all(fourier_input_rows, "wide", split_axis=2, concat_axis=1, tiled=True)
    half_count = wave_rows.shape[1]
    slot_count = wave_rows.shape[2]
    field_count = wave_rows.shape[3]
    column_count = wave_rows.shape[4]
    degree_count = legendre.shape[1] * lax.axis_size(("lev", "fld"))
    weights = latitude_weights(half_count)[:, None, None, None]
    north_half = wave_rows[0].astype(jnp.float32)
    south_half = wave_rows[1].astype(jnp.float32)
    symmetric = (weights * (north_half + south_half)).astype(jnp.bfloat16)
    antisym = (weights * (north_half - south_half)).astype(jnp.bfloat16)
    paired = jnp.concatenate((symmetric, antisym), axis=3)

    def direct_rows(section, first_row):
        row_count = section.shape[1]
        degree = first_row + jnp.arange(row_count, dtype=jnp.int32)
        relative = degree[None, :] - slot_wave[:, None]
        product = jnp.einsum("snj,jsfc->snfc", section, paired, preferred_element_type=jnp.float32)
        is_even = (relative % 2 == 0)[:, :, None, None]
        is_live = (relative >= 0)[:, :, None, None]
        picked = jnp.where(is_even, product[..., :column_count], product[..., column_count:])
        return jnp.where(is_live, picked, jnp.zeros_like(picked))

    full_table = lax.all_gather(legendre, ("lev", "fld"), axis=1, tiled=True)
    block_rows = 128
    block_count = degree_count // block_rows

    def direct_step(block_index, buffer):
        first_row = block_index * block_rows
        section = lax.dynamic_slice_in_dim(full_table, first_row, block_rows, 1)
        result = direct_rows(section, first_row).astype(jnp.bfloat16)
        return lax.dynamic_update_slice_in_dim(buffer, result, first_row, 1)

    initial_raw = jnp.zeros((slot_count, degree_count, field_count, column_count), jnp.bfloat16)
    raw_spectral = lax.fori_loop(0, block_count, direct_step, initial_raw)
    own_levels = column_count // 2
    first_level = lax.axis_index("lev") * own_levels
    degree_real = jnp.arange(degree_count, dtype=jnp.float32)
    all_levels = lax.all_gather(raw_spectral, "lev", axis=3, tiled=True)
    level_count = all_levels.shape[3] // 2
    level_grid = all_levels.reshape(slot_count, degree_count, field_count, level_count, 2)
    weight_rows = lax.dynamic_slice_in_dim(to_modes, first_level, own_levels, 0)
    rate_rows = lax.dynamic_slice_in_dim(mode_rate, first_level, own_levels, 0)
    own_modes = project(level_grid, degree_real, weight_rows, rate_rows, degree_count).reshape(
        slot_count, degree_count, field_count, column_count
    )
    mode_values = lax.all_gather(own_modes, "lev", axis=3, tiled=True).reshape(
        slot_count, degree_count, field_count, level_count, 2
    )
    back_rows = lax.dynamic_slice_in_dim(from_modes, first_level, own_levels, 0)
    spectral = jnp.einsum(
        "lk,snfkr->snflr", back_rows, mode_values, preferred_element_type=jnp.float32
    )
    spectral = spectral.astype(jnp.bfloat16).reshape(
        slot_count, degree_count, field_count, column_count
    )

    def inverse_rows(running, section, first_row):
        row_count = section.shape[1]
        degree = first_row + jnp.arange(row_count, dtype=jnp.int32)
        relative = degree[None, :] - slot_wave[:, None]
        spec_rows = lax.dynamic_slice_in_dim(spectral, first_row, row_count, 1)
        even_mask = ((relative >= 0) & (relative % 2 == 0))[:, :, None, None]
        odd_mask = ((relative >= 0) & (relative % 2 == 1))[:, :, None, None]
        empty_rows = jnp.zeros_like(spec_rows)
        parity_split = jnp.concatenate(
            (
                jnp.where(even_mask, spec_rows, empty_rows),
                jnp.where(odd_mask, spec_rows, empty_rows),
            ),
            axis=3,
        )
        return running + jnp.einsum(
            "snj,snfc->jsfc", section, parity_split, preferred_element_type=jnp.float32
        )

    initial_sum = jnp.zeros((half_count, slot_count, field_count, 2 * column_count), jnp.float32)

    def inverse_step(block_index, running):
        first_row = block_index * block_rows
        section = lax.dynamic_slice_in_dim(full_table, first_row, block_rows, 1)
        return inverse_rows(running, section, first_row)

    running = lax.fori_loop(0, block_count, inverse_step, initial_sum)
    even_sum = running[..., :column_count]
    odd_sum = running[..., column_count:]
    fourier_wave = jnp.stack((even_sum + odd_sum, even_sum - odd_sum), axis=0).astype(jnp.bfloat16)
    fourier_out = lax.all_to_all(fourier_wave, "wide", split_axis=1, concat_axis=2, tiled=True)
    return (fourier_out, spectral)


def solution(mesh):
    in_specs = (
        P("ens", "wide", None, "fld", "lev"),
        P("wide", ("lev", "fld"), None),
        P("wide"),
        P(),
        P(),
        P(),
    )
    out_specs = (P("ens", "wide", None, "fld", "lev"), P(("ens", "wide"), None, "fld", "lev"))

    def body(fourier_input_rows, legendre, *rest):
        _, latitudes, slots, fields, lanes = fourier_input_rows.shape
        whole_tiles = (
            latitudes % 32 == 0
            and fields == 2
            and slots == mesh.shape["wide"] == 4
            and mesh.shape["lev"] == mesh.shape["fld"] == 2
            and lanes == 128
            and legendre.shape[1] % 64 == 0
            and legendre.shape[2] % 256 == 0
        )
        form = shards if whole_tiles else plain_shards
        return form(fourier_input_rows, legendre, *rest)

    return jax.shard_map(body, mesh=mesh, in_specs=in_specs, out_specs=out_specs, check_vma=False)
```

```python
import functools
import math

import jax
import jax.numpy as jnp
from jax import lax
from jax.experimental import pallas as pl
from jax.experimental.pallas import tpu as pltpu
from jax.sharding import PartitionSpec as P

VMEM_BYTES = 8 * 1024 * 1024


def latitude_weights(count):
    position = jnp.arange(count, dtype=jnp.float32)
    return jnp.sin(math.pi * (position + 0.5) / (2 * count))


def iota2(shape, dim):
    return lax.broadcasted_iota(jnp.int32, shape, dim)


def picks(condition):
    return jnp.where(condition, 1.0, 0.0).astype(jnp.bfloat16)


def dot32(a, b):
    return jnp.dot(a, b, preferred_element_type=jnp.float32)


def call(body, out_shape, name, flops, scratch=(), scalars=1, after=()):
    smem = pl.BlockSpec(memory_space=pltpu.SMEM)
    vmem = pl.BlockSpec(memory_space=pltpu.VMEM)

    def run(*operands):
        used = len(operands)

        def kernel(*refs):
            body(*refs[:used], *refs[used + len(after) :])

        return pl.pallas_call(
            kernel,
            out_shape=out_shape,
            in_specs=[smem] * scalars
            + [vmem] * (used - scalars)
            + [pl.BlockSpec(memory_space=pl.ANY)] * len(after),
            out_specs=jax.tree.map(lambda _: vmem, out_shape),
            scratch_shapes=list(scratch),
            compiler_params=pltpu.CompilerParams(vmem_limit_bytes=VMEM_BYTES),
            cost_estimate=pl.CostEstimate(flops=flops, bytes_accessed=0, transcendentals=0),
            name=name,
        )(*operands, *after)

    return run


def lane_order(lanes, lev, old, new):
    levels = lanes // 4
    part = lax.rem(new // (lanes // 2) + lev, 2)
    field = (new // levels) % 2
    return old == field * (lanes // 2) + 2 * (new % levels) + part


HALFWAY = 2


def entry(refs, k, half):
    if k == HALFWAY:
        return refs[half - 2], ()
    return refs[k - (k > HALFWAY)], (half,)


def split_body(slots, fields, block, meta_ref, rows_ref, weight_ref, *outs):
    latitudes = weight_ref.shape[0]
    group = slots * fields
    size = block * group
    out_row, in_row = iota2((size, size), 0), iota2((size, size), 1)
    pair = out_row // block
    slot = lax.rem(meta_ref[1] + pair // fields, slots)
    order = picks(in_row == (out_row % block) * group + slot * fields + pair % fields)
    lanes = fields * 128
    parts = picks(lane_order(lanes, meta_ref[2], iota2((lanes, lanes), 0), iota2((lanes, lanes), 1)))
    for first in range(0, latitudes, block):
        north = rows_ref[0, first * group : first * group + size, :]
        south = rows_ref[1, first * group : first * group + size, :]
        sorted_rows = dot32(order, jnp.concatenate((north, south), axis=1))
        up, down = sorted_rows[:, :128], sorted_rows[:, 128:]
        weight = weight_ref[first : first + block, :]
        halves = []
        for mixed in (up + down, up - down):
            for shift in range(slots):
                at = shift * fields * block
                halves.append(jnp.concatenate(
                    [
                        (weight * mixed[at + f * block : at + f * block + block]).astype(jnp.bfloat16)
                        for f in range(fields)
                    ],
                    axis=1,
                ))
        turned = dot32(jnp.concatenate(halves, axis=0), parts).astype(jnp.bfloat16)
        for odd in range(2):
            for shift in range(slots):
                at = (odd * slots + shift) * block
                out_ref, index = entry(outs, shift, odd)
                out_ref[(*index, slice(first, first + block))] = turned[at : at + block, :]


def by_parity(meta_ref, rows):
    half = rows // 2
    out_row, in_row = iota2((rows, rows), 0), iota2((rows, rows), 1)
    odd = jnp.where(out_row < half, 0, 1)
    return picks(in_row == 2 * (out_row - odd * half) + (meta_ref[0] + odd) % 2)


def table_body(meta_ref, own_ref, beside_ref, even_ref, odd_ref):
    rows, columns = own_ref.shape
    half = rows // 2
    order = by_parity(meta_ref, rows)
    for g, table_ref in enumerate((own_ref, beside_ref)):
        at = slice(g * half, g * half + half)
        for first in range(0, columns, 256):
            lanes = slice(first, first + 256)
            result = dot32(order, table_ref[:, lanes]).astype(jnp.bfloat16)
            even_ref[at, lanes] = result[:half]
            odd_ref[at, lanes] = result[half:]


def modes_body(sizes, degree_total, meta_ref, to_ref, from_ref, rate_ref, in_ref, out_ref, scale_ref):
    levels = to_ref.shape[0]
    wide = 2 * levels
    own = levels // 2
    lane, row = iota2((levels, wide), 1), iota2((levels, wide), 0)
    owner = lax.rem(meta_ref[2] + lane // levels, 2)
    spread = picks(row == owner * own + lane % own)
    plain = picks(row == lane % levels)
    old, new = iota2((wide, wide), 0), iota2((wide, wide), 1)

    def turned(first, matrix, last):
        half = lax.dot_general(first, matrix, (((0,), (1,)), ((), ())), preferred_element_type=jnp.float32)
        return dot32(half.astype(jnp.bfloat16), last)

    same = (old // own) % 2 == new // levels
    in_ref[...] = jnp.where(same, turned(spread, to_ref[...], plain), 0.0).astype(jnp.bfloat16)
    same = old // levels == (new // own) % 2
    out_ref[...] = jnp.where(same, turned(plain, from_ref[...], spread), 0.0).astype(jnp.bfloat16)
    wide, levs, flds = sizes
    rows = degree_total // (2 * levs * flds)
    for odd in range(2):
        for d in range(levs):
            for g in range(flds):
                block = lax.rem(meta_ref[2] + d, levs) * flds + lax.rem(meta_ref[3] + g, flds)
                degree = block * (2 * rows) + 2 * iota2((rows, 1), 0) + (meta_ref[0] + odd) % 2
                real = degree.astype(jnp.float32)
                factor = 1.0 + real * (real + 1.0) * rate_ref[...] / (degree_total * degree_total)
                at = ((d * 2 + odd) * flds + g) * rows
                scale_ref[at : at + rows, :] = jnp.where(degree >= meta_ref[0], 1.0 / factor, 0.0)


def transform(even_ref, odd_ref, data_ref, own_ref, other_ref):
    rows, lanes = even_ref.shape[0], own_ref.shape[1]
    for odd, table_ref in enumerate((even_ref, odd_ref)):
        at = slice(odd * rows, odd * rows + rows)
        raw = dot32(table_ref[...], data_ref[odd]).astype(jnp.bfloat16)
        own_ref[at, :] = raw[:, :lanes]
        other_ref[at, :] = raw[:, lanes:]


def near_body(meta_ref, *refs):
    parts, (even_ref, odd_ref, own_ref, other_ref, data_ref) = refs[:-5], refs[-5:]
    wide, latitudes = len(parts) - 1, parts[0].shape[1]
    for shift in range(wide):
        owner = lax.rem(meta_ref[1] - shift + wide, wide)
        at = pl.ds(pl.multiple_of(owner * latitudes, latitudes), latitudes)
        for odd in range(2):
            part, index = entry(parts, shift, odd)
            data_ref[odd, at, :] = part[(*index, Ellipsis)]
    transform(even_ref, odd_ref, data_ref, own_ref, other_ref)


def far_body(data_ref, even_ref, odd_ref, own_ref, other_ref):
    transform(even_ref, odd_ref, data_ref, own_ref, other_ref)


def solve_body(far, in_ref, out_ref, scale_ref, mine_ref, theirs_ref, own_ref, other_ref):
    rows, lanes = mine_ref.shape
    raw = jnp.concatenate((mine_ref[...], theirs_ref[...]), axis=1)
    scale = jnp.concatenate([scale_ref[far * rows : far * rows + rows, :]] * 2, axis=1)
    modes = (dot32(raw, in_ref[...]) * scale).astype(jnp.bfloat16)
    spectral = dot32(modes, out_ref[...]).astype(jnp.bfloat16)
    own_ref[...] = spectral[:, :lanes]
    other_ref[...] = spectral[:, lanes:]


def hemispheres(own_ref, other_ref, even_ref, odd_ref, chunk):
    rows = even_ref.shape[0]
    even, odd = (
        lax.dot_general(
            table_ref[:, chunk],
            jnp.concatenate((own_ref[at : at + rows, :], other_ref[at : at + rows, :]), axis=1),
            (((0,), (0,)), ((), ())),
            preferred_element_type=jnp.float32,
        )
        for table_ref, at in ((even_ref, 0), (odd_ref, rows))
    )
    return even + odd, even - odd


def inverse_far_body(own_ref, other_ref, even_ref, odd_ref, out_ref):
    for first in range(0, out_ref.shape[1], 256):
        chunk = slice(first, first + 256)
        out_ref[0, chunk, :], out_ref[1, chunk, :] = hemispheres(own_ref, other_ref, even_ref, odd_ref, chunk)


def inverse_near_body(wide, meta_ref, sum_ref, own_ref, other_ref, even_ref, odd_ref, *refs):
    outs, total = refs[:-1], refs[-1]
    latitudes, lanes = outs[0].shape[1:]
    for first in range(0, total.shape[1], 256):
        chunk = slice(first, first + 256)
        for half, more in enumerate(hemispheres(own_ref, other_ref, even_ref, odd_ref, chunk)):
            total[half, chunk, :] = (sum_ref[half, chunk, :] + more).astype(jnp.bfloat16)
    for shift in range(wide):
        owner = lax.rem(meta_ref[1] + shift, wide)
        at = pl.ds(pl.multiple_of(owner * latitudes, latitudes), latitudes)
        for d in range(2):
            for half in range(2):
                out_ref, index = entry(outs[d * (wide + 1) : (d + 1) * (wide + 1)], shift, half)
                out_ref[(*index, Ellipsis)] = total[half, at, d * lanes : d * lanes + lanes]


def join_body(slots, block, meta_ref, *refs):
    parts, out_ref = refs[:-1], refs[-1]
    latitudes, lanes = parts[0].shape[1:]
    fields = 2

    def rows_of(d, k, half, at):
        part, index = entry(parts[d * (slots + 1) : (d + 1) * (slots + 1)], k, half)
        return part[(*index, at)]

    group = slots * fields
    size = block * group
    out_row, in_row = iota2((size, size), 0), iota2((size, size), 1)
    place = out_row % group
    shift = lax.rem(meta_ref[1] - place // fields + slots, slots)
    order = picks(in_row == (shift * fields + place % fields) * block + out_row // group)
    both = 2 * lanes
    turn = picks(lane_order(both, meta_ref[2], iota2((both, both), 1), iota2((both, both), 0)))
    for first in range(0, latitudes, block):
        at = slice(first, first + block)
        stacked = jnp.concatenate(
            [
                jnp.concatenate([rows_of(d, shift, half, at) for d in range(2)], axis=1)
                for half in range(2)
                for shift in range(slots)
            ],
            axis=0,
        )
        turned = dot32(stacked, turn).astype(jnp.bfloat16)
        halves = [
            jnp.concatenate(
                [
                    turned[
                        (half * slots + shift) * block : (half * slots + shift + 1) * block,
                        field * lanes : field * lanes + lanes,
                    ]
                    for shift in range(slots)
                    for field in range(fields)
                ],
                axis=0,
            )
            for half in range(2)
        ]
        result = dot32(order, jnp.concatenate(halves, axis=1)).astype(jnp.bfloat16)
        for half in range(2):
            out_ref[half, first * group : first * group + size, :] = result[:, half * lanes : half * lanes + lanes]


def rows_body(sizes, block, meta_ref, *refs):
    wide, levs, flds = sizes
    own_refs, other_refs, out_ref = refs[:2], refs[2:4], refs[4]
    total_rows, lanes = own_refs[0].shape
    rows = total_rows // (2 * flds)
    fields = 2
    group = 2 * fields
    size = block * group
    out_row, in_row = iota2((size, size), 0), iota2((size, size), 1)
    place = out_row % group
    odd = (place // fields + meta_ref[0] % 2) % 2
    order = picks(in_row == (odd * fields + place % fields) * block + out_row // group)
    both = 2 * lanes
    turn = picks(lane_order(both, meta_ref[2], iota2((both, both), 1), iota2((both, both), 0)))
    for d in range(levs):
        for g in range(flds):
            index = lax.rem(meta_ref[2] + d, levs) * flds + lax.rem(meta_ref[3] + g, flds)
            halves = []
            for odd in range(2):
                at = slice((odd * flds + g) * rows, (odd * flds + g + 1) * rows)
                halves.append(jnp.concatenate((own_refs[d][at, :], other_refs[1 - d][at, :]), axis=1))
            turned = dot32(jnp.concatenate(halves, axis=0), turn).astype(jnp.bfloat16)
            for first in range(0, rows, block):
                stacked = jnp.concatenate(
                    [
                        turned[
                            odd * rows + first : odd * rows + first + block, field * lanes : field * lanes + lanes
                        ]
                        for odd in range(2)
                        for field in range(fields)
                    ],
                    axis=0,
                )
                start = pl.multiple_of(index * (rows * group), rows * group) + first * group
                out_ref[pl.ds(start, size), :] = dot32(order, stacked).astype(jnp.bfloat16)


def shards(fourier_input_rows, legendre, slot_wave, to_modes, from_modes, mode_rate):
    wide, levs, flds = (lax.axis_size(axis) for axis in ("wide", "lev", "fld"))
    sizes = (wide, levs, flds)
    _, latitudes, slots, fields, lanes = fourier_input_rows.shape
    _, shard_rows, half_count = legendre.shape
    degree_count = shard_rows * levs * flds
    group = slots * fields
    columns = fields * lanes
    block = 256 // group
    levels = to_modes.shape[0]
    bf16 = jnp.bfloat16

    def shape(*dims):
        return jax.ShapeDtypeStruct(dims, bf16)

    def shifted(value, axis, count, step):
        return lax.ppermute(value, axis, [(i, (i + step) % count) for i in range(count)])

    def moved(value, k, d):
        pairs = [(w * levs + l, (w + k) % wide * levs + (l + d) % levs) for w in range(wide) for l in range(levs)]
        return lax.ppermute(value, ("wide", "lev"), pairs)

    def over_lev(value):
        return shifted(value, "lev", levs, 1)

    def beside(value):
        return shifted(value, "fld", flds, 1)

    def behind(value, *others):
        return lax.optimization_barrier((value, *others))

    wide_at, lev_at, fld_at = (lax.axis_index(axis) for axis in ("wide", "lev", "fld"))
    meta = jnp.stack((slot_wave[0], wide_at, lev_at, fld_at)).astype(jnp.int32)
    position = (wide_at * latitudes + jnp.arange(latitudes, dtype=jnp.int32)).astype(jnp.float32)
    weights = jnp.sin(math.pi * (position + 0.5) / (2 * half_count))
    weights = jnp.broadcast_to(weights[:, None], (latitudes, lanes))
    move_flops = 8 * group * latitudes * 128 * 256
    transform_flops = 2 * degree_count * half_count * columns

    def split_table(first, second, after=()):
        return call(
            table_body, (shape(shard_rows, half_count),) * 2, "split_table",
            4 * shard_rows * shard_rows * half_count, after=after,
        )(meta, first, second)

    steps = [k for k in range(wide) if k != HALFWAY] + [HALFWAY] * 2

    def in_halves(count):
        return tuple(shape(*(() if k == HALFWAY else (2,)), latitudes, count) for k in steps)

    table_far, table_beside = over_lev(legendre[0]), beside(legendre[0])
    blocks = call(
        functools.partial(split_body, slots, fields, block), in_halves(columns),
        "split_hemispheres", move_flops,
    )(meta, fourier_input_rows.reshape(2, latitudes * group, lanes), weights)
    table_beside, *blocks = behind(table_beside, *blocks)
    data = [moved(one, k, 0) if k else one for k, one in zip(steps, blocks)]
    *matrices, scale = call(
        functools.partial(modes_body, sizes, degree_count),
        (shape(2 * levels, 2 * levels),) * 2 + (jax.ShapeDtypeStruct((degree_count, levels), jnp.float32),),
        "spread_modes", 12 * levels * levels * levels, after=(blocks[0],),
    )(meta, to_modes, from_modes, mode_rate[None, :])
    near = split_table(legendre[0], table_beside, (scale,))
    table_far, scale, *near = behind(table_far, scale, *near)
    table_far, *arrived = behind(table_far, *data[1:])
    data[1:] = arrived
    far = split_table(table_far, beside(table_far))

    half_rows = degree_count // 2
    raw = (shape(half_rows, lanes),) * 2
    *near_raw, gathered = call(
        near_body, raw + (shape(2, half_count, columns),), "direct_legendre_near", transform_flops // 2
    )(meta, *data, *near)
    far_raw = call(far_body, raw, "direct_legendre_far", transform_flops // 2, scalars=0)(gathered, *far)
    spectral = [
        call(functools.partial(solve_body, i), raw, "vertical_solve", move_flops, scalars=0)(
            *matrices, scale, mine, over_lev(other)
        )
        for i, (mine, other) in enumerate(((near_raw[0], far_raw[1]), (far_raw[0], near_raw[1])))
    ]
    far_sum = call(
        inverse_far_body, jax.ShapeDtypeStruct((2, half_count, columns), jnp.float32), "inverse_legendre_far",
        transform_flops // 2, scalars=0,
    )(*spectral[1], *far)
    grid = call(
        functools.partial(inverse_near_body, wide), in_halves(lanes) * levs,
        "inverse_legendre_near", transform_flops // 2, scratch=[pltpu.VMEM((2, half_count, columns), bf16)],
    )(meta, far_sum, *spectral[0], *near)

    straight, turning = grid[: len(steps)], grid[len(steps) :]
    straight = [moved(one, k, 0) if k else one for k, one in zip(steps, straight)]
    across_lev = moved(turning[0], 0, 1)
    diagonal = []
    for i, (k, one) in enumerate(zip(steps[1:], turning[1:]), 1):
        one, straight[i] = behind(one, straight[i])
        if i == 1:
            one, across_lev = behind(one, across_lev)
        diagonal.append(moved(one, k, 1))
    result = [*straight, across_lev, *diagonal]
    spectral_rows = call(
        functools.partial(rows_body, sizes, 32), shape(degree_count * fields, lanes), "order_spectral", move_flops,
    )(meta, *(own for own, _ in spectral), *(over_lev(other) for _, other in spectral))
    fourier_rows = call(
        functools.partial(join_body, slots, 256 // group), shape(2, latitudes * group, lanes),
        "join_hemispheres", move_flops,
    )(meta, *result)
    return (
        fourier_rows.reshape(2, latitudes, slots, fields, lanes),
        spectral_rows.reshape(1, degree_count, fields, lanes),
    )


def project(level_grid, degree_real, weight_rows, rate_rows, degree_total):
    projected = jnp.einsum(
        "kl,snflr->snfkr", weight_rows, level_grid, preferred_element_type=jnp.float32
    )
    factor = 1.0 + degree_real[:, None] * (degree_real[:, None] + 1.0) * rate_rows[None, :] / (
        degree_total * degree_total
    )
    return (projected / factor[None, :, None, :, None]).astype(jnp.bfloat16)


def plain_shards(fourier_input_rows, legendre, slot_wave, to_modes, from_modes, mode_rate):
    wave_rows = lax.all_to_all(fourier_input_rows, "wide", split_axis=2, concat_axis=1, tiled=True)
    half_count = wave_rows.shape[1]
    slot_count = wave_rows.shape[2]
    field_count = wave_rows.shape[3]
    column_count = wave_rows.shape[4]
    degree_count = legendre.shape[1] * lax.axis_size(("lev", "fld"))
    weights = latitude_weights(half_count)[:, None, None, None]
    north_half = wave_rows[0].astype(jnp.float32)
    south_half = wave_rows[1].astype(jnp.float32)
    symmetric = (weights * (north_half + south_half)).astype(jnp.bfloat16)
    antisym = (weights * (north_half - south_half)).astype(jnp.bfloat16)
    paired = jnp.concatenate((symmetric, antisym), axis=3)

    def direct_rows(section, first_row):
        row_count = section.shape[1]
        degree = first_row + jnp.arange(row_count, dtype=jnp.int32)
        relative = degree[None, :] - slot_wave[:, None]
        product = jnp.einsum("snj,jsfc->snfc", section, paired, preferred_element_type=jnp.float32)
        is_even = (relative % 2 == 0)[:, :, None, None]
        is_live = (relative >= 0)[:, :, None, None]
        picked = jnp.where(is_even, product[..., :column_count], product[..., column_count:])
        return jnp.where(is_live, picked, jnp.zeros_like(picked))

    full_table = lax.all_gather(legendre, ("lev", "fld"), axis=1, tiled=True)
    block_rows = 128
    block_count = degree_count // block_rows

    def direct_step(block_index, buffer):
        first_row = block_index * block_rows
        section = lax.dynamic_slice_in_dim(full_table, first_row, block_rows, 1)
        result = direct_rows(section, first_row).astype(jnp.bfloat16)
        return lax.dynamic_update_slice_in_dim(buffer, result, first_row, 1)

    initial_raw = jnp.zeros((slot_count, degree_count, field_count, column_count), jnp.bfloat16)
    raw_spectral = lax.fori_loop(0, block_count, direct_step, initial_raw)
    own_levels = column_count // 2
    first_level = lax.axis_index("lev") * own_levels
    degree_real = jnp.arange(degree_count, dtype=jnp.float32)
    all_levels = lax.all_gather(raw_spectral, "lev", axis=3, tiled=True)
    level_count = all_levels.shape[3] // 2
    level_grid = all_levels.reshape(slot_count, degree_count, field_count, level_count, 2)
    weight_rows = lax.dynamic_slice_in_dim(to_modes, first_level, own_levels, 0)
    rate_rows = lax.dynamic_slice_in_dim(mode_rate, first_level, own_levels, 0)
    own_modes = project(level_grid, degree_real, weight_rows, rate_rows, degree_count).reshape(
        slot_count, degree_count, field_count, column_count
    )
    mode_values = lax.all_gather(own_modes, "lev", axis=3, tiled=True).reshape(
        slot_count, degree_count, field_count, level_count, 2
    )
    back_rows = lax.dynamic_slice_in_dim(from_modes, first_level, own_levels, 0)
    spectral = jnp.einsum(
        "lk,snfkr->snflr", back_rows, mode_values, preferred_element_type=jnp.float32
    )
    spectral = spectral.astype(jnp.bfloat16).reshape(
        slot_count, degree_count, field_count, column_count
    )

    def inverse_rows(running, section, first_row):
        row_count = section.shape[1]
        degree = first_row + jnp.arange(row_count, dtype=jnp.int32)
        relative = degree[None, :] - slot_wave[:, None]
        spec_rows = lax.dynamic_slice_in_dim(spectral, first_row, row_count, 1)
        even_mask = ((relative >= 0) & (relative % 2 == 0))[:, :, None, None]
        odd_mask = ((relative >= 0) & (relative % 2 == 1))[:, :, None, None]
        empty_rows = jnp.zeros_like(spec_rows)
        parity_split = jnp.concatenate(
            (
                jnp.where(even_mask, spec_rows, empty_rows),
                jnp.where(odd_mask, spec_rows, empty_rows),
            ),
            axis=3,
        )
        return running + jnp.einsum(
            "snj,snfc->jsfc", section, parity_split, preferred_element_type=jnp.float32
        )

    initial_sum = jnp.zeros((half_count, slot_count, field_count, 2 * column_count), jnp.float32)

    def inverse_step(block_index, running):
        first_row = block_index * block_rows
        section = lax.dynamic_slice_in_dim(full_table, first_row, block_rows, 1)
        return inverse_rows(running, section, first_row)

    running = lax.fori_loop(0, block_count, inverse_step, initial_sum)
    even_sum = running[..., :column_count]
    odd_sum = running[..., column_count:]
    fourier_wave = jnp.stack((even_sum + odd_sum, even_sum - odd_sum), axis=0).astype(jnp.bfloat16)
    fourier_out = lax.all_to_all(fourier_wave, "wide", split_axis=1, concat_axis=2, tiled=True)
    return (fourier_out, spectral)


def solution(mesh):
    in_specs = (
        P("ens", "wide", None, "fld", "lev"),
        P("wide", ("lev", "fld"), None),
        P("wide"),
        P(),
        P(),
        P(),
    )
    out_specs = (P("ens", "wide", None, "fld", "lev"), P(("ens", "wide"), None, "fld", "lev"))

    def body(fourier_input_rows, legendre, *rest):
        _, latitudes, slots, fields, lanes = fourier_input_rows.shape
        whole_tiles = (
            latitudes % 32 == 0
            and fields == 2
            and slots == mesh.shape["wide"] == 4
            and mesh.shape["lev"] == mesh.shape["fld"] == 2
            and lanes == 128
            and legendre.shape[1] % 64 == 0
            and legendre.shape[2] % 256 == 0
        )
        form = shards if whole_tiles else plain_shards
        return form(fourier_input_rows, legendre, *rest)

    return jax.shard_map(body, mesh=mesh, in_specs=in_specs, out_specs=out_specs, check_vma=False)
```

```python
import functools
import math

import jax
import jax.numpy as jnp
from jax import lax
from jax.experimental import pallas as pl
from jax.experimental.pallas import tpu as pltpu
from jax.sharding import PartitionSpec as P

VMEM_BYTES = 8 * 1024 * 1024


def latitude_weights(count):
    position = jnp.arange(count, dtype=jnp.float32)
    return jnp.sin(math.pi * (position + 0.5) / (2 * count))


def iota2(shape, dim):
    return lax.broadcasted_iota(jnp.int32, shape, dim)


def picks(condition):
    return jnp.where(condition, 1.0, 0.0).astype(jnp.bfloat16)


def dot32(a, b):
    return jnp.dot(a, b, preferred_element_type=jnp.float32)


PIECES = 5


def copy_pieces(source, target, semaphores):
    rows = target.shape[1] // PIECES
    return [
        pltpu.make_async_copy(
            source.at[:, pl.ds(i * rows, rows), :], target.at[:, pl.ds(i * rows, rows), :], semaphores.at[i]
        )
        for i in range(PIECES)
    ]


def call(body, out_shape, name, flops, scratch=(), scalars=1, after=(), out_hbm=False):
    smem = pl.BlockSpec(memory_space=pltpu.SMEM)
    vmem = pl.BlockSpec(memory_space=pltpu.VMEM)
    hbm = pl.BlockSpec(memory_space=pltpu.HBM)

    def run(*operands):
        used = len(operands)

        def kernel(*refs):
            body(*refs[:used], *refs[used + len(after) :])

        return pl.pallas_call(
            kernel,
            out_shape=out_shape,
            in_specs=[smem] * scalars
            + [vmem] * (used - scalars)
            + [pl.BlockSpec(memory_space=pl.ANY)] * len(after),
            out_specs=jax.tree.map(lambda _: hbm if out_hbm else vmem, out_shape),
            scratch_shapes=list(scratch),
            compiler_params=pltpu.CompilerParams(vmem_limit_bytes=VMEM_BYTES),
            cost_estimate=pl.CostEstimate(flops=flops, bytes_accessed=0, transcendentals=0),
            name=name,
        )(*operands, *after)

    return run


def lane_order(lanes, lev, old, new):
    levels = lanes // 4
    part = lax.rem(new // (lanes // 2) + lev, 2)
    field = (new // levels) % 2
    return old == field * (lanes // 2) + 2 * (new % levels) + part


def split_body(slots, fields, block, meta_ref, rows_ref, weight_ref, *outs):
    latitudes = weight_ref.shape[0]
    group = slots * fields
    size = block * group
    out_row, in_row = iota2((size, size), 0), iota2((size, size), 1)
    pair = out_row // block
    slot = lax.rem(meta_ref[1] + pair // fields, slots)
    order = picks(in_row == (out_row % block) * group + slot * fields + pair % fields)
    lanes = fields * 128
    parts = picks(lane_order(lanes, meta_ref[2], iota2((lanes, lanes), 0), iota2((lanes, lanes), 1)))
    for first in range(0, latitudes, block):
        north = rows_ref[0, first * group : first * group + size, :]
        south = rows_ref[1, first * group : first * group + size, :]
        sorted_rows = dot32(order, jnp.concatenate((north, south), axis=1))
        up, down = sorted_rows[:, :128], sorted_rows[:, 128:]
        weight = weight_ref[first : first + block, :]
        halves = []
        for mixed in (up + down, up - down):
            for shift in range(slots):
                at = shift * fields * block
                halves.append(jnp.concatenate(
                    [
                        (weight * mixed[at + f * block : at + f * block + block]).astype(jnp.bfloat16)
                        for f in range(fields)
                    ],
                    axis=1,
                ))
        turned = dot32(jnp.concatenate(halves, axis=0), parts).astype(jnp.bfloat16)
        for odd in range(2):
            for shift in range(slots):
                at = (odd * slots + shift) * block
                for d in range(2):
                    outs[shift * 2 + d][odd, first : first + block, :] = turned[
                        at : at + block, d * 128 : d * 128 + 128
                    ]


def by_parity(meta_ref, rows):
    half = rows // 2
    out_row, in_row = iota2((rows, rows), 0), iota2((rows, rows), 1)
    odd = jnp.where(out_row < half, 0, 1)
    return picks(in_row == 2 * (out_row - odd * half) + (meta_ref[0] + odd) % 2)


def near_table_body(meta_ref, own_ref, beside_ref, even_ref, odd_ref):
    rows, columns = own_ref.shape
    half = rows // 2
    order = by_parity(meta_ref, rows)
    for g, table_ref in enumerate((own_ref, beside_ref)):
        at = slice(g * half, g * half + half)
        for first in range(0, columns, 256):
            lanes = slice(first, first + 256)
            result = dot32(order, table_ref[:, lanes]).astype(jnp.bfloat16)
            even_ref[at, lanes] = result[:half]
            odd_ref[at, lanes] = result[half:]


def far_table_body(meta_ref, first_ref, second_ref, out_ref, whole):
    half, columns = first_ref.shape
    for ens, ref in ((meta_ref[4], first_ref), (1 - meta_ref[4], second_ref)):
        whole[pl.ds(pl.multiple_of(ens * half, half), half), :] = ref[...]
    order = by_parity(meta_ref, 2 * half)
    for first in range(0, columns, 256):
        lanes = slice(first, first + 256)
        out_ref[:, lanes] = dot32(order, whole[:, lanes]).astype(jnp.bfloat16)


def modes_body(sizes, degree_total, meta_ref, to_ref, from_ref, rate_ref, in_ref, out_ref, scale_ref):
    levels = to_ref.shape[0]
    wide = 2 * levels
    own = levels // 2
    lane, row = iota2((levels, wide), 1), iota2((levels, wide), 0)
    owner = lax.rem(meta_ref[2] + lane // levels, 2)
    spread = picks(row == owner * own + lane % own)
    plain = picks(row == lane % levels)
    old, new = iota2((wide, wide), 0), iota2((wide, wide), 1)

    def turned(first, matrix, last):
        half = lax.dot_general(first, matrix, (((0,), (1,)), ((), ())), preferred_element_type=jnp.float32)
        return dot32(half.astype(jnp.bfloat16), last)

    same = (old // own) % 2 == new // levels
    in_ref[...] = jnp.where(same, turned(spread, to_ref[...], plain), 0.0).astype(jnp.bfloat16)
    same = old // levels == (new // own) % 2
    out_ref[...] = jnp.where(same, turned(plain, from_ref[...], spread), 0.0).astype(jnp.bfloat16)
    wide, levs, flds = sizes
    rows = degree_total // (2 * levs * flds)
    for odd in range(2):
        for d in range(levs):
            for g in range(flds):
                block = lax.rem(meta_ref[2] + d, levs) * flds + lax.rem(meta_ref[3] + g, flds)
                degree = block * (2 * rows) + 2 * iota2((rows, 1), 0) + (meta_ref[0] + odd) % 2
                real = degree.astype(jnp.float32)
                factor = 1.0 + real * (real + 1.0) * rate_ref[...] / (degree_total * degree_total)
                at = ((d * 2 + odd) * flds + g) * rows
                scale_ref[at : at + rows, :] = jnp.where(degree >= meta_ref[0], 1.0 / factor, 0.0)


def transform(tables, data, scale_ref, in_ref, out_ref, own_ref, other_ref):
    lanes = own_ref.shape[1]
    rows = own_ref.shape[0] // 2
    for odd in range(2):
        at = slice(odd * rows, odd * rows + rows)
        raw = dot32(tables[odd], data[odd]).astype(jnp.bfloat16)
        scale = jnp.concatenate([scale_ref[at, :]] * 2, axis=1)
        modes = (dot32(raw, in_ref[...]) * scale).astype(jnp.bfloat16)
        spectral = dot32(modes, out_ref[...]).astype(jnp.bfloat16)
        own_ref[at, :] = spectral[:, :lanes]
        other_ref[at, :] = spectral[:, lanes:]


def near_body(wide, meta_ref, in_ref, out_ref, scale_ref, even_ref, odd_ref, *refs):
    parts, (own_ref, other_ref, data_ref) = refs[:-3], refs[-3:]
    latitudes, lanes = parts[0].shape[1:]
    for shift in range(wide):
        owner = lax.rem(meta_ref[1] - shift + wide, wide)
        at = pl.ds(pl.multiple_of(owner * latitudes, latitudes), latitudes)
        for d in range(2):
            data_ref[:, at, d * lanes : d * lanes + lanes] = parts[shift * 2 + d][...]
    scale = scale_ref.at[: scale_ref.shape[0] // 2]
    transform((even_ref[...], odd_ref[...]), data_ref, scale, in_ref, out_ref, own_ref, other_ref)


def far_body(in_ref, out_ref, scale_ref, first_ref, second_ref, data_ref, own_ref, other_ref):
    rows = first_ref.shape[0] // 2
    tables = [
        jnp.concatenate([ref[odd * rows : odd * rows + rows, :] for ref in (first_ref, second_ref)], axis=0)
        for odd in range(2)
    ]
    scale = scale_ref.at[scale_ref.shape[0] // 2 :]
    transform(tables, data_ref, scale, in_ref, out_ref, own_ref, other_ref)


def inverse_body(wide, meta_ref, *refs):
    parts, near, far, outs, total = refs[:4], refs[4:6], refs[6:8], refs[8:-1], refs[-1]
    latitudes, lanes = outs[0].shape[1:]
    rows = parts[0].shape[0] // 2
    spectral = [
        jnp.concatenate(
            [
                jnp.concatenate([ref[odd * rows : odd * rows + rows, :] for ref in pair], axis=1)
                for pair in (parts[:2], parts[2:])
            ],
            axis=0,
        )
        for odd in range(2)
    ]
    for first in range(0, total.shape[1], 256):
        chunk = slice(first, first + 256)
        sums = []
        for odd in range(2):
            at = slice(odd * (rows // 2), (odd + 1) * (rows // 2))
            table = jnp.concatenate([near[odd][:, chunk]] + [ref[at, chunk] for ref in far], axis=0)
            sums.append(lax.dot_general(
                table, spectral[odd], (((0,), (0,)), ((), ())), preferred_element_type=jnp.float32
            ))
        total[0, chunk, :] = (sums[0] + sums[1]).astype(jnp.bfloat16)
        total[1, chunk, :] = (sums[0] - sums[1]).astype(jnp.bfloat16)
    for shift in range(wide):
        owner = lax.rem(meta_ref[1] + shift, wide)
        at = pl.ds(pl.multiple_of(owner * latitudes, latitudes), latitudes)
        for d in range(2):
            outs[shift * 2 + d][...] = total[:, at, d * lanes : d * lanes + lanes]


def join_body(slots, block, meta_ref, *refs):
    parts, out_hbm, out_ref, semaphores = refs[:-3], *refs[-3:]
    copies = copy_pieces(out_ref, out_hbm, semaphores)
    latitudes, lanes = parts[0].shape[1:]
    fields = 2
    group = slots * fields
    size = block * group
    out_row, in_row = iota2((size, size), 0), iota2((size, size), 1)
    place = out_row % group
    shift = lax.rem(meta_ref[1] - place // fields + slots, slots)
    order = picks(in_row == (shift * fields + place % fields) * block + out_row // group)
    both = 2 * lanes
    turn = picks(lane_order(both, meta_ref[2], iota2((both, both), 1), iota2((both, both), 0)))
    for first in range(0, latitudes, block):
        at = slice(first, first + block)
        stacked = jnp.concatenate(
            [
                jnp.concatenate([parts[shift * 2 + d][half, at, :] for d in range(2)], axis=1)
                for half in range(2)
                for shift in range(slots)
            ],
            axis=0,
        )
        turned = dot32(stacked, turn).astype(jnp.bfloat16)
        halves = [
            jnp.concatenate(
                [
                    turned[
                        (half * slots + shift) * block : (half * slots + shift + 1) * block,
                        field * lanes : field * lanes + lanes,
                    ]
                    for shift in range(slots)
                    for field in range(fields)
                ],
                axis=0,
            )
            for half in range(2)
        ]
        result = dot32(order, jnp.concatenate(halves, axis=1)).astype(jnp.bfloat16)
        for half in range(2):
            out_ref[half, first * group : first * group + size, :] = result[:, half * lanes : half * lanes + lanes]
        done = first + block
        if done * PIECES % latitudes == 0:
            copies[done * PIECES // latitudes - 1].start()
    for copy in copies:
        copy.wait()


def rows_body(sizes, block, meta_ref, *refs):
    wide, levs, flds = sizes
    own_refs, other_refs, out_ref = refs[:2], refs[2:4], refs[4]
    total_rows, lanes = own_refs[0].shape
    rows = total_rows // (2 * flds)
    fields = 2
    group = 2 * fields
    size = block * group
    out_row, in_row = iota2((size, size), 0), iota2((size, size), 1)
    place = out_row % group
    odd = (place // fields + meta_ref[0] % 2) % 2
    order = picks(in_row == (odd * fields + place % fields) * block + out_row // group)
    both = 2 * lanes
    turn = picks(lane_order(both, meta_ref[2], iota2((both, both), 1), iota2((both, both), 0)))
    for d in range(levs):
        for g in range(flds):
            index = lax.rem(meta_ref[2] + d, levs) * flds + lax.rem(meta_ref[3] + g, flds)
            halves = []
            for odd in range(2):
                at = slice((odd * flds + g) * rows, (odd * flds + g + 1) * rows)
                halves.append(jnp.concatenate((own_refs[d][at, :], other_refs[1 - d][at, :]), axis=1))
            turned = dot32(jnp.concatenate(halves, axis=0), turn).astype(jnp.bfloat16)
            for first in range(0, rows, block):
                stacked = jnp.concatenate(
                    [
                        turned[
                            odd * rows + first : odd * rows + first + block, field * lanes : field * lanes + lanes
                        ]
                        for odd in range(2)
                        for field in range(fields)
                    ],
                    axis=0,
                )
                start = pl.multiple_of(index * (rows * group), rows * group) + first * group
                out_ref[pl.ds(start, size), :] = dot32(order, stacked).astype(jnp.bfloat16)


def shards(fourier_input_rows, legendre, slot_wave, to_modes, from_modes, mode_rate):
    wide, levs, flds = (lax.axis_size(axis) for axis in ("wide", "lev", "fld"))
    sizes = (wide, levs, flds)
    _, latitudes, slots, fields, lanes = fourier_input_rows.shape
    _, shard_rows, half_count = legendre.shape
    degree_count = shard_rows * levs * flds
    group = slots * fields
    columns = fields * lanes
    block = 256 // group
    levels = to_modes.shape[0]
    bf16 = jnp.bfloat16

    def shape(*dims):
        return jax.ShapeDtypeStruct(dims, bf16)

    def shifted(value, axis, count, step):
        return lax.ppermute(value, axis, [(i, (i + step) % count) for i in range(count)])

    def over_lev(value):
        return shifted(value, "lev", levs, 1)

    def beside(value):
        return shifted(value, "fld", flds, 1)

    def moved(value, k, d):
        pairs = [(w * levs + l, (w + k) % wide * levs + (l + d) % levs) for w in range(wide) for l in range(levs)]
        return lax.ppermute(value, ("wide", "lev"), pairs)

    def behind(value, *others):
        return lax.optimization_barrier((value, *others))

    wide_at, lev_at, fld_at = (lax.axis_index(axis) for axis in ("wide", "lev", "fld"))
    meta = jnp.stack((slot_wave[0], wide_at, lev_at, fld_at, lax.axis_index("ens"))).astype(jnp.int32)
    position = (wide_at * latitudes + jnp.arange(latitudes, dtype=jnp.int32)).astype(jnp.float32)
    weights = jnp.sin(math.pi * (position + 0.5) / (2 * half_count))
    weights = jnp.broadcast_to(weights[:, None], (latitudes, lanes))
    move_flops = 8 * group * latitudes * 128 * 256
    transform_flops = 2 * degree_count * half_count * columns

    table_beside = beside(legendre[0])
    blocks = call(
        functools.partial(split_body, slots, fields, block), (shape(2, latitudes, lanes),) * (wide * levs),
        "split_hemispheres", move_flops,
    )(meta, fourier_input_rows.reshape(2, latitudes * group, lanes), weights)
    table_beside, *blocks = behind(table_beside, *blocks)
    *matrices, scale = call(
        functools.partial(modes_body, sizes, degree_count),
        (shape(2 * levels, 2 * levels),) * 2 + (jax.ShapeDtypeStruct((degree_count, levels), jnp.float32),),
        "spread_modes", 12 * levels * levels * levels, after=(blocks[0],),
    )(meta, to_modes, from_modes, mode_rate[None, :])
    near = call(
        near_table_body, (shape(shard_rows, half_count),) * 2, "split_table",
        4 * shard_rows * shard_rows * half_count, after=(scale,),
    )(meta, legendre[0], table_beside)

    def exchanged(blocks, ahead):
        arrived = {(0, 0): blocks[0]}
        for k, d in ((2, 0), (1, 0), (3, 0), (0, 1)):
            arrived[k, d] = moved(blocks[k * levs + d], k, d)
        for k, first in ((2, (0, 1)), (1, (1, 0)), (3, (3, 0))):
            value, arrived[first], *_ = behind(blocks[k * levs + 1], arrived[first], *ahead)
            arrived[k, 1] = moved(value, k, 1)
        return arrived

    def listed(arrived):
        return [arrived[k, d] for k in range(wide) for d in range(levs)]

    arrived = exchanged(blocks, (near[0], scale))
    half_shard = shard_rows // 2
    own_table, _ = behind(legendre[0], blocks[0])
    first = over_lev(lax.dynamic_slice_in_dim(own_table, lax.axis_index("ens") * half_shard, half_shard, 0))
    steps = [(1, 0), (2, 0), (3, 0), (0, 1)]
    first, *ahead = behind(first, *(arrived[step] for step in steps))
    arrived |= dict(zip(steps, ahead))
    second = shifted(first, "ens", 2, 1)
    far = call(
        far_table_body, shape(shard_rows, half_count), "split_table", 2 * shard_rows * shard_rows * half_count,
        scratch=[pltpu.VMEM((shard_rows, half_count), bf16)],
    )(meta, first, second)
    steps = [(1, 1), (2, 1), (3, 1)]
    far, *ahead = behind(far, *(arrived[step] for step in steps))
    arrived |= dict(zip(steps, ahead))
    far = [far, beside(far)]

    half_rows = degree_count // 2
    *near_spectral, data = call(
        functools.partial(near_body, wide), (shape(half_rows, lanes),) * 2 + (shape(2, half_count, columns),),
        "direct_legendre_and_solve", transform_flops // 2,
    )(meta, *matrices, scale, *near, *listed(arrived))
    far_spectral = call(
        far_body, (shape(half_rows, lanes),) * 2, "direct_legendre_and_solve", transform_flops // 2, scalars=0,
    )(*matrices, scale, *far, data)
    spectral = (near_spectral, far_spectral)
    grid = call(
        functools.partial(inverse_body, wide), (shape(2, latitudes, lanes),) * (wide * levs),
        "inverse_legendre", transform_flops, scratch=[pltpu.VMEM((2, half_count, columns), bf16)],
    )(meta, *near_spectral, *far_spectral, *near, *far)
    arrived = exchanged(grid, ())
    others = [other for _, other in spectral]
    arrived[0, 1], *others = behind(arrived[0, 1], *others)
    result = listed(arrived)
    spectral_rows = call(
        functools.partial(rows_body, sizes, 32), shape(degree_count * fields, lanes), "order_spectral", move_flops,
    )(meta, *(own for own, _ in spectral), *(over_lev(other) for other in others))
    fourier_rows = call(
        functools.partial(join_body, slots, 256 // group), shape(2, latitudes * group, lanes),
        "join_hemispheres", move_flops, out_hbm=True,
        scratch=[pltpu.VMEM((2, latitudes * group, lanes), bf16), pltpu.SemaphoreType.DMA((PIECES,))],
    )(meta, *result)
    return (
        fourier_rows.reshape(2, latitudes, slots, fields, lanes),
        spectral_rows.reshape(1, degree_count, fields, lanes),
    )


def project(level_grid, degree_real, weight_rows, rate_rows, degree_total):
    projected = jnp.einsum(
        "kl,snflr->snfkr", weight_rows, level_grid, preferred_element_type=jnp.float32
    )
    factor = 1.0 + degree_real[:, None] * (degree_real[:, None] + 1.0) * rate_rows[None, :] / (
        degree_total * degree_total
    )
    return (projected / factor[None, :, None, :, None]).astype(jnp.bfloat16)


def plain_shards(fourier_input_rows, legendre, slot_wave, to_modes, from_modes, mode_rate):
    wave_rows = lax.all_to_all(fourier_input_rows, "wide", split_axis=2, concat_axis=1, tiled=True)
    half_count = wave_rows.shape[1]
    slot_count = wave_rows.shape[2]
    field_count = wave_rows.shape[3]
    column_count = wave_rows.shape[4]
    degree_count = legendre.shape[1] * lax.axis_size(("lev", "fld"))
    weights = latitude_weights(half_count)[:, None, None, None]
    north_half = wave_rows[0].astype(jnp.float32)
    south_half = wave_rows[1].astype(jnp.float32)
    symmetric = (weights * (north_half + south_half)).astype(jnp.bfloat16)
    antisym = (weights * (north_half - south_half)).astype(jnp.bfloat16)
    paired = jnp.concatenate((symmetric, antisym), axis=3)

    def direct_rows(section, first_row):
        row_count = section.shape[1]
        degree = first_row + jnp.arange(row_count, dtype=jnp.int32)
        relative = degree[None, :] - slot_wave[:, None]
        product = jnp.einsum("snj,jsfc->snfc", section, paired, preferred_element_type=jnp.float32)
        is_even = (relative % 2 == 0)[:, :, None, None]
        is_live = (relative >= 0)[:, :, None, None]
        picked = jnp.where(is_even, product[..., :column_count], product[..., column_count:])
        return jnp.where(is_live, picked, jnp.zeros_like(picked))

    full_table = lax.all_gather(legendre, ("lev", "fld"), axis=1, tiled=True)
    block_rows = 128
    block_count = degree_count // block_rows

    def direct_step(block_index, buffer):
        first_row = block_index * block_rows
        section = lax.dynamic_slice_in_dim(full_table, first_row, block_rows, 1)
        result = direct_rows(section, first_row).astype(jnp.bfloat16)
        return lax.dynamic_update_slice_in_dim(buffer, result, first_row, 1)

    initial_raw = jnp.zeros((slot_count, degree_count, field_count, column_count), jnp.bfloat16)
    raw_spectral = lax.fori_loop(0, block_count, direct_step, initial_raw)
    own_levels = column_count // 2
    first_level = lax.axis_index("lev") * own_levels
    degree_real = jnp.arange(degree_count, dtype=jnp.float32)
    all_levels = lax.all_gather(raw_spectral, "lev", axis=3, tiled=True)
    level_count = all_levels.shape[3] // 2
    level_grid = all_levels.reshape(slot_count, degree_count, field_count, level_count, 2)
    weight_rows = lax.dynamic_slice_in_dim(to_modes, first_level, own_levels, 0)
    rate_rows = lax.dynamic_slice_in_dim(mode_rate, first_level, own_levels, 0)
    own_modes = project(level_grid, degree_real, weight_rows, rate_rows, degree_count).reshape(
        slot_count, degree_count, field_count, column_count
    )
    mode_values = lax.all_gather(own_modes, "lev", axis=3, tiled=True).reshape(
        slot_count, degree_count, field_count, level_count, 2
    )
    back_rows = lax.dynamic_slice_in_dim(from_modes, first_level, own_levels, 0)
    spectral = jnp.einsum(
        "lk,snfkr->snflr", back_rows, mode_values, preferred_element_type=jnp.float32
    )
    spectral = spectral.astype(jnp.bfloat16).reshape(
        slot_count, degree_count, field_count, column_count
    )

    def inverse_rows(running, section, first_row):
        row_count = section.shape[1]
        degree = first_row + jnp.arange(row_count, dtype=jnp.int32)
        relative = degree[None, :] - slot_wave[:, None]
        spec_rows = lax.dynamic_slice_in_dim(spectral, first_row, row_count, 1)
        even_mask = ((relative >= 0) & (relative % 2 == 0))[:, :, None, None]
        odd_mask = ((relative >= 0) & (relative % 2 == 1))[:, :, None, None]
        empty_rows = jnp.zeros_like(spec_rows)
        parity_split = jnp.concatenate(
            (
                jnp.where(even_mask, spec_rows, empty_rows),
                jnp.where(odd_mask, spec_rows, empty_rows),
            ),
            axis=3,
        )
        return running + jnp.einsum(
            "snj,snfc->jsfc", section, parity_split, preferred_element_type=jnp.float32
        )

    initial_sum = jnp.zeros((half_count, slot_count, field_count, 2 * column_count), jnp.float32)

    def inverse_step(block_index, running):
        first_row = block_index * block_rows
        section = lax.dynamic_slice_in_dim(full_table, first_row, block_rows, 1)
        return inverse_rows(running, section, first_row)

    running = lax.fori_loop(0, block_count, inverse_step, initial_sum)
    even_sum = running[..., :column_count]
    odd_sum = running[..., column_count:]
    fourier_wave = jnp.stack((even_sum + odd_sum, even_sum - odd_sum), axis=0).astype(jnp.bfloat16)
    fourier_out = lax.all_to_all(fourier_wave, "wide", split_axis=1, concat_axis=2, tiled=True)
    return (fourier_out, spectral)


def solution(mesh):
    in_specs = (
        P("ens", "wide", None, "fld", "lev"),
        P("wide", ("lev", "fld"), None),
        P("wide"),
        P(),
        P(),
        P(),
    )
    out_specs = (P("ens", "wide", None, "fld", "lev"), P(("ens", "wide"), None, "fld", "lev"))

    def body(fourier_input_rows, legendre, *rest):
        _, latitudes, slots, fields, lanes = fourier_input_rows.shape
        whole_tiles = (
            latitudes % (32 * PIECES) == 0
            and fields == 2
            and slots == mesh.shape["wide"] == 4
            and mesh.shape["ens"] == mesh.shape["lev"] == mesh.shape["fld"] == 2
            and lanes == 128
            and legendre.shape[1] % 64 == 0
            and legendre.shape[2] % 256 == 0
        )
        form = shards if whole_tiles else plain_shards
        return form(fourier_input_rows, legendre, *rest)

    return jax.shard_map(body, mesh=mesh, in_specs=in_specs, out_specs=out_specs, check_vma=False)
```

```python
import functools
import math

import jax
import jax.numpy as jnp
from jax import lax
from jax.experimental import pallas as pl
from jax.experimental.pallas import tpu as pltpu
from jax.sharding import PartitionSpec as P

VMEM_BYTES = 8 * 1024 * 1024


def latitude_weights(count):
    position = jnp.arange(count, dtype=jnp.float32)
    return jnp.sin(math.pi * (position + 0.5) / (2 * count))


def iota2(shape, dim):
    return lax.broadcasted_iota(jnp.int32, shape, dim)


def picks(condition):
    return jnp.where(condition, 1.0, 0.0).astype(jnp.bfloat16)


def dot32(a, b):
    return jnp.dot(a, b, preferred_element_type=jnp.float32)


PIECES = 5


def copy_pieces(source, target, semaphores):
    rows = target.shape[1] // PIECES
    return [
        pltpu.make_async_copy(
            source.at[:, pl.ds(i * rows, rows), :], target.at[:, pl.ds(i * rows, rows), :], semaphores.at[i]
        )
        for i in range(PIECES)
    ]


def call(body, out_shape, name, flops, scratch=(), scalars=1, after=(), out_hbm=False):
    smem = pl.BlockSpec(memory_space=pltpu.SMEM)
    vmem = pl.BlockSpec(memory_space=pltpu.VMEM)
    hbm = pl.BlockSpec(memory_space=pltpu.HBM)

    def run(*operands):
        used = len(operands)

        def kernel(*refs):
            body(*refs[:used], *refs[used + len(after) :])

        return pl.pallas_call(
            kernel,
            out_shape=out_shape,
            in_specs=[smem] * scalars
            + [vmem] * (used - scalars)
            + [pl.BlockSpec(memory_space=pl.ANY)] * len(after),
            out_specs=jax.tree.map(lambda _: hbm if out_hbm else vmem, out_shape),
            scratch_shapes=list(scratch),
            compiler_params=pltpu.CompilerParams(vmem_limit_bytes=VMEM_BYTES),
            cost_estimate=pl.CostEstimate(flops=flops, bytes_accessed=0, transcendentals=0),
            name=name,
        )(*operands, *after)

    return run


def split_body(slots, fields, block, meta_ref, rows_ref, weight_ref, *outs):
    latitudes = weight_ref.shape[0]
    group = slots * fields
    size = block * group
    out_row, in_row = iota2((size, size), 0), iota2((size, size), 1)
    pair = out_row // block
    slot = lax.rem(meta_ref[1] + pair // fields, slots)
    field = (meta_ref[2] + pair) % fields
    order = picks(in_row == (out_row % block) * group + slot * fields + field)
    for first in range(0, latitudes, block):
        north = rows_ref[0, first * group : first * group + size, :]
        south = rows_ref[1, first * group : first * group + size, :]
        sorted_rows = dot32(order, jnp.concatenate((north, south), axis=1))
        up, down = sorted_rows[:, :128], sorted_rows[:, 128:]
        weight = weight_ref[first : first + block, :]
        for odd, mixed in enumerate((up + down, up - down)):
            for i, out_ref in enumerate(outs):
                out_ref[odd, first : first + block, :] = (weight * mixed[i * block : i * block + block]).astype(
                    jnp.bfloat16
                )


def by_parity(meta_ref, rows):
    half = rows // 2
    out_row, in_row = iota2((rows, rows), 0), iota2((rows, rows), 1)
    odd = jnp.where(out_row < half, 0, 1)
    return picks(in_row == 2 * (out_row - odd * half) + (meta_ref[0] + odd) % 2)


def near_table_body(meta_ref, own_ref, beside_ref, even_ref, odd_ref):
    rows, columns = own_ref.shape
    half = rows // 2
    order = by_parity(meta_ref, rows)
    for g, table_ref in enumerate((own_ref, beside_ref)):
        at = slice(g * half, g * half + half)
        for first in range(0, columns, 256):
            lanes = slice(first, first + 256)
            result = dot32(order, table_ref[:, lanes]).astype(jnp.bfloat16)
            even_ref[at, lanes] = result[:half]
            odd_ref[at, lanes] = result[half:]


def far_table_body(meta_ref, first_ref, second_ref, out_ref, whole):
    half, columns = first_ref.shape
    for ens, ref in ((meta_ref[4], first_ref), (1 - meta_ref[4], second_ref)):
        whole[pl.ds(pl.multiple_of(ens * half, half), half), :] = ref[...]
    order = by_parity(meta_ref, 2 * half)
    for first in range(0, columns, 256):
        lanes = slice(first, first + 256)
        out_ref[:, lanes] = dot32(order, whole[:, lanes]).astype(jnp.bfloat16)


def modes_body(sizes, degree_total, meta_ref, to_ref, from_ref, rate_ref, in_ref, out_ref, scale_ref):
    levels = to_ref.shape[0]
    wide = 2 * levels
    own = levels // 2
    lane, row = iota2((levels, wide), 1), iota2((levels, wide), 0)
    owner = lax.rem(meta_ref[2] + lane // levels, 2)
    spread = picks(row == owner * own + lane % levels // 2)
    plain = picks(row == lane % levels)
    old, new = iota2((wide, wide), 0), iota2((wide, wide), 1)

    def turned(first, matrix, last):
        half = lax.dot_general(first, matrix, (((0,), (1,)), ((), ())), preferred_element_type=jnp.float32)
        return dot32(half.astype(jnp.bfloat16), last)

    same = old % 2 == new // levels
    in_ref[...] = jnp.where(same, turned(spread, to_ref[...], plain), 0.0).astype(jnp.bfloat16)
    same = old // levels == new % 2
    out_ref[...] = jnp.where(same, turned(plain, from_ref[...], spread), 0.0).astype(jnp.bfloat16)
    wide, levs, flds = sizes
    rows = degree_total // (2 * levs * flds)
    for odd in range(2):
        for d in range(levs):
            for g in range(flds):
                block = lax.rem(meta_ref[2] + d, levs) * flds + lax.rem(meta_ref[3] + g, flds)
                degree = block * (2 * rows) + 2 * iota2((rows, 1), 0) + (meta_ref[0] + odd) % 2
                real = degree.astype(jnp.float32)
                factor = 1.0 + real * (real + 1.0) * rate_ref[...] / (degree_total * degree_total)
                at = ((d * 2 + odd) * flds + g) * rows
                scale_ref[at : at + rows, :] = jnp.where(degree >= meta_ref[0], 1.0 / factor, 0.0)


def transform(tables, data, scale_ref, in_ref, out_ref, own_ref, other_ref):
    lanes = own_ref.shape[1]
    rows = own_ref.shape[0] // 2
    for odd in range(2):
        at = slice(odd * rows, odd * rows + rows)
        raw = dot32(tables[odd], data[odd]).astype(jnp.bfloat16)
        scale = jnp.concatenate([scale_ref[at, :]] * 2, axis=1)
        modes = (dot32(raw, in_ref[...]) * scale).astype(jnp.bfloat16)
        spectral = dot32(modes, out_ref[...]).astype(jnp.bfloat16)
        own_ref[at, :] = spectral[:, :lanes]
        other_ref[at, :] = spectral[:, lanes:]


def near_body(wide, meta_ref, in_ref, out_ref, scale_ref, even_ref, odd_ref, *refs):
    parts, (own_ref, other_ref, data_ref) = refs[:-3], refs[-3:]
    latitudes, lanes = parts[0].shape[1:]
    for shift in range(wide):
        owner = lax.rem(meta_ref[1] - shift + wide, wide)
        at = pl.ds(pl.multiple_of(owner * latitudes, latitudes), latitudes)
        for d in range(2):
            data_ref[:, at, d * lanes : d * lanes + lanes] = parts[shift * 2 + d][...]
    scale = scale_ref.at[: scale_ref.shape[0] // 2]
    transform((even_ref[...], odd_ref[...]), data_ref, scale, in_ref, out_ref, own_ref, other_ref)


def far_body(in_ref, out_ref, scale_ref, first_ref, second_ref, data_ref, own_ref, other_ref):
    rows = first_ref.shape[0] // 2
    tables = [
        jnp.concatenate([ref[odd * rows : odd * rows + rows, :] for ref in (first_ref, second_ref)], axis=0)
        for odd in range(2)
    ]
    scale = scale_ref.at[scale_ref.shape[0] // 2 :]
    transform(tables, data_ref, scale, in_ref, out_ref, own_ref, other_ref)


def inverse_body(wide, meta_ref, *refs):
    parts, near, far, outs, total = refs[:4], refs[4:6], refs[6:8], refs[8:-1], refs[-1]
    latitudes, lanes = outs[0].shape[1:]
    rows = parts[0].shape[0] // 2
    spectral = [
        jnp.concatenate(
            [
                jnp.concatenate([ref[odd * rows : odd * rows + rows, :] for ref in pair], axis=1)
                for pair in (parts[:2], parts[2:])
            ],
            axis=0,
        )
        for odd in range(2)
    ]
    for first in range(0, total.shape[1], 256):
        chunk = slice(first, first + 256)
        sums = []
        for odd in range(2):
            at = slice(odd * (rows // 2), (odd + 1) * (rows // 2))
            table = jnp.concatenate([near[odd][:, chunk]] + [ref[at, chunk] for ref in far], axis=0)
            sums.append(lax.dot_general(
                table, spectral[odd], (((0,), (0,)), ((), ())), preferred_element_type=jnp.float32
            ))
        total[0, chunk, :] = (sums[0] + sums[1]).astype(jnp.bfloat16)
        total[1, chunk, :] = (sums[0] - sums[1]).astype(jnp.bfloat16)
    for shift in range(wide):
        owner = lax.rem(meta_ref[1] + shift, wide)
        at = pl.ds(pl.multiple_of(owner * latitudes, latitudes), latitudes)
        for d in range(2):
            outs[shift * 2 + d][...] = total[:, at, d * lanes : d * lanes + lanes]


def join_body(slots, block, meta_ref, *refs):
    parts, out_hbm, out_ref, semaphores = refs[:-3], *refs[-3:]
    copies = copy_pieces(out_ref, out_hbm, semaphores)
    latitudes, lanes = parts[0].shape[1:]
    fields = 2
    group = slots * fields
    size = block * group
    out_row, in_row = iota2((size, size), 0), iota2((size, size), 1)
    place = out_row % group
    shift = lax.rem(meta_ref[1] - place // fields + slots, slots)
    order = picks(in_row == (shift * fields + (place + meta_ref[2]) % fields) * block + out_row // group)
    for first in range(0, latitudes, block):
        at = slice(first, first + block)
        stacked = [jnp.concatenate([part[half, at, :] for part in parts], axis=0) for half in range(2)]
        result = dot32(order, jnp.concatenate(stacked, axis=1)).astype(jnp.bfloat16)
        for half in range(2):
            out_ref[half, first * group : first * group + size, :] = result[:, half * lanes : half * lanes + lanes]
        done = first + block
        if done * PIECES % latitudes == 0:
            copies[done * PIECES // latitudes - 1].start()
    for copy in copies:
        copy.wait()


def rows_body(sizes, block, meta_ref, *refs):
    wide, levs, flds = sizes
    own_refs, other_refs, out_ref = refs[:2], refs[2:4], refs[4]
    rows = own_refs[0].shape[0] // (2 * flds)
    fields = 2
    group = 2 * fields
    size = block * group
    out_row, in_row = iota2((size, size), 0), iota2((size, size), 1)
    place = out_row % group
    odd = (place // fields + meta_ref[0] % 2) % 2
    order = picks(in_row == (odd * fields + (place + meta_ref[2]) % fields) * block + out_row // group)
    for d in range(levs):
        for g in range(flds):
            index = lax.rem(meta_ref[2] + d, levs) * flds + lax.rem(meta_ref[3] + g, flds)
            for first in range(0, rows, block):
                stacked = jnp.concatenate(
                    [
                        ref[(odd * flds + g) * rows + first : (odd * flds + g) * rows + first + block, :]
                        for odd in range(2)
                        for ref in (own_refs[d], other_refs[1 - d])
                    ],
                    axis=0,
                )
                start = pl.multiple_of(index * (rows * group), rows * group) + first * group
                out_ref[pl.ds(start, size), :] = dot32(order, stacked).astype(jnp.bfloat16)


def shards(fourier_input_rows, legendre, slot_wave, to_modes, from_modes, mode_rate):
    wide, levs, flds = (lax.axis_size(axis) for axis in ("wide", "lev", "fld"))
    sizes = (wide, levs, flds)
    _, latitudes, slots, fields, lanes = fourier_input_rows.shape
    _, shard_rows, half_count = legendre.shape
    degree_count = shard_rows * levs * flds
    group = slots * fields
    columns = fields * lanes
    block = 256 // group
    levels = to_modes.shape[0]
    bf16 = jnp.bfloat16

    def shape(*dims):
        return jax.ShapeDtypeStruct(dims, bf16)

    def shifted(value, axis, count, step):
        return lax.ppermute(value, axis, [(i, (i + step) % count) for i in range(count)])

    def over_lev(value):
        return shifted(value, "lev", levs, 1)

    def beside(value):
        return shifted(value, "fld", flds, 1)

    def moved(value, k, d):
        pairs = [(w * levs + l, (w + k) % wide * levs + (l + d) % levs) for w in range(wide) for l in range(levs)]
        return lax.ppermute(value, ("wide", "lev"), pairs)

    def behind(value, *others):
        return lax.optimization_barrier((value, *others))

    wide_at, lev_at, fld_at = (lax.axis_index(axis) for axis in ("wide", "lev", "fld"))
    meta = jnp.stack((slot_wave[0], wide_at, lev_at, fld_at, lax.axis_index("ens"))).astype(jnp.int32)
    position = (wide_at * latitudes + jnp.arange(latitudes, dtype=jnp.int32)).astype(jnp.float32)
    weights = jnp.sin(math.pi * (position + 0.5) / (2 * half_count))
    weights = jnp.broadcast_to(weights[:, None], (latitudes, lanes))
    move_flops = 8 * group * latitudes * 128 * 256
    transform_flops = 2 * degree_count * half_count * columns

    table_beside = beside(legendre[0])
    blocks = call(
        functools.partial(split_body, slots, fields, block), (shape(2, latitudes, lanes),) * (wide * levs),
        "split_hemispheres", move_flops,
    )(meta, fourier_input_rows.reshape(2, latitudes * group, lanes), weights)
    table_beside, *blocks = behind(table_beside, *blocks)
    *matrices, scale = call(
        functools.partial(modes_body, sizes, degree_count),
        (shape(2 * levels, 2 * levels),) * 2 + (jax.ShapeDtypeStruct((degree_count, levels), jnp.float32),),
        "spread_modes", 12 * levels * levels * levels, after=(blocks[0],),
    )(meta, to_modes, from_modes, mode_rate[None, :])
    near = call(
        near_table_body, (shape(shard_rows, half_count),) * 2, "split_table",
        4 * shard_rows * shard_rows * half_count, after=(scale,),
    )(meta, legendre[0], table_beside)

    def exchanged(blocks, ahead):
        arrived = {(0, 0): blocks[0]}
        for k, d in ((2, 0), (1, 0), (3, 0), (0, 1)):
            arrived[k, d] = moved(blocks[k * levs + d], k, d)
        for k, first in ((2, (0, 1)), (1, (1, 0)), (3, (3, 0))):
            value, arrived[first], *_ = behind(blocks[k * levs + 1], arrived[first], *ahead)
            arrived[k, 1] = moved(value, k, 1)
        return arrived

    def listed(arrived):
        return [arrived[k, d] for k in range(wide) for d in range(levs)]

    arrived = exchanged(blocks, (near[0], scale))
    half_shard = shard_rows // 2
    own_table, _ = behind(legendre[0], blocks[0])
    first = over_lev(lax.dynamic_slice_in_dim(own_table, lax.axis_index("ens") * half_shard, half_shard, 0))
    steps = [(1, 0), (2, 0), (3, 0), (0, 1)]
    first, *ahead = behind(first, *(arrived[step] for step in steps))
    arrived |= dict(zip(steps, ahead))
    second = shifted(first, "ens", 2, 1)
    far = call(
        far_table_body, shape(shard_rows, half_count), "split_table", 2 * shard_rows * shard_rows * half_count,
        scratch=[pltpu.VMEM((shard_rows, half_count), bf16)],
    )(meta, first, second)
    steps = [(1, 1), (2, 1), (3, 1)]
    far, *ahead = behind(far, *(arrived[step] for step in steps))
    arrived |= dict(zip(steps, ahead))
    far = [far, beside(far)]

    half_rows = degree_count // 2
    *near_spectral, data = call(
        functools.partial(near_body, wide), (shape(half_rows, lanes),) * 2 + (shape(2, half_count, columns),),
        "direct_legendre_and_solve", transform_flops // 2,
    )(meta, *matrices, scale, *near, *listed(arrived))
    far_spectral = call(
        far_body, (shape(half_rows, lanes),) * 2, "direct_legendre_and_solve", transform_flops // 2, scalars=0,
    )(*matrices, scale, *far, data)
    spectral = (near_spectral, far_spectral)
    grid = call(
        functools.partial(inverse_body, wide), (shape(2, latitudes, lanes),) * (wide * levs),
        "inverse_legendre", transform_flops, scratch=[pltpu.VMEM((2, half_count, columns), bf16)],
    )(meta, *near_spectral, *far_spectral, *near, *far)
    arrived = exchanged(grid, ())
    others = [other for _, other in spectral]
    arrived[0, 1], *others = behind(arrived[0, 1], *others)
    result = listed(arrived)
    spectral_rows = call(
        functools.partial(rows_body, sizes, 32), shape(degree_count * fields, lanes), "order_spectral", move_flops,
    )(meta, *(own for own, _ in spectral), *(over_lev(other) for other in others))
    fourier_rows = call(
        functools.partial(join_body, slots, 256 // group), shape(2, latitudes * group, lanes),
        "join_hemispheres", move_flops, out_hbm=True,
        scratch=[pltpu.VMEM((2, latitudes * group, lanes), bf16), pltpu.SemaphoreType.DMA((PIECES,))],
    )(meta, *result)
    return (
        fourier_rows.reshape(2, latitudes, slots, fields, lanes),
        spectral_rows.reshape(1, degree_count, fields, lanes),
    )


def project(level_grid, degree_real, weight_rows, rate_rows, degree_total):
    projected = jnp.einsum(
        "kl,snflr->snfkr", weight_rows, level_grid, preferred_element_type=jnp.float32
    )
    factor = 1.0 + degree_real[:, None] * (degree_real[:, None] + 1.0) * rate_rows[None, :] / (
        degree_total * degree_total
    )
    return (projected / factor[None, :, None, :, None]).astype(jnp.bfloat16)


def plain_shards(fourier_input_rows, legendre, slot_wave, to_modes, from_modes, mode_rate):
    wave_rows = lax.all_to_all(fourier_input_rows, "wide", split_axis=2, concat_axis=1, tiled=True)
    half_count = wave_rows.shape[1]
    slot_count = wave_rows.shape[2]
    field_count = wave_rows.shape[3]
    column_count = wave_rows.shape[4]
    degree_count = legendre.shape[1] * lax.axis_size(("lev", "fld"))
    weights = latitude_weights(half_count)[:, None, None, None]
    north_half = wave_rows[0].astype(jnp.float32)
    south_half = wave_rows[1].astype(jnp.float32)
    symmetric = (weights * (north_half + south_half)).astype(jnp.bfloat16)
    antisym = (weights * (north_half - south_half)).astype(jnp.bfloat16)
    paired = jnp.concatenate((symmetric, antisym), axis=3)

    def direct_rows(section, first_row):
        row_count = section.shape[1]
        degree = first_row + jnp.arange(row_count, dtype=jnp.int32)
        relative = degree[None, :] - slot_wave[:, None]
        product = jnp.einsum("snj,jsfc->snfc", section, paired, preferred_element_type=jnp.float32)
        is_even = (relative % 2 == 0)[:, :, None, None]
        is_live = (relative >= 0)[:, :, None, None]
        picked = jnp.where(is_even, product[..., :column_count], product[..., column_count:])
        return jnp.where(is_live, picked, jnp.zeros_like(picked))

    full_table = lax.all_gather(legendre, ("lev", "fld"), axis=1, tiled=True)
    block_rows = 128
    block_count = degree_count // block_rows

    def direct_step(block_index, buffer):
        first_row = block_index * block_rows
        section = lax.dynamic_slice_in_dim(full_table, first_row, block_rows, 1)
        result = direct_rows(section, first_row).astype(jnp.bfloat16)
        return lax.dynamic_update_slice_in_dim(buffer, result, first_row, 1)

    initial_raw = jnp.zeros((slot_count, degree_count, field_count, column_count), jnp.bfloat16)
    raw_spectral = lax.fori_loop(0, block_count, direct_step, initial_raw)
    own_levels = column_count // 2
    first_level = lax.axis_index("lev") * own_levels
    degree_real = jnp.arange(degree_count, dtype=jnp.float32)
    all_levels = lax.all_gather(raw_spectral, "lev", axis=3, tiled=True)
    level_count = all_levels.shape[3] // 2
    level_grid = all_levels.reshape(slot_count, degree_count, field_count, level_count, 2)
    weight_rows = lax.dynamic_slice_in_dim(to_modes, first_level, own_levels, 0)
    rate_rows = lax.dynamic_slice_in_dim(mode_rate, first_level, own_levels, 0)
    own_modes = project(level_grid, degree_real, weight_rows, rate_rows, degree_count).reshape(
        slot_count, degree_count, field_count, column_count
    )
    mode_values = lax.all_gather(own_modes, "lev", axis=3, tiled=True).reshape(
        slot_count, degree_count, field_count, level_count, 2
    )
    back_rows = lax.dynamic_slice_in_dim(from_modes, first_level, own_levels, 0)
    spectral = jnp.einsum(
        "lk,snfkr->snflr", back_rows, mode_values, preferred_element_type=jnp.float32
    )
    spectral = spectral.astype(jnp.bfloat16).reshape(
        slot_count, degree_count, field_count, column_count
    )

    def inverse_rows(running, section, first_row):
        row_count = section.shape[1]
        degree = first_row + jnp.arange(row_count, dtype=jnp.int32)
        relative = degree[None, :] - slot_wave[:, None]
        spec_rows = lax.dynamic_slice_in_dim(spectral, first_row, row_count, 1)
        even_mask = ((relative >= 0) & (relative % 2 == 0))[:, :, None, None]
        odd_mask = ((relative >= 0) & (relative % 2 == 1))[:, :, None, None]
        empty_rows = jnp.zeros_like(spec_rows)
        parity_split = jnp.concatenate(
            (
                jnp.where(even_mask, spec_rows, empty_rows),
                jnp.where(odd_mask, spec_rows, empty_rows),
            ),
            axis=3,
        )
        return running + jnp.einsum(
            "snj,snfc->jsfc", section, parity_split, preferred_element_type=jnp.float32
        )

    initial_sum = jnp.zeros((half_count, slot_count, field_count, 2 * column_count), jnp.float32)

    def inverse_step(block_index, running):
        first_row = block_index * block_rows
        section = lax.dynamic_slice_in_dim(full_table, first_row, block_rows, 1)
        return inverse_rows(running, section, first_row)

    running = lax.fori_loop(0, block_count, inverse_step, initial_sum)
    even_sum = running[..., :column_count]
    odd_sum = running[..., column_count:]
    fourier_wave = jnp.stack((even_sum + odd_sum, even_sum - odd_sum), axis=0).astype(jnp.bfloat16)
    fourier_out = lax.all_to_all(fourier_wave, "wide", split_axis=1, concat_axis=2, tiled=True)
    return (fourier_out, spectral)


def solution(mesh):
    in_specs = (
        P("ens", "wide", None, "fld", "lev"),
        P("wide", ("lev", "fld"), None),
        P("wide"),
        P(),
        P(),
        P(),
    )
    out_specs = (P("ens", "wide", None, "fld", "lev"), P(("ens", "wide"), None, "fld", "lev"))

    def body(fourier_input_rows, legendre, *rest):
        _, latitudes, slots, fields, lanes = fourier_input_rows.shape
        whole_tiles = (
            latitudes % (32 * PIECES) == 0
            and fields == 2
            and slots == mesh.shape["wide"] == 4
            and mesh.shape["ens"] == mesh.shape["lev"] == mesh.shape["fld"] == 2
            and lanes == 128
            and legendre.shape[1] % 64 == 0
            and legendre.shape[2] % 256 == 0
        )
        form = shards if whole_tiles else plain_shards
        return form(fourier_input_rows, legendre, *rest)

    return jax.shard_map(body, mesh=mesh, in_specs=in_specs, out_specs=out_specs, check_vma=False)
```

```python
import functools
import math

import jax
import jax.numpy as jnp
from jax import lax
from jax.experimental import pallas as pl
from jax.experimental.pallas import tpu as pltpu
from jax.sharding import PartitionSpec as P

VMEM_BYTES = 8 * 1024 * 1024


def latitude_weights(count):
    position = jnp.arange(count, dtype=jnp.float32)
    return jnp.sin(math.pi * (position + 0.5) / (2 * count))


def iota2(shape, dim):
    return lax.broadcasted_iota(jnp.int32, shape, dim)


def picks(condition):
    return jnp.where(condition, 1.0, 0.0).astype(jnp.bfloat16)


def dot32(a, b):
    return jnp.dot(a, b, preferred_element_type=jnp.float32)


PIECES = 5


def copy_pieces(source, target, semaphores):
    rows = target.shape[1] // PIECES
    return [
        pltpu.make_async_copy(
            source.at[:, pl.ds(i * rows, rows), :], target.at[:, pl.ds(i * rows, rows), :], semaphores.at[i]
        )
        for i in range(PIECES)
    ]


def call(body, out_shape, name, flops, scratch=(), scalars=1, after=(), out_hbm=False):
    smem = pl.BlockSpec(memory_space=pltpu.SMEM)
    vmem = pl.BlockSpec(memory_space=pltpu.VMEM)
    hbm = pl.BlockSpec(memory_space=pltpu.HBM)

    def run(*operands):
        used = len(operands)

        def kernel(*refs):
            body(*refs[:used], *refs[used + len(after) :])

        return pl.pallas_call(
            kernel,
            out_shape=out_shape,
            in_specs=[smem] * scalars
            + [vmem] * (used - scalars)
            + [pl.BlockSpec(memory_space=pl.ANY)] * len(after),
            out_specs=jax.tree.map(lambda _: hbm if out_hbm else vmem, out_shape),
            scratch_shapes=list(scratch),
            compiler_params=pltpu.CompilerParams(vmem_limit_bytes=VMEM_BYTES),
            cost_estimate=pl.CostEstimate(flops=flops, bytes_accessed=0, transcendentals=0),
            name=name,
        )(*operands, *after)

    return run


def split_body(slots, fields, block, meta_ref, rows_ref, weight_ref, *outs):
    latitudes = weight_ref.shape[0]
    group = slots * fields
    size = block * group
    out_row, in_row = iota2((size, size), 0), iota2((size, size), 1)
    pair = out_row // block
    slot = lax.rem(meta_ref[1] + pair // fields, slots)
    field = (meta_ref[2] + pair) % fields
    order = picks(in_row == (out_row % block) * group + slot * fields + field)
    for first in range(0, latitudes, block):
        north = rows_ref[0, first * group : first * group + size, :]
        south = rows_ref[1, first * group : first * group + size, :]
        sorted_rows = dot32(order, jnp.concatenate((north, south), axis=1))
        up, down = sorted_rows[:, :128], sorted_rows[:, 128:]
        weight = weight_ref[first : first + block, :]
        for odd, mixed in enumerate((up + down, up - down)):
            for i, out_ref in enumerate(outs):
                out_ref[odd, first : first + block, :] = (weight * mixed[i * block : i * block + block]).astype(
                    jnp.bfloat16
                )


def by_parity(meta_ref, rows):
    half = rows // 2
    out_row, in_row = iota2((rows, rows), 0), iota2((rows, rows), 1)
    odd = jnp.where(out_row < half, 0, 1)
    return picks(in_row == 2 * (out_row - odd * half) + (meta_ref[0] + odd) % 2)


def near_table_body(meta_ref, own_ref, beside_ref, even_ref, odd_ref):
    rows, columns = own_ref.shape
    half = rows // 2
    order = by_parity(meta_ref, rows)
    for g, table_ref in enumerate((own_ref, beside_ref)):
        at = slice(g * half, g * half + half)
        for first in range(0, columns, 256):
            lanes = slice(first, first + 256)
            result = dot32(order, table_ref[:, lanes]).astype(jnp.bfloat16)
            even_ref[at, lanes] = result[:half]
            odd_ref[at, lanes] = result[half:]


def far_table_body(meta_ref, first_ref, second_ref, out_ref, whole):
    half, columns = first_ref.shape
    for ens, ref in ((meta_ref[4], first_ref), (1 - meta_ref[4], second_ref)):
        whole[pl.ds(pl.multiple_of(ens * half, half), half), :] = ref[...]
    order = by_parity(meta_ref, 2 * half)
    for first in range(0, columns, 256):
        lanes = slice(first, first + 256)
        out_ref[:, lanes] = dot32(order, whole[:, lanes]).astype(jnp.bfloat16)


def modes_body(sizes, degree_total, meta_ref, to_ref, from_ref, rate_ref, in_ref, out_ref, scale_ref):
    levels = to_ref.shape[0]
    wide = 2 * levels
    own = levels // 2
    lane, row = iota2((levels, wide), 1), iota2((levels, wide), 0)
    owner = lax.rem(meta_ref[2] + lane // levels, 2)
    spread = picks(row == owner * own + lane % levels // 2)
    plain = picks(row == lane % levels)
    old, new = iota2((wide, wide), 0), iota2((wide, wide), 1)

    def turned(first, matrix, last):
        half = lax.dot_general(first, matrix, (((0,), (1,)), ((), ())), preferred_element_type=jnp.float32)
        return dot32(half.astype(jnp.bfloat16), last)

    same = old % 2 == new // levels
    in_ref[...] = jnp.where(same, turned(spread, to_ref[...], plain), 0.0).astype(jnp.bfloat16)
    same = old // levels == new % 2
    out_ref[...] = jnp.where(same, turned(plain, from_ref[...], spread), 0.0).astype(jnp.bfloat16)
    wide, levs, flds = sizes
    rows = degree_total // (2 * levs * flds)
    for odd in range(2):
        for d in range(levs):
            for g in range(flds):
                block = lax.rem(meta_ref[2] + d, levs) * flds + lax.rem(meta_ref[3] + g, flds)
                degree = block * (2 * rows) + 2 * iota2((rows, 1), 0) + (meta_ref[0] + odd) % 2
                real = degree.astype(jnp.float32)
                factor = 1.0 + real * (real + 1.0) * rate_ref[...] / (degree_total * degree_total)
                at = ((d * 2 + odd) * flds + g) * rows
                scale_ref[at : at + rows, :] = jnp.where(degree >= meta_ref[0], 1.0 / factor, 0.0)


def transform(tables, data, scale_ref, in_ref, out_ref, own_ref, other_ref):
    lanes = own_ref.shape[1]
    rows = own_ref.shape[0] // 2
    for odd in range(2):
        at = slice(odd * rows, odd * rows + rows)
        raw = dot32(tables[odd], data[odd]).astype(jnp.bfloat16)
        scale = jnp.concatenate([scale_ref[at, :]] * 2, axis=1)
        modes = (dot32(raw, in_ref[...]) * scale).astype(jnp.bfloat16)
        spectral = dot32(modes, out_ref[...]).astype(jnp.bfloat16)
        own_ref[at, :] = spectral[:, :lanes]
        other_ref[at, :] = spectral[:, lanes:]


def near_body(wide, meta_ref, in_ref, out_ref, scale_ref, even_ref, odd_ref, *refs):
    parts, (own_ref, other_ref, data_ref) = refs[:-3], refs[-3:]
    latitudes, lanes = parts[0].shape[1:]
    for shift in range(wide):
        owner = lax.rem(meta_ref[1] - shift + wide, wide)
        at = pl.ds(pl.multiple_of(owner * latitudes, latitudes), latitudes)
        for d in range(2):
            data_ref[:, at, d * lanes : d * lanes + lanes] = parts[shift * 2 + d][...]
    scale = scale_ref.at[: scale_ref.shape[0] // 2]
    transform((even_ref[...], odd_ref[...]), data_ref, scale, in_ref, out_ref, own_ref, other_ref)


def far_body(in_ref, out_ref, scale_ref, first_ref, second_ref, data_ref, own_ref, other_ref):
    rows = first_ref.shape[0] // 2
    tables = [
        jnp.concatenate([ref[odd * rows : odd * rows + rows, :] for ref in (first_ref, second_ref)], axis=0)
        for odd in range(2)
    ]
    scale = scale_ref.at[scale_ref.shape[0] // 2 :]
    transform(tables, data_ref, scale, in_ref, out_ref, own_ref, other_ref)


def inverse_body(wide, meta_ref, *refs):
    parts, near, far, outs, total = refs[:4], refs[4:6], refs[6:8], refs[8:-1], refs[-1]
    latitudes, lanes = outs[0].shape[1:]
    rows = parts[0].shape[0] // 2
    spectral = [
        jnp.concatenate(
            [
                jnp.concatenate([ref[odd * rows : odd * rows + rows, :] for ref in pair], axis=1)
                for pair in (parts[:2], parts[2:])
            ],
            axis=0,
        )
        for odd in range(2)
    ]
    for first in range(0, total.shape[1], 256):
        chunk = slice(first, first + 256)
        sums = []
        for odd in range(2):
            at = slice(odd * (rows // 2), (odd + 1) * (rows // 2))
            table = jnp.concatenate([near[odd][:, chunk]] + [ref[at, chunk] for ref in far], axis=0)
            sums.append(lax.dot_general(
                table, spectral[odd], (((0,), (0,)), ((), ())), preferred_element_type=jnp.float32
            ))
        total[0, chunk, :] = (sums[0] + sums[1]).astype(jnp.bfloat16)
        total[1, chunk, :] = (sums[0] - sums[1]).astype(jnp.bfloat16)
    for shift in range(wide):
        owner = lax.rem(meta_ref[1] + shift, wide)
        at = pl.ds(pl.multiple_of(owner * latitudes, latitudes), latitudes)
        for d in range(2):
            outs[shift * 2 + d][...] = total[:, at, d * lanes : d * lanes + lanes]


def join_body(slots, block, meta_ref, *refs):
    parts, out_hbm, out_ref, semaphores = refs[:-3], *refs[-3:]
    copies = copy_pieces(out_ref, out_hbm, semaphores)
    latitudes, lanes = parts[0].shape[1:]
    fields = 2
    group = slots * fields
    size = block * group
    out_row, in_row = iota2((size, size), 0), iota2((size, size), 1)
    place = out_row % group
    shift = lax.rem(meta_ref[1] - place // fields + slots, slots)
    order = picks(in_row == (shift * fields + (place + meta_ref[2]) % fields) * block + out_row // group)
    for first in range(0, latitudes, block):
        at = slice(first, first + block)
        stacked = [jnp.concatenate([part[half, at, :] for part in parts], axis=0) for half in range(2)]
        result = dot32(order, jnp.concatenate(stacked, axis=1)).astype(jnp.bfloat16)
        for half in range(2):
            out_ref[half, first * group : first * group + size, :] = result[:, half * lanes : half * lanes + lanes]
        done = first + block
        if done * PIECES % latitudes == 0:
            copies[done * PIECES // latitudes - 1].start()
    for copy in copies:
        copy.wait()


def rows_body(sizes, block, meta_ref, *refs):
    wide, levs, flds = sizes
    own_refs, other_refs, out_ref = refs[:2], refs[2:4], refs[4]
    rows = own_refs[0].shape[0] // (2 * flds)
    fields = 2
    group = 2 * fields
    size = block * group
    out_row, in_row = iota2((size, size), 0), iota2((size, size), 1)
    place = out_row % group
    odd = (place // fields + meta_ref[0] % 2) % 2
    order = picks(in_row == (odd * fields + (place + meta_ref[2]) % fields) * block + out_row // group)
    for d in range(levs):
        for g in range(flds):
            index = lax.rem(meta_ref[2] + d, levs) * flds + lax.rem(meta_ref[3] + g, flds)
            for first in range(0, rows, block):
                stacked = jnp.concatenate(
                    [
                        ref[(odd * flds + g) * rows + first : (odd * flds + g) * rows + first + block, :]
                        for odd in range(2)
                        for ref in (own_refs[d], other_refs[1 - d])
                    ],
                    axis=0,
                )
                start = pl.multiple_of(index * (rows * group), rows * group) + first * group
                out_ref[pl.ds(start, size), :] = dot32(order, stacked).astype(jnp.bfloat16)


def shards(fourier_input_rows, legendre, slot_wave, to_modes, from_modes, mode_rate):
    wide, levs, flds = (lax.axis_size(axis) for axis in ("wide", "lev", "fld"))
    sizes = (wide, levs, flds)
    _, latitudes, slots, fields, lanes = fourier_input_rows.shape
    _, shard_rows, half_count = legendre.shape
    degree_count = shard_rows * levs * flds
    group = slots * fields
    columns = fields * lanes
    block = 256 // group
    levels = to_modes.shape[0]
    bf16 = jnp.bfloat16

    def shape(*dims):
        return jax.ShapeDtypeStruct(dims, bf16)

    def shifted(value, axis, count, step):
        return lax.ppermute(value, axis, [(i, (i + step) % count) for i in range(count)])

    def over_lev(value):
        return shifted(value, "lev", levs, 1)

    def beside(value):
        return shifted(value, "fld", flds, 1)

    def moved(value, k, d):
        pairs = [(w * levs + l, (w + k) % wide * levs + (l + d) % levs) for w in range(wide) for l in range(levs)]
        return lax.ppermute(value, ("wide", "lev"), pairs)

    def behind(value, *others):
        return lax.optimization_barrier((value, *others))

    wide_at, lev_at, fld_at = (lax.axis_index(axis) for axis in ("wide", "lev", "fld"))
    meta = jnp.stack((slot_wave[0], wide_at, lev_at, fld_at, lax.axis_index("ens"))).astype(jnp.int32)
    place = jnp.stack((jnp.zeros_like(wide_at), wide_at, lev_at, fld_at)).astype(jnp.int32)
    position = (wide_at * latitudes + jnp.arange(latitudes, dtype=jnp.int32)).astype(jnp.float32)
    weights = jnp.sin(math.pi * (position + 0.5) / (2 * half_count))
    weights = jnp.broadcast_to(weights[:, None], (latitudes, lanes))
    move_flops = 8 * group * latitudes * 128 * 256
    transform_flops = 2 * degree_count * half_count * columns

    table_beside = beside(legendre[0])
    blocks = call(
        functools.partial(split_body, slots, fields, block), (shape(2, latitudes, lanes),) * (wide * levs),
        "split_hemispheres", move_flops,
    )(place, fourier_input_rows.reshape(2, latitudes * group, lanes), weights)
    table_beside, *blocks = behind(table_beside, *blocks)
    *matrices, scale = call(
        functools.partial(modes_body, sizes, degree_count),
        (shape(2 * levels, 2 * levels),) * 2 + (jax.ShapeDtypeStruct((degree_count, levels), jnp.float32),),
        "spread_modes", 12 * levels * levels * levels, after=(blocks[0],),
    )(meta, to_modes, from_modes, mode_rate[None, :])
    near = call(
        near_table_body, (shape(shard_rows, half_count),) * 2, "split_table",
        4 * shard_rows * shard_rows * half_count, after=(scale,),
    )(meta, legendre[0], table_beside)

    def exchanged(blocks, ahead):
        arrived = {(0, 0): blocks[0]}
        for k, d in ((2, 0), (1, 0), (3, 0), (0, 1)):
            arrived[k, d] = moved(blocks[k * levs + d], k, d)
        for k, first in ((2, (0, 1)), (1, (1, 0)), (3, (3, 0))):
            value, arrived[first], *_ = behind(blocks[k * levs + 1], arrived[first], *ahead)
            arrived[k, 1] = moved(value, k, 1)
        return arrived

    def listed(arrived):
        return [arrived[k, d] for k in range(wide) for d in range(levs)]

    arrived = exchanged(blocks, (near[0], scale))
    half_shard = shard_rows // 2
    own_table, _ = behind(legendre[0], blocks[0])
    first = over_lev(lax.dynamic_slice_in_dim(own_table, lax.axis_index("ens") * half_shard, half_shard, 0))
    steps = [(1, 0), (2, 0), (3, 0), (0, 1)]
    first, *ahead = behind(first, *(arrived[step] for step in steps))
    arrived |= dict(zip(steps, ahead))
    second = shifted(first, "ens", 2, 1)
    far = call(
        far_table_body, shape(shard_rows, half_count), "split_table", 2 * shard_rows * shard_rows * half_count,
        scratch=[pltpu.VMEM((shard_rows, half_count), bf16)],
    )(meta, first, second)
    steps = [(1, 1), (2, 1), (3, 1)]
    far, *ahead = behind(far, *(arrived[step] for step in steps))
    arrived |= dict(zip(steps, ahead))
    far = [far, beside(far)]

    half_rows = degree_count // 2
    *near_spectral, data = call(
        functools.partial(near_body, wide), (shape(half_rows, lanes),) * 2 + (shape(2, half_count, columns),),
        "direct_legendre_and_solve", transform_flops // 2,
    )(meta, *matrices, scale, *near, *listed(arrived))
    far_spectral = call(
        far_body, (shape(half_rows, lanes),) * 2, "direct_legendre_and_solve", transform_flops // 2, scalars=0,
    )(*matrices, scale, *far, data)
    spectral = (near_spectral, far_spectral)
    grid = call(
        functools.partial(inverse_body, wide), (shape(2, latitudes, lanes),) * (wide * levs),
        "inverse_legendre", transform_flops, scratch=[pltpu.VMEM((2, half_count, columns), bf16)],
    )(meta, *near_spectral, *far_spectral, *near, *far)
    arrived = exchanged(grid, ())
    result = listed(arrived)
    spectral_rows = call(
        functools.partial(rows_body, sizes, 32), shape(degree_count * fields, lanes), "order_spectral", move_flops,
    )(meta, *(own for own, _ in spectral), *(over_lev(other) for _, other in spectral))
    fourier_rows = call(
        functools.partial(join_body, slots, 256 // group), shape(2, latitudes * group, lanes),
        "join_hemispheres", move_flops, out_hbm=True,
        scratch=[pltpu.VMEM((2, latitudes * group, lanes), bf16), pltpu.SemaphoreType.DMA((PIECES,))],
    )(meta, *result)
    return (
        fourier_rows.reshape(2, latitudes, slots, fields, lanes),
        spectral_rows.reshape(1, degree_count, fields, lanes),
    )


def project(level_grid, degree_real, weight_rows, rate_rows, degree_total):
    projected = jnp.einsum(
        "kl,snflr->snfkr", weight_rows, level_grid, preferred_element_type=jnp.float32
    )
    factor = 1.0 + degree_real[:, None] * (degree_real[:, None] + 1.0) * rate_rows[None, :] / (
        degree_total * degree_total
    )
    return (projected / factor[None, :, None, :, None]).astype(jnp.bfloat16)


def plain_shards(fourier_input_rows, legendre, slot_wave, to_modes, from_modes, mode_rate):
    wave_rows = lax.all_to_all(fourier_input_rows, "wide", split_axis=2, concat_axis=1, tiled=True)
    half_count = wave_rows.shape[1]
    slot_count = wave_rows.shape[2]
    field_count = wave_rows.shape[3]
    column_count = wave_rows.shape[4]
    degree_count = legendre.shape[1] * lax.axis_size(("lev", "fld"))
    weights = latitude_weights(half_count)[:, None, None, None]
    north_half = wave_rows[0].astype(jnp.float32)
    south_half = wave_rows[1].astype(jnp.float32)
    symmetric = (weights * (north_half + south_half)).astype(jnp.bfloat16)
    antisym = (weights * (north_half - south_half)).astype(jnp.bfloat16)
    paired = jnp.concatenate((symmetric, antisym), axis=3)

    def direct_rows(section, first_row):
        row_count = section.shape[1]
        degree = first_row + jnp.arange(row_count, dtype=jnp.int32)
        relative = degree[None, :] - slot_wave[:, None]
        product = jnp.einsum("snj,jsfc->snfc", section, paired, preferred_element_type=jnp.float32)
        is_even = (relative % 2 == 0)[:, :, None, None]
        is_live = (relative >= 0)[:, :, None, None]
        picked = jnp.where(is_even, product[..., :column_count], product[..., column_count:])
        return jnp.where(is_live, picked, jnp.zeros_like(picked))

    full_table = lax.all_gather(legendre, ("lev", "fld"), axis=1, tiled=True)
    block_rows = 128
    block_count = degree_count // block_rows

    def direct_step(block_index, buffer):
        first_row = block_index * block_rows
        section = lax.dynamic_slice_in_dim(full_table, first_row, block_rows, 1)
        result = direct_rows(section, first_row).astype(jnp.bfloat16)
        return lax.dynamic_update_slice_in_dim(buffer, result, first_row, 1)

    initial_raw = jnp.zeros((slot_count, degree_count, field_count, column_count), jnp.bfloat16)
    raw_spectral = lax.fori_loop(0, block_count, direct_step, initial_raw)
    own_levels = column_count // 2
    first_level = lax.axis_index("lev") * own_levels
    degree_real = jnp.arange(degree_count, dtype=jnp.float32)
    all_levels = lax.all_gather(raw_spectral, "lev", axis=3, tiled=True)
    level_count = all_levels.shape[3] // 2
    level_grid = all_levels.reshape(slot_count, degree_count, field_count, level_count, 2)
    weight_rows = lax.dynamic_slice_in_dim(to_modes, first_level, own_levels, 0)
    rate_rows = lax.dynamic_slice_in_dim(mode_rate, first_level, own_levels, 0)
    own_modes = project(level_grid, degree_real, weight_rows, rate_rows, degree_count).reshape(
        slot_count, degree_count, field_count, column_count
    )
    mode_values = lax.all_gather(own_modes, "lev", axis=3, tiled=True).reshape(
        slot_count, degree_count, field_count, level_count, 2
    )
    back_rows = lax.dynamic_slice_in_dim(from_modes, first_level, own_levels, 0)
    spectral = jnp.einsum(
        "lk,snfkr->snflr", back_rows, mode_values, preferred_element_type=jnp.float32
    )
    spectral = spectral.astype(jnp.bfloat16).reshape(
        slot_count, degree_count, field_count, column_count
    )

    def inverse_rows(running, section, first_row):
        row_count = section.shape[1]
        degree = first_row + jnp.arange(row_count, dtype=jnp.int32)
        relative = degree[None, :] - slot_wave[:, None]
        spec_rows = lax.dynamic_slice_in_dim(spectral, first_row, row_count, 1)
        even_mask = ((relative >= 0) & (relative % 2 == 0))[:, :, None, None]
        odd_mask = ((relative >= 0) & (relative % 2 == 1))[:, :, None, None]
        empty_rows = jnp.zeros_like(spec_rows)
        parity_split = jnp.concatenate(
            (
                jnp.where(even_mask, spec_rows, empty_rows),
                jnp.where(odd_mask, spec_rows, empty_rows),
            ),
            axis=3,
        )
        return running + jnp.einsum(
            "snj,snfc->jsfc", section, parity_split, preferred_element_type=jnp.float32
        )

    initial_sum = jnp.zeros((half_count, slot_count, field_count, 2 * column_count), jnp.float32)

    def inverse_step(block_index, running):
        first_row = block_index * block_rows
        section = lax.dynamic_slice_in_dim(full_table, first_row, block_rows, 1)
        return inverse_rows(running, section, first_row)

    running = lax.fori_loop(0, block_count, inverse_step, initial_sum)
    even_sum = running[..., :column_count]
    odd_sum = running[..., column_count:]
    fourier_wave = jnp.stack((even_sum + odd_sum, even_sum - odd_sum), axis=0).astype(jnp.bfloat16)
    fourier_out = lax.all_to_all(fourier_wave, "wide", split_axis=1, concat_axis=2, tiled=True)
    return (fourier_out, spectral)


def solution(mesh):
    in_specs = (
        P("ens", "wide", None, "fld", "lev"),
        P("wide", ("lev", "fld"), None),
        P("wide"),
        P(),
        P(),
        P(),
    )
    out_specs = (P("ens", "wide", None, "fld", "lev"), P(("ens", "wide"), None, "fld", "lev"))

    def body(fourier_input_rows, legendre, *rest):
        _, latitudes, slots, fields, lanes = fourier_input_rows.shape
        whole_tiles = (
            latitudes % (32 * PIECES) == 0
            and fields == 2
            and slots == mesh.shape["wide"] == 4
            and mesh.shape["ens"] == mesh.shape["lev"] == mesh.shape["fld"] == 2
            and lanes == 128
            and legendre.shape[1] % 64 == 0
            and legendre.shape[2] % 256 == 0
        )
        form = shards if whole_tiles else plain_shards
        return form(fourier_input_rows, legendre, *rest)

    return jax.shard_map(body, mesh=mesh, in_specs=in_specs, out_specs=out_specs, check_vma=False)
```

```python
import functools
import math

import jax
import jax.numpy as jnp
from jax import lax
from jax.experimental import pallas as pl
from jax.experimental.pallas import tpu as pltpu
from jax.sharding import PartitionSpec as P

VMEM_BYTES = 8 * 1024 * 1024


def latitude_weights(count):
    position = jnp.arange(count, dtype=jnp.float32)
    return jnp.sin(math.pi * (position + 0.5) / (2 * count))


def iota2(shape, dim):
    return lax.broadcasted_iota(jnp.int32, shape, dim)


def picks(condition):
    return jnp.where(condition, 1.0, 0.0).astype(jnp.bfloat16)


def dot32(a, b):
    return jnp.dot(a, b, preferred_element_type=jnp.float32)


PIECES = 5


def copy_pieces(source, target, semaphores):
    rows = target.shape[1] // PIECES
    return [
        pltpu.make_async_copy(
            source.at[:, pl.ds(i * rows, rows), :], target.at[:, pl.ds(i * rows, rows), :], semaphores.at[i]
        )
        for i in range(PIECES)
    ]


def call(body, out_shape, name, flops, scratch=(), scalars=1, after=(), out_hbm=False):
    smem = pl.BlockSpec(memory_space=pltpu.SMEM)
    vmem = pl.BlockSpec(memory_space=pltpu.VMEM)
    hbm = pl.BlockSpec(memory_space=pltpu.HBM)

    def run(*operands):
        used = len(operands)

        def kernel(*refs):
            body(*refs[:used], *refs[used + len(after) :])

        return pl.pallas_call(
            kernel,
            out_shape=out_shape,
            in_specs=[smem] * scalars
            + [vmem] * (used - scalars)
            + [pl.BlockSpec(memory_space=pl.ANY)] * len(after),
            out_specs=jax.tree.map(lambda _: hbm if out_hbm else vmem, out_shape),
            scratch_shapes=list(scratch),
            compiler_params=pltpu.CompilerParams(vmem_limit_bytes=VMEM_BYTES),
            cost_estimate=pl.CostEstimate(flops=flops, bytes_accessed=0, transcendentals=0),
            name=name,
        )(*operands, *after)

    return run


def split_body(slots, fields, block, meta_ref, rows_ref, weight_ref, *outs):
    latitudes = weight_ref.shape[0]
    group = slots * fields
    size = block * group
    out_row, in_row = iota2((size, size), 0), iota2((size, size), 1)
    pair = out_row // block
    slot = lax.rem(meta_ref[1] + pair // fields, slots)
    field = (meta_ref[2] + pair) % fields
    order = picks(in_row == (out_row % block) * group + slot * fields + field)
    for first in range(0, latitudes, block):
        north = rows_ref[0, first * group : first * group + size, :]
        south = rows_ref[1, first * group : first * group + size, :]
        sorted_rows = dot32(order, jnp.concatenate((north, south), axis=1))
        up, down = sorted_rows[:, :128], sorted_rows[:, 128:]
        weight = weight_ref[first : first + block, :]
        for odd, mixed in enumerate((up + down, up - down)):
            for i, out_ref in enumerate(outs):
                out_ref[odd, first : first + block, :] = (weight * mixed[i * block : i * block + block]).astype(
                    jnp.bfloat16
                )


def by_parity(meta_ref, rows):
    half = rows // 2
    out_row, in_row = iota2((rows, rows), 0), iota2((rows, rows), 1)
    odd = jnp.where(out_row < half, 0, 1)
    return picks(in_row == 2 * (out_row - odd * half) + (meta_ref[0] + odd) % 2)


def near_table_body(meta_ref, own_ref, beside_ref, even_ref, odd_ref):
    rows, columns = own_ref.shape
    half = rows // 2
    order = by_parity(meta_ref, rows)
    for g, table_ref in enumerate((own_ref, beside_ref)):
        at = slice(g * half, g * half + half)
        for first in range(0, columns, 256):
            lanes = slice(first, first + 256)
            result = dot32(order, table_ref[:, lanes]).astype(jnp.bfloat16)
            even_ref[at, lanes] = result[:half]
            odd_ref[at, lanes] = result[half:]


def far_table_body(meta_ref, first_ref, second_ref, out_ref, whole):
    half, columns = first_ref.shape
    for ens, ref in ((meta_ref[4], first_ref), (1 - meta_ref[4], second_ref)):
        whole[pl.ds(pl.multiple_of(ens * half, half), half), :] = ref[...]
    order = by_parity(meta_ref, 2 * half)
    for first in range(0, columns, 256):
        lanes = slice(first, first + 256)
        out_ref[:, lanes] = dot32(order, whole[:, lanes]).astype(jnp.bfloat16)


def modes_body(sizes, degree_total, meta_ref, to_ref, from_ref, rate_ref, in_ref, out_ref, scale_ref):
    levels = to_ref.shape[0]
    wide = 2 * levels
    own = levels // 2
    lane, row = iota2((levels, wide), 1), iota2((levels, wide), 0)
    owner = lax.rem(meta_ref[2] + lane // levels, 2)
    spread = picks(row == owner * own + lane % levels // 2)
    plain = picks(row == lane % levels)
    old, new = iota2((wide, wide), 0), iota2((wide, wide), 1)

    def turned(first, matrix, last):
        half = lax.dot_general(first, matrix, (((0,), (1,)), ((), ())), preferred_element_type=jnp.float32)
        return dot32(half.astype(jnp.bfloat16), last)

    same = old % 2 == new // levels
    in_ref[...] = jnp.where(same, turned(spread, to_ref[...], plain), 0.0).astype(jnp.bfloat16)
    same = old // levels == new % 2
    out_ref[...] = jnp.where(same, turned(plain, from_ref[...], spread), 0.0).astype(jnp.bfloat16)
    wide, levs, flds = sizes
    rows = degree_total // (2 * levs * flds)
    for odd in range(2):
        for d in range(levs):
            for g in range(flds):
                block = lax.rem(meta_ref[2] + d, levs) * flds + lax.rem(meta_ref[3] + g, flds)
                degree = block * (2 * rows) + 2 * iota2((rows, 1), 0) + (meta_ref[0] + odd) % 2
                real = degree.astype(jnp.float32)
                factor = 1.0 + real * (real + 1.0) * rate_ref[...] / (degree_total * degree_total)
                at = ((d * 2 + odd) * flds + g) * rows
                scale_ref[at : at + rows, :] = jnp.where(degree >= meta_ref[0], 1.0 / factor, 0.0)


def transform(tables, data, scale_ref, in_ref, out_ref, own_ref, other_ref):
    lanes = own_ref.shape[1]
    rows = own_ref.shape[0] // 2
    for odd in range(2):
        at = slice(odd * rows, odd * rows + rows)
        raw = dot32(tables[odd], data[odd]).astype(jnp.bfloat16)
        scale = jnp.concatenate([scale_ref[at, :]] * 2, axis=1)
        modes = (dot32(raw, in_ref[...]) * scale).astype(jnp.bfloat16)
        spectral = dot32(modes, out_ref[...]).astype(jnp.bfloat16)
        own_ref[at, :] = spectral[:, :lanes]
        other_ref[at, :] = spectral[:, lanes:]


def near_body(wide, meta_ref, in_ref, out_ref, scale_ref, even_ref, odd_ref, *refs):
    parts, (own_ref, other_ref, data_ref) = refs[:-3], refs[-3:]
    latitudes, lanes = parts[0].shape[1:]
    for shift in range(wide):
        owner = lax.rem(meta_ref[1] - shift + wide, wide)
        at = pl.ds(pl.multiple_of(owner * latitudes, latitudes), latitudes)
        for d in range(2):
            data_ref[:, at, d * lanes : d * lanes + lanes] = parts[shift * 2 + d][...]
    scale = scale_ref.at[: scale_ref.shape[0] // 2]
    transform((even_ref[...], odd_ref[...]), data_ref, scale, in_ref, out_ref, own_ref, other_ref)


def far_body(in_ref, out_ref, scale_ref, first_ref, second_ref, data_ref, own_ref, other_ref):
    rows = first_ref.shape[0] // 2
    tables = [
        jnp.concatenate([ref[odd * rows : odd * rows + rows, :] for ref in (first_ref, second_ref)], axis=0)
        for odd in range(2)
    ]
    scale = scale_ref.at[scale_ref.shape[0] // 2 :]
    transform(tables, data_ref, scale, in_ref, out_ref, own_ref, other_ref)


def inverse_body(wide, meta_ref, *refs):
    parts, near, far, outs, total = refs[:4], refs[4:6], refs[6:8], refs[8:-1], refs[-1]
    latitudes, lanes = outs[0].shape[1:]
    rows = parts[0].shape[0] // 2
    spectral = [
        jnp.concatenate(
            [
                jnp.concatenate([ref[odd * rows : odd * rows + rows, :] for ref in pair], axis=1)
                for pair in (parts[:2], parts[2:])
            ],
            axis=0,
        )
        for odd in range(2)
    ]
    for first in range(0, total.shape[1], 256):
        chunk = slice(first, first + 256)
        sums = []
        for odd in range(2):
            at = slice(odd * (rows // 2), (odd + 1) * (rows // 2))
            table = jnp.concatenate([near[odd][:, chunk]] + [ref[at, chunk] for ref in far], axis=0)
            sums.append(lax.dot_general(
                table, spectral[odd], (((0,), (0,)), ((), ())), preferred_element_type=jnp.float32
            ))
        total[0, chunk, :] = (sums[0] + sums[1]).astype(jnp.bfloat16)
        total[1, chunk, :] = (sums[0] - sums[1]).astype(jnp.bfloat16)
    for shift in range(wide):
        owner = lax.rem(meta_ref[1] + shift, wide)
        at = pl.ds(pl.multiple_of(owner * latitudes, latitudes), latitudes)
        for d in range(2):
            outs[shift * 2 + d][...] = total[:, at, d * lanes : d * lanes + lanes]


def join_body(slots, block, meta_ref, *refs):
    parts, out_hbm, out_ref, semaphores = refs[:-3], *refs[-3:]
    copies = copy_pieces(out_ref, out_hbm, semaphores)
    latitudes, lanes = parts[0].shape[1:]
    fields = 2
    group = slots * fields
    size = block * group
    out_row, in_row = iota2((size, size), 0), iota2((size, size), 1)
    place = out_row % group
    shift = lax.rem(meta_ref[1] - place // fields + slots, slots)
    order = picks(in_row == (shift * fields + (place + meta_ref[2]) % fields) * block + out_row // group)
    for first in range(0, latitudes, block):
        at = slice(first, first + block)
        stacked = [jnp.concatenate([part[half, at, :] for part in parts], axis=0) for half in range(2)]
        result = dot32(order, jnp.concatenate(stacked, axis=1)).astype(jnp.bfloat16)
        for half in range(2):
            out_ref[half, first * group : first * group + size, :] = result[:, half * lanes : half * lanes + lanes]
        done = first + block
        if done * PIECES % latitudes == 0:
            copies[done * PIECES // latitudes - 1].start()
    for copy in copies:
        copy.wait()


def rows_body(sizes, block, meta_ref, *refs):
    wide, levs, flds = sizes
    own_refs, other_refs, out_ref = refs[:2], refs[2:4], refs[4]
    rows = own_refs[0].shape[0] // (2 * flds)
    fields = 2
    group = 2 * fields
    size = block * group
    out_row, in_row = iota2((size, size), 0), iota2((size, size), 1)
    place = out_row % group
    odd = (place // fields + meta_ref[0] % 2) % 2
    order = picks(in_row == (odd * fields + (place + meta_ref[2]) % fields) * block + out_row // group)
    for d in range(levs):
        for g in range(flds):
            index = lax.rem(meta_ref[2] + d, levs) * flds + lax.rem(meta_ref[3] + g, flds)
            for first in range(0, rows, block):
                stacked = jnp.concatenate(
                    [
                        ref[(odd * flds + g) * rows + first : (odd * flds + g) * rows + first + block, :]
                        for odd in range(2)
                        for ref in (own_refs[d], other_refs[1 - d])
                    ],
                    axis=0,
                )
                start = pl.multiple_of(index * (rows * group), rows * group) + first * group
                out_ref[pl.ds(start, size), :] = dot32(order, stacked).astype(jnp.bfloat16)


def shards(fourier_input_rows, legendre, slot_wave, to_modes, from_modes, mode_rate):
    wide, levs, flds = (lax.axis_size(axis) for axis in ("wide", "lev", "fld"))
    sizes = (wide, levs, flds)
    _, latitudes, slots, fields, lanes = fourier_input_rows.shape
    _, shard_rows, half_count = legendre.shape
    degree_count = shard_rows * levs * flds
    group = slots * fields
    columns = fields * lanes
    block = 256 // group
    levels = to_modes.shape[0]
    bf16 = jnp.bfloat16

    def shape(*dims):
        return jax.ShapeDtypeStruct(dims, bf16)

    def shifted(value, axis, count, step):
        return lax.ppermute(value, axis, [(i, (i + step) % count) for i in range(count)])

    def over_lev(value):
        return shifted(value, "lev", levs, 1)

    def beside(value):
        return shifted(value, "fld", flds, 1)

    def moved(value, k, d):
        pairs = [(w * levs + l, (w + k) % wide * levs + (l + d) % levs) for w in range(wide) for l in range(levs)]
        return lax.ppermute(value, ("wide", "lev"), pairs)

    def behind(value, *others):
        return lax.optimization_barrier((value, *others))

    wide_at, lev_at, fld_at = (lax.axis_index(axis) for axis in ("wide", "lev", "fld"))
    meta = jnp.stack((slot_wave[0], wide_at, lev_at, fld_at, lax.axis_index("ens"))).astype(jnp.int32)
    position = (wide_at * latitudes + jnp.arange(latitudes, dtype=jnp.int32)).astype(jnp.float32)
    weights = jnp.sin(math.pi * (position + 0.5) / (2 * half_count))
    weights = jnp.broadcast_to(weights[:, None], (latitudes, lanes))
    move_flops = 8 * group * latitudes * 128 * 256
    transform_flops = 2 * degree_count * half_count * columns

    table_beside = beside(legendre[0])
    blocks = call(
        functools.partial(split_body, slots, fields, block), (shape(2, latitudes, lanes),) * (wide * levs),
        "split_hemispheres", move_flops,
    )(meta, fourier_input_rows.reshape(2, latitudes * group, lanes), weights)
    table_beside, *blocks = behind(table_beside, *blocks)
    *matrices, scale = call(
        functools.partial(modes_body, sizes, degree_count),
        (shape(2 * levels, 2 * levels),) * 2 + (jax.ShapeDtypeStruct((degree_count, levels), jnp.float32),),
        "spread_modes", 12 * levels * levels * levels, after=(blocks[0],),
    )(meta, to_modes, from_modes, mode_rate[None, :])
    near = call(
        near_table_body, (shape(shard_rows, half_count),) * 2, "split_table",
        4 * shard_rows * shard_rows * half_count, after=(scale,),
    )(meta, legendre[0], table_beside)

    def exchanged(blocks, ahead):
        arrived = {(0, 0): blocks[0]}
        for k, d in ((2, 0), (1, 0), (3, 0), (0, 1)):
            arrived[k, d] = moved(blocks[k * levs + d], k, d)
        for k, first in ((2, (0, 1)), (1, (1, 0)), (3, (3, 0))):
            value, arrived[first], *_ = behind(blocks[k * levs + 1], arrived[first], *ahead)
            arrived[k, 1] = moved(value, k, 1)
        return arrived

    def listed(arrived):
        return [arrived[k, d] for k in range(wide) for d in range(levs)]

    arrived = exchanged(blocks, (near[0], scale))
    half_shard = shard_rows // 2
    own_table, _ = behind(legendre[0], blocks[0])
    first = over_lev(lax.dynamic_slice_in_dim(own_table, lax.axis_index("ens") * half_shard, half_shard, 0))
    steps = [(1, 0), (2, 0), (3, 0), (0, 1)]
    first, *ahead = behind(first, *(arrived[step] for step in steps))
    arrived |= dict(zip(steps, ahead))
    second = shifted(first, "ens", 2, 1)
    far = call(
        far_table_body, shape(shard_rows, half_count), "split_table", 2 * shard_rows * shard_rows * half_count,
        scratch=[pltpu.VMEM((shard_rows, half_count), bf16)],
    )(meta, first, second)
    steps = [(1, 1), (2, 1), (3, 1)]
    far, *ahead = behind(far, *(arrived[step] for step in steps))
    arrived |= dict(zip(steps, ahead))
    far = [far, beside(far)]

    half_rows = degree_count // 2
    *near_spectral, data = call(
        functools.partial(near_body, wide), (shape(half_rows, lanes),) * 2 + (shape(2, half_count, columns),),
        "direct_legendre_and_solve", transform_flops // 2,
    )(meta, *matrices, scale, *near, *listed(arrived))
    far_spectral = call(
        far_body, (shape(half_rows, lanes),) * 2, "direct_legendre_and_solve", transform_flops // 2, scalars=0,
    )(*matrices, scale, *far, data)
    spectral = (near_spectral, far_spectral)
    grid = call(
        functools.partial(inverse_body, wide), (shape(2, latitudes, lanes),) * (wide * levs),
        "inverse_legendre", transform_flops, scratch=[pltpu.VMEM((2, half_count, columns), bf16)],
    )(meta, *near_spectral, *far_spectral, *near, *far)
    arrived = exchanged(grid, ())
    result = listed(arrived)
    spectral_rows = call(
        functools.partial(rows_body, sizes, 32), shape(degree_count * fields, lanes), "order_spectral", move_flops,
    )(meta, *(own for own, _ in spectral), *(over_lev(other) for _, other in spectral))
    fourier_rows = call(
        functools.partial(join_body, slots, 256 // group), shape(2, latitudes * group, lanes),
        "join_hemispheres", move_flops, out_hbm=True,
        scratch=[pltpu.VMEM((2, latitudes * group, lanes), bf16), pltpu.SemaphoreType.DMA((PIECES,))],
    )(meta, *result)
    return (
        fourier_rows.reshape(2, latitudes, slots, fields, lanes),
        spectral_rows.reshape(1, degree_count, fields, lanes),
    )


def project(level_grid, degree_real, weight_rows, rate_rows, degree_total):
    projected = jnp.einsum(
        "kl,snflr->snfkr", weight_rows, level_grid, preferred_element_type=jnp.float32
    )
    factor = 1.0 + degree_real[:, None] * (degree_real[:, None] + 1.0) * rate_rows[None, :] / (
        degree_total * degree_total
    )
    return (projected / factor[None, :, None, :, None]).astype(jnp.bfloat16)


def plain_shards(fourier_input_rows, legendre, slot_wave, to_modes, from_modes, mode_rate):
    wave_rows = lax.all_to_all(fourier_input_rows, "wide", split_axis=2, concat_axis=1, tiled=True)
    half_count = wave_rows.shape[1]
    slot_count = wave_rows.shape[2]
    field_count = wave_rows.shape[3]
    column_count = wave_rows.shape[4]
    degree_count = legendre.shape[1] * lax.axis_size(("lev", "fld"))
    weights = latitude_weights(half_count)[:, None, None, None]
    north_half = wave_rows[0].astype(jnp.float32)
    south_half = wave_rows[1].astype(jnp.float32)
    symmetric = (weights * (north_half + south_half)).astype(jnp.bfloat16)
    antisym = (weights * (north_half - south_half)).astype(jnp.bfloat16)
    paired = jnp.concatenate((symmetric, antisym), axis=3)

    def direct_rows(section, first_row):
        row_count = section.shape[1]
        degree = first_row + jnp.arange(row_count, dtype=jnp.int32)
        relative = degree[None, :] - slot_wave[:, None]
        product = jnp.einsum("snj,jsfc->snfc", section, paired, preferred_element_type=jnp.float32)
        is_even = (relative % 2 == 0)[:, :, None, None]
        is_live = (relative >= 0)[:, :, None, None]
        picked = jnp.where(is_even, product[..., :column_count], product[..., column_count:])
        return jnp.where(is_live, picked, jnp.zeros_like(picked))

    full_table = lax.all_gather(legendre, ("lev", "fld"), axis=1, tiled=True)
    block_rows = 128
    block_count = degree_count // block_rows

    def direct_step(block_index, buffer):
        first_row = block_index * block_rows
        section = lax.dynamic_slice_in_dim(full_table, first_row, block_rows, 1)
        result = direct_rows(section, first_row).astype(jnp.bfloat16)
        return lax.dynamic_update_slice_in_dim(buffer, result, first_row, 1)

    initial_raw = jnp.zeros((slot_count, degree_count, field_count, column_count), jnp.bfloat16)
    raw_spectral = lax.fori_loop(0, block_count, direct_step, initial_raw)
    own_levels = column_count // 2
    first_level = lax.axis_index("lev") * own_levels
    degree_real = jnp.arange(degree_count, dtype=jnp.float32)
    all_levels = lax.all_gather(raw_spectral, "lev", axis=3, tiled=True)
    level_count = all_levels.shape[3] // 2
    level_grid = all_levels.reshape(slot_count, degree_count, field_count, level_count, 2)
    weight_rows = lax.dynamic_slice_in_dim(to_modes, first_level, own_levels, 0)
    rate_rows = lax.dynamic_slice_in_dim(mode_rate, first_level, own_levels, 0)
    own_modes = project(level_grid, degree_real, weight_rows, rate_rows, degree_count).reshape(
        slot_count, degree_count, field_count, column_count
    )
    mode_values = lax.all_gather(own_modes, "lev", axis=3, tiled=True).reshape(
        slot_count, degree_count, field_count, level_count, 2
    )
    back_rows = lax.dynamic_slice_in_dim(from_modes, first_level, own_levels, 0)
    spectral = jnp.einsum(
        "lk,snfkr->snflr", back_rows, mode_values, preferred_element_type=jnp.float32
    )
    spectral = spectral.astype(jnp.bfloat16).reshape(
        slot_count, degree_count, field_count, column_count
    )

    def inverse_rows(running, section, first_row):
        row_count = section.shape[1]
        degree = first_row + jnp.arange(row_count, dtype=jnp.int32)
        relative = degree[None, :] - slot_wave[:, None]
        spec_rows = lax.dynamic_slice_in_dim(spectral, first_row, row_count, 1)
        even_mask = ((relative >= 0) & (relative % 2 == 0))[:, :, None, None]
        odd_mask = ((relative >= 0) & (relative % 2 == 1))[:, :, None, None]
        empty_rows = jnp.zeros_like(spec_rows)
        parity_split = jnp.concatenate(
            (
                jnp.where(even_mask, spec_rows, empty_rows),
                jnp.where(odd_mask, spec_rows, empty_rows),
            ),
            axis=3,
        )
        return running + jnp.einsum(
            "snj,snfc->jsfc", section, parity_split, preferred_element_type=jnp.float32
        )

    initial_sum = jnp.zeros((half_count, slot_count, field_count, 2 * column_count), jnp.float32)

    def inverse_step(block_index, running):
        first_row = block_index * block_rows
        section = lax.dynamic_slice_in_dim(full_table, first_row, block_rows, 1)
        return inverse_rows(running, section, first_row)

    running = lax.fori_loop(0, block_count, inverse_step, initial_sum)
    even_sum = running[..., :column_count]
    odd_sum = running[..., column_count:]
    fourier_wave = jnp.stack((even_sum + odd_sum, even_sum - odd_sum), axis=0).astype(jnp.bfloat16)
    fourier_out = lax.all_to_all(fourier_wave, "wide", split_axis=1, concat_axis=2, tiled=True)
    return (fourier_out, spectral)


def solution(mesh):
    in_specs = (
        P("ens", "wide", None, "fld", "lev"),
        P("wide", ("lev", "fld"), None),
        P("wide"),
        P(),
        P(),
        P(),
    )
    out_specs = (P("ens", "wide", None, "fld", "lev"), P(("ens", "wide"), None, "fld", "lev"))

    def body(fourier_input_rows, legendre, *rest):
        _, latitudes, slots, fields, lanes = fourier_input_rows.shape
        whole_tiles = (
            latitudes % (32 * PIECES) == 0
            and fields == 2
            and slots == mesh.shape["wide"] == 4
            and mesh.shape["ens"] == mesh.shape["lev"] == mesh.shape["fld"] == 2
            and lanes == 128
            and legendre.shape[1] % 64 == 0
            and legendre.shape[2] % 256 == 0
        )
        form = shards if whole_tiles else plain_shards
        return form(fourier_input_rows, legendre, *rest)

    return jax.shard_map(body, mesh=mesh, in_specs=in_specs, out_specs=out_specs, check_vma=False)
```

```python
import functools
import math

import jax
import jax.numpy as jnp
from jax import lax
from jax.experimental import pallas as pl
from jax.experimental.pallas import tpu as pltpu
from jax.sharding import PartitionSpec as P

VMEM_BYTES = 8 * 1024 * 1024


def latitude_weights(count):
    position = jnp.arange(count, dtype=jnp.float32)
    return jnp.sin(math.pi * (position + 0.5) / (2 * count))


def iota2(shape, dim):
    return lax.broadcasted_iota(jnp.int32, shape, dim)


def picks(condition):
    return jnp.where(condition, 1.0, 0.0).astype(jnp.bfloat16)


def dot32(a, b):
    return jnp.dot(a, b, preferred_element_type=jnp.float32)


PIECES = 5


def copy_pieces(source, target, semaphores):
    rows = target.shape[1] // PIECES
    return [
        pltpu.make_async_copy(
            source.at[:, pl.ds(i * rows, rows), :], target.at[:, pl.ds(i * rows, rows), :], semaphores.at[i]
        )
        for i in range(PIECES)
    ]


def call(body, out_shape, name, flops, scratch=(), scalars=1, after=(), out_hbm=False):
    smem = pl.BlockSpec(memory_space=pltpu.SMEM)
    vmem = pl.BlockSpec(memory_space=pltpu.VMEM)
    hbm = pl.BlockSpec(memory_space=pltpu.HBM)

    def run(*operands):
        used = len(operands)

        def kernel(*refs):
            body(*refs[:used], *refs[used + len(after) :])

        return pl.pallas_call(
            kernel,
            out_shape=out_shape,
            in_specs=[smem] * scalars
            + [vmem] * (used - scalars)
            + [pl.BlockSpec(memory_space=pl.ANY)] * len(after),
            out_specs=jax.tree.map(lambda _: hbm if out_hbm else vmem, out_shape),
            scratch_shapes=list(scratch),
            compiler_params=pltpu.CompilerParams(vmem_limit_bytes=VMEM_BYTES),
            cost_estimate=pl.CostEstimate(flops=flops, bytes_accessed=0, transcendentals=0),
            name=name,
        )(*operands, *after)

    return run


def split_body(slots, fields, block, meta_ref, rows_ref, weight_ref, *outs):
    latitudes = weight_ref.shape[0]
    group = slots * fields
    size = block * group
    out_row, in_row = iota2((size, size), 0), iota2((size, size), 1)
    pair = out_row // block
    slot = lax.rem(meta_ref[1] + pair // fields, slots)
    field = (meta_ref[2] + pair) % fields
    order = picks(in_row == (out_row % block) * group + slot * fields + field)
    for first in range(0, latitudes, block):
        north = rows_ref[0, first * group : first * group + size, :]
        south = rows_ref[1, first * group : first * group + size, :]
        sorted_rows = dot32(order, jnp.concatenate((north, south), axis=1))
        up, down = sorted_rows[:, :128], sorted_rows[:, 128:]
        weight = weight_ref[first : first + block, :]
        for odd, mixed in enumerate((up + down, up - down)):
            for i, out_ref in enumerate(outs):
                out_ref[odd, first : first + block, :] = (weight * mixed[i * block : i * block + block]).astype(
                    jnp.bfloat16
                )


def by_parity(meta_ref, rows):
    half = rows // 2
    out_row, in_row = iota2((rows, rows), 0), iota2((rows, rows), 1)
    odd = jnp.where(out_row < half, 0, 1)
    return picks(in_row == 2 * (out_row - odd * half) + (meta_ref[0] + odd) % 2)


def near_table_body(meta_ref, own_ref, beside_ref, even_ref, odd_ref):
    rows, columns = own_ref.shape
    half = rows // 2
    order = by_parity(meta_ref, rows)
    for g, table_ref in enumerate((own_ref, beside_ref)):
        at = slice(g * half, g * half + half)
        for first in range(0, columns, 256):
            lanes = slice(first, first + 256)
            result = dot32(order, table_ref[:, lanes]).astype(jnp.bfloat16)
            even_ref[at, lanes] = result[:half]
            odd_ref[at, lanes] = result[half:]


def far_table_body(meta_ref, first_ref, second_ref, out_ref, whole):
    half, columns = first_ref.shape
    for ens, ref in ((meta_ref[4], first_ref), (1 - meta_ref[4], second_ref)):
        whole[pl.ds(pl.multiple_of(ens * half, half), half), :] = ref[...]
    order = by_parity(meta_ref, 2 * half)
    for first in range(0, columns, 256):
        lanes = slice(first, first + 256)
        out_ref[:, lanes] = dot32(order, whole[:, lanes]).astype(jnp.bfloat16)


def modes_body(sizes, degree_total, meta_ref, to_ref, from_ref, rate_ref, in_ref, out_ref, scale_ref):
    levels = to_ref.shape[0]
    wide = 2 * levels
    own = levels // 2
    lane, row = iota2((levels, wide), 1), iota2((levels, wide), 0)
    owner = lax.rem(meta_ref[2] + lane // levels, 2)
    spread = picks(row == owner * own + lane % levels // 2)
    plain = picks(row == lane % levels)
    old, new = iota2((wide, wide), 0), iota2((wide, wide), 1)

    def turned(first, matrix, last):
        half = lax.dot_general(first, matrix, (((0,), (1,)), ((), ())), preferred_element_type=jnp.float32)
        return dot32(half.astype(jnp.bfloat16), last)

    same = old % 2 == new // levels
    in_ref[...] = jnp.where(same, turned(spread, to_ref[...], plain), 0.0).astype(jnp.bfloat16)
    same = old // levels == new % 2
    out_ref[...] = jnp.where(same, turned(plain, from_ref[...], spread), 0.0).astype(jnp.bfloat16)
    wide, levs, flds = sizes
    rows = degree_total // (2 * levs * flds)
    for odd in range(2):
        for d in range(levs):
            for g in range(flds):
                block = lax.rem(meta_ref[2] + d, levs) * flds + lax.rem(meta_ref[3] + g, flds)
                degree = block * (2 * rows) + 2 * iota2((rows, 1), 0) + (meta_ref[0] + odd) % 2
                real = degree.astype(jnp.float32)
                factor = 1.0 + real * (real + 1.0) * rate_ref[...] / (degree_total * degree_total)
                at = ((d * 2 + odd) * flds + g) * rows
                scale_ref[at : at + rows, :] = jnp.where(degree >= meta_ref[0], 1.0 / factor, 0.0)


def transform(tables, data, scale_ref, in_ref, out_ref, own_ref, other_ref):
    lanes = own_ref.shape[1]
    rows = own_ref.shape[0] // 2
    for odd in range(2):
        at = slice(odd * rows, odd * rows + rows)
        raw = dot32(tables[odd], data[odd]).astype(jnp.bfloat16)
        scale = jnp.concatenate([scale_ref[at, :]] * 2, axis=1)
        modes = (dot32(raw, in_ref[...]) * scale).astype(jnp.bfloat16)
        spectral = dot32(modes, out_ref[...]).astype(jnp.bfloat16)
        own_ref[at, :] = spectral[:, :lanes]
        other_ref[at, :] = spectral[:, lanes:]


def near_body(wide, meta_ref, in_ref, out_ref, scale_ref, even_ref, odd_ref, *refs):
    parts, (own_ref, other_ref, data_ref) = refs[:-3], refs[-3:]
    latitudes, lanes = parts[0].shape[1:]
    for shift in range(wide):
        owner = lax.rem(meta_ref[1] - shift + wide, wide)
        at = pl.ds(pl.multiple_of(owner * latitudes, latitudes), latitudes)
        for d in range(2):
            data_ref[:, at, d * lanes : d * lanes + lanes] = parts[shift * 2 + d][...]
    scale = scale_ref.at[: scale_ref.shape[0] // 2]
    transform((even_ref[...], odd_ref[...]), data_ref, scale, in_ref, out_ref, own_ref, other_ref)


def far_body(in_ref, out_ref, scale_ref, first_ref, second_ref, data_ref, own_ref, other_ref):
    rows = first_ref.shape[0] // 2
    tables = [
        jnp.concatenate([ref[odd * rows : odd * rows + rows, :] for ref in (first_ref, second_ref)], axis=0)
        for odd in range(2)
    ]
    scale = scale_ref.at[scale_ref.shape[0] // 2 :]
    transform(tables, data_ref, scale, in_ref, out_ref, own_ref, other_ref)


def inverse_body(wide, meta_ref, *refs):
    parts, near, far, outs, total = refs[:4], refs[4:6], refs[6:8], refs[8:-1], refs[-1]
    latitudes, lanes = outs[0].shape[1:]
    rows = parts[0].shape[0] // 2
    spectral = [
        jnp.concatenate(
            [
                jnp.concatenate([ref[odd * rows : odd * rows + rows, :] for ref in pair], axis=1)
                for pair in (parts[:2], parts[2:])
            ],
            axis=0,
        )
        for odd in range(2)
    ]
    for first in range(0, total.shape[1], 256):
        chunk = slice(first, first + 256)
        sums = []
        for odd in range(2):
            at = slice(odd * (rows // 2), (odd + 1) * (rows // 2))
            table = jnp.concatenate([near[odd][:, chunk]] + [ref[at, chunk] for ref in far], axis=0)
            sums.append(lax.dot_general(
                table, spectral[odd], (((0,), (0,)), ((), ())), preferred_element_type=jnp.float32
            ))
        total[0, chunk, :] = (sums[0] + sums[1]).astype(jnp.bfloat16)
        total[1, chunk, :] = (sums[0] - sums[1]).astype(jnp.bfloat16)
    for shift in range(wide):
        owner = lax.rem(meta_ref[1] + shift, wide)
        at = pl.ds(pl.multiple_of(owner * latitudes, latitudes), latitudes)
        for d in range(2):
            outs[shift * 2 + d][...] = total[:, at, d * lanes : d * lanes + lanes]


def join_body(slots, block, meta_ref, *refs):
    parts, out_hbm, out_ref, semaphores = refs[:-3], *refs[-3:]
    copies = copy_pieces(out_ref, out_hbm, semaphores)
    latitudes, lanes = parts[0].shape[1:]
    fields = 2
    group = slots * fields
    size = block * group
    out_row, in_row = iota2((size, size), 0), iota2((size, size), 1)
    place = out_row % group
    shift = lax.rem(meta_ref[1] - place // fields + slots, slots)
    order = picks(in_row == (shift * fields + (place + meta_ref[2]) % fields) * block + out_row // group)
    for first in range(0, latitudes, block):
        at = slice(first, first + block)
        stacked = [jnp.concatenate([part[half, at, :] for part in parts], axis=0) for half in range(2)]
        result = dot32(order, jnp.concatenate(stacked, axis=1)).astype(jnp.bfloat16)
        for half in range(2):
            out_ref[half, first * group : first * group + size, :] = result[:, half * lanes : half * lanes + lanes]
        done = first + block
        if done * PIECES % latitudes == 0:
            copies[done * PIECES // latitudes - 1].start()
    for copy in copies:
        copy.wait()


def rows_body(sizes, block, meta_ref, *refs):
    wide, levs, flds = sizes
    own_refs, other_refs, out_ref = refs[:2], refs[2:4], refs[4]
    rows = own_refs[0].shape[0] // (2 * flds)
    fields = 2
    group = 2 * fields
    size = block * group
    out_row, in_row = iota2((size, size), 0), iota2((size, size), 1)
    place = out_row % group
    odd = (place // fields + meta_ref[0] % 2) % 2
    order = picks(in_row == (odd * fields + (place + meta_ref[2]) % fields) * block + out_row // group)
    for d in range(levs):
        for g in range(flds):
            index = lax.rem(meta_ref[2] + d, levs) * flds + lax.rem(meta_ref[3] + g, flds)
            for first in range(0, rows, block):
                stacked = jnp.concatenate(
                    [
                        ref[(odd * flds + g) * rows + first : (odd * flds + g) * rows + first + block, :]
                        for odd in range(2)
                        for ref in (own_refs[d], other_refs[1 - d])
                    ],
                    axis=0,
                )
                start = pl.multiple_of(index * (rows * group), rows * group) + first * group
                out_ref[pl.ds(start, size), :] = dot32(order, stacked).astype(jnp.bfloat16)


def shards(fourier_input_rows, legendre, slot_wave, to_modes, from_modes, mode_rate):
    wide, levs, flds = (lax.axis_size(axis) for axis in ("wide", "lev", "fld"))
    sizes = (wide, levs, flds)
    _, latitudes, slots, fields, lanes = fourier_input_rows.shape
    _, shard_rows, half_count = legendre.shape
    degree_count = shard_rows * levs * flds
    group = slots * fields
    columns = fields * lanes
    block = 256 // group
    levels = to_modes.shape[0]
    bf16 = jnp.bfloat16

    def shape(*dims):
        return jax.ShapeDtypeStruct(dims, bf16)

    def shifted(value, axis, count, step):
        return lax.ppermute(value, axis, [(i, (i + step) % count) for i in range(count)])

    def over_lev(value):
        return shifted(value, "lev", levs, 1)

    def beside(value):
        return shifted(value, "fld", flds, 1)

    def moved(value, k, d):
        pairs = [(w * levs + l, (w + k) % wide * levs + (l + d) % levs) for w in range(wide) for l in range(levs)]
        return lax.ppermute(value, ("wide", "lev"), pairs)

    def behind(value, *others):
        return lax.optimization_barrier((value, *others))

    wide_at, lev_at, fld_at = (lax.axis_index(axis) for axis in ("wide", "lev", "fld"))
    meta = jnp.stack((slot_wave[0], wide_at, lev_at, fld_at, lax.axis_index("ens"))).astype(jnp.int32)
    position = (wide_at * latitudes + jnp.arange(latitudes, dtype=jnp.int32)).astype(jnp.float32)
    weights = jnp.sin(math.pi * (position + 0.5) / (2 * half_count))
    weights = jnp.broadcast_to(weights[:, None], (latitudes, lanes))
    move_flops = 8 * group * latitudes * 128 * 256
    transform_flops = 2 * degree_count * half_count * columns

    blocks = call(
        functools.partial(split_body, slots, fields, block), (shape(2, latitudes, lanes),) * (wide * levs),
        "split_hemispheres", move_flops,
    )(meta, fourier_input_rows.reshape(2, latitudes * group, lanes), weights)
    *matrices, scale = call(
        functools.partial(modes_body, sizes, degree_count),
        (shape(2 * levels, 2 * levels),) * 2 + (jax.ShapeDtypeStruct((degree_count, levels), jnp.float32),),
        "spread_modes", 12 * levels * levels * levels, after=(blocks[0],),
    )(meta, to_modes, from_modes, mode_rate[None, :])
    def exchanged(blocks, ahead):
        arrived = {(0, 0): blocks[0]}
        for k, d in ((2, 0), (1, 0), (3, 0), (0, 1)):
            arrived[k, d] = moved(blocks[k * levs + d], k, d)
        for k, first in ((2, (0, 1)), (1, (1, 0)), (3, (3, 0))):
            value, arrived[first], *_ = behind(blocks[k * levs + 1], arrived[first], *ahead)
            arrived[k, 1] = moved(value, k, 1)
        return arrived

    def listed(arrived):
        return [arrived[k, d] for k in range(wide) for d in range(levs)]

    arrived = exchanged(blocks, (scale,))
    half_shard = shard_rows // 2
    own_table, _ = behind(legendre[0], blocks[0])
    first = over_lev(lax.dynamic_slice_in_dim(own_table, lax.axis_index("ens") * half_shard, half_shard, 0))
    steps = [(1, 0), (2, 0), (3, 0), (0, 1)]
    first, *ahead = behind(first, *(arrived[step] for step in steps))
    arrived |= dict(zip(steps, ahead))
    second = shifted(first, "ens", 2, 1)
    own_table, second = behind(legendre[0], second)
    near = call(
        near_table_body, (shape(shard_rows, half_count),) * 2, "split_table",
        4 * shard_rows * shard_rows * half_count, after=(scale,),
    )(meta, legendre[0], beside(own_table))
    near = list(near)

    far = call(
        far_table_body, shape(shard_rows, half_count), "split_table", 2 * shard_rows * shard_rows * half_count,
        scratch=[pltpu.VMEM((shard_rows, half_count), bf16)],
    )(meta, first, second)
    steps = [(1, 1), (2, 1), (3, 1)]
    far, near[0], near[1], *ahead = behind(far, *near, *(arrived[step] for step in steps))
    arrived |= dict(zip(steps, ahead))
    far = [far, beside(far)]

    half_rows = degree_count // 2
    *near_spectral, data = call(
        functools.partial(near_body, wide), (shape(half_rows, lanes),) * 2 + (shape(2, half_count, columns),),
        "direct_legendre_and_solve", transform_flops // 2,
    )(meta, *matrices, scale, *near, *listed(arrived))
    far_spectral = call(
        far_body, (shape(half_rows, lanes),) * 2, "direct_legendre_and_solve", transform_flops // 2, scalars=0,
    )(*matrices, scale, *far, data)
    spectral = (near_spectral, far_spectral)
    grid = call(
        functools.partial(inverse_body, wide), (shape(2, latitudes, lanes),) * (wide * levs),
        "inverse_legendre", transform_flops, scratch=[pltpu.VMEM((2, half_count, columns), bf16)],
    )(meta, *near_spectral, *far_spectral, *near, *far)
    arrived = exchanged(grid, ())
    result = listed(arrived)
    spectral_rows = call(
        functools.partial(rows_body, sizes, 32), shape(degree_count * fields, lanes), "order_spectral", move_flops,
    )(meta, *(own for own, _ in spectral), *(over_lev(other) for _, other in spectral))
    fourier_rows = call(
        functools.partial(join_body, slots, 256 // group), shape(2, latitudes * group, lanes),
        "join_hemispheres", move_flops, out_hbm=True,
        scratch=[pltpu.VMEM((2, latitudes * group, lanes), bf16), pltpu.SemaphoreType.DMA((PIECES,))],
    )(meta, *result)
    return (
        fourier_rows.reshape(2, latitudes, slots, fields, lanes),
        spectral_rows.reshape(1, degree_count, fields, lanes),
    )


def project(level_grid, degree_real, weight_rows, rate_rows, degree_total):
    projected = jnp.einsum(
        "kl,snflr->snfkr", weight_rows, level_grid, preferred_element_type=jnp.float32
    )
    factor = 1.0 + degree_real[:, None] * (degree_real[:, None] + 1.0) * rate_rows[None, :] / (
        degree_total * degree_total
    )
    return (projected / factor[None, :, None, :, None]).astype(jnp.bfloat16)


def plain_shards(fourier_input_rows, legendre, slot_wave, to_modes, from_modes, mode_rate):
    wave_rows = lax.all_to_all(fourier_input_rows, "wide", split_axis=2, concat_axis=1, tiled=True)
    half_count = wave_rows.shape[1]
    slot_count = wave_rows.shape[2]
    field_count = wave_rows.shape[3]
    column_count = wave_rows.shape[4]
    degree_count = legendre.shape[1] * lax.axis_size(("lev", "fld"))
    weights = latitude_weights(half_count)[:, None, None, None]
    north_half = wave_rows[0].astype(jnp.float32)
    south_half = wave_rows[1].astype(jnp.float32)
    symmetric = (weights * (north_half + south_half)).astype(jnp.bfloat16)
    antisym = (weights * (north_half - south_half)).astype(jnp.bfloat16)
    paired = jnp.concatenate((symmetric, antisym), axis=3)

    def direct_rows(section, first_row):
        row_count = section.shape[1]
        degree = first_row + jnp.arange(row_count, dtype=jnp.int32)
        relative = degree[None, :] - slot_wave[:, None]
        product = jnp.einsum("snj,jsfc->snfc", section, paired, preferred_element_type=jnp.float32)
        is_even = (relative % 2 == 0)[:, :, None, None]
        is_live = (relative >= 0)[:, :, None, None]
        picked = jnp.where(is_even, product[..., :column_count], product[..., column_count:])
        return jnp.where(is_live, picked, jnp.zeros_like(picked))

    full_table = lax.all_gather(legendre, ("lev", "fld"), axis=1, tiled=True)
    block_rows = 128
    block_count = degree_count // block_rows

    def direct_step(block_index, buffer):
        first_row = block_index * block_rows
        section = lax.dynamic_slice_in_dim(full_table, first_row, block_rows, 1)
        result = direct_rows(section, first_row).astype(jnp.bfloat16)
        return lax.dynamic_update_slice_in_dim(buffer, result, first_row, 1)

    initial_raw = jnp.zeros((slot_count, degree_count, field_count, column_count), jnp.bfloat16)
    raw_spectral = lax.fori_loop(0, block_count, direct_step, initial_raw)
    own_levels = column_count // 2
    first_level = lax.axis_index("lev") * own_levels
    degree_real = jnp.arange(degree_count, dtype=jnp.float32)
    all_levels = lax.all_gather(raw_spectral, "lev", axis=3, tiled=True)
    level_count = all_levels.shape[3] // 2
    level_grid = all_levels.reshape(slot_count, degree_count, field_count, level_count, 2)
    weight_rows = lax.dynamic_slice_in_dim(to_modes, first_level, own_levels, 0)
    rate_rows = lax.dynamic_slice_in_dim(mode_rate, first_level, own_levels, 0)
    own_modes = project(level_grid, degree_real, weight_rows, rate_rows, degree_count).reshape(
        slot_count, degree_count, field_count, column_count
    )
    mode_values = lax.all_gather(own_modes, "lev", axis=3, tiled=True).reshape(
        slot_count, degree_count, field_count, level_count, 2
    )
    back_rows = lax.dynamic_slice_in_dim(from_modes, first_level, own_levels, 0)
    spectral = jnp.einsum(
        "lk,snfkr->snflr", back_rows, mode_values, preferred_element_type=jnp.float32
    )
    spectral = spectral.astype(jnp.bfloat16).reshape(
        slot_count, degree_count, field_count, column_count
    )

    def inverse_rows(running, section, first_row):
        row_count = section.shape[1]
        degree = first_row + jnp.arange(row_count, dtype=jnp.int32)
        relative = degree[None, :] - slot_wave[:, None]
        spec_rows = lax.dynamic_slice_in_dim(spectral, first_row, row_count, 1)
        even_mask = ((relative >= 0) & (relative % 2 == 0))[:, :, None, None]
        odd_mask = ((relative >= 0) & (relative % 2 == 1))[:, :, None, None]
        empty_rows = jnp.zeros_like(spec_rows)
        parity_split = jnp.concatenate(
            (
                jnp.where(even_mask, spec_rows, empty_rows),
                jnp.where(odd_mask, spec_rows, empty_rows),
            ),
            axis=3,
        )
        return running + jnp.einsum(
            "snj,snfc->jsfc", section, parity_split, preferred_element_type=jnp.float32
        )

    initial_sum = jnp.zeros((half_count, slot_count, field_count, 2 * column_count), jnp.float32)

    def inverse_step(block_index, running):
        first_row = block_index * block_rows
        section = lax.dynamic_slice_in_dim(full_table, first_row, block_rows, 1)
        return inverse_rows(running, section, first_row)

    running = lax.fori_loop(0, block_count, inverse_step, initial_sum)
    even_sum = running[..., :column_count]
    odd_sum = running[..., column_count:]
    fourier_wave = jnp.stack((even_sum + odd_sum, even_sum - odd_sum), axis=0).astype(jnp.bfloat16)
    fourier_out = lax.all_to_all(fourier_wave, "wide", split_axis=1, concat_axis=2, tiled=True)
    return (fourier_out, spectral)


def solution(mesh):
    in_specs = (
        P("ens", "wide", None, "fld", "lev"),
        P("wide", ("lev", "fld"), None),
        P("wide"),
        P(),
        P(),
        P(),
    )
    out_specs = (P("ens", "wide", None, "fld", "lev"), P(("ens", "wide"), None, "fld", "lev"))

    def body(fourier_input_rows, legendre, *rest):
        _, latitudes, slots, fields, lanes = fourier_input_rows.shape
        whole_tiles = (
            latitudes % (32 * PIECES) == 0
            and fields == 2
            and slots == mesh.shape["wide"] == 4
            and mesh.shape["ens"] == mesh.shape["lev"] == mesh.shape["fld"] == 2
            and lanes == 128
            and legendre.shape[1] % 64 == 0
            and legendre.shape[2] % 256 == 0
        )
        form = shards if whole_tiles else plain_shards
        return form(fourier_input_rows, legendre, *rest)

    return jax.shard_map(body, mesh=mesh, in_specs=in_specs, out_specs=out_specs, check_vma=False)
```

```python
import functools
import math

import jax
import jax.numpy as jnp
from jax import lax
from jax.experimental import pallas as pl
from jax.experimental.pallas import tpu as pltpu
from jax.sharding import PartitionSpec as P

VMEM_BYTES = 8 * 1024 * 1024


def latitude_weights(count):
    position = jnp.arange(count, dtype=jnp.float32)
    return jnp.sin(math.pi * (position + 0.5) / (2 * count))


def iota2(shape, dim):
    return lax.broadcasted_iota(jnp.int32, shape, dim)


def picks(condition):
    return jnp.where(condition, 1.0, 0.0).astype(jnp.bfloat16)


def dot32(a, b):
    return jnp.dot(a, b, preferred_element_type=jnp.float32)


PIECES = 5


def copy_pieces(source, target, semaphores):
    rows = target.shape[1] // PIECES
    return [
        pltpu.make_async_copy(
            source.at[:, pl.ds(i * rows, rows), :], target.at[:, pl.ds(i * rows, rows), :], semaphores.at[i]
        )
        for i in range(PIECES)
    ]


def call(body, out_shape, name, flops, scratch=(), scalars=1, after=(), out_hbm=False):
    smem = pl.BlockSpec(memory_space=pltpu.SMEM)
    vmem = pl.BlockSpec(memory_space=pltpu.VMEM)
    hbm = pl.BlockSpec(memory_space=pltpu.HBM)

    def run(*operands):
        used = len(operands)

        def kernel(*refs):
            body(*refs[:used], *refs[used + len(after) :])

        return pl.pallas_call(
            kernel,
            out_shape=out_shape,
            in_specs=[smem] * scalars
            + [vmem] * (used - scalars)
            + [pl.BlockSpec(memory_space=pl.ANY)] * len(after),
            out_specs=jax.tree.map(lambda _: hbm if out_hbm else vmem, out_shape),
            scratch_shapes=list(scratch),
            compiler_params=pltpu.CompilerParams(vmem_limit_bytes=VMEM_BYTES),
            cost_estimate=pl.CostEstimate(flops=flops, bytes_accessed=0, transcendentals=0),
            name=name,
        )(*operands, *after)

    return run


def split_body(slots, fields, block, meta_ref, rows_ref, weight_ref, *outs):
    latitudes = weight_ref.shape[0]
    group = slots * fields
    size = block * group
    out_row, in_row = iota2((size, size), 0), iota2((size, size), 1)
    pair = out_row // block
    slot = lax.rem(meta_ref[1] + pair // fields, slots)
    field = (meta_ref[2] + pair) % fields
    order = picks(in_row == (out_row % block) * group + slot * fields + field)
    for first in range(0, latitudes, block):
        north = rows_ref[0, first * group : first * group + size, :]
        south = rows_ref[1, first * group : first * group + size, :]
        sorted_rows = dot32(order, jnp.concatenate((north, south), axis=1))
        up, down = sorted_rows[:, :128], sorted_rows[:, 128:]
        weight = weight_ref[first : first + block, :]
        for odd, mixed in enumerate((up + down, up - down)):
            for i, out_ref in enumerate(outs):
                out_ref[odd, first : first + block, :] = (weight * mixed[i * block : i * block + block]).astype(
                    jnp.bfloat16
                )


def by_parity(meta_ref, rows):
    half = rows // 2
    out_row, in_row = iota2((rows, rows), 0), iota2((rows, rows), 1)
    odd = jnp.where(out_row < half, 0, 1)
    return picks(in_row == 2 * (out_row - odd * half) + (meta_ref[0] + odd) % 2)


def near_table_body(meta_ref, own_ref, beside_ref, even_ref, odd_ref):
    rows, columns = own_ref.shape
    half = rows // 2
    order = by_parity(meta_ref, rows)
    for g, table_ref in enumerate((own_ref, beside_ref)):
        at = slice(g * half, g * half + half)
        for first in range(0, columns, 256):
            lanes = slice(first, first + 256)
            result = dot32(order, table_ref[:, lanes]).astype(jnp.bfloat16)
            even_ref[at, lanes] = result[:half]
            odd_ref[at, lanes] = result[half:]


def far_table_body(meta_ref, first_ref, second_ref, out_ref, whole):
    half, columns = first_ref.shape
    for ens, ref in ((meta_ref[4], first_ref), (1 - meta_ref[4], second_ref)):
        whole[pl.ds(pl.multiple_of(ens * half, half), half), :] = ref[...]
    order = by_parity(meta_ref, 2 * half)
    for first in range(0, columns, 256):
        lanes = slice(first, first + 256)
        out_ref[:, lanes] = dot32(order, whole[:, lanes]).astype(jnp.bfloat16)


def modes_body(sizes, degree_total, meta_ref, to_ref, from_ref, rate_ref, in_ref, out_ref, scale_ref):
    levels = to_ref.shape[0]
    wide = 2 * levels
    own = levels // 2
    lane, row = iota2((levels, wide), 1), iota2((levels, wide), 0)
    owner = lax.rem(meta_ref[2] + lane // levels, 2)
    spread = picks(row == owner * own + lane % levels // 2)
    plain = picks(row == lane % levels)
    old, new = iota2((wide, wide), 0), iota2((wide, wide), 1)

    def turned(first, matrix, last):
        half = lax.dot_general(first, matrix, (((0,), (1,)), ((), ())), preferred_element_type=jnp.float32)
        return dot32(half.astype(jnp.bfloat16), last)

    same = old % 2 == new // levels
    in_ref[...] = jnp.where(same, turned(spread, to_ref[...], plain), 0.0).astype(jnp.bfloat16)
    same = old // levels == new % 2
    out_ref[...] = jnp.where(same, turned(plain, from_ref[...], spread), 0.0).astype(jnp.bfloat16)
    wide, levs, flds = sizes
    rows = degree_total // (2 * levs * flds)
    for odd in range(2):
        for d in range(levs):
            for g in range(flds):
                block = lax.rem(meta_ref[2] + d, levs) * flds + lax.rem(meta_ref[3] + g, flds)
                degree = block * (2 * rows) + 2 * iota2((rows, 1), 0) + (meta_ref[0] + odd) % 2
                real = degree.astype(jnp.float32)
                factor = 1.0 + real * (real + 1.0) * rate_ref[...] / (degree_total * degree_total)
                at = ((d * 2 + odd) * flds + g) * rows
                scale_ref[at : at + rows, :] = jnp.where(degree >= meta_ref[0], 1.0 / factor, 0.0)


def transform(tables, data, scale_ref, in_ref, out_ref, own_ref, other_ref):
    lanes = own_ref.shape[1]
    rows = own_ref.shape[0] // 2
    for odd in range(2):
        at = slice(odd * rows, odd * rows + rows)
        raw = dot32(tables[odd], data[odd]).astype(jnp.bfloat16)
        scale = jnp.concatenate([scale_ref[at, :]] * 2, axis=1)
        modes = (dot32(raw, in_ref[...]) * scale).astype(jnp.bfloat16)
        spectral = dot32(modes, out_ref[...]).astype(jnp.bfloat16)
        own_ref[at, :] = spectral[:, :lanes]
        other_ref[at, :] = spectral[:, lanes:]


def near_body(wide, meta_ref, in_ref, out_ref, scale_ref, even_ref, odd_ref, *refs):
    parts, (own_ref, other_ref, data_ref) = refs[:-3], refs[-3:]
    latitudes, lanes = parts[0].shape[1:]
    for shift in range(wide):
        owner = lax.rem(meta_ref[1] - shift + wide, wide)
        at = pl.ds(pl.multiple_of(owner * latitudes, latitudes), latitudes)
        for d in range(2):
            data_ref[:, at, d * lanes : d * lanes + lanes] = parts[shift * 2 + d][...]
    scale = scale_ref.at[: scale_ref.shape[0] // 2]
    transform((even_ref[...], odd_ref[...]), data_ref, scale, in_ref, out_ref, own_ref, other_ref)


def far_body(in_ref, out_ref, scale_ref, first_ref, second_ref, data_ref, own_ref, other_ref):
    rows = first_ref.shape[0] // 2
    tables = [
        jnp.concatenate([ref[odd * rows : odd * rows + rows, :] for ref in (first_ref, second_ref)], axis=0)
        for odd in range(2)
    ]
    scale = scale_ref.at[scale_ref.shape[0] // 2 :]
    transform(tables, data_ref, scale, in_ref, out_ref, own_ref, other_ref)


def inverse_body(wide, meta_ref, *refs):
    parts, near, far, outs, total = refs[:4], refs[4:6], refs[6:8], refs[8:-1], refs[-1]
    latitudes, lanes = outs[0].shape[1:]
    rows = parts[0].shape[0] // 2
    spectral = [
        jnp.concatenate(
            [
                jnp.concatenate([ref[odd * rows : odd * rows + rows, :] for ref in pair], axis=1)
                for pair in (parts[:2], parts[2:])
            ],
            axis=0,
        )
        for odd in range(2)
    ]
    for first in range(0, total.shape[1], 256):
        chunk = slice(first, first + 256)
        sums = []
        for odd in range(2):
            at = slice(odd * (rows // 2), (odd + 1) * (rows // 2))
            table = jnp.concatenate([near[odd][:, chunk]] + [ref[at, chunk] for ref in far], axis=0)
            sums.append(lax.dot_general(
                table, spectral[odd], (((0,), (0,)), ((), ())), preferred_element_type=jnp.float32
            ))
        total[0, chunk, :] = (sums[0] + sums[1]).astype(jnp.bfloat16)
        total[1, chunk, :] = (sums[0] - sums[1]).astype(jnp.bfloat16)
    for shift in range(wide):
        owner = lax.rem(meta_ref[1] + shift, wide)
        at = pl.ds(pl.multiple_of(owner * latitudes, latitudes), latitudes)
        for d in range(2):
            outs[shift * 2 + d][...] = total[:, at, d * lanes : d * lanes + lanes]


def join_body(slots, block, meta_ref, *refs):
    parts, out_hbm, out_ref, semaphores = refs[:-3], *refs[-3:]
    copies = copy_pieces(out_ref, out_hbm, semaphores)
    latitudes, lanes = parts[0].shape[1:]
    fields = 2
    group = slots * fields
    size = block * group
    out_row, in_row = iota2((size, size), 0), iota2((size, size), 1)
    place = out_row % group
    shift = lax.rem(meta_ref[1] - place // fields + slots, slots)
    order = picks(in_row == (shift * fields + (place + meta_ref[2]) % fields) * block + out_row // group)
    for first in range(0, latitudes, block):
        at = slice(first, first + block)
        stacked = [jnp.concatenate([part[half, at, :] for part in parts], axis=0) for half in range(2)]
        result = dot32(order, jnp.concatenate(stacked, axis=1)).astype(jnp.bfloat16)
        for half in range(2):
            out_ref[half, first * group : first * group + size, :] = result[:, half * lanes : half * lanes + lanes]
        done = first + block
        if done * PIECES % latitudes == 0:
            copies[done * PIECES // latitudes - 1].start()
    for copy in copies:
        copy.wait()


def rows_body(sizes, block, meta_ref, *refs):
    wide, levs, flds = sizes
    own_refs, other_refs, out_ref = refs[:2], refs[2:4], refs[4]
    rows = own_refs[0].shape[0] // (2 * flds)
    fields = 2
    group = 2 * fields
    size = block * group
    out_row, in_row = iota2((size, size), 0), iota2((size, size), 1)
    place = out_row % group
    odd = (place // fields + meta_ref[0] % 2) % 2
    order = picks(in_row == (odd * fields + (place + meta_ref[2]) % fields) * block + out_row // group)
    for d in range(levs):
        for g in range(flds):
            index = lax.rem(meta_ref[2] + d, levs) * flds + lax.rem(meta_ref[3] + g, flds)
            for first in range(0, rows, block):
                stacked = jnp.concatenate(
                    [
                        ref[(odd * flds + g) * rows + first : (odd * flds + g) * rows + first + block, :]
                        for odd in range(2)
                        for ref in (own_refs[d], other_refs[1 - d])
                    ],
                    axis=0,
                )
                start = pl.multiple_of(index * (rows * group), rows * group) + first * group
                out_ref[pl.ds(start, size), :] = dot32(order, stacked).astype(jnp.bfloat16)


def shards(fourier_input_rows, legendre, slot_wave, to_modes, from_modes, mode_rate):
    wide, levs, flds = (lax.axis_size(axis) for axis in ("wide", "lev", "fld"))
    sizes = (wide, levs, flds)
    _, latitudes, slots, fields, lanes = fourier_input_rows.shape
    _, shard_rows, half_count = legendre.shape
    degree_count = shard_rows * levs * flds
    group = slots * fields
    columns = fields * lanes
    block = 256 // group
    levels = to_modes.shape[0]
    bf16 = jnp.bfloat16

    def shape(*dims):
        return jax.ShapeDtypeStruct(dims, bf16)

    def shifted(value, axis, count, step):
        return lax.ppermute(value, axis, [(i, (i + step) % count) for i in range(count)])

    def over_lev(value):
        return shifted(value, "lev", levs, 1)

    def beside(value):
        return shifted(value, "fld", flds, 1)

    def moved(value, k, d):
        pairs = [(w * levs + l, (w + k) % wide * levs + (l + d) % levs) for w in range(wide) for l in range(levs)]
        return lax.ppermute(value, ("wide", "lev"), pairs)

    def behind(value, *others):
        return lax.optimization_barrier((value, *others))

    wide_at, lev_at, fld_at = (lax.axis_index(axis) for axis in ("wide", "lev", "fld"))
    meta = jnp.stack((slot_wave[0], wide_at, lev_at, fld_at, lax.axis_index("ens"))).astype(jnp.int32)
    position = (wide_at * latitudes + jnp.arange(latitudes, dtype=jnp.int32)).astype(jnp.float32)
    weights = jnp.sin(math.pi * (position + 0.5) / (2 * half_count))
    weights = jnp.broadcast_to(weights[:, None], (latitudes, lanes))
    move_flops = 8 * group * latitudes * 128 * 256
    transform_flops = 2 * degree_count * half_count * columns

    table_beside = beside(legendre[0])
    blocks = call(
        functools.partial(split_body, slots, fields, block), (shape(2, latitudes, lanes),) * (wide * levs),
        "split_hemispheres", move_flops,
    )(meta, fourier_input_rows.reshape(2, latitudes * group, lanes), weights)
    table_beside, *blocks = behind(table_beside, *blocks)
    *matrices, scale = call(
        functools.partial(modes_body, sizes, degree_count),
        (shape(2 * levels, 2 * levels),) * 2 + (jax.ShapeDtypeStruct((degree_count, levels), jnp.float32),),
        "spread_modes", 12 * levels * levels * levels, after=(blocks[0],),
    )(meta, to_modes, from_modes, mode_rate[None, :])
    near = call(
        near_table_body, (shape(shard_rows, half_count),) * 2, "split_table",
        4 * shard_rows * shard_rows * half_count, after=(scale,),
    )(meta, legendre[0], table_beside)

    def exchanged(blocks, ahead, leads):
        arrived = {(0, 0): blocks[0]}
        for k, d in ((2, 0), (1, 0), (3, 0), (0, 1)):
            arrived[k, d] = moved(blocks[k * levs + d], k, d)
        for k, steps in leads:
            value, *lead = behind(blocks[k * levs + 1], *(arrived[step] for step in steps), *ahead)
            arrived |= dict(zip(steps, lead))
            arrived[k, 1] = moved(value, k, 1)
        return arrived

    def listed(arrived):
        return [arrived[k, d] for k in range(wide) for d in range(levs)]

    arrived = exchanged(blocks, (near[0], scale), ((2, [(0, 1)]), (1, [(1, 0)]), (3, [(3, 0)])))
    half_shard = shard_rows // 2
    own_table, _ = behind(legendre[0], blocks[0])
    first = over_lev(lax.dynamic_slice_in_dim(own_table, lax.axis_index("ens") * half_shard, half_shard, 0))
    steps = [(1, 0), (2, 0), (3, 0), (0, 1)]
    first, *ahead = behind(first, *(arrived[step] for step in steps))
    arrived |= dict(zip(steps, ahead))
    second = shifted(first, "ens", 2, 1)
    far = call(
        far_table_body, shape(shard_rows, half_count), "split_table", 2 * shard_rows * shard_rows * half_count,
        scratch=[pltpu.VMEM((shard_rows, half_count), bf16)],
    )(meta, first, second)
    steps = [(1, 1), (2, 1), (3, 1)]
    far, *ahead = behind(far, *(arrived[step] for step in steps))
    arrived |= dict(zip(steps, ahead))
    far = [far, beside(far)]

    half_rows = degree_count // 2
    *near_spectral, data = call(
        functools.partial(near_body, wide), (shape(half_rows, lanes),) * 2 + (shape(2, half_count, columns),),
        "direct_legendre_and_solve", transform_flops // 2,
    )(meta, *matrices, scale, *near, *listed(arrived))
    far_spectral = call(
        far_body, (shape(half_rows, lanes),) * 2, "direct_legendre_and_solve", transform_flops // 2, scalars=0,
    )(*matrices, scale, *far, data)
    spectral = (near_spectral, far_spectral)
    grid = call(
        functools.partial(inverse_body, wide), (shape(2, latitudes, lanes),) * (wide * levs),
        "inverse_legendre", transform_flops, scratch=[pltpu.VMEM((2, half_count, columns), bf16)],
    )(meta, *near_spectral, *far_spectral, *near, *far)
    arrived = exchanged(grid, (), ((2, [(2, 0)]), (1, [(1, 0), (0, 1)]), (3, [(3, 0)])))
    result = listed(arrived)
    spectral_rows = call(
        functools.partial(rows_body, sizes, 32), shape(degree_count * fields, lanes), "order_spectral", move_flops,
    )(meta, *(own for own, _ in spectral), *(over_lev(other) for _, other in spectral))
    fourier_rows = call(
        functools.partial(join_body, slots, 256 // group), shape(2, latitudes * group, lanes),
        "join_hemispheres", move_flops, out_hbm=True,
        scratch=[pltpu.VMEM((2, latitudes * group, lanes), bf16), pltpu.SemaphoreType.DMA((PIECES,))],
    )(meta, *result)
    return (
        fourier_rows.reshape(2, latitudes, slots, fields, lanes),
        spectral_rows.reshape(1, degree_count, fields, lanes),
    )


def project(level_grid, degree_real, weight_rows, rate_rows, degree_total):
    projected = jnp.einsum(
        "kl,snflr->snfkr", weight_rows, level_grid, preferred_element_type=jnp.float32
    )
    factor = 1.0 + degree_real[:, None] * (degree_real[:, None] + 1.0) * rate_rows[None, :] / (
        degree_total * degree_total
    )
    return (projected / factor[None, :, None, :, None]).astype(jnp.bfloat16)


def plain_shards(fourier_input_rows, legendre, slot_wave, to_modes, from_modes, mode_rate):
    wave_rows = lax.all_to_all(fourier_input_rows, "wide", split_axis=2, concat_axis=1, tiled=True)
    half_count = wave_rows.shape[1]
    slot_count = wave_rows.shape[2]
    field_count = wave_rows.shape[3]
    column_count = wave_rows.shape[4]
    degree_count = legendre.shape[1] * lax.axis_size(("lev", "fld"))
    weights = latitude_weights(half_count)[:, None, None, None]
    north_half = wave_rows[0].astype(jnp.float32)
    south_half = wave_rows[1].astype(jnp.float32)
    symmetric = (weights * (north_half + south_half)).astype(jnp.bfloat16)
    antisym = (weights * (north_half - south_half)).astype(jnp.bfloat16)
    paired = jnp.concatenate((symmetric, antisym), axis=3)

    def direct_rows(section, first_row):
        row_count = section.shape[1]
        degree = first_row + jnp.arange(row_count, dtype=jnp.int32)
        relative = degree[None, :] - slot_wave[:, None]
        product = jnp.einsum("snj,jsfc->snfc", section, paired, preferred_element_type=jnp.float32)
        is_even = (relative % 2 == 0)[:, :, None, None]
        is_live = (relative >= 0)[:, :, None, None]
        picked = jnp.where(is_even, product[..., :column_count], product[..., column_count:])
        return jnp.where(is_live, picked, jnp.zeros_like(picked))

    full_table = lax.all_gather(legendre, ("lev", "fld"), axis=1, tiled=True)
    block_rows = 128
    block_count = degree_count // block_rows

    def direct_step(block_index, buffer):
        first_row = block_index * block_rows
        section = lax.dynamic_slice_in_dim(full_table, first_row, block_rows, 1)
        result = direct_rows(section, first_row).astype(jnp.bfloat16)
        return lax.dynamic_update_slice_in_dim(buffer, result, first_row, 1)

    initial_raw = jnp.zeros((slot_count, degree_count, field_count, column_count), jnp.bfloat16)
    raw_spectral = lax.fori_loop(0, block_count, direct_step, initial_raw)
    own_levels = column_count // 2
    first_level = lax.axis_index("lev") * own_levels
    degree_real = jnp.arange(degree_count, dtype=jnp.float32)
    all_levels = lax.all_gather(raw_spectral, "lev", axis=3, tiled=True)
    level_count = all_levels.shape[3] // 2
    level_grid = all_levels.reshape(slot_count, degree_count, field_count, level_count, 2)
    weight_rows = lax.dynamic_slice_in_dim(to_modes, first_level, own_levels, 0)
    rate_rows = lax.dynamic_slice_in_dim(mode_rate, first_level, own_levels, 0)
    own_modes = project(level_grid, degree_real, weight_rows, rate_rows, degree_count).reshape(
        slot_count, degree_count, field_count, column_count
    )
    mode_values = lax.all_gather(own_modes, "lev", axis=3, tiled=True).reshape(
        slot_count, degree_count, field_count, level_count, 2
    )
    back_rows = lax.dynamic_slice_in_dim(from_modes, first_level, own_levels, 0)
    spectral = jnp.einsum(
        "lk,snfkr->snflr", back_rows, mode_values, preferred_element_type=jnp.float32
    )
    spectral = spectral.astype(jnp.bfloat16).reshape(
        slot_count, degree_count, field_count, column_count
    )

    def inverse_rows(running, section, first_row):
        row_count = section.shape[1]
        degree = first_row + jnp.arange(row_count, dtype=jnp.int32)
        relative = degree[None, :] - slot_wave[:, None]
        spec_rows = lax.dynamic_slice_in_dim(spectral, first_row, row_count, 1)
        even_mask = ((relative >= 0) & (relative % 2 == 0))[:, :, None, None]
        odd_mask = ((relative >= 0) & (relative % 2 == 1))[:, :, None, None]
        empty_rows = jnp.zeros_like(spec_rows)
        parity_split = jnp.concatenate(
            (
                jnp.where(even_mask, spec_rows, empty_rows),
                jnp.where(odd_mask, spec_rows, empty_rows),
            ),
            axis=3,
        )
        return running + jnp.einsum(
            "snj,snfc->jsfc", section, parity_split, preferred_element_type=jnp.float32
        )

    initial_sum = jnp.zeros((half_count, slot_count, field_count, 2 * column_count), jnp.float32)

    def inverse_step(block_index, running):
        first_row = block_index * block_rows
        section = lax.dynamic_slice_in_dim(full_table, first_row, block_rows, 1)
        return inverse_rows(running, section, first_row)

    running = lax.fori_loop(0, block_count, inverse_step, initial_sum)
    even_sum = running[..., :column_count]
    odd_sum = running[..., column_count:]
    fourier_wave = jnp.stack((even_sum + odd_sum, even_sum - odd_sum), axis=0).astype(jnp.bfloat16)
    fourier_out = lax.all_to_all(fourier_wave, "wide", split_axis=1, concat_axis=2, tiled=True)
    return (fourier_out, spectral)


def solution(mesh):
    in_specs = (
        P("ens", "wide", None, "fld", "lev"),
        P("wide", ("lev", "fld"), None),
        P("wide"),
        P(),
        P(),
        P(),
    )
    out_specs = (P("ens", "wide", None, "fld", "lev"), P(("ens", "wide"), None, "fld", "lev"))

    def body(fourier_input_rows, legendre, *rest):
        _, latitudes, slots, fields, lanes = fourier_input_rows.shape
        whole_tiles = (
            latitudes % (32 * PIECES) == 0
            and fields == 2
            and slots == mesh.shape["wide"] == 4
            and mesh.shape["ens"] == mesh.shape["lev"] == mesh.shape["fld"] == 2
            and lanes == 128
            and legendre.shape[1] % 64 == 0
            and legendre.shape[2] % 256 == 0
        )
        form = shards if whole_tiles else plain_shards
        return form(fourier_input_rows, legendre, *rest)

    return jax.shard_map(body, mesh=mesh, in_specs=in_specs, out_specs=out_specs, check_vma=False)
```

```python
import functools
import math

import jax
import jax.numpy as jnp
from jax import lax
from jax.experimental import pallas as pl
from jax.experimental.pallas import tpu as pltpu
from jax.sharding import PartitionSpec as P

VMEM_BYTES = 8 * 1024 * 1024


def latitude_weights(count):
    position = jnp.arange(count, dtype=jnp.float32)
    return jnp.sin(math.pi * (position + 0.5) / (2 * count))


def iota2(shape, dim):
    return lax.broadcasted_iota(jnp.int32, shape, dim)


def picks(condition):
    return jnp.where(condition, 1.0, 0.0).astype(jnp.bfloat16)


def dot32(a, b):
    return jnp.dot(a, b, preferred_element_type=jnp.float32)


PIECES = 5


def copy_pieces(source, target, semaphores):
    rows = target.shape[1] // PIECES
    return [
        pltpu.make_async_copy(
            source.at[:, pl.ds(i * rows, rows), :], target.at[:, pl.ds(i * rows, rows), :], semaphores.at[i]
        )
        for i in range(PIECES)
    ]


def call(body, out_shape, name, flops, scratch=(), scalars=1, after=(), out_hbm=False):
    smem = pl.BlockSpec(memory_space=pltpu.SMEM)
    vmem = pl.BlockSpec(memory_space=pltpu.VMEM)
    hbm = pl.BlockSpec(memory_space=pltpu.HBM)

    def run(*operands):
        used = len(operands)

        def kernel(*refs):
            body(*refs[:used], *refs[used + len(after) :])

        return pl.pallas_call(
            kernel,
            out_shape=out_shape,
            in_specs=[smem] * scalars
            + [vmem] * (used - scalars)
            + [pl.BlockSpec(memory_space=pl.ANY)] * len(after),
            out_specs=jax.tree.map(lambda _: hbm if out_hbm else vmem, out_shape),
            scratch_shapes=list(scratch),
            compiler_params=pltpu.CompilerParams(vmem_limit_bytes=VMEM_BYTES),
            cost_estimate=pl.CostEstimate(flops=flops, bytes_accessed=0, transcendentals=0),
            name=name,
        )(*operands, *after)

    return run


def split_body(slots, fields, block, meta_ref, rows_ref, weight_ref, *outs):
    latitudes = weight_ref.shape[0]
    group = slots * fields
    size = block * group
    out_row, in_row = iota2((size, size), 0), iota2((size, size), 1)
    pair = out_row // block
    slot = lax.rem(meta_ref[1] + pair // fields, slots)
    field = (meta_ref[2] + pair) % fields
    order = picks(in_row == (out_row % block) * group + slot * fields + field)
    for first in range(0, latitudes, block):
        north = rows_ref[0, first * group : first * group + size, :]
        south = rows_ref[1, first * group : first * group + size, :]
        sorted_rows = dot32(order, jnp.concatenate((north, south), axis=1))
        up, down = sorted_rows[:, :128], sorted_rows[:, 128:]
        weight = weight_ref[first : first + block, :]
        for odd, mixed in enumerate((up + down, up - down)):
            for i, out_ref in enumerate(outs):
                out_ref[odd, first : first + block, :] = (weight * mixed[i * block : i * block + block]).astype(
                    jnp.bfloat16
                )


def by_parity(meta_ref, rows):
    half = rows // 2
    out_row, in_row = iota2((rows, rows), 0), iota2((rows, rows), 1)
    odd = jnp.where(out_row < half, 0, 1)
    return picks(in_row == 2 * (out_row - odd * half) + (meta_ref[0] + odd) % 2)


def near_table_body(meta_ref, own_ref, beside_ref, even_ref, odd_ref):
    rows, columns = own_ref.shape
    half = rows // 2
    order = by_parity(meta_ref, rows)
    for g, table_ref in enumerate((own_ref, beside_ref)):
        at = slice(g * half, g * half + half)
        for first in range(0, columns, 256):
            lanes = slice(first, first + 256)
            result = dot32(order, table_ref[:, lanes]).astype(jnp.bfloat16)
            even_ref[at, lanes] = result[:half]
            odd_ref[at, lanes] = result[half:]


def far_table_body(meta_ref, first_ref, second_ref, out_ref, whole):
    half, columns = first_ref.shape
    for ens, ref in ((meta_ref[4], first_ref), (1 - meta_ref[4], second_ref)):
        whole[pl.ds(pl.multiple_of(ens * half, half), half), :] = ref[...]
    order = by_parity(meta_ref, 2 * half)
    for first in range(0, columns, 256):
        lanes = slice(first, first + 256)
        out_ref[:, lanes] = dot32(order, whole[:, lanes]).astype(jnp.bfloat16)


def modes_body(sizes, degree_total, meta_ref, to_ref, from_ref, rate_ref, in_ref, out_ref, scale_ref):
    levels = to_ref.shape[0]
    wide = 2 * levels
    own = levels // 2
    lane, row = iota2((levels, wide), 1), iota2((levels, wide), 0)
    owner = lax.rem(meta_ref[2] + lane // levels, 2)
    spread = picks(row == owner * own + lane % levels // 2)
    plain = picks(row == lane % levels)
    old, new = iota2((wide, wide), 0), iota2((wide, wide), 1)

    def turned(first, matrix, last):
        half = lax.dot_general(first, matrix, (((0,), (1,)), ((), ())), preferred_element_type=jnp.float32)
        return dot32(half.astype(jnp.bfloat16), last)

    same = old % 2 == new // levels
    in_ref[...] = jnp.where(same, turned(spread, to_ref[...], plain), 0.0).astype(jnp.bfloat16)
    same = old // levels == new % 2
    out_ref[...] = jnp.where(same, turned(plain, from_ref[...], spread), 0.0).astype(jnp.bfloat16)
    wide, levs, flds = sizes
    rows = degree_total // (2 * levs * flds)
    for odd in range(2):
        for d in range(levs):
            for g in range(flds):
                block = lax.rem(meta_ref[2] + d, levs) * flds + lax.rem(meta_ref[3] + g, flds)
                degree = block * (2 * rows) + 2 * iota2((rows, 1), 0) + (meta_ref[0] + odd) % 2
                real = degree.astype(jnp.float32)
                factor = 1.0 + real * (real + 1.0) * rate_ref[...] / (degree_total * degree_total)
                at = ((d * 2 + odd) * flds + g) * rows
                scale_ref[at : at + rows, :] = jnp.where(degree >= meta_ref[0], 1.0 / factor, 0.0)


def transform(tables, data, scale_ref, in_ref, out_ref, own_ref, other_ref):
    lanes = own_ref.shape[1]
    rows = own_ref.shape[0] // 2
    for odd in range(2):
        at = slice(odd * rows, odd * rows + rows)
        raw = dot32(tables[odd], data[odd]).astype(jnp.bfloat16)
        scale = jnp.concatenate([scale_ref[at, :]] * 2, axis=1)
        modes = (dot32(raw, in_ref[...]) * scale).astype(jnp.bfloat16)
        spectral = dot32(modes, out_ref[...]).astype(jnp.bfloat16)
        own_ref[at, :] = spectral[:, :lanes]
        other_ref[at, :] = spectral[:, lanes:]


def near_body(wide, meta_ref, in_ref, out_ref, scale_ref, even_ref, odd_ref, *refs):
    parts, (own_ref, other_ref, data_ref) = refs[:-3], refs[-3:]
    latitudes, lanes = parts[0].shape[1:]
    for shift in range(wide):
        owner = lax.rem(meta_ref[1] - shift + wide, wide)
        at = pl.ds(pl.multiple_of(owner * latitudes, latitudes), latitudes)
        for d in range(2):
            data_ref[:, at, d * lanes : d * lanes + lanes] = parts[shift * 2 + d][...]
    scale = scale_ref.at[: scale_ref.shape[0] // 2]
    transform((even_ref[...], odd_ref[...]), data_ref, scale, in_ref, out_ref, own_ref, other_ref)


def far_body(in_ref, out_ref, scale_ref, first_ref, second_ref, data_ref, own_ref, other_ref):
    rows = first_ref.shape[0] // 2
    tables = [
        jnp.concatenate([ref[odd * rows : odd * rows + rows, :] for ref in (first_ref, second_ref)], axis=0)
        for odd in range(2)
    ]
    scale = scale_ref.at[scale_ref.shape[0] // 2 :]
    transform(tables, data_ref, scale, in_ref, out_ref, own_ref, other_ref)


def inverse_body(wide, meta_ref, *refs):
    parts, near, far, outs, total = refs[:4], refs[4:6], refs[6:8], refs[8:-1], refs[-1]
    latitudes, lanes = outs[0].shape[1:]
    rows = parts[0].shape[0] // 2
    spectral = [
        jnp.concatenate(
            [
                jnp.concatenate([ref[odd * rows : odd * rows + rows, :] for ref in pair], axis=1)
                for pair in (parts[:2], parts[2:])
            ],
            axis=0,
        )
        for odd in range(2)
    ]
    for first in range(0, total.shape[1], 256):
        chunk = slice(first, first + 256)
        sums = []
        for odd in range(2):
            at = slice(odd * (rows // 2), (odd + 1) * (rows // 2))
            table = jnp.concatenate([near[odd][:, chunk]] + [ref[at, chunk] for ref in far], axis=0)
            sums.append(lax.dot_general(
                table, spectral[odd], (((0,), (0,)), ((), ())), preferred_element_type=jnp.float32
            ))
        total[0, chunk, :] = (sums[0] + sums[1]).astype(jnp.bfloat16)
        total[1, chunk, :] = (sums[0] - sums[1]).astype(jnp.bfloat16)
    for shift in range(wide):
        owner = lax.rem(meta_ref[1] + shift, wide)
        at = pl.ds(pl.multiple_of(owner * latitudes, latitudes), latitudes)
        for d in range(2):
            outs[shift * 2 + d][...] = total[:, at, d * lanes : d * lanes + lanes]


def join_body(slots, block, meta_ref, *refs):
    parts, out_hbm, out_ref, semaphores = refs[:-3], *refs[-3:]
    copies = copy_pieces(out_ref, out_hbm, semaphores)
    latitudes, lanes = parts[0].shape[1:]
    fields = 2
    group = slots * fields
    size = block * group
    out_row, in_row = iota2((size, size), 0), iota2((size, size), 1)
    place = out_row % group
    shift = lax.rem(meta_ref[1] - place // fields + slots, slots)
    order = picks(in_row == (shift * fields + (place + meta_ref[2]) % fields) * block + out_row // group)
    for first in range(0, latitudes, block):
        at = slice(first, first + block)
        stacked = [jnp.concatenate([part[half, at, :] for part in parts], axis=0) for half in range(2)]
        result = dot32(order, jnp.concatenate(stacked, axis=1)).astype(jnp.bfloat16)
        for half in range(2):
            out_ref[half, first * group : first * group + size, :] = result[:, half * lanes : half * lanes + lanes]
        done = first + block
        if done * PIECES % latitudes == 0:
            copies[done * PIECES // latitudes - 1].start()
    for copy in copies:
        copy.wait()


def rows_body(sizes, block, meta_ref, *refs):
    wide, levs, flds = sizes
    own_refs, other_refs, out_ref = refs[:2], refs[2:4], refs[4]
    rows = own_refs[0].shape[0] // (2 * flds)
    fields = 2
    group = 2 * fields
    size = block * group
    out_row, in_row = iota2((size, size), 0), iota2((size, size), 1)
    place = out_row % group
    odd = (place // fields + meta_ref[0] % 2) % 2
    order = picks(in_row == (odd * fields + (place + meta_ref[2]) % fields) * block + out_row // group)
    for d in range(levs):
        for g in range(flds):
            index = lax.rem(meta_ref[2] + d, levs) * flds + lax.rem(meta_ref[3] + g, flds)
            for first in range(0, rows, block):
                stacked = jnp.concatenate(
                    [
                        ref[(odd * flds + g) * rows + first : (odd * flds + g) * rows + first + block, :]
                        for odd in range(2)
                        for ref in (own_refs[d], other_refs[1 - d])
                    ],
                    axis=0,
                )
                start = pl.multiple_of(index * (rows * group), rows * group) + first * group
                out_ref[pl.ds(start, size), :] = dot32(order, stacked).astype(jnp.bfloat16)


def shards(fourier_input_rows, legendre, slot_wave, to_modes, from_modes, mode_rate):
    wide, levs, flds = (lax.axis_size(axis) for axis in ("wide", "lev", "fld"))
    sizes = (wide, levs, flds)
    _, latitudes, slots, fields, lanes = fourier_input_rows.shape
    _, shard_rows, half_count = legendre.shape
    degree_count = shard_rows * levs * flds
    group = slots * fields
    columns = fields * lanes
    block = 256 // group
    levels = to_modes.shape[0]
    bf16 = jnp.bfloat16

    def shape(*dims):
        return jax.ShapeDtypeStruct(dims, bf16)

    def shifted(value, axis, count, step):
        return lax.ppermute(value, axis, [(i, (i + step) % count) for i in range(count)])

    def over_lev(value):
        return shifted(value, "lev", levs, 1)

    def beside(value):
        return shifted(value, "fld", flds, 1)

    def moved(value, k, d):
        pairs = [(w * levs + l, (w + k) % wide * levs + (l + d) % levs) for w in range(wide) for l in range(levs)]
        return lax.ppermute(value, ("wide", "lev"), pairs)

    def behind(value, *others):
        return lax.optimization_barrier((value, *others))

    wide_at, lev_at, fld_at = (lax.axis_index(axis) for axis in ("wide", "lev", "fld"))
    meta = jnp.stack((slot_wave[0], wide_at, lev_at, fld_at, lax.axis_index("ens"))).astype(jnp.int32)
    position = (wide_at * latitudes + jnp.arange(latitudes, dtype=jnp.int32)).astype(jnp.float32)
    weights = jnp.sin(math.pi * (position + 0.5) / (2 * half_count))
    weights = jnp.broadcast_to(weights[:, None], (latitudes, lanes))
    move_flops = 8 * group * latitudes * 128 * 256
    transform_flops = 2 * degree_count * half_count * columns

    table_beside = beside(legendre[0])
    blocks = call(
        functools.partial(split_body, slots, fields, block), (shape(2, latitudes, lanes),) * (wide * levs),
        "split_hemispheres", move_flops,
    )(meta, fourier_input_rows.reshape(2, latitudes * group, lanes), weights)
    table_beside, *blocks = behind(table_beside, *blocks)
    *matrices, scale = call(
        functools.partial(modes_body, sizes, degree_count),
        (shape(2 * levels, 2 * levels),) * 2 + (jax.ShapeDtypeStruct((degree_count, levels), jnp.float32),),
        "spread_modes", 12 * levels * levels * levels, after=(blocks[0],),
    )(meta, to_modes, from_modes, mode_rate[None, :])
    near = call(
        near_table_body, (shape(shard_rows, half_count),) * 2, "split_table",
        4 * shard_rows * shard_rows * half_count, after=(scale,),
    )(meta, legendre[0], table_beside)

    def exchanged(blocks, ahead, leads):
        arrived = {(0, 0): blocks[0]}
        for k, d in ((2, 0), (1, 0), (3, 0), (0, 1)):
            arrived[k, d] = moved(blocks[k * levs + d], k, d)
        for k, first in zip((2, 1, 3), leads):
            value, arrived[first], *_ = behind(blocks[k * levs + 1], arrived[first], *ahead)
            arrived[k, 1] = moved(value, k, 1)
        return arrived

    def listed(arrived):
        return [arrived[k, d] for k in range(wide) for d in range(levs)]

    arrived = exchanged(blocks, (near[0], scale), ((0, 1), (2, 0), (3, 0)))
    half_shard = shard_rows // 2
    own_table, _ = behind(legendre[0], blocks[0])
    first = over_lev(lax.dynamic_slice_in_dim(own_table, lax.axis_index("ens") * half_shard, half_shard, 0))
    steps = [(2, 0), (3, 0), (0, 1)]
    first, *ahead = behind(first, *(arrived[step] for step in steps))
    arrived |= dict(zip(steps, ahead))
    second = shifted(first, "ens", 2, 1)
    far = call(
        far_table_body, shape(shard_rows, half_count), "split_table", 2 * shard_rows * shard_rows * half_count,
        scratch=[pltpu.VMEM((shard_rows, half_count), bf16)],
    )(meta, first, second)
    steps = [(1, 0), (1, 1), (2, 1), (3, 1)]
    far, *ahead = behind(far, *(arrived[step] for step in steps))
    arrived |= dict(zip(steps, ahead))
    far = [far, beside(far)]

    half_rows = degree_count // 2
    *near_spectral, data = call(
        functools.partial(near_body, wide), (shape(half_rows, lanes),) * 2 + (shape(2, half_count, columns),),
        "direct_legendre_and_solve", transform_flops // 2,
    )(meta, *matrices, scale, *near, *listed(arrived))
    far_spectral = call(
        far_body, (shape(half_rows, lanes),) * 2, "direct_legendre_and_solve", transform_flops // 2, scalars=0,
    )(*matrices, scale, *far, data)
    spectral = (near_spectral, far_spectral)
    grid = call(
        functools.partial(inverse_body, wide), (shape(2, latitudes, lanes),) * (wide * levs),
        "inverse_legendre", transform_flops, scratch=[pltpu.VMEM((2, half_count, columns), bf16)],
    )(meta, *near_spectral, *far_spectral, *near, *far)
    arrived = exchanged(grid, (), ((0, 1), (1, 0), (3, 0)))
    result = listed(arrived)
    spectral_rows = call(
        functools.partial(rows_body, sizes, 32), shape(degree_count * fields, lanes), "order_spectral", move_flops,
    )(meta, *(own for own, _ in spectral), *(over_lev(other) for _, other in spectral))
    fourier_rows = call(
        functools.partial(join_body, slots, 256 // group), shape(2, latitudes * group, lanes),
        "join_hemispheres", move_flops, out_hbm=True,
        scratch=[pltpu.VMEM((2, latitudes * group, lanes), bf16), pltpu.SemaphoreType.DMA((PIECES,))],
    )(meta, *result)
    return (
        fourier_rows.reshape(2, latitudes, slots, fields, lanes),
        spectral_rows.reshape(1, degree_count, fields, lanes),
    )


def project(level_grid, degree_real, weight_rows, rate_rows, degree_total):
    projected = jnp.einsum(
        "kl,snflr->snfkr", weight_rows, level_grid, preferred_element_type=jnp.float32
    )
    factor = 1.0 + degree_real[:, None] * (degree_real[:, None] + 1.0) * rate_rows[None, :] / (
        degree_total * degree_total
    )
    return (projected / factor[None, :, None, :, None]).astype(jnp.bfloat16)


def plain_shards(fourier_input_rows, legendre, slot_wave, to_modes, from_modes, mode_rate):
    wave_rows = lax.all_to_all(fourier_input_rows, "wide", split_axis=2, concat_axis=1, tiled=True)
    half_count = wave_rows.shape[1]
    slot_count = wave_rows.shape[2]
    field_count = wave_rows.shape[3]
    column_count = wave_rows.shape[4]
    degree_count = legendre.shape[1] * lax.axis_size(("lev", "fld"))
    weights = latitude_weights(half_count)[:, None, None, None]
    north_half = wave_rows[0].astype(jnp.float32)
    south_half = wave_rows[1].astype(jnp.float32)
    symmetric = (weights * (north_half + south_half)).astype(jnp.bfloat16)
    antisym = (weights * (north_half - south_half)).astype(jnp.bfloat16)
    paired = jnp.concatenate((symmetric, antisym), axis=3)

    def direct_rows(section, first_row):
        row_count = section.shape[1]
        degree = first_row + jnp.arange(row_count, dtype=jnp.int32)
        relative = degree[None, :] - slot_wave[:, None]
        product = jnp.einsum("snj,jsfc->snfc", section, paired, preferred_element_type=jnp.float32)
        is_even = (relative % 2 == 0)[:, :, None, None]
        is_live = (relative >= 0)[:, :, None, None]
        picked = jnp.where(is_even, product[..., :column_count], product[..., column_count:])
        return jnp.where(is_live, picked, jnp.zeros_like(picked))

    full_table = lax.all_gather(legendre, ("lev", "fld"), axis=1, tiled=True)
    block_rows = 128
    block_count = degree_count // block_rows

    def direct_step(block_index, buffer):
        first_row = block_index * block_rows
        section = lax.dynamic_slice_in_dim(full_table, first_row, block_rows, 1)
        result = direct_rows(section, first_row).astype(jnp.bfloat16)
        return lax.dynamic_update_slice_in_dim(buffer, result, first_row, 1)

    initial_raw = jnp.zeros((slot_count, degree_count, field_count, column_count), jnp.bfloat16)
    raw_spectral = lax.fori_loop(0, block_count, direct_step, initial_raw)
    own_levels = column_count // 2
    first_level = lax.axis_index("lev") * own_levels
    degree_real = jnp.arange(degree_count, dtype=jnp.float32)
    all_levels = lax.all_gather(raw_spectral, "lev", axis=3, tiled=True)
    level_count = all_levels.shape[3] // 2
    level_grid = all_levels.reshape(slot_count, degree_count, field_count, level_count, 2)
    weight_rows = lax.dynamic_slice_in_dim(to_modes, first_level, own_levels, 0)
    rate_rows = lax.dynamic_slice_in_dim(mode_rate, first_level, own_levels, 0)
    own_modes = project(level_grid, degree_real, weight_rows, rate_rows, degree_count).reshape(
        slot_count, degree_count, field_count, column_count
    )
    mode_values = lax.all_gather(own_modes, "lev", axis=3, tiled=True).reshape(
        slot_count, degree_count, field_count, level_count, 2
    )
    back_rows = lax.dynamic_slice_in_dim(from_modes, first_level, own_levels, 0)
    spectral = jnp.einsum(
        "lk,snfkr->snflr", back_rows, mode_values, preferred_element_type=jnp.float32
    )
    spectral = spectral.astype(jnp.bfloat16).reshape(
        slot_count, degree_count, field_count, column_count
    )

    def inverse_rows(running, section, first_row):
        row_count = section.shape[1]
        degree = first_row + jnp.arange(row_count, dtype=jnp.int32)
        relative = degree[None, :] - slot_wave[:, None]
        spec_rows = lax.dynamic_slice_in_dim(spectral, first_row, row_count, 1)
        even_mask = ((relative >= 0) & (relative % 2 == 0))[:, :, None, None]
        odd_mask = ((relative >= 0) & (relative % 2 == 1))[:, :, None, None]
        empty_rows = jnp.zeros_like(spec_rows)
        parity_split = jnp.concatenate(
            (
                jnp.where(even_mask, spec_rows, empty_rows),
                jnp.where(odd_mask, spec_rows, empty_rows),
            ),
            axis=3,
        )
        return running + jnp.einsum(
            "snj,snfc->jsfc", section, parity_split, preferred_element_type=jnp.float32
        )

    initial_sum = jnp.zeros((half_count, slot_count, field_count, 2 * column_count), jnp.float32)

    def inverse_step(block_index, running):
        first_row = block_index * block_rows
        section = lax.dynamic_slice_in_dim(full_table, first_row, block_rows, 1)
        return inverse_rows(running, section, first_row)

    running = lax.fori_loop(0, block_count, inverse_step, initial_sum)
    even_sum = running[..., :column_count]
    odd_sum = running[..., column_count:]
    fourier_wave = jnp.stack((even_sum + odd_sum, even_sum - odd_sum), axis=0).astype(jnp.bfloat16)
    fourier_out = lax.all_to_all(fourier_wave, "wide", split_axis=1, concat_axis=2, tiled=True)
    return (fourier_out, spectral)


def solution(mesh):
    in_specs = (
        P("ens", "wide", None, "fld", "lev"),
        P("wide", ("lev", "fld"), None),
        P("wide"),
        P(),
        P(),
        P(),
    )
    out_specs = (P("ens", "wide", None, "fld", "lev"), P(("ens", "wide"), None, "fld", "lev"))

    def body(fourier_input_rows, legendre, *rest):
        _, latitudes, slots, fields, lanes = fourier_input_rows.shape
        whole_tiles = (
            latitudes % (32 * PIECES) == 0
            and fields == 2
            and slots == mesh.shape["wide"] == 4
            and mesh.shape["ens"] == mesh.shape["lev"] == mesh.shape["fld"] == 2
            and lanes == 128
            and legendre.shape[1] % 64 == 0
            and legendre.shape[2] % 256 == 0
        )
        form = shards if whole_tiles else plain_shards
        return form(fourier_input_rows, legendre, *rest)

    return jax.shard_map(body, mesh=mesh, in_specs=in_specs, out_specs=out_specs, check_vma=False)
```

```python
import functools
import math

import jax
import jax.numpy as jnp
from jax import lax
from jax.experimental import pallas as pl
from jax.experimental.pallas import tpu as pltpu
from jax.sharding import PartitionSpec as P

VMEM_BYTES = 8 * 1024 * 1024


def latitude_weights(count):
    position = jnp.arange(count, dtype=jnp.float32)
    return jnp.sin(math.pi * (position + 0.5) / (2 * count))


def iota2(shape, dim):
    return lax.broadcasted_iota(jnp.int32, shape, dim)


def picks(condition):
    return jnp.where(condition, 1.0, 0.0).astype(jnp.bfloat16)


def dot32(a, b):
    return jnp.dot(a, b, preferred_element_type=jnp.float32)


PIECES = 5


def copy_pieces(source, target, semaphores):
    rows = target.shape[1] // PIECES
    return [
        pltpu.make_async_copy(
            source.at[:, pl.ds(i * rows, rows), :], target.at[:, pl.ds(i * rows, rows), :], semaphores.at[i]
        )
        for i in range(PIECES)
    ]


def call(body, out_shape, name, flops, scratch=(), scalars=1, after=(), out_hbm=False):
    smem = pl.BlockSpec(memory_space=pltpu.SMEM)
    vmem = pl.BlockSpec(memory_space=pltpu.VMEM)
    hbm = pl.BlockSpec(memory_space=pltpu.HBM)

    def run(*operands):
        used = len(operands)

        def kernel(*refs):
            body(*refs[:used], *refs[used + len(after) :])

        return pl.pallas_call(
            kernel,
            out_shape=out_shape,
            in_specs=[smem] * scalars
            + [vmem] * (used - scalars)
            + [pl.BlockSpec(memory_space=pl.ANY)] * len(after),
            out_specs=jax.tree.map(lambda _: hbm if out_hbm else vmem, out_shape),
            scratch_shapes=list(scratch),
            compiler_params=pltpu.CompilerParams(vmem_limit_bytes=VMEM_BYTES),
            cost_estimate=pl.CostEstimate(flops=flops, bytes_accessed=0, transcendentals=0),
            name=name,
        )(*operands, *after)

    return run


def split_body(slots, fields, block, meta_ref, rows_ref, weight_ref, *outs):
    latitudes = weight_ref.shape[0]
    group = slots * fields
    size = block * group
    out_row, in_row = iota2((size, size), 0), iota2((size, size), 1)
    pair = out_row // block
    slot = lax.rem(meta_ref[1] + pair // fields, slots)
    field = (meta_ref[2] + pair) % fields
    order = picks(in_row == (out_row % block) * group + slot * fields + field)
    for first in range(0, latitudes, block):
        north = rows_ref[0, first * group : first * group + size, :]
        south = rows_ref[1, first * group : first * group + size, :]
        sorted_rows = dot32(order, jnp.concatenate((north, south), axis=1))
        up, down = sorted_rows[:, :128], sorted_rows[:, 128:]
        weight = weight_ref[first : first + block, :]
        for odd, mixed in enumerate((up + down, up - down)):
            for i, out_ref in enumerate(outs):
                out_ref[odd, first : first + block, :] = (weight * mixed[i * block : i * block + block]).astype(
                    jnp.bfloat16
                )


def by_parity(meta_ref, rows):
    half = rows // 2
    out_row, in_row = iota2((rows, rows), 0), iota2((rows, rows), 1)
    odd = jnp.where(out_row < half, 0, 1)
    return picks(in_row == 2 * (out_row - odd * half) + (meta_ref[0] + odd) % 2)


def near_table_body(meta_ref, own_ref, beside_ref, even_ref, odd_ref):
    rows, columns = own_ref.shape
    half = rows // 2
    order = by_parity(meta_ref, rows)
    for g, table_ref in enumerate((own_ref, beside_ref)):
        at = slice(g * half, g * half + half)
        for first in range(0, columns, 256):
            lanes = slice(first, first + 256)
            result = dot32(order, table_ref[:, lanes]).astype(jnp.bfloat16)
            even_ref[at, lanes] = result[:half]
            odd_ref[at, lanes] = result[half:]


def far_table_body(meta_ref, first_ref, second_ref, out_ref, whole):
    half, columns = first_ref.shape
    for ens, ref in ((meta_ref[4], first_ref), (1 - meta_ref[4], second_ref)):
        whole[pl.ds(pl.multiple_of(ens * half, half), half), :] = ref[...]
    order = by_parity(meta_ref, 2 * half)
    for first in range(0, columns, 256):
        lanes = slice(first, first + 256)
        out_ref[:, lanes] = dot32(order, whole[:, lanes]).astype(jnp.bfloat16)


def modes_body(sizes, degree_total, meta_ref, to_ref, from_ref, rate_ref, in_ref, out_ref, scale_ref):
    levels = to_ref.shape[0]
    wide = 2 * levels
    own = levels // 2
    lane, row = iota2((levels, wide), 1), iota2((levels, wide), 0)
    owner = lax.rem(meta_ref[2] + lane // levels, 2)
    spread = picks(row == owner * own + lane % levels // 2)
    plain = picks(row == lane % levels)
    old, new = iota2((wide, wide), 0), iota2((wide, wide), 1)

    def turned(first, matrix, last):
        half = lax.dot_general(first, matrix, (((0,), (1,)), ((), ())), preferred_element_type=jnp.float32)
        return dot32(half.astype(jnp.bfloat16), last)

    same = old % 2 == new // levels
    in_ref[...] = jnp.where(same, turned(spread, to_ref[...], plain), 0.0).astype(jnp.bfloat16)
    same = old // levels == new % 2
    out_ref[...] = jnp.where(same, turned(plain, from_ref[...], spread), 0.0).astype(jnp.bfloat16)
    wide, levs, flds = sizes
    rows = degree_total // (2 * levs * flds)
    for odd in range(2):
        for d in range(levs):
            for g in range(flds):
                block = lax.rem(meta_ref[2] + d, levs) * flds + lax.rem(meta_ref[3] + g, flds)
                degree = block * (2 * rows) + 2 * iota2((rows, 1), 0) + (meta_ref[0] + odd) % 2
                real = degree.astype(jnp.float32)
                factor = 1.0 + real * (real + 1.0) * rate_ref[...] / (degree_total * degree_total)
                at = ((d * 2 + odd) * flds + g) * rows
                scale_ref[at : at + rows, :] = jnp.where(degree >= meta_ref[0], 1.0 / factor, 0.0)


def transform(tables, data, scale_ref, in_ref, out_ref, own_ref, other_ref):
    lanes = own_ref.shape[1]
    rows = own_ref.shape[0] // 2
    for odd in range(2):
        at = slice(odd * rows, odd * rows + rows)
        columns = jnp.concatenate([ref[odd] for ref in data], axis=1)
        raw = dot32(tables[odd], columns).astype(jnp.bfloat16)
        scale = jnp.concatenate([scale_ref[at, :]] * 2, axis=1)
        modes = (dot32(raw, in_ref[...]) * scale).astype(jnp.bfloat16)
        spectral = dot32(modes, out_ref[...]).astype(jnp.bfloat16)
        own_ref[at, :] = spectral[:, :lanes]
        other_ref[at, :] = spectral[:, lanes:]


def gather(wide, meta_ref, *refs):
    parts, data_ref = refs[:-1], refs[-1]
    latitudes = parts[0].shape[1]
    for shift in range(wide):
        owner = lax.rem(meta_ref[1] - shift + wide, wide)
        at = pl.ds(pl.multiple_of(owner * latitudes, latitudes), latitudes)
        data_ref[:, at, :] = parts[shift][...]


def near_body(wide, meta_ref, in_ref, out_ref, scale_ref, even_ref, odd_ref, gathered_ref, *refs):
    parts, (own_ref, other_ref, data_ref) = refs[:-3], refs[-3:]
    gather(wide, meta_ref, *parts, data_ref)
    scale = scale_ref.at[: scale_ref.shape[0] // 2]
    transform((even_ref[...], odd_ref[...]), (gathered_ref, data_ref), scale, in_ref, out_ref, own_ref, other_ref)


def far_body(in_ref, out_ref, scale_ref, first_ref, second_ref, gathered_ref, data_ref, own_ref, other_ref):
    rows = first_ref.shape[0] // 2
    tables = [
        jnp.concatenate([ref[odd * rows : odd * rows + rows, :] for ref in (first_ref, second_ref)], axis=0)
        for odd in range(2)
    ]
    scale = scale_ref.at[scale_ref.shape[0] // 2 :]
    transform(tables, (gathered_ref, data_ref), scale, in_ref, out_ref, own_ref, other_ref)


def inverse_body(wide, meta_ref, *refs):
    parts, near, far, outs, total = refs[:4], refs[4:6], refs[6:8], refs[8:-1], refs[-1]
    latitudes, lanes = outs[0].shape[1:]
    rows = parts[0].shape[0] // 2
    spectral = [
        jnp.concatenate(
            [
                jnp.concatenate([ref[odd * rows : odd * rows + rows, :] for ref in pair], axis=1)
                for pair in (parts[:2], parts[2:])
            ],
            axis=0,
        )
        for odd in range(2)
    ]
    for first in range(0, total.shape[1], 256):
        chunk = slice(first, first + 256)
        sums = []
        for odd in range(2):
            at = slice(odd * (rows // 2), (odd + 1) * (rows // 2))
            table = jnp.concatenate([near[odd][:, chunk]] + [ref[at, chunk] for ref in far], axis=0)
            sums.append(lax.dot_general(
                table, spectral[odd], (((0,), (0,)), ((), ())), preferred_element_type=jnp.float32
            ))
        total[0, chunk, :] = (sums[0] + sums[1]).astype(jnp.bfloat16)
        total[1, chunk, :] = (sums[0] - sums[1]).astype(jnp.bfloat16)
    for shift in range(wide):
        owner = lax.rem(meta_ref[1] + shift, wide)
        at = pl.ds(pl.multiple_of(owner * latitudes, latitudes), latitudes)
        for d in range(2):
            outs[shift * 2 + d][...] = total[:, at, d * lanes : d * lanes + lanes]


def join_body(slots, block, meta_ref, *refs):
    parts, out_hbm, out_ref, semaphores = refs[:-3], *refs[-3:]
    copies = copy_pieces(out_ref, out_hbm, semaphores)
    latitudes, lanes = parts[0].shape[1:]
    fields = 2
    group = slots * fields
    size = block * group
    out_row, in_row = iota2((size, size), 0), iota2((size, size), 1)
    place = out_row % group
    shift = lax.rem(meta_ref[1] - place // fields + slots, slots)
    order = picks(in_row == (shift * fields + (place + meta_ref[2]) % fields) * block + out_row // group)
    for first in range(0, latitudes, block):
        at = slice(first, first + block)
        stacked = [jnp.concatenate([part[half, at, :] for part in parts], axis=0) for half in range(2)]
        result = dot32(order, jnp.concatenate(stacked, axis=1)).astype(jnp.bfloat16)
        for half in range(2):
            out_ref[half, first * group : first * group + size, :] = result[:, half * lanes : half * lanes + lanes]
        done = first + block
        if done * PIECES % latitudes == 0:
            copies[done * PIECES // latitudes - 1].start()
    for copy in copies:
        copy.wait()


def rows_body(sizes, block, meta_ref, *refs):
    wide, levs, flds = sizes
    own_refs, other_refs, out_ref = refs[:2], refs[2:4], refs[4]
    rows = own_refs[0].shape[0] // (2 * flds)
    fields = 2
    group = 2 * fields
    size = block * group
    out_row, in_row = iota2((size, size), 0), iota2((size, size), 1)
    place = out_row % group
    odd = (place // fields + meta_ref[0] % 2) % 2
    order = picks(in_row == (odd * fields + (place + meta_ref[2]) % fields) * block + out_row // group)
    for d in range(levs):
        for g in range(flds):
            index = lax.rem(meta_ref[2] + d, levs) * flds + lax.rem(meta_ref[3] + g, flds)
            for first in range(0, rows, block):
                stacked = jnp.concatenate(
                    [
                        ref[(odd * flds + g) * rows + first : (odd * flds + g) * rows + first + block, :]
                        for odd in range(2)
                        for ref in (own_refs[d], other_refs[1 - d])
                    ],
                    axis=0,
                )
                start = pl.multiple_of(index * (rows * group), rows * group) + first * group
                out_ref[pl.ds(start, size), :] = dot32(order, stacked).astype(jnp.bfloat16)


def shards(fourier_input_rows, legendre, slot_wave, to_modes, from_modes, mode_rate):
    wide, levs, flds = (lax.axis_size(axis) for axis in ("wide", "lev", "fld"))
    sizes = (wide, levs, flds)
    _, latitudes, slots, fields, lanes = fourier_input_rows.shape
    _, shard_rows, half_count = legendre.shape
    degree_count = shard_rows * levs * flds
    group = slots * fields
    columns = fields * lanes
    block = 256 // group
    levels = to_modes.shape[0]
    bf16 = jnp.bfloat16

    def shape(*dims):
        return jax.ShapeDtypeStruct(dims, bf16)

    def shifted(value, axis, count, step):
        return lax.ppermute(value, axis, [(i, (i + step) % count) for i in range(count)])

    def over_lev(value):
        return shifted(value, "lev", levs, 1)

    def beside(value):
        return shifted(value, "fld", flds, 1)

    def moved(value, k, d):
        pairs = [(w * levs + l, (w + k) % wide * levs + (l + d) % levs) for w in range(wide) for l in range(levs)]
        return lax.ppermute(value, ("wide", "lev"), pairs)

    def behind(value, *others):
        return lax.optimization_barrier((value, *others))

    wide_at, lev_at, fld_at = (lax.axis_index(axis) for axis in ("wide", "lev", "fld"))
    meta = jnp.stack((slot_wave[0], wide_at, lev_at, fld_at, lax.axis_index("ens"))).astype(jnp.int32)
    position = (wide_at * latitudes + jnp.arange(latitudes, dtype=jnp.int32)).astype(jnp.float32)
    weights = jnp.sin(math.pi * (position + 0.5) / (2 * half_count))
    weights = jnp.broadcast_to(weights[:, None], (latitudes, lanes))
    move_flops = 8 * group * latitudes * 128 * 256
    transform_flops = 2 * degree_count * half_count * columns

    table_beside = beside(legendre[0])
    blocks = call(
        functools.partial(split_body, slots, fields, block), (shape(2, latitudes, lanes),) * (wide * levs),
        "split_hemispheres", move_flops,
    )(meta, fourier_input_rows.reshape(2, latitudes * group, lanes), weights)
    table_beside, *blocks = behind(table_beside, *blocks)
    *matrices, scale = call(
        functools.partial(modes_body, sizes, degree_count),
        (shape(2 * levels, 2 * levels),) * 2 + (jax.ShapeDtypeStruct((degree_count, levels), jnp.float32),),
        "spread_modes", 12 * levels * levels * levels, after=(blocks[0],),
    )(meta, to_modes, from_modes, mode_rate[None, :])
    near = call(
        near_table_body, (shape(shard_rows, half_count),) * 2, "split_table",
        4 * shard_rows * shard_rows * half_count, after=(scale,),
    )(meta, legendre[0], table_beside)

    def exchanged(blocks, ahead):
        arrived = {(0, 0): blocks[0]}
        for k, d in ((2, 0), (1, 0), (3, 0), (0, 1)):
            arrived[k, d] = moved(blocks[k * levs + d], k, d)
        for k, first in ((2, (0, 1)), (1, (1, 0)), (3, (3, 0))):
            value, arrived[first], *_ = behind(blocks[k * levs + 1], arrived[first], *ahead)
            arrived[k, 1] = moved(value, k, 1)
        return arrived

    def listed(arrived):
        return [arrived[k, d] for k in range(wide) for d in range(levs)]

    arrived = exchanged(blocks, (near[0], scale))
    half_shard = shard_rows // 2
    own_table, _ = behind(legendre[0], blocks[0])
    first = over_lev(lax.dynamic_slice_in_dim(own_table, lax.axis_index("ens") * half_shard, half_shard, 0))
    steps = [(1, 0), (2, 0), (3, 0), (0, 1)]
    first, *ahead = behind(first, *(arrived[step] for step in steps))
    arrived |= dict(zip(steps, ahead))
    second = shifted(first, "ens", 2, 1)
    far = call(
        far_table_body, shape(shard_rows, half_count), "split_table", 2 * shard_rows * shard_rows * half_count,
        scratch=[pltpu.VMEM((shard_rows, half_count), bf16)],
    )(meta, first, second)
    steps = [(1, 1), (2, 1), (3, 1)]
    gathered = call(
        functools.partial(gather, wide), shape(2, half_count, lanes), "gather_latitudes", 0,
    )(meta, *(arrived[k, 0] for k in range(wide)))
    far, gathered, *ahead = behind(far, gathered, *(arrived[step] for step in steps))
    arrived |= dict(zip(steps, ahead))
    far = [far, beside(far)]

    half_rows = degree_count // 2
    *near_spectral, data = call(
        functools.partial(near_body, wide), (shape(half_rows, lanes),) * 2 + (shape(2, half_count, lanes),),
        "direct_legendre_and_solve", transform_flops // 2,
    )(meta, *matrices, scale, *near, gathered, *(arrived[k, 1] for k in range(wide)))
    far_spectral = call(
        far_body, (shape(half_rows, lanes),) * 2, "direct_legendre_and_solve", transform_flops // 2, scalars=0,
    )(*matrices, scale, *far, gathered, data)
    spectral = (near_spectral, far_spectral)
    grid = call(
        functools.partial(inverse_body, wide), (shape(2, latitudes, lanes),) * (wide * levs),
        "inverse_legendre", transform_flops, scratch=[pltpu.VMEM((2, half_count, columns), bf16)],
    )(meta, *near_spectral, *far_spectral, *near, *far)
    arrived = exchanged(grid, ())
    result = listed(arrived)
    spectral_rows = call(
        functools.partial(rows_body, sizes, 32), shape(degree_count * fields, lanes), "order_spectral", move_flops,
    )(meta, *(own for own, _ in spectral), *(over_lev(other) for _, other in spectral))
    fourier_rows = call(
        functools.partial(join_body, slots, 256 // group), shape(2, latitudes * group, lanes),
        "join_hemispheres", move_flops, out_hbm=True,
        scratch=[pltpu.VMEM((2, latitudes * group, lanes), bf16), pltpu.SemaphoreType.DMA((PIECES,))],
    )(meta, *result)
    return (
        fourier_rows.reshape(2, latitudes, slots, fields, lanes),
        spectral_rows.reshape(1, degree_count, fields, lanes),
    )


def project(level_grid, degree_real, weight_rows, rate_rows, degree_total):
    projected = jnp.einsum(
        "kl,snflr->snfkr", weight_rows, level_grid, preferred_element_type=jnp.float32
    )
    factor = 1.0 + degree_real[:, None] * (degree_real[:, None] + 1.0) * rate_rows[None, :] / (
        degree_total * degree_total
    )
    return (projected / factor[None, :, None, :, None]).astype(jnp.bfloat16)


def plain_shards(fourier_input_rows, legendre, slot_wave, to_modes, from_modes, mode_rate):
    wave_rows = lax.all_to_all(fourier_input_rows, "wide", split_axis=2, concat_axis=1, tiled=True)
    half_count = wave_rows.shape[1]
    slot_count = wave_rows.shape[2]
    field_count = wave_rows.shape[3]
    column_count = wave_rows.shape[4]
    degree_count = legendre.shape[1] * lax.axis_size(("lev", "fld"))
    weights = latitude_weights(half_count)[:, None, None, None]
    north_half = wave_rows[0].astype(jnp.float32)
    south_half = wave_rows[1].astype(jnp.float32)
    symmetric = (weights * (north_half + south_half)).astype(jnp.bfloat16)
    antisym = (weights * (north_half - south_half)).astype(jnp.bfloat16)
    paired = jnp.concatenate((symmetric, antisym), axis=3)

    def direct_rows(section, first_row):
        row_count = section.shape[1]
        degree = first_row + jnp.arange(row_count, dtype=jnp.int32)
        relative = degree[None, :] - slot_wave[:, None]
        product = jnp.einsum("snj,jsfc->snfc", section, paired, preferred_element_type=jnp.float32)
        is_even = (relative % 2 == 0)[:, :, None, None]
        is_live = (relative >= 0)[:, :, None, None]
        picked = jnp.where(is_even, product[..., :column_count], product[..., column_count:])
        return jnp.where(is_live, picked, jnp.zeros_like(picked))

    full_table = lax.all_gather(legendre, ("lev", "fld"), axis=1, tiled=True)
    block_rows = 128
    block_count = degree_count // block_rows

    def direct_step(block_index, buffer):
        first_row = block_index * block_rows
        section = lax.dynamic_slice_in_dim(full_table, first_row, block_rows, 1)
        result = direct_rows(section, first_row).astype(jnp.bfloat16)
        return lax.dynamic_update_slice_in_dim(buffer, result, first_row, 1)

    initial_raw = jnp.zeros((slot_count, degree_count, field_count, column_count), jnp.bfloat16)
    raw_spectral = lax.fori_loop(0, block_count, direct_step, initial_raw)
    own_levels = column_count // 2
    first_level = lax.axis_index("lev") * own_levels
    degree_real = jnp.arange(degree_count, dtype=jnp.float32)
    all_levels = lax.all_gather(raw_spectral, "lev", axis=3, tiled=True)
    level_count = all_levels.shape[3] // 2
    level_grid = all_levels.reshape(slot_count, degree_count, field_count, level_count, 2)
    weight_rows = lax.dynamic_slice_in_dim(to_modes, first_level, own_levels, 0)
    rate_rows = lax.dynamic_slice_in_dim(mode_rate, first_level, own_levels, 0)
    own_modes = project(level_grid, degree_real, weight_rows, rate_rows, degree_count).reshape(
        slot_count, degree_count, field_count, column_count
    )
    mode_values = lax.all_gather(own_modes, "lev", axis=3, tiled=True).reshape(
        slot_count, degree_count, field_count, level_count, 2
    )
    back_rows = lax.dynamic_slice_in_dim(from_modes, first_level, own_levels, 0)
    spectral = jnp.einsum(
        "lk,snfkr->snflr", back_rows, mode_values, preferred_element_type=jnp.float32
    )
    spectral = spectral.astype(jnp.bfloat16).reshape(
        slot_count, degree_count, field_count, column_count
    )

    def inverse_rows(running, section, first_row):
        row_count = section.shape[1]
        degree = first_row + jnp.arange(row_count, dtype=jnp.int32)
        relative = degree[None, :] - slot_wave[:, None]
        spec_rows = lax.dynamic_slice_in_dim(spectral, first_row, row_count, 1)
        even_mask = ((relative >= 0) & (relative % 2 == 0))[:, :, None, None]
        odd_mask = ((relative >= 0) & (relative % 2 == 1))[:, :, None, None]
        empty_rows = jnp.zeros_like(spec_rows)
        parity_split = jnp.concatenate(
            (
                jnp.where(even_mask, spec_rows, empty_rows),
                jnp.where(odd_mask, spec_rows, empty_rows),
            ),
            axis=3,
        )
        return running + jnp.einsum(
            "snj,snfc->jsfc", section, parity_split, preferred_element_type=jnp.float32
        )

    initial_sum = jnp.zeros((half_count, slot_count, field_count, 2 * column_count), jnp.float32)

    def inverse_step(block_index, running):
        first_row = block_index * block_rows
        section = lax.dynamic_slice_in_dim(full_table, first_row, block_rows, 1)
        return inverse_rows(running, section, first_row)

    running = lax.fori_loop(0, block_count, inverse_step, initial_sum)
    even_sum = running[..., :column_count]
    odd_sum = running[..., column_count:]
    fourier_wave = jnp.stack((even_sum + odd_sum, even_sum - odd_sum), axis=0).astype(jnp.bfloat16)
    fourier_out = lax.all_to_all(fourier_wave, "wide", split_axis=1, concat_axis=2, tiled=True)
    return (fourier_out, spectral)


def solution(mesh):
    in_specs = (
        P("ens", "wide", None, "fld", "lev"),
        P("wide", ("lev", "fld"), None),
        P("wide"),
        P(),
        P(),
        P(),
    )
    out_specs = (P("ens", "wide", None, "fld", "lev"), P(("ens", "wide"), None, "fld", "lev"))

    def body(fourier_input_rows, legendre, *rest):
        _, latitudes, slots, fields, lanes = fourier_input_rows.shape
        whole_tiles = (
            latitudes % (32 * PIECES) == 0
            and fields == 2
            and slots == mesh.shape["wide"] == 4
            and mesh.shape["ens"] == mesh.shape["lev"] == mesh.shape["fld"] == 2
            and lanes == 128
            and legendre.shape[1] % 64 == 0
            and legendre.shape[2] % 256 == 0
        )
        form = shards if whole_tiles else plain_shards
        return form(fourier_input_rows, legendre, *rest)

    return jax.shard_map(body, mesh=mesh, in_specs=in_specs, out_specs=out_specs, check_vma=False)
```
